32 devices in a mesh: leaf: 8 (over y, x, core), sub: 4 (over z).
Axes of the slice: x: 2, y: 2, z: 4, core: 2. Of those that a mesh axis runs over, the one named last changes fastest.
Arguments:
- charges: bfloat16 [32, 524288], P(None, ('leaf', 'sub')), may hold values from -0.59765625 to 0.59765625
- points: float32 [3, 524288], P(None, ('leaf', 'sub')), as said below
- basis: bfloat16 [4096, 64, 128], P(('leaf', 'sub')), may hold values from -0.5 to 0.5
- transfer: float32 [2, 64, 64], replicated, may hold values from -0.625 to 0.625
- near_list: int32 [4096, 8], P(('leaf', 'sub')), may hold values from -1 to 4095, as said below
- coupling_list: int32 [4096, 8], P(('leaf', 'sub')), may hold values from -1 to 4095, as said below
Outputs:
- potential: float32 [32, 524288], P(None, ('leaf', 'sub'))
The draws below stay inside these ranges and needn't reach their ends.
Inputs may be any that keep to these rules, and one draw needn't show every extreme that they name: `near_list`: every live slot of row i holds a leaf j with |j - i| <= 64 whose unit box touches the box of leaf i (the box corners differ by at most 1 in every coordinate); slot 0 holds i itself, slot 1 the leaf whose index differs from i in the lowest bit, slot 2 the leaf i - 4 (i + 4 where i < 4), slot 3 the leaf i + 4 (i - 4 where i + 4 >= 4096); other slots may repeat leaves; empty slots hold -1 and come after the live ones; at least four slots of every row are live, and how many are live varies from device to device. `coupling_list`: every live slot of row i holds a leaf j with 1 <= |j - i| <= 64 whose unit box does not touch the box of leaf i (the box corners differ by 2 or more in some coordinate); slot 1 holds a leaf exactly 64 away from i; other slots may repeat leaves; empty slots hold -1 and come after the live ones; at least two slots of every row are live, and how many are live varies from device to device. The points of leaf c lie in the unit box whose lower corner is (c % 2, (c // 2) % 2, c // 4).
All inputs are finite; a program needn't handle non-finite values.
Results may differ from the reference program's by a relative error of at most 0.00065.
The reference program's roundings to bfloat16 on the way (of `near_tile` and `down_leaf`) count: a program that leaves them out, or rounds other values in their place, can miss the bound.
Values may be sent and summed in bfloat16 or wider, within the bound.
No kernel may reach another device: no remote copies, remote signals or barrier semaphores. Data moves between devices by JAX's collectives and lax.ppermute only.
A program may use at most 128 MiB of HBM per device.

```python
import math
import jax
import jax.numpy as jnp
from jax import lax

P_SIZE = 128
K = 64
R = 32
LD = 128
NEAR = 8
COUP = 8
NBAND = 64
LEAVES = 4096
POINTS = 524288


def axis_extent(axis_id):
    return 2 if axis_id < 2 else LEAVES // 4


def box_coords(leaf_ids):
    return [leaf_ids % 2, leaf_ids // 2 % 2, leaf_ids // 4]


def box_index(coords):
    return coords[0] + 2 * coords[1] + 4 * coords[2]


def live_counts(key, slots, least):
    leaf_ids = jnp.arange(LEAVES, dtype=jnp.int32)
    key_cap, key_count = jax.random.split(key, 2)
    owners = LEAVES // LD
    caps = jax.random.randint(key_cap, (owners,), least, slots + 1)
    caps = caps.at[0].set(least)
    owner_of = leaf_ids // LD
    counts = jnp.minimum(jax.random.randint(key_count, (LEAVES,), least, slots + 1), caps[owner_of])
    return jnp.where(owner_of == owners - 1, slots, counts)


def draw_near_list(key, part):
    key = jax.random.fold_in(key, 21)
    key_step, key_count = jax.random.split(key, 2)
    leaf_ids = jnp.arange(LEAVES, dtype=jnp.int32)[:, None]
    column = jnp.arange(NEAR, dtype=jnp.int32)[None, :]
    own = box_coords(jnp.broadcast_to(leaf_ids, (LEAVES, NEAR)))
    steps_drawn = jax.random.randint(key_step, (3, LEAVES, NEAR), -1, 2)
    moved = [own[axis_id] + steps_drawn[axis_id] for axis_id in range(3)]
    inside = jnp.ones((LEAVES, NEAR), bool)
    for axis_id in range(3):
        inside = inside & (moved[axis_id] >= 0) & (moved[axis_id] < axis_extent(axis_id))
    clamped = [jnp.clip(moved[axis_id], 0, axis_extent(axis_id) - 1) for axis_id in range(3)]
    target = box_index(clamped)
    sibling = leaf_ids + 1 - 2 * (leaf_ids % 2)
    below = jnp.where(leaf_ids >= 4, leaf_ids - 4, leaf_ids + 4)
    above = jnp.where(leaf_ids + 4 < LEAVES, leaf_ids + 4, leaf_ids - 4)
    valid = inside & (target != leaf_ids) & (jnp.abs(target - leaf_ids) <= NBAND)
    target = jnp.where(valid, target, sibling)
    target = jnp.where(column == 3, above, target)
    target = jnp.where(column == 2, below, target)
    target = jnp.where(column == 1, sibling, target)
    target = jnp.where(column == 0, leaf_ids, target)
    counts = live_counts(key_count, NEAR, 4)
    return jnp.where(column < counts[:, None], target, -1).astype(jnp.int32)


def draw_coupling_list(key, part):
    key = jax.random.fold_in(key, 22)
    key_offset, key_sign, key_count = jax.random.split(key, 3)
    leaf_ids = jnp.arange(LEAVES, dtype=jnp.int32)[:, None]
    column = jnp.arange(COUP, dtype=jnp.int32)[None, :]
    band_bit = leaf_ids // NBAND % 2
    exact = jnp.where(band_bit == 0, leaf_ids + NBAND, leaf_ids - NBAND)
    distance = jax.random.randint(key_offset, (LEAVES, COUP), 1, NBAND + 1)
    signs = 2 * jax.random.randint(key_sign, (LEAVES, COUP), 0, 2) - 1
    target = leaf_ids + signs * distance
    target = jnp.where((target < 0) | (target >= LEAVES), leaf_ids - signs * distance, target)
    own = box_coords(jnp.broadcast_to(leaf_ids, (LEAVES, COUP)))
    other = box_coords(target)
    apart = jnp.zeros((LEAVES, COUP), bool)
    for axis_id in range(3):
        apart = apart | (jnp.abs(own[axis_id] - other[axis_id]) >= 2)
    target = jnp.where(apart, target, exact)
    target = jnp.where(column == 1, exact, target)
    counts = live_counts(key_count, COUP, 2)
    return jnp.where(column < counts[:, None], target, -1).astype(jnp.int32)


def draw_points(key, part):
    key = jax.random.fold_in(key, 23)
    leaf_ids = jnp.arange(LEAVES, dtype=jnp.int32)
    corner = jnp.stack(box_coords(leaf_ids)).astype(jnp.float32)
    spread = jax.random.uniform(key, (3, LEAVES, P_SIZE), jnp.float32)
    return (corner[:, :, None] + spread).reshape(3, LEAVES * P_SIZE)


def block_scale(stream_key, dims, cuts, smallest, top_value):
    def one(position, shards_of):
        draws = jax.random.uniform(jax.random.fold_in(jax.random.fold_in(stream_key, 6), position), (shards_of,), jnp.float32, smallest / len(cuts), top_value / len(cuts))
        return jnp.repeat(jnp.exp(draws), dims[position] // shards_of).reshape((-1,) + (1,) * (len(dims) - position - 1))

    factor_of = one(*cuts[0])
    for cut in cuts[1:]:
        factor_of = factor_of * one(*cut)
    return factor_of


def gaussian(stream_key, shape, width, bound, cuts=(), kind=jnp.bfloat16):
    array = jax.random.normal(stream_key, shape, jnp.float32) * width
    if len(cuts) > 0:
        array = block_scale(stream_key, shape, cuts, -0.22, 0.18) * array
    return jnp.clip(array, min=-bound, max=bound).astype(kind)


def setup_inputs(seed: int = 0) -> dict:
    seeds = jax.random.split(jax.random.key(seed), 7)
    charges = gaussian(seeds[0], (R, POINTS), 0.1, 0.59765625, ((1, 32),))
    points = draw_points(jax.random.fold_in(seeds[6], 71), 0)
    basis = gaussian(seeds[2], (LEAVES, K, P_SIZE), P_SIZE ** -0.5, 0.5, ((0, 32),))
    transfer = gaussian(seeds[3], (2, K, K), (K + K // 2) ** -0.5, 0.625, (), jnp.float32)
    near_list = draw_near_list(jax.random.fold_in(seeds[6], 71), 0)
    coupling_list = draw_coupling_list(jax.random.fold_in(seeds[6], 71), 0)
    return {"charges": charges, "points": points, "basis": basis, "transfer": transfer, "near_list": near_list, "coupling_list": coupling_list}


LENGTH_SCALE = 2.0
NUGGET_VARIANCE = 1.0
HIGHEST = lax.Precision.HIGHEST

def unit_nodes():
    index_row = jnp.arange(64, dtype=jnp.int32)

    def axis_value(digit):
        return jnp.cos((2.0 * digit.astype(jnp.float32) + 1.0) * (math.pi / 8.0))
    return jnp.stack([axis_value(index_row // 16), axis_value(index_row // 4 % 4), axis_value(index_row % 4)])

def covariance(first, second):
    separation = first[..., :, None] - second[..., None, :]
    return jnp.exp(-jnp.sqrt(lax.optimization_barrier(jnp.sum(separation * separation, axis=0))) / LENGTH_SCALE)

def cluster_nodes(centers, radii, reference_nodes):
    extra = (1,) * (centers.ndim - 1)
    shaped = reference_nodes.reshape((3,) + extra + (reference_nodes.shape[1],))
    return centers[..., None] + radii[None, ..., None] * shaped

def leaf_shapes(leaf_points):
    centers = lax.optimization_barrier(jnp.mean(leaf_points, axis=2))
    offsets = leaf_points - centers[:, :, None]
    radii = lax.optimization_barrier(jnp.max(jnp.sqrt(lax.optimization_barrier(jnp.sum(offsets * offsets, axis=0))), axis=1))
    return (centers, radii)

def merge_shapes(centers, radii):
    paired = centers.reshape(3, -1, 2)
    spread = radii.reshape(-1, 2)
    separation = paired[:, :, 0] - paired[:, :, 1]
    joined = 0.5 * (paired[:, :, 0] + paired[:, :, 1])
    return (joined, jnp.maximum(spread[:, 0], spread[:, 1]) + 0.5 * jnp.sqrt(lax.optimization_barrier(jnp.sum(separation * separation, axis=0))))

def merge_coefficients(coefficient, transfer):
    paired = coefficient.reshape(coefficient.shape[0], -1, 2, coefficient.shape[2])
    return jnp.einsum('rcsk,skj->rcj', paired, transfer, precision=HIGHEST)

def descend(downward, transfer):
    spread = jnp.einsum('rcj,skj->rcsk', downward, transfer, precision=HIGHEST)
    return spread.reshape(downward.shape[0], -1, downward.shape[2])

def sibling_coupling(coefficient, centers, radii, reference_nodes):
    nodes = cluster_nodes(centers, radii, reference_nodes)
    paired = nodes.reshape(3, -1, 2, nodes.shape[2])
    kernel_tile = covariance(paired[:, :, 0], paired[:, :, 1])
    coef_pairs = coefficient.reshape(coefficient.shape[0], -1, 2, coefficient.shape[2])
    to_left = jnp.einsum('rcq,cpq->rcp', coef_pairs[:, :, 1], kernel_tile, precision=HIGHEST)
    to_right = jnp.einsum('rcp,cpq->rcq', coef_pairs[:, :, 0], kernel_tile, precision=HIGHEST)
    return jnp.stack([to_left, to_right], axis=2).reshape(coefficient.shape)

def listed_coupling(all_coef, all_centers, all_radii, own_centers, own_radii, slot_rows, reference_nodes):
    is_live = slot_rows >= 0
    safe_rows = jnp.where(is_live, slot_rows, 0).astype(jnp.int32)
    own_nodes = cluster_nodes(own_centers, own_radii, reference_nodes)
    far_nodes = cluster_nodes(jnp.take(all_centers, safe_rows, axis=1), jnp.take(all_radii, safe_rows, axis=0), reference_nodes)
    kernel_tile = covariance(own_nodes[:, :, None, :], far_nodes) * is_live.astype(jnp.float32)[:, :, None, None]
    far_coef = jnp.take(all_coef, safe_rows, axis=1)
    return jnp.einsum('wspq,rwsq->rwp', kernel_tile, far_coef, precision=HIGHEST)

def near_tile(all_x, all_points, own_x, own_points, slot_rows):
    is_live = slot_rows >= 0
    safe_rows = jnp.where(is_live, slot_rows, 0).astype(jnp.int32)
    far_points = jnp.take(all_points, safe_rows, axis=1)
    kernel_tile = (covariance(own_points[:, :, None, :], far_points) * is_live.astype(jnp.float32)[:, :, None, None]).astype(jnp.bfloat16)
    far_x = jnp.take(all_x, safe_rows, axis=1)
    summed = jnp.einsum('wspq,rwsq->rwp', kernel_tile.astype(jnp.float32), far_x.astype(jnp.float32))
    return summed + NUGGET_VARIANCE * own_x.astype(jnp.float32)

def blocked(function, total_rows, block_size):
    starts = jnp.arange(total_rows // block_size, dtype=jnp.int32) * block_size
    pieces = lax.map(function, starts)
    return jnp.moveaxis(pieces, 0, 1).reshape(pieces.shape[1], total_rows, pieces.shape[3])

def reference(charges, points, basis, transfer, near_list, coupling_list):
    reference_nodes = unit_nodes()
    leaf_x = charges.reshape(R, LEAVES, P_SIZE)
    leaf_points = points.reshape(3, LEAVES, P_SIZE)

    def near_block(start_leaf):
        return near_tile(leaf_x, leaf_points, lax.dynamic_slice_in_dim(leaf_x, start_leaf, 64, 1), lax.dynamic_slice_in_dim(leaf_points, start_leaf, 64, 1), lax.dynamic_slice_in_dim(near_list, start_leaf, 64, 0))
    near = blocked(near_block, LEAVES, 64)
    coefficient = jnp.einsum('rcp,ckp->rck', leaf_x.astype(jnp.float32), basis.astype(jnp.float32))
    centers, radii = leaf_shapes(leaf_points)

    def couple_block(start_leaf):
        return listed_coupling(coefficient, centers, radii, lax.dynamic_slice_in_dim(centers, start_leaf, 64, 1), lax.dynamic_slice_in_dim(radii, start_leaf, 64, 0), lax.dynamic_slice_in_dim(coupling_list, start_leaf, 64, 0), reference_nodes)
    leaf_couple = blocked(couple_block, LEAVES, 64)
    levels = [(coefficient, centers, radii)]
    while levels[-1][0].shape[1] > 1:
        last_coef, last_centers, last_radii = levels[-1]
        joined_centers, joined_radii = merge_shapes(last_centers, last_radii)
        levels.append((merge_coefficients(last_coef, transfer), joined_centers, joined_radii))
    downward = jnp.zeros((R, 1, K), jnp.float32)
    for level_index in range(len(levels) - 2, 0, -1):
        level_coef, level_centers, level_radii = levels[level_index]
        downward = descend(downward, transfer) + sibling_coupling(level_coef, level_centers, level_radii, reference_nodes)
    downward = descend(downward, transfer) + leaf_couple
    down_leaf = downward.astype(jnp.bfloat16)
    far = jnp.einsum('rck,ckp->rcp', down_leaf.astype(jnp.float32), basis.astype(jnp.float32))
    return (near + far).reshape(R, POINTS)
```

```python
import functools
import math

import jax
import jax.numpy as jnp
from jax import lax
from jax.experimental import pallas as pl
from jax.experimental.pallas import tpu as pltpu
from jax.sharding import PartitionSpec as P

P_SIZE = 128
K = 64
R = 32
LD = 128
PAIRS = LD // 2
GROUPS = LD // 4
HALF = LD // 2
NEAR_REACH = 8
FEATS = 48
BATCH = 8
LIST = 896
SEND = 40
SCALE = 0.5 * math.log2(math.e)
NODE = [math.cos((2 * a + 1) * math.pi / 8) for a in range(4)]
AXES = ("leaf", "sub")
F32 = jnp.float32
BF16 = jnp.bfloat16
NT = (((1,), (1,)), ((), ()))
TINY = 1e-30
VMEM_LIMIT = 56 * 1024 * 1024


def lanes(shape):
    return lax.broadcasted_iota(jnp.int32, shape, len(shape) - 1)


def rows(shape):
    return lax.broadcasted_iota(jnp.int32, shape, len(shape) - 2)


def dot(a, b):
    return jnp.dot(a, b, preferred_element_type=F32)


def dot_nt(a, b):
    return lax.dot_general(a, b, NT, preferred_element_type=F32)


def halves(value):
    high = value.astype(BF16)
    return high, (value - high.astype(F32)).astype(BF16)


def thirds(value):
    first = value.astype(BF16).astype(F32)
    rest = value - first
    second = rest.astype(BF16).astype(F32)
    return first, second, rest - second


def unit_node(index):
    return jnp.where(
        index == 0,
        NODE[0],
        jnp.where(index == 1, NODE[1], jnp.where(index == 2, NODE[2], NODE[3])),
    ).astype(F32)


def lane_nodes():
    b = lanes((8, 128)) & 63
    return [unit_node(b >> 4), unit_node((b >> 2) & 3), unit_node(b & 3)]


def row_nodes():
    r = rows((8, 128))
    return [unit_node(r >> 2), unit_node((r >> 2) + 2)], unit_node(r & 3)


def decay(t):
    t = jnp.maximum(t, TINY)
    return jnp.exp2(-(t * lax.rsqrt(t)))


def tile_from_axes(x_sq, y_sq, z_sq):
    yz = [y_sq[0] + z_sq, y_sq[1] + z_sq]
    return decay(jnp.concatenate([x_sq[k // 2] + yz[k % 2] for k in range(8)], axis=0))


def doubled_transfer(t_ref):
    flat = t_ref[...].reshape(2 * K, K)
    return jnp.concatenate([flat, flat], axis=1)


def device_index():
    return lax.axis_index("leaf") * lax.axis_size("sub") + lax.axis_index("sub")


def merge_up(pairs, t_high, t_low):
    n = pairs.shape[0]
    high, low = halves(pairs.reshape(n * R, 128))
    out = dot(high, t_high) + dot(high, t_low) + dot(low, t_high)
    return out.reshape(n, R, 128)


def pair_lanes(clusters):
    n = clusters.shape[0]
    split = clusters.reshape(n // 2, 2, R, 128)
    return jnp.where(lanes((1, R, 128)) < K, split[:, 0], split[:, 1])


def push_down(value, t_high, t_low):
    n = value.shape[0]
    high, low = halves(value.reshape(n * R, 128))
    out = dot_nt(high, t_high) + dot_nt(high, t_low) + dot_nt(low, t_high)
    return out.reshape(n, R, 128)


def children_of(pairs):
    lane = lanes((1, R, 128))
    left = jnp.where(lane < K, pairs, 0.0)
    right = jnp.where(lane < K, 0.0, pairs)
    return jnp.stack([left, right], axis=1).reshape(2 * pairs.shape[0], R, 128)


def merge_shape_rows(left, right):
    lane = lanes(left.shape)
    sep = left - right
    gap = jnp.sqrt(jnp.sum(jnp.where(lane < 3, sep * sep, 0.0), axis=1, keepdims=True))
    radius = jnp.maximum(left, right) + 0.5 * gap
    return jnp.where(lane == 3, radius, jnp.where(lane < 3, 0.5 * (left + right), 0.0))


def sibling_tile(left, right, lane_u, row_y, row_z):
    low = lanes((8, 128)) < K
    alpha = jnp.where(low, left[3], right[3])
    beta = jnp.where(low, right[3], left[3])
    base = [jnp.where(low, left[d] - right[d], right[d] - left[d]) - beta * lane_u[d] for d in range(3)]
    x_sq = [jnp.square(base[0] + alpha * NODE[a]) for a in range(4)]
    y_sq = [jnp.square(base[1] + alpha * row_y[h]) for h in range(2)]
    z_sq = jnp.square(base[2] + alpha * row_z)
    return tile_from_axes(x_sq, y_sq, z_sq)


def sibling_apply(tile, pair):
    low = lanes((R, 128)) < K
    swapped = pltpu.roll(pair, K, 1)
    stacked = jnp.concatenate(
        [jnp.where(low, swapped, 0.0), jnp.where(low, 0.0, swapped)], axis=0
    )
    high, low_part = halves(stacked)
    t_high, t_low = halves(tile)
    t_high = jnp.concatenate([t_high, t_high], axis=0)
    t_low = jnp.concatenate([t_low, t_low], axis=0)
    out = dot_nt(high, t_high) + dot_nt(high, t_low) + dot_nt(low_part, t_high)
    return jnp.where(low, out[:R], out[R:])


LEVEL_OFFSETS = [0, 128, 192, 224, 240, 248, 252, 254]
PAIR_OFFSETS = [0, 0, 32, 48, 56, 60, 62]


def leaf_kernel(
    x_ref, p_ref, b_ref, t_ref, near_ref,
    send_next, send_prev, coef_ref, lev_ref, root_ref, shape_ref, list_ref,
    pts, shapes,
):
    first_leaf = device_index() * LD
    origin = (first_leaf // 4).astype(F32)
    zero = jnp.zeros((K, P_SIZE), BF16)

    def leaf_pair(c, carry):
        x = x_ref[:, pl.ds(pl.multiple_of(c * 256, 256), 256)]
        weights = jnp.concatenate(
            [
                jnp.concatenate([b_ref[2 * c], zero], axis=1),
                jnp.concatenate([zero, b_ref[2 * c + 1]], axis=1),
            ],
            axis=0,
        )
        coef_ref[c] = dot_nt(x, weights)
        return carry

    lax.fori_loop(0, PAIRS, leaf_pair, 0, unroll=8)

    t_high, t_low = halves(doubled_transfer(t_ref))
    pairs = coef_ref[...]
    for level in range(1, 7):
        pairs = pair_lanes(merge_up(pairs, t_high, t_low))
        lev_ref[pl.ds(PAIR_OFFSETS[level], pairs.shape[0])] = pairs
    root = merge_up(pairs, t_high, t_low)[0]

    for i in range(LD):
        for d in range(3):
            pts[d, i : i + 1, :] = p_ref[d : d + 1, i * P_SIZE : (i + 1) * P_SIZE]
    centers, squares = [], 0.0
    for d in range(3):
        coords = pts[d] - origin if d == 2 else pts[d]
        center = jnp.sum(coords, axis=1, keepdims=True) * (1.0 / P_SIZE)
        centers.append(center)
        squares = squares + jnp.square(coords - center)
    radius = jnp.sqrt(jnp.max(squares, axis=1, keepdims=True))
    lane = lanes((LD, 128))
    shapes[0:LD, :] = jnp.where(
        lane == 0,
        centers[0],
        jnp.where(
            lane == 1,
            centers[1],
            jnp.where(lane == 2, centers[2], jnp.where(lane == 3, radius, 0.0)),
        ),
    )
    count = LD // 2
    for level in range(1, 8):
        source = LEVEL_OFFSETS[level - 1]
        joined = merge_shape_rows(
            shapes[pl.ds(source, count, stride=2), :],
            shapes[pl.ds(source + 1, count, stride=2), :],
        )
        shapes[pl.ds(LEVEL_OFFSETS[level], count), :] = joined
        count //= 2
    shape_rows = jnp.concatenate(
        [jnp.transpose(shapes[0:128, :])[0:8], jnp.transpose(shapes[128:256, :])[0:8]], axis=1
    )
    shape_ref[...] = shape_rows
    root_ref[0:R, :] = root
    root_ref[R : R + 8, :] = jnp.broadcast_to(shapes[254:255, :], (8, 128))

    for send, first_pair, first_group_leaf in ((send_next, PAIRS // 2, LD - 4), (send_prev, 0, 0)):
        send[0 : PAIRS // 2] = coef_ref[pl.ds(first_pair, PAIRS // 2)]
        send[32, 0:8, :] = shape_rows[:, 0:128]
        send[32, 8:32, :] = jnp.zeros((24, 128), F32)
        for k in range(4):
            place = (first_group_leaf + k) * P_SIZE
            send[33 + k] = x_ref[:, place : place + P_SIZE].astype(F32)
            send[32, 8 + 4 * k : 11 + 4 * k, :] = p_ref[:, place : place + P_SIZE]
        for k in range(37, SEND):
            send[k] = jnp.zeros((R, 128), F32)

    lane8 = lanes((8, 128))
    row8 = rows((8, 128))
    offset = jnp.where(near_ref[...] >= 0, near_ref[...] - first_leaf - lane8, 1000)

    def slots_at(delta):
        return jnp.sum(jnp.where(offset == delta, 1.0, 0.0), axis=0, keepdims=True)

    forward = jnp.concatenate([slots_at(delta) for delta in range(8)], axis=0)
    backward = jnp.concatenate(
        [jnp.zeros((1, 128), F32)]
        + [pltpu.roll(slots_at(-delta), 128 - delta, 1) for delta in range(1, 8)],
        axis=0,
    )
    inside = lane8 + row8 < LD
    flags = jnp.where(inside & (forward + backward > 0.0), 1.0, 0.0)
    earlier = jnp.where(rows((128, 128)) < lanes((128, 128)), 1.0, 0.0).astype(BF16)
    place = dot(flags.astype(BF16), earlier)
    totals = jnp.sum(flags, axis=1, keepdims=True)
    before = jnp.full((1, 1), 2.0 * BATCH, F32)
    starts = []
    for delta in range(8):
        starts.append(before)
        before = before + totals[delta : delta + 1, :]
    place = jnp.where(flags > 0.0, place + jnp.concatenate(starts, axis=0), -1.0)
    task_rows = []
    for delta in range(8):
        first = lane8.astype(F32)
        task_rows.append(
            jnp.where(
                row8 == 0,
                first,
                jnp.where(
                    row8 == 1,
                    first + delta,
                    jnp.where(
                        row8 == 2,
                        forward[delta : delta + 1, :],
                        jnp.where(row8 == 3, backward[delta : delta + 1, :], 0.0),
                    ),
                ),
            ).astype(BF16)
        )
    tasks = jnp.concatenate(task_rows, axis=1)
    slot_row = rows((128, 128)).astype(F32)
    for m in range(LIST // 128):
        chosen = jnp.concatenate(
            [
                jnp.where(place[delta : delta + 1, :] == slot_row + 128.0 * m, 1.0, 0.0).astype(BF16)
                for delta in range(8)
            ],
            axis=1,
        )
        part = dot_nt(tasks, chosen)
        part = jnp.where(row8 == 4, before - 2.0 * BATCH, part)
        list_ref[:, m * 128 : (m + 1) * 128] = part.astype(jnp.int32)


def point_features(points8, origin_z):
    row = rows(points8.shape)
    center = jnp.where(row == 2, origin_z + 0.5, 1.0)
    v = jnp.where(row < 3, (points8 - center) * SCALE, 0.0)
    norm = jnp.sum(v * v, axis=0, keepdims=True)
    far = jnp.where(row == 3, norm, jnp.where(row == 4, 1.0, v))
    own = jnp.where(row == 3, 1.0, jnp.where(row == 4, norm, -2.0 * v))
    return far, own


def far_stack(value):
    first, second, third = thirds(value)
    return jnp.concatenate([first, first, first, second, second, third], axis=0)


def own_stack(value):
    first, second, third = thirds(value)
    return jnp.concatenate([first, second, third, first, second, first], axis=0).astype(BF16)


def near_kernel(
    list_ref, shape_ref, x_ref, p_ref, lev_ref, out_ref, couple_ref,
    p8, far_feat, own_feat, dist0, dist1, tile0, tile1,
):
    first_group = device_index() * GROUPS
    p8[...] = jnp.zeros((8, 512), F32)

    def features(g, carry):
        p8[0:3, :] = p_ref[:, pl.ds(pl.multiple_of(g * 512, 512), 512)]
        coords = p8[...]
        origin_z = (first_group + g).astype(F32)
        far, own = point_features(coords, origin_z)
        _, own_up = point_features(coords, origin_z + 1.0)
        far = far_stack(far)
        own = own_stack(own)
        own_up = own_stack(own_up)
        for k in range(4):
            part = slice(k * P_SIZE, (k + 1) * P_SIZE)
            far_feat[4 * g + k] = jnp.transpose(far[:, part]).astype(BF16)
            own_feat[4 * g + k] = own[:, part]
            own_feat[LD + 4 * g + k] = own_up[:, part]
        return carry

    lax.fori_loop(0, GROUPS, features, 0)

    out_ref[...] = x_ref[...].astype(F32)
    for ref in (dist0, dist1, tile0, tile1):
        ref[...] = jnp.zeros(ref.shape, ref.dtype)

    total = list_ref[4, 0]
    steps = (total + BATCH - 1) // BATCH + 2

    def leaf_slice(i):
        return pl.ds(pl.multiple_of(i * P_SIZE, P_SIZE), P_SIZE)

    def phase(n, dist_new, dist_old, tile_new, tile_old):
        results = []
        for u in range(BATCH):
            k = n * BATCH + u
            i, j = list_ref[0, k], list_ref[1, k]
            tile = tile_old[u]
            results.append(
                (
                    i,
                    j,
                    dot(x_ref[:, leaf_slice(j)], tile) * list_ref[2, k].astype(F32),
                    dot_nt(x_ref[:, leaf_slice(i)], tile) * list_ref[3, k].astype(F32),
                )
            )
        for u in range(BATCH):
            k = (n + 2) * BATCH + u
            i, j = list_ref[0, k], list_ref[1, k]
            variant = ((j >> 2) - (i >> 2)) * LD
            dist_new[u] = dot(far_feat[j], own_feat[variant + i])
        for u in range(BATCH):
            tile_new[u] = decay(dist_old[u]).astype(BF16)
        for i, j, to_i, to_j in results:
            out_ref[:, leaf_slice(i)] += to_i
            out_ref[:, leaf_slice(j)] += to_j

    def two_phases(m, carry):
        phase(2 * m, dist0, dist1, tile1, tile0)
        phase(2 * m + 1, dist1, dist0, tile0, tile1)
        return carry

    lax.fori_loop(0, (steps + 1) // 2, two_phases, 0)

    lane_u = lane_nodes()
    row_y, row_z = row_nodes()

    def sibling(pair, cluster):
        left = [shape_ref[d, cluster] * SCALE for d in range(4)]
        right = [shape_ref[d, cluster + 1] * SCALE for d in range(4)]
        tile = sibling_tile(left, right, lane_u, row_y, row_z)
        couple_ref[pair] = sibling_apply(tile, lev_ref[pair])

    def siblings(m, carry):
        for u in range(9):
            pair = 9 * m + u
            sibling(pair, LD + 2 * pair)
        return carry

    lax.fori_loop(0, 7, siblings, 0)


def top_merge_kernel(blocks_ref, t_ref, root_ref, shapes):
    t_high, t_low = halves(doubled_transfer(t_ref))
    n = blocks_ref.shape[0]
    clusters = blocks_ref[:, 0:R, :]
    for k in range(n):
        shift = lanes((1, 128)) == 2
        shapes[k : k + 1, :] = blocks_ref[k, R : R + 1, :] + jnp.where(shift, (k * GROUPS) * 1.0, 0.0)
    source, count = 0, n // 2
    while count >= 1:
        clusters = merge_up(pair_lanes(clusters), t_high, t_low)
        joined = merge_shape_rows(
            shapes[pl.ds(source, count, stride=2), :], shapes[pl.ds(source + 1, count, stride=2), :]
        )
        source += 2 * count
        shapes[pl.ds(source, count), :] = joined
        count //= 2
    root_ref[0:R, :] = clusters[0]
    root_ref[R : R + 8, :] = jnp.broadcast_to(shapes[source : source + 1, :], (8, 128))


def top_down(blocks_ref, member, spacing, incoming, t_high, t_low, pairs_scr, shapes):
    n = blocks_ref.shape[0]
    clusters = blocks_ref[:, 0:R, :]
    for k in range(n):
        shift = lanes((1, 128)) == 2
        shapes[k : k + 1, :] = (
            blocks_ref[k, R : R + 1, :] + jnp.where(shift, (k * spacing) * 1.0, 0.0)
        ) * SCALE
    source, count, pair_source = 0, n // 2, 0
    levels = []
    while count >= 1:
        pairs = pair_lanes(clusters)
        pairs_scr[pl.ds(pair_source, count)] = pairs
        levels.append((source, pair_source))
        if count > 1:
            clusters = merge_up(pairs, t_high, t_low)
            joined = merge_shape_rows(
                shapes[pl.ds(source, count, stride=2), :],
                shapes[pl.ds(source + 1, count, stride=2), :],
            )
            shapes[pl.ds(source + 2 * count, count), :] = joined
        source += 2 * count
        pair_source += count
        count //= 2
    lane_u = lane_nodes()
    row_y, row_z = row_nodes()
    couples = []
    for level, (source, pair_source) in enumerate(levels):
        pair = member >> (level + 1)
        left_row = shapes[pl.ds(source + 2 * pair, 1), :]
        right_row = shapes[pl.ds(source + 2 * pair + 1, 1), :]
        left = [jnp.broadcast_to(left_row[:, d : d + 1], (8, 128)) for d in range(4)]
        right = [jnp.broadcast_to(right_row[:, d : d + 1], (8, 128)) for d in range(4)]
        tile = sibling_tile(left, right, lane_u, row_y, row_z)
        couples.append(sibling_apply(tile, pairs_scr[pair_source + pair]))
    low = lanes((R, 128)) < K
    for level in reversed(range(len(levels))):
        value = couples[level]
        if incoming is not None:
            value = value + push_down(incoming[None], t_high, t_low)[0]
        side = (member >> level) & 1
        keep_low = jnp.where(low, 1, 0) == (1 - side)
        incoming = jnp.where(keep_low, value, 0.0)
    return incoming


def final_kernel(
    near_list, coupling_list, shape_ref,
    near_ref, x_ref, p_ref, b_ref, t_ref, prev_ref, next_ref, coef_ref, couple_ref,
    sub_ref, leaf_ref,
    out_ref,
    pairs_scr, top_shapes, down, leaf_couple, node_tab, high_tab, low_tab,
    halo_shape, sems, p8,
    tile_h0, tile_l0, lhs0, tile_h1, tile_l1, lhs1,
):
    device = device_index()
    first_leaf = device * LD
    lane32 = lanes((R, 128))
    low32 = lane32 < K
    copies = [
        pltpu.make_async_copy(prev_ref.at[32, 0:8], halo_shape.at[0], sems.at[0]),
        pltpu.make_async_copy(next_ref.at[32, 0:8], halo_shape.at[1], sems.at[1]),
    ]
    for copy in copies:
        copy.start()

    t_high, t_low = halves(doubled_transfer(t_ref))
    sub_count = lax.axis_size("sub")
    incoming = top_down(
        leaf_ref, lax.axis_index("leaf"), sub_count * GROUPS, None, t_high, t_low, pairs_scr, top_shapes
    )
    incoming = top_down(
        sub_ref, lax.axis_index("sub"), GROUPS, incoming, t_high, t_low, pairs_scr, top_shapes
    )
    value = couple_ref[pl.ds(PAIR_OFFSETS[6], 1)] + push_down(incoming[None], t_high, t_low)
    for level in range(5, 0, -1):
        n = PAIRS >> level
        value = couple_ref[pl.ds(PAIR_OFFSETS[level], n)] + push_down(
            children_of(value), t_high, t_low
        )
    down[...] = push_down(children_of(value), t_high, t_low)

    p8[...] = jnp.zeros((8, 512), F32)
    out_ref[...] = near_ref[...]
    for halo_ref, group, step in ((prev_ref, 0, -1), (next_ref, GROUPS - 1, 1)):
        origin_z = (device * GROUPS + group).astype(F32)
        span = slice(group * 512, group * 512 + 512)
        p8[0:3, :] = p_ref[:, span]
        _, own = point_features(p8[...], origin_z)
        own = own_stack(own)
        for k in range(4):
            p8[0:3, k * P_SIZE : (k + 1) * P_SIZE] = halo_ref[32, 8 + 4 * k : 11 + 4 * k, :]
        far, _ = point_features(p8[...], origin_z)
        far = far_stack(far)
        for k in range(4):
            far_k = jnp.transpose(far[:, k * P_SIZE : (k + 1) * P_SIZE]).astype(BF16)
            tiles = decay(dot(far_k, own)).astype(BF16)
            x_k = halo_ref[33 + k].astype(BF16)
            target = first_leaf + 4 * (group + step) + k
            products = dot(x_k, tiles)
            for i in range(4):
                leaf = 4 * group + i
                weight = jnp.int32(0)
                for s in range(8):
                    weight = weight + jnp.where(near_list[s, leaf] == target, 1, 0)
                place = slice(leaf * P_SIZE, (leaf + 1) * P_SIZE)
                out_ref[:, place] += products[:, i * P_SIZE : (i + 1) * P_SIZE] * weight.astype(F32)

    def table(first_pair, source_ref, first, count):
        def one(m, carry):
            pair = source_ref[first + m]
            high, low = halves(pair)
            high_tab[0, first_pair + m] = high
            low_tab[0, first_pair + m] = low
            high, low = halves(pltpu.roll(pair, K, 1))
            high_tab[1, first_pair + m] = high
            low_tab[1, first_pair + m] = low
            return carry

        lax.fori_loop(0, count, one, 0, unroll=4)

    table(0, prev_ref, 0, PAIRS // 2)
    table(PAIRS // 2, coef_ref, 0, PAIRS)
    table(PAIRS // 2 + PAIRS, next_ref, 0, PAIRS // 2)
    for swap in range(2):
        high_tab[swap, 2 * PAIRS] = jnp.zeros((R, 128), BF16)
        low_tab[swap, 2 * PAIRS] = jnp.zeros((R, 128), BF16)

    for copy in copies:
        copy.wait()
    lane_u = lane_nodes()
    row8 = rows((8, 128))
    low8 = lanes((8, 128)) < K
    unit8 = jnp.where(row8 == 0, lane_u[0], jnp.where(row8 == 1, lane_u[1], lane_u[2])) * SCALE

    def nodes(first_pair, read, shift, count):
        def one(m, carry):
            left = [read(d, 2 * m) for d in range(4)]
            right = [read(d, 2 * m + 1) for d in range(4)]
            left[2] = left[2] + shift
            right[2] = right[2] + shift

            def column(c):
                return jnp.where(row8 == 0, c[0], jnp.where(row8 == 1, c[1], c[2])) * SCALE

            left_nodes = column(left) + left[3] * unit8
            right_nodes = column(right) + right[3] * unit8
            node_tab[0, first_pair + m] = jnp.where(low8, left_nodes, right_nodes)
            node_tab[1, first_pair + m] = jnp.where(low8, right_nodes, left_nodes)
            return carry

        lax.fori_loop(0, count, one, 0, unroll=4)

    nodes(0, lambda d, k: halo_shape[0, d, HALF + k], -1.0 * GROUPS, PAIRS // 2)
    nodes(PAIRS // 2, lambda d, k: shape_ref[d, k], 0.0, PAIRS)
    nodes(PAIRS // 2 + PAIRS, lambda d, k: halo_shape[1, d, k], 1.0 * GROUPS, PAIRS // 2)

    row_y, row_z = row_nodes()

    def couple_tiles(i, u, tile_h, tile_l, lhs):
        radius = shape_ref[3, i] * SCALE
        center = [shape_ref[d, i] * SCALE for d in range(3)]
        own_x = [center[0] + radius * NODE[a] for a in range(4)]
        own_y = [center[1] + radius * row_y[h] for h in range(2)]
        own_z = center[2] + radius * row_z
        for q in range(4):
            picks = []
            for h in range(2):
                j = coupling_list[2 * q + h, i]
                e = jnp.where(j >= 0, j - first_leaf + HALF, 0)
                swap = (e & 1) ^ h
                picks.append((swap, e >> 1, jnp.where(j >= 0, e >> 1, 2 * PAIRS)))
            (s0, n0, c0), (s1, n1, c1) = picks
            base = jnp.where(low8, node_tab[s0, n0], node_tab[s1, n1])
            bx = jnp.broadcast_to(base[0:1], (8, 128))
            by = jnp.broadcast_to(base[1:2], (8, 128))
            bz = jnp.broadcast_to(base[2:3], (8, 128))
            tile = tile_from_axes(
                [jnp.square(bx - own_x[a]) for a in range(4)],
                [jnp.square(by - own_y[h]) for h in range(2)],
                jnp.square(bz - own_z),
            )
            high, low = halves(tile)
            span = slice(q * 128, (q + 1) * 128)
            tile_h[u, :, span] = high
            tile_l[u, :, span] = low
            lhs[u, 0:R, span] = jnp.where(low32, high_tab[s0, c0], high_tab[s1, c1])
            lhs[u, R : 2 * R, span] = jnp.where(low32, low_tab[s0, c0], low_tab[s1, c1])

    def couple_apply(u, tile_h, tile_l, lhs):
        both = dot_nt(lhs[u], tile_h[u])
        cross = dot_nt(lhs[u, 0:R], tile_l[u])
        return both[0:R] + both[R : 2 * R] + cross

    UNIT = 4

    def couple_phase(n, new, old):
        for v in range(UNIT // 2):
            pair = (n - 1) * (UNIT // 2) + v + 2
            value = jnp.concatenate(
                [couple_apply(2 * v, *old), couple_apply(2 * v + 1, *old)], axis=1
            )
            leaf_couple[pair] = value
        for u in range(UNIT):
            leaf = jnp.minimum(n * UNIT + u, LD - 1)
            couple_tiles(leaf, u, *new)

    buffers = ((tile_h0, tile_l0, lhs0), (tile_h1, tile_l1, lhs1))
    for ref in buffers[1]:
        ref[...] = jnp.zeros(ref.shape, ref.dtype)

    def couple_two(m, carry):
        couple_phase(2 * m, buffers[0], buffers[1])
        couple_phase(2 * m + 1, buffers[1], buffers[0])
        return carry

    lax.fori_loop(0, LD // UNIT // 2 + 1, couple_two, 0)

    zero = jnp.zeros((K, P_SIZE), BF16)

    def finish(c, carry):
        value = (down[c] + leaf_couple[c + 2]).astype(BF16)
        weights = jnp.concatenate(
            [
                jnp.concatenate([b_ref[2 * c], zero], axis=1),
                jnp.concatenate([zero, b_ref[2 * c + 1]], axis=1),
            ],
            axis=0,
        )
        out_ref[:, pl.ds(pl.multiple_of(c * 256, 256), 256)] += dot(value, weights)
        return carry

    lax.fori_loop(0, PAIRS, finish, 0, unroll=8)


def shaped(*shape, dtype=F32):
    return jax.ShapeDtypeStruct(shape, dtype)


def vmem():
    return pl.BlockSpec(memory_space=pltpu.VMEM)


def smem():
    return pl.BlockSpec(memory_space=pltpu.SMEM)


PARAMS = pltpu.CompilerParams(vmem_limit_bytes=VMEM_LIMIT)


def per_device(charges, points, basis, transfer, near_list, coupling_list):
    near_rows = near_list.T
    coupling_rows = coupling_list.T
    n_sub = lax.axis_size("sub")
    n_leaf = lax.axis_size("leaf")
    devices = n_sub * n_leaf
    send_next, send_prev, coef, lev, root, shapes, tasks = pl.pallas_call(
        leaf_kernel,
        name="leaf_up",
        out_shape=(
            shaped(SEND, R, 128),
            shaped(SEND, R, 128),
            shaped(PAIRS, R, 128),
            shaped(PAIRS - 1, R, 128),
            shaped(R + 8, 128),
            shaped(8, 256),
            shaped(8, LIST, dtype=jnp.int32),
        ),
        in_specs=[vmem()] * 5,
        out_specs=[vmem()] * 7,
        scratch_shapes=[pltpu.VMEM((3, LD, 128), F32), pltpu.VMEM((256, 128), F32)],
        compiler_params=PARAMS,
    )(charges, points, basis, transfer, near_rows)

    sub_blocks = lax.all_to_all(
        jnp.broadcast_to(root[None], (n_sub,) + root.shape), "sub", 0, 0, tiled=True
    )
    merged = pl.pallas_call(
        top_merge_kernel,
        name="top_merge",
        out_shape=shaped(R + 8, 128),
        in_specs=[vmem()] * 2,
        out_specs=vmem(),
        scratch_shapes=[pltpu.VMEM((2 * n_sub, 128), F32)],
        compiler_params=PARAMS,
    )(sub_blocks, transfer)
    leaf_blocks = lax.all_to_all(
        jnp.broadcast_to(merged[None], (n_leaf,) + merged.shape), "leaf", 0, 0, tiled=True
    )
    forward = [(i, i + 1) for i in range(devices - 1)]
    backward = [(i + 1, i) for i in range(devices - 1)]
    from_prev = lax.ppermute(send_next, AXES, forward)
    from_next = lax.ppermute(send_prev, AXES, backward)

    near, couple = pl.pallas_call(
        near_kernel,
        name="near_field",
        out_shape=(shaped(R, LD * P_SIZE), shaped(PAIRS - 1, R, 128)),
        in_specs=[smem(), smem(), vmem(), vmem(), vmem()],
        out_specs=[vmem()] * 2,
        scratch_shapes=[
            pltpu.VMEM((8, 512), F32),
            pltpu.VMEM((LD, P_SIZE, FEATS), BF16),
            pltpu.VMEM((2 * LD, FEATS, P_SIZE), BF16),
            pltpu.VMEM((BATCH, 128, 128), F32),
            pltpu.VMEM((BATCH, 128, 128), F32),
            pltpu.VMEM((BATCH, 128, 128), BF16),
            pltpu.VMEM((BATCH, 128, 128), BF16),
        ],
        compiler_params=PARAMS,
        cost_estimate=pl.CostEstimate(
            flops=2 * 460 * 128 * 128 * 128, bytes_accessed=4 << 20, transcendentals=460 * 32768
        ),
    )(tasks, shapes, charges, points, lev)

    n_top = max(n_sub, n_leaf)
    unit = 4
    stages = [
        pltpu.VMEM((unit, K, 512), BF16),
        pltpu.VMEM((unit, K, 512), BF16),
        pltpu.VMEM((unit, 2 * R, 512), BF16),
    ]
    return pl.pallas_call(
        final_kernel,
        name="couple_down",
        out_shape=shaped(R, LD * P_SIZE),
        in_specs=[smem()] * 3 + [vmem()] * 11,
        out_specs=vmem(),
        scratch_shapes=[
            pltpu.VMEM((n_top, R, 128), F32),
            pltpu.VMEM((2 * n_top, 128), F32),
            pltpu.VMEM((PAIRS, R, 128), F32),
            pltpu.VMEM((PAIRS + 8, R, 128), F32),
            pltpu.VMEM((2, 2 * PAIRS, 8, 128), F32),
            pltpu.VMEM((2, 2 * PAIRS + 1, R, 128), BF16),
            pltpu.VMEM((2, 2 * PAIRS + 1, R, 128), BF16),
            pltpu.SMEM((2, 8, 128), F32),
            pltpu.SemaphoreType.DMA((2,)),
            pltpu.VMEM((8, 512), F32),
        ]
        + stages
        + stages,
        compiler_params=PARAMS,
    )(
        near_rows, coupling_rows, shapes,
        near, charges, points, basis, transfer, from_prev, from_next, coef, couple,
        sub_blocks, leaf_blocks,
    )


def solution(mesh):
    in_specs = (
        P(None, AXES),
        P(None, AXES),
        P(AXES, None, None),
        P(),
        P(AXES, None),
        P(AXES, None),
    )
    return jax.shard_map(
        per_device, mesh=mesh, in_specs=in_specs, out_specs=P(None, AXES), check_vma=False
    )
```

```python
import functools
import math

import jax
import jax.numpy as jnp
from jax import lax
from jax.experimental import pallas as pl
from jax.experimental.pallas import tpu as pltpu
from jax.sharding import PartitionSpec as P

P_SIZE = 128
K = 64
R = 32
LD = 128
PAIRS = LD // 2
GROUPS = LD // 4
HALF = LD // 2
NEAR_REACH = 8
FEATS = 64
BATCH = 8
LIST = 896
SEND = 40
SCALE = 0.5 * math.log2(math.e)
NODE = [math.cos((2 * a + 1) * math.pi / 8) for a in range(4)]
AXES = ("leaf", "sub")
F32 = jnp.float32
BF16 = jnp.bfloat16
NT = (((1,), (1,)), ((), ()))
TINY = 1e-30
VMEM_LIMIT = 56 * 1024 * 1024


def lanes(shape):
    return lax.broadcasted_iota(jnp.int32, shape, len(shape) - 1)


def rows(shape):
    return lax.broadcasted_iota(jnp.int32, shape, len(shape) - 2)


def dot(a, b):
    return jnp.dot(a, b, preferred_element_type=F32)


def dot_nt(a, b):
    return lax.dot_general(a, b, NT, preferred_element_type=F32)


def halves(value):
    high = value.astype(BF16)
    return high, (value - high.astype(F32)).astype(BF16)


def thirds(value):
    first = value.astype(BF16).astype(F32)
    rest = value - first
    second = rest.astype(BF16).astype(F32)
    return first, second, rest - second


def unit_node(index):
    return jnp.where(
        index == 0,
        NODE[0],
        jnp.where(index == 1, NODE[1], jnp.where(index == 2, NODE[2], NODE[3])),
    ).astype(F32)


def lane_nodes():
    b = lanes((8, 128)) & 63
    return [unit_node(b >> 4), unit_node((b >> 2) & 3), unit_node(b & 3)]


def row_nodes():
    r = rows((8, 128))
    return [unit_node(r >> 2), unit_node((r >> 2) + 2)], unit_node(r & 3)


def decay(t):
    t = jnp.maximum(t, TINY)
    return jnp.exp2(-(t * lax.rsqrt(t)))


def tile_from_axes(x_sq, y_sq, z_sq):
    yz = [y_sq[0] + z_sq, y_sq[1] + z_sq]
    return decay(jnp.concatenate([x_sq[k // 2] + yz[k % 2] for k in range(8)], axis=0))


def doubled_transfer(t_ref):
    flat = t_ref[...].reshape(2 * K, K)
    return jnp.concatenate([flat, flat], axis=1)


def device_index():
    return lax.axis_index("leaf") * lax.axis_size("sub") + lax.axis_index("sub")


def merge_up(pairs, t_high, t_low):
    n = pairs.shape[0]
    high, low = halves(pairs.reshape(n * R, 128))
    out = dot(high, t_high) + dot(high, t_low) + dot(low, t_high)
    return out.reshape(n, R, 128)


def pair_lanes(clusters):
    n = clusters.shape[0]
    split = clusters.reshape(n // 2, 2, R, 128)
    return jnp.where(lanes((1, R, 128)) < K, split[:, 0], split[:, 1])


def push_down(value, t_high, t_low):
    n = value.shape[0]
    high, low = halves(value.reshape(n * R, 128))
    out = dot_nt(high, t_high) + dot_nt(high, t_low) + dot_nt(low, t_high)
    return out.reshape(n, R, 128)


def children_of(pairs):
    lane = lanes((1, R, 128))
    left = jnp.where(lane < K, pairs, 0.0)
    right = jnp.where(lane < K, 0.0, pairs)
    return jnp.stack([left, right], axis=1).reshape(2 * pairs.shape[0], R, 128)


def merge_shape_rows(left, right):
    lane = lanes(left.shape)
    sep = left - right
    gap = jnp.sqrt(jnp.sum(jnp.where(lane < 3, sep * sep, 0.0), axis=1, keepdims=True))
    radius = jnp.maximum(left, right) + 0.5 * gap
    return jnp.where(lane == 3, radius, jnp.where(lane < 3, 0.5 * (left + right), 0.0))


def sibling_tile(left, right, lane_u, row_y, row_z):
    low = lanes((8, 128)) < K
    alpha = jnp.where(low, left[3], right[3])
    beta = jnp.where(low, right[3], left[3])
    base = [jnp.where(low, left[d] - right[d], right[d] - left[d]) - beta * lane_u[d] for d in range(3)]
    x_sq = [jnp.square(base[0] + alpha * NODE[a]) for a in range(4)]
    y_sq = [jnp.square(base[1] + alpha * row_y[h]) for h in range(2)]
    z_sq = jnp.square(base[2] + alpha * row_z)
    return tile_from_axes(x_sq, y_sq, z_sq)


def sibling_apply(tile, pair):
    low = lanes((R, 128)) < K
    swapped = pltpu.roll(pair, K, 1)
    stacked = jnp.concatenate(
        [jnp.where(low, swapped, 0.0), jnp.where(low, 0.0, swapped)], axis=0
    )
    high, low_part = halves(stacked)
    t_high, t_low = halves(tile)
    t_high = jnp.concatenate([t_high, t_high], axis=0)
    t_low = jnp.concatenate([t_low, t_low], axis=0)
    out = dot_nt(high, t_high) + dot_nt(high, t_low) + dot_nt(low_part, t_high)
    return jnp.where(low, out[:R], out[R:])


LEVEL_OFFSETS = [0, 128, 192, 224, 240, 248, 252, 254]
PAIR_OFFSETS = [0, 0, 32, 48, 56, 60, 62]


def block_diagonal(left, right):
    zero = jnp.zeros(left.shape, left.dtype)
    return jnp.concatenate(
        [jnp.concatenate([left, zero], axis=1), jnp.concatenate([zero, right], axis=1)], axis=0
    )


def leaf_kernel(
    x_ref, p_ref, b_ref, t_ref,
    send_next, send_prev, coef_ref, lev_ref, root_ref, shape_ref,
    pts, shapes, p8,
):
    origin = (device_index() * GROUPS).astype(F32)

    def leaf_pair(c, carry):
        x = x_ref[:, pl.ds(pl.multiple_of(c * 256, 256), 256)]
        coef_ref[c] = dot_nt(x, block_diagonal(b_ref[2 * c], b_ref[2 * c + 1]))
        return carry

    lax.fori_loop(0, PAIRS, leaf_pair, 0, unroll=8)

    t_high, t_low = halves(doubled_transfer(t_ref))
    pairs = coef_ref[...]
    for level in range(1, 7):
        pairs = pair_lanes(merge_up(pairs, t_high, t_low))
        lev_ref[pl.ds(PAIR_OFFSETS[level], pairs.shape[0])] = pairs
    root = merge_up(pairs, t_high, t_low)[0]

    for i in range(LD):
        for d in range(3):
            pts[d, i : i + 1, :] = p_ref[d : d + 1, i * P_SIZE : (i + 1) * P_SIZE]
    centers, squares = [], 0.0
    for d in range(3):
        coords = pts[d] - origin if d == 2 else pts[d]
        center = jnp.sum(coords, axis=1, keepdims=True) * (1.0 / P_SIZE)
        centers.append(center)
        squares = squares + jnp.square(coords - center)
    radius = jnp.sqrt(jnp.max(squares, axis=1, keepdims=True))
    lane = lanes((LD, 128))
    shapes[0:LD, :] = jnp.where(
        lane == 0,
        centers[0],
        jnp.where(
            lane == 1,
            centers[1],
            jnp.where(lane == 2, centers[2], jnp.where(lane == 3, radius, 0.0)),
        ),
    )
    count = LD // 2
    for level in range(1, 8):
        source = LEVEL_OFFSETS[level - 1]
        joined = merge_shape_rows(
            shapes[pl.ds(source, count, stride=2), :],
            shapes[pl.ds(source + 1, count, stride=2), :],
        )
        shapes[pl.ds(LEVEL_OFFSETS[level], count), :] = joined
        count //= 2
    shape_rows = jnp.concatenate(
        [jnp.transpose(shapes[0:128, :])[0:8], jnp.transpose(shapes[128:256, :])[0:8]], axis=1
    )
    shape_ref[...] = shape_rows
    low = lanes((R // 2, 128)) < K
    block = jnp.concatenate(
        [
            jnp.where(low, root[0 : R // 2], root[R // 2 : R]),
            jnp.broadcast_to(shapes[254:255, :], (8, 128)),
        ],
        axis=0,
    )
    root_ref[...] = jnp.broadcast_to(block[None], root_ref.shape)

    p8[...] = jnp.zeros((8, 512), F32)
    for send, first_pair, group in ((send_next, PAIRS // 2, GROUPS - 1), (send_prev, 0, 0)):
        send[0 : PAIRS // 2] = coef_ref[pl.ds(first_pair, PAIRS // 2)].astype(BF16)
        parts = thirds(shape_rows[:, 0:128])
        send[36] = jnp.concatenate(list(parts) + [jnp.zeros((8, 128), F32)], axis=0).astype(BF16)
        p8[0:3, :] = p_ref[:, group * 512 : group * 512 + 512]
        parts = thirds(p8[...])
        for k in range(4):
            span = slice(k * P_SIZE, (k + 1) * P_SIZE)
            send[32 + k] = x_ref[:, group * 512 + k * P_SIZE : group * 512 + (k + 1) * P_SIZE]
        for part in range(3):
            send[37 + part] = jnp.concatenate(
                [parts[part][:, k * P_SIZE : (k + 1) * P_SIZE] for k in range(4)], axis=0
            ).astype(BF16)


def list_kernel(near_ref, list_ref):
    first_leaf = device_index() * LD
    lane8 = lanes((8, 128))
    row8 = rows((8, 128))
    offset = jnp.where(near_ref[...] >= 0, near_ref[...] - first_leaf - lane8, 1000)

    def slots_at(delta):
        return jnp.sum(jnp.where(offset == delta, 1.0, 0.0), axis=0, keepdims=True)

    forward = jnp.concatenate([slots_at(delta) for delta in range(8)], axis=0)
    backward = jnp.concatenate(
        [jnp.zeros((1, 128), F32)]
        + [pltpu.roll(slots_at(-delta), 128 - delta, 1) for delta in range(1, 8)],
        axis=0,
    )
    inside = lane8 + row8 < LD
    flags = jnp.where(inside & (forward + backward > 0.0), 1.0, 0.0)
    earlier = jnp.where(rows((128, 128)) < lanes((128, 128)), 1.0, 0.0).astype(BF16)
    place = dot(flags.astype(BF16), earlier)
    totals = jnp.sum(flags, axis=1, keepdims=True)
    before = jnp.full((1, 1), 2.0 * BATCH, F32)
    starts = []
    for delta in range(8):
        starts.append(before)
        before = before + totals[delta : delta + 1, :]
    place = jnp.where(flags > 0.0, place + jnp.concatenate(starts, axis=0), -1.0)
    task_rows = []
    for delta in range(8):
        first = lane8.astype(F32)
        task_rows.append(
            jnp.where(
                row8 == 0,
                first,
                jnp.where(
                    row8 == 1,
                    first + delta,
                    jnp.where(
                        row8 == 2,
                        forward[delta : delta + 1, :],
                        jnp.where(row8 == 3, backward[delta : delta + 1, :], 0.0),
                    ),
                ),
            ).astype(BF16)
        )
    tasks = jnp.concatenate(task_rows, axis=1)
    slot_row = rows((128, 128)).astype(F32)
    for m in range(LIST // 128):
        chosen = jnp.concatenate(
            [
                jnp.where(place[delta : delta + 1, :] == slot_row + 128.0 * m, 1.0, 0.0).astype(BF16)
                for delta in range(8)
            ],
            axis=1,
        )
        part = dot_nt(tasks, chosen)
        part = jnp.where(row8 == 4, before - 2.0 * BATCH, part)
        list_ref[:, m * 128 : (m + 1) * 128] = part.astype(jnp.int32)


def point_features(points8, origin_z):
    row = rows(points8.shape)
    center = jnp.where(row == 2, origin_z + 0.5, 1.0)
    v = jnp.where(row < 3, (points8 - center) * SCALE, 0.0)
    norm = jnp.sum(v * v, axis=0, keepdims=True)
    far = jnp.where(row == 3, norm, jnp.where(row == 4, 1.0, v))
    own = jnp.where(row == 3, 1.0, jnp.where(row == 4, norm, -2.0 * v))
    return far, own


def far_stack(value):
    first, second, third = thirds(value)
    none = jnp.zeros(value.shape, F32)
    return jnp.concatenate(
        [first, first, first, second, second, third, none, none], axis=0
    ).astype(BF16)


def own_stack(value):
    first, second, third = thirds(value)
    none = jnp.zeros(value.shape, F32)
    return jnp.concatenate(
        [first, second, third, first, second, first, none, none], axis=0
    ).astype(BF16)


def identity():
    return jnp.where(rows((128, 128)) == lanes((128, 128)), 1.0, 0.0).astype(BF16)


def near_kernel(
    list_ref, x_ref, p_ref, out_ref,
    p8, far_feat, own_feat, back, dist0, dist1, tile0, tile1,
):
    first_group = device_index() * GROUPS
    p8[...] = jnp.zeros(p8.shape, F32)
    eye = identity()

    def features(m, carry):
        for v in range(2):
            g = 2 * m + v
            p8[v, 0:3, :] = p_ref[:, pl.ds(pl.multiple_of(g * 512, 512), 512)]
            coords = p8[v]
            origin_z = (first_group + g).astype(F32)
            far, own = point_features(coords, origin_z)
            _, own_up = point_features(coords, origin_z + 1.0)
            far = far_stack(far)
            own = own_stack(own)
            own_up = own_stack(own_up)
            parts = [far[:, k * P_SIZE : (k + 1) * P_SIZE] for k in range(4)]
            for swap in range(2):
                stacked = jnp.concatenate([parts[k ^ swap] for k in range(4)], axis=0)
                turned = dot_nt(eye, stacked).astype(BF16)
                far_feat[swap, 2 * g] = turned[:, 0:128]
                far_feat[swap, 2 * g + 1] = turned[:, 128:256]
            for k in range(4):
                part = slice(k * P_SIZE, (k + 1) * P_SIZE)
                own_feat[4 * g + k] = own[:, part]
                own_feat[LD + 4 * g + k] = own_up[:, part]
        return carry

    lax.fori_loop(0, GROUPS // 2, features, 0)

    out_ref[...] = x_ref[...].astype(F32)
    for ref in (back, dist0, dist1, tile0, tile1):
        ref[...] = jnp.zeros(ref.shape, ref.dtype)

    total = list_ref[4, 0]
    steps = (total + BATCH - 1) // BATCH + 2
    low = lanes((128, 128)) < K

    def leaf_slice(i):
        return pl.ds(pl.multiple_of(i * P_SIZE, P_SIZE), P_SIZE)

    def phase(n, dist_new, dist_old, tile_new, tile_old):
        results = []
        for u in range(BATCH):
            k = n * BATCH + u
            i, j = list_ref[0, k], list_ref[1, k]
            tile = tile_old[u // 2, :, (u % 2) * 128 : (u % 2) * 128 + 128]
            results.append(
                (
                    i,
                    j,
                    dot(x_ref[:, leaf_slice(j)], tile) * list_ref[2, k].astype(F32),
                    dot_nt(x_ref[:, leaf_slice(i)], tile) * list_ref[3, k].astype(F32),
                )
            )
        for u in range(BATCH // 2):
            far, own = [], []
            for h in range(2):
                k = (n + 2) * BATCH + 2 * u + h
                i, j = list_ref[0, k], list_ref[1, k]
                variant = ((j >> 2) - (i >> 2)) * LD
                far.append(far_feat[(j & 1) ^ h, j >> 1])
                own.append(own_feat[variant + i])
            dist_new[u] = dot(jnp.where(low, far[0], far[1]), block_diagonal(own[0], own[1]))
        for u in range(BATCH // 2):
            tile_new[u] = decay(dist_old[u]).astype(BF16)
        for i, j, to_i, to_j in results:
            out_ref[:, leaf_slice(i)] += to_i
            back[:, leaf_slice(j)] += to_j

    def two_phases(m, carry):
        phase(2 * m, dist0, dist1, tile1, tile0)
        phase(2 * m + 1, dist1, dist0, tile0, tile1)
        return carry

    lax.fori_loop(0, (steps + 1) // 2, two_phases, 0)
    out_ref[...] += back[...]


def down_kernel(
    shape_ref, lev_ref, t_ref, root_ref, down_ref, couple, pairs_scr, shapes,
):
    lane_u = lane_nodes()
    row_y, row_z = row_nodes()

    def sibling(pair, cluster):
        left = [shape_ref[d, cluster] * SCALE for d in range(4)]
        right = [shape_ref[d, cluster + 1] * SCALE for d in range(4)]
        tile = sibling_tile(left, right, lane_u, row_y, row_z)
        couple[pair] = sibling_apply(tile, lev_ref[pair])

    def siblings(m, carry):
        for u in range(9):
            pair = 9 * m + u
            sibling(pair, LD + 2 * pair)
        return carry

    lax.fori_loop(0, 7, siblings, 0)

    t_high, t_low = halves(doubled_transfer(t_ref))
    device = device_index()
    n = root_ref.shape[0]
    low = lanes((R, 128)) < K
    for k in range(n):
        shift = lanes((1, 128)) == 2
        shapes[k : k + 1, :] = (
            root_ref[k, R // 2 : R // 2 + 1, :] + jnp.where(shift, (k * GROUPS) * 1.0, 0.0)
        ) * SCALE
    for k in range(n // 2):
        left = root_ref[2 * k, 0 : R // 2, :]
        right = root_ref[2 * k + 1, 0 : R // 2, :]
        left = jnp.concatenate([left, pltpu.roll(left, K, 1)], axis=0)
        right = jnp.concatenate([pltpu.roll(right, K, 1), right], axis=0)
        pairs_scr[k] = jnp.where(low, left, right)
    source, count, pair_source = 0, n // 2, 0
    levels = []
    while count >= 1:
        levels.append((source, pair_source))
        if count > 1:
            pairs = pair_lanes(merge_up(pairs_scr[pl.ds(pair_source, count)], t_high, t_low))
            pairs_scr[pl.ds(pair_source + count, count // 2)] = pairs
            joined = merge_shape_rows(
                shapes[pl.ds(source, count, stride=2), :],
                shapes[pl.ds(source + 1, count, stride=2), :],
            )
            shapes[pl.ds(source + 2 * count, count), :] = joined
        source += 2 * count
        pair_source += count
        count //= 2
    couples = []
    for level, (source, pair_source) in enumerate(levels):
        pair = device >> (level + 1)
        left_row = shapes[pl.ds(source + 2 * pair, 1), :]
        right_row = shapes[pl.ds(source + 2 * pair + 1, 1), :]
        left = [jnp.broadcast_to(left_row[:, d : d + 1], (8, 128)) for d in range(4)]
        right = [jnp.broadcast_to(right_row[:, d : d + 1], (8, 128)) for d in range(4)]
        tile = sibling_tile(left, right, lane_u, row_y, row_z)
        couples.append(sibling_apply(tile, pairs_scr[pair_source + pair]))
    incoming = None
    for level in reversed(range(len(levels))):
        value = couples[level]
        if incoming is not None:
            value = value + push_down(incoming[None], t_high, t_low)[0]
        side = (device >> level) & 1
        keep_low = jnp.where(low, 1, 0) == (1 - side)
        incoming = jnp.where(keep_low, value, 0.0)
    value = couple[pl.ds(PAIR_OFFSETS[6], 1)] + push_down(incoming[None], t_high, t_low)
    for level in range(5, 0, -1):
        n = PAIRS >> level
        value = couple[pl.ds(PAIR_OFFSETS[level], n)] + push_down(
            children_of(value), t_high, t_low
        )
    down_ref[...] = push_down(children_of(value), t_high, t_low)


UNIT = 4


def couple_kernel(
    coupling_list, shape_ref, prev_ref, next_ref, coef_ref,
    leaf_couple,
    node_tab, high_tab, low_tab, halo_rows, halo_shape, sems,
    tile_h0, tile_l0, lhs0, tile_h1, tile_l1, lhs1,
):
    first_leaf = device_index() * LD
    low32 = lanes((R, 128)) < K
    copies = []
    for k, ref in enumerate((prev_ref, next_ref)):
        parts = ref[36].astype(F32)
        halo_rows[k] = parts[0:8] + parts[8:16] + parts[16:24]
        copies.append(pltpu.make_async_copy(halo_rows.at[k], halo_shape.at[k], sems.at[k]))
        copies[k].start()

    def own_table(m, carry):
        pair = coef_ref[m]
        high, low = halves(pair)
        high_tab[0, PAIRS // 2 + m] = high
        low_tab[0, m] = low
        high, low = halves(pltpu.roll(pair, K, 1))
        high_tab[1, PAIRS // 2 + m] = high
        low_tab[1, m] = low
        return carry

    lax.fori_loop(0, PAIRS, own_table, 0, unroll=4)
    for first_pair, ref in ((0, prev_ref), (PAIRS // 2 + PAIRS, next_ref)):

        def halo_table(m, carry):
            pair = ref[m]
            high_tab[0, first_pair + m] = pair
            high_tab[1, first_pair + m] = pltpu.roll(pair.astype(F32), K, 1).astype(BF16)
            return carry

        lax.fori_loop(0, PAIRS // 2, halo_table, 0, unroll=4)
    for swap in range(2):
        high_tab[swap, 2 * PAIRS] = jnp.zeros((R, 128), BF16)
        low_tab[swap, PAIRS] = jnp.zeros((R, 128), BF16)

    lane_u = lane_nodes()
    row8 = rows((8, 128))
    low8 = lanes((8, 128)) < K
    unit8 = jnp.where(row8 == 0, lane_u[0], jnp.where(row8 == 1, lane_u[1], lane_u[2])) * SCALE
    for copy in copies:
        copy.wait()

    def nodes(first_pair, read, shift, count):
        def one(m, carry):
            left = [read(d, 2 * m) for d in range(4)]
            right = [read(d, 2 * m + 1) for d in range(4)]
            left[2] = left[2] + shift
            right[2] = right[2] + shift

            def column(c):
                return jnp.where(row8 == 0, c[0], jnp.where(row8 == 1, c[1], c[2])) * SCALE

            left_nodes = column(left) + left[3] * unit8
            right_nodes = column(right) + right[3] * unit8
            node_tab[0, first_pair + m] = jnp.where(low8, left_nodes, right_nodes)
            node_tab[1, first_pair + m] = jnp.where(low8, right_nodes, left_nodes)
            return carry

        lax.fori_loop(0, count, one, 0, unroll=4)

    nodes(0, lambda d, k: halo_shape[0, d, HALF + k], -1.0 * GROUPS, PAIRS // 2)
    nodes(PAIRS // 2, lambda d, k: shape_ref[d, k], 0.0, PAIRS)
    nodes(PAIRS // 2 + PAIRS, lambda d, k: halo_shape[1, d, k], 1.0 * GROUPS, PAIRS // 2)

    row_y, row_z = row_nodes()

    def couple_tiles(i, u, tile_h, tile_l, lhs):
        radius = shape_ref[3, i] * SCALE
        center = [shape_ref[d, i] * SCALE for d in range(3)]
        own_x = [center[0] + radius * NODE[a] for a in range(4)]
        own_y = [center[1] + radius * row_y[h] for h in range(2)]
        own_z = center[2] + radius * row_z
        for q in range(4):
            picks = []
            for h in range(2):
                j = coupling_list[2 * q + h, i]
                e = jnp.where(j >= 0, j - first_leaf + HALF, 0)
                p = e >> 1
                own = (p >= PAIRS // 2) & (p < PAIRS // 2 + PAIRS) & (j >= 0)
                picks.append(
                    (
                        (e & 1) ^ h,
                        p,
                        jnp.where(j >= 0, p, 2 * PAIRS),
                        jnp.where(own, p - PAIRS // 2, PAIRS),
                    )
                )
            (s0, n0, c0, l0), (s1, n1, c1, l1) = picks
            base = jnp.where(low8, node_tab[s0, n0], node_tab[s1, n1])
            bx = jnp.broadcast_to(base[0:1], (8, 128))
            by = jnp.broadcast_to(base[1:2], (8, 128))
            bz = jnp.broadcast_to(base[2:3], (8, 128))
            tile = tile_from_axes(
                [jnp.square(bx - own_x[a]) for a in range(4)],
                [jnp.square(by - own_y[h]) for h in range(2)],
                jnp.square(bz - own_z),
            )
            high, low = halves(tile)
            span = slice(q * 128, (q + 1) * 128)
            tile_h[u, :, span] = high
            tile_l[u, :, span] = low
            lhs[u, 0:R, span] = jnp.where(low32, high_tab[s0, c0], high_tab[s1, c1])
            lhs[u, R : 2 * R, span] = jnp.where(low32, low_tab[s0, l0], low_tab[s1, l1])

    def couple_apply(u, tile_h, tile_l, lhs):
        both = dot_nt(lhs[u], tile_h[u])
        cross = dot_nt(lhs[u, 0:R], tile_l[u])
        return both[0:R] + both[R : 2 * R] + cross

    def couple_phase(n, new, old):
        for v in range(UNIT // 2):
            pair = (n - 1) * (UNIT // 2) + v + 2
            leaf_couple[pair] = jnp.concatenate(
                [couple_apply(2 * v, *old), couple_apply(2 * v + 1, *old)], axis=1
            )
        for u in range(UNIT):
            leaf = jnp.minimum(n * UNIT + u, LD - 1)
            couple_tiles(leaf, u, *new)

    buffers = ((tile_h0, tile_l0, lhs0), (tile_h1, tile_l1, lhs1))
    for ref in buffers[1]:
        ref[...] = jnp.zeros(ref.shape, ref.dtype)

    def couple_two(m, carry):
        couple_phase(2 * m, buffers[0], buffers[1])
        couple_phase(2 * m + 1, buffers[1], buffers[0])
        return carry

    lax.fori_loop(0, LD // UNIT // 2 + 1, couple_two, 0)


def finish_kernel(
    near_list, near_ref, p_ref, b_ref, prev_ref, next_ref, down_ref, leaf_couple,
    out_ref,
    p8,
):
    device = device_index()
    first_leaf = device * LD

    def finish(c, carry):
        value = (down_ref[c] + leaf_couple[c + 2]).astype(BF16)
        span = pl.ds(pl.multiple_of(c * 256, 256), 256)
        out_ref[:, span] = near_ref[:, span] + dot(
            value, block_diagonal(b_ref[2 * c], b_ref[2 * c + 1])
        )
        return carry

    lax.fori_loop(0, PAIRS, finish, 0, unroll=8)

    p8[...] = jnp.zeros(p8.shape, F32)
    eye = identity()
    for side, (halo_ref, group, step) in enumerate(((prev_ref, 0, -1), (next_ref, GROUPS - 1, 1))):
        origin_z = (device * GROUPS + group).astype(F32)
        p8[side, 0:3, :] = p_ref[:, group * 512 : group * 512 + 512]
        _, own = point_features(p8[side], origin_z)
        own = own_stack(own)
        coords = halo_ref[37].astype(F32) + halo_ref[38].astype(F32) + halo_ref[39].astype(F32)
        for k in range(4):
            far, _ = point_features(coords[8 * k : 8 * k + 8], origin_z)
            far_k = dot_nt(eye, far_stack(far)).astype(BF16)
            tiles = decay(dot(far_k, own)).astype(BF16)
            target = first_leaf + 4 * (group + step) + k
            products = dot(halo_ref[32 + k], tiles)
            for i in range(4):
                leaf = 4 * group + i
                weight = jnp.int32(0)
                for s in range(8):
                    weight = weight + jnp.where(near_list[s, leaf] == target, 1, 0)
                place = slice(leaf * P_SIZE, (leaf + 1) * P_SIZE)
                out_ref[:, place] += products[:, i * P_SIZE : (i + 1) * P_SIZE] * weight.astype(F32)


def shaped(*shape, dtype=F32):
    return jax.ShapeDtypeStruct(shape, dtype)


def vmem():
    return pl.BlockSpec(memory_space=pltpu.VMEM)


def smem():
    return pl.BlockSpec(memory_space=pltpu.SMEM)


PARAMS = pltpu.CompilerParams(vmem_limit_bytes=VMEM_LIMIT)


def per_device(charges, points, basis, transfer, near_list, coupling_list):
    near_rows = near_list.T
    coupling_rows = coupling_list.T
    devices = lax.axis_size("sub") * lax.axis_size("leaf")
    send_next, send_prev, coef, lev, root, shapes = pl.pallas_call(
        leaf_kernel,
        name="leaf_up",
        out_shape=(
            shaped(SEND, R, 128, dtype=BF16),
            shaped(SEND, R, 128, dtype=BF16),
            shaped(PAIRS, R, 128),
            shaped(PAIRS - 1, R, 128),
            shaped(devices, R // 2 + 8, 128),
            shaped(8, 256),
        ),
        in_specs=[vmem()] * 4,
        out_specs=[vmem()] * 6,
        scratch_shapes=[
            pltpu.VMEM((3, LD, 128), F32),
            pltpu.VMEM((256, 128), F32),
            pltpu.VMEM((8, 512), F32),
        ],
        compiler_params=PARAMS,
    )(charges, points, basis, transfer)

    roots = lax.all_to_all(root, AXES, 0, 0, tiled=True)
    forward = [(i, i + 1) for i in range(devices - 1)]
    backward = [(i + 1, i) for i in range(devices - 1)]
    from_prev = lax.ppermute(send_next, AXES, forward)
    from_next = lax.ppermute(send_prev, AXES, backward)

    tasks = pl.pallas_call(
        list_kernel,
        name="near_tasks",
        out_shape=shaped(8, LIST, dtype=jnp.int32),
        in_specs=[vmem()],
        out_specs=vmem(),
        compiler_params=PARAMS,
        cost_estimate=pl.CostEstimate(flops=1 << 24, bytes_accessed=1 << 16, transcendentals=0),
    )(near_rows)
    near = pl.pallas_call(
        near_kernel,
        name="near_field",
        out_shape=shaped(R, LD * P_SIZE),
        in_specs=[smem(), vmem(), vmem()],
        out_specs=vmem(),
        scratch_shapes=[
            pltpu.VMEM((2, 8, 512), F32),
            pltpu.VMEM((2, PAIRS, P_SIZE, 2 * FEATS), BF16),
            pltpu.VMEM((2 * LD, FEATS, P_SIZE), BF16),
            pltpu.VMEM((R, LD * P_SIZE), F32),
            pltpu.VMEM((BATCH // 2, 128, 256), F32),
            pltpu.VMEM((BATCH // 2, 128, 256), F32),
            pltpu.VMEM((BATCH // 2, 128, 256), BF16),
            pltpu.VMEM((BATCH // 2, 128, 256), BF16),
        ],
        compiler_params=PARAMS,
        cost_estimate=pl.CostEstimate(
            flops=2 * 460 * 128 * 128 * 128, bytes_accessed=4 << 20, transcendentals=460 * 32768
        ),
    )(tasks, charges, points)

    down = pl.pallas_call(
        down_kernel,
        name="tree_down",
        out_shape=shaped(PAIRS, R, 128),
        in_specs=[smem()] + [vmem()] * 3,
        out_specs=vmem(),
        scratch_shapes=[
            pltpu.VMEM((PAIRS - 1, R, 128), F32),
            pltpu.VMEM((devices, R, 128), F32),
            pltpu.VMEM((2 * devices, 128), F32),
        ],
        compiler_params=PARAMS,
    )(shapes, lev, transfer, roots)

    stages = [
        pltpu.VMEM((UNIT, K, 512), BF16),
        pltpu.VMEM((UNIT, K, 512), BF16),
        pltpu.VMEM((UNIT, 2 * R, 512), BF16),
    ]
    leaf_couple = pl.pallas_call(
        couple_kernel,
        name="leaf_couple",
        out_shape=shaped(PAIRS + 8, R, 128),
        in_specs=[smem()] * 2 + [vmem()] * 3,
        out_specs=vmem(),
        scratch_shapes=[
            pltpu.VMEM((2, 2 * PAIRS, 8, 128), F32),
            pltpu.VMEM((2, 2 * PAIRS + 1, R, 128), BF16),
            pltpu.VMEM((2, PAIRS + 1, R, 128), BF16),
            pltpu.VMEM((2, 8, 128), F32),
            pltpu.SMEM((2, 8, 128), F32),
            pltpu.SemaphoreType.DMA((2,)),
        ]
        + stages
        + stages,
        compiler_params=PARAMS,
    )(coupling_rows, shapes, from_prev, from_next, coef)

    return pl.pallas_call(
        finish_kernel,
        name="finish",
        out_shape=shaped(R, LD * P_SIZE),
        in_specs=[smem()] + [vmem()] * 7,
        out_specs=vmem(),
        scratch_shapes=[pltpu.VMEM((2, 8, 512), F32)],
        compiler_params=PARAMS,
    )(near_rows, near, points, basis, from_prev, from_next, down, leaf_couple)


def solution(mesh):
    in_specs = (
        P(None, AXES),
        P(None, AXES),
        P(AXES, None, None),
        P(),
        P(AXES, None),
        P(AXES, None),
    )
    return jax.shard_map(
        per_device, mesh=mesh, in_specs=in_specs, out_specs=P(None, AXES), check_vma=False
    )
```

```python
import functools
import math

import jax
import jax.numpy as jnp
from jax import lax
from jax.experimental import pallas as pl
from jax.experimental.pallas import tpu as pltpu
from jax.sharding import PartitionSpec as P

P_SIZE = 128
K = 64
R = 32
LD = 128
PAIRS = LD // 2
GROUPS = LD // 4
TABLE = 257
HALF = LD // 2
NEAR_REACH = 8
FEATS = 64
BATCH = 8
LIST = 896
SEND = 72
SCALE = 0.5 * math.log2(math.e)
NODE = [math.cos((2 * a + 1) * math.pi / 8) for a in range(4)]
AXES = ("leaf", "sub")
F32 = jnp.float32
BF16 = jnp.bfloat16
NT = (((1,), (1,)), ((), ()))
TINY = 1e-30
VMEM_LIMIT = 32 * 1024 * 1024


def lanes(shape):
    return lax.broadcasted_iota(jnp.int32, shape, len(shape) - 1)


def rows(shape):
    return lax.broadcasted_iota(jnp.int32, shape, len(shape) - 2)


def dot(a, b):
    return jnp.dot(a, b, preferred_element_type=F32)


def dot_nt(a, b):
    return lax.dot_general(a, b, NT, preferred_element_type=F32)


def halves(value):
    high = value.astype(BF16)
    return high, (value - high.astype(F32)).astype(BF16)


def thirds(value):
    first = value.astype(BF16).astype(F32)
    rest = value - first
    second = rest.astype(BF16).astype(F32)
    return first, second, rest - second


def unit_node(index):
    return jnp.where(
        index == 0,
        NODE[0],
        jnp.where(index == 1, NODE[1], jnp.where(index == 2, NODE[2], NODE[3])),
    ).astype(F32)


def lane_nodes():
    b = lanes((8, 128)) & 63
    return [unit_node(b >> 4), unit_node((b >> 2) & 3), unit_node(b & 3)]


def row_nodes():
    r = rows((8, 128))
    return [unit_node(r >> 2), unit_node((r >> 2) + 2)], unit_node(r & 3)


def decay(t):
    t = jnp.maximum(t, TINY)
    return jnp.exp2(-(t * lax.rsqrt(t)))


def tile_from_axes(x_sq, y_sq, z_sq):
    yz = [y_sq[0] + z_sq, y_sq[1] + z_sq]
    return decay(jnp.concatenate([x_sq[k // 2] + yz[k % 2] for k in range(8)], axis=0))


def doubled_transfer(t_ref):
    flat = t_ref[...].reshape(2 * K, K)
    return jnp.concatenate([flat, flat], axis=1)


def device_index():
    return lax.axis_index("leaf") * lax.axis_size("sub") + lax.axis_index("sub")


def merge_up(pairs, t_high, t_low):
    n = pairs.shape[0]
    high, low = halves(pairs.reshape(n * R, 128))
    out = dot(high, t_high) + dot(high, t_low) + dot(low, t_high)
    return out.reshape(n, R, 128)


def pair_lanes(clusters):
    n = clusters.shape[0]
    split = clusters.reshape(n // 2, 2, R, 128)
    return jnp.where(lanes((1, R, 128)) < K, split[:, 0], split[:, 1])


def push_down(value, t_high, t_low):
    n = value.shape[0]
    high, low = halves(value.reshape(n * R, 128))
    out = dot_nt(high, t_high) + dot_nt(high, t_low) + dot_nt(low, t_high)
    return out.reshape(n, R, 128)


def children_of(pairs):
    lane = lanes((1, R, 128))
    left = jnp.where(lane < K, pairs, 0.0)
    right = jnp.where(lane < K, 0.0, pairs)
    return jnp.stack([left, right], axis=1).reshape(2 * pairs.shape[0], R, 128)


def merge_shape_rows(left, right):
    lane = lanes(left.shape)
    sep = left - right
    gap = jnp.sqrt(jnp.sum(jnp.where(lane < 3, sep * sep, 0.0), axis=1, keepdims=True))
    radius = jnp.maximum(left, right) + 0.5 * gap
    return jnp.where(lane == 3, radius, jnp.where(lane < 3, 0.5 * (left + right), 0.0))


def sibling_tile(left, right, lane_u, row_y, row_z):
    low = lanes((8, 128)) < K
    alpha = jnp.where(low, left[3], right[3])
    beta = jnp.where(low, right[3], left[3])
    base = [jnp.where(low, left[d] - right[d], right[d] - left[d]) - beta * lane_u[d] for d in range(3)]
    x_sq = [jnp.square(base[0] + alpha * NODE[a]) for a in range(4)]
    y_sq = [jnp.square(base[1] + alpha * row_y[h]) for h in range(2)]
    z_sq = jnp.square(base[2] + alpha * row_z)
    return tile_from_axes(x_sq, y_sq, z_sq)


def sibling_apply(tile, pair):
    low = lanes((R, 128)) < K
    swapped = pltpu.roll(pair, K, 1)
    stacked = jnp.concatenate(
        [jnp.where(low, swapped, 0.0), jnp.where(low, 0.0, swapped)], axis=0
    )
    high, low_part = halves(stacked)
    t_high, t_low = halves(tile)
    t_high = jnp.concatenate([t_high, t_high], axis=0)
    t_low = jnp.concatenate([t_low, t_low], axis=0)
    out = dot_nt(high, t_high) + dot_nt(high, t_low) + dot_nt(low_part, t_high)
    return jnp.where(low, out[:R], out[R:])


LEVEL_OFFSETS = [0, 128, 192, 224, 240, 248, 252, 254]
PAIR_OFFSETS = [0, 0, 32, 48, 56, 60, 62]


def block_diagonal(left, right):
    zero = jnp.zeros(left.shape, left.dtype)
    return jnp.concatenate(
        [jnp.concatenate([left, zero], axis=1), jnp.concatenate([zero, right], axis=1)], axis=0
    )


def leaf_kernel(
    x_ref, p_ref, b_ref, t_ref,
    send_next, send_prev, high_ref, low_ref, lev_ref, root_ref, shape_ref,
    coef, pts, shapes, p8,
):
    origin = (device_index() * GROUPS).astype(F32)
    low32 = lanes((R, 128)) < K

    def leaf_pair(c, carry):
        both = []
        for side in range(2):
            leaf = 2 * c + side
            x = x_ref[:, pl.ds(pl.multiple_of(leaf * P_SIZE, P_SIZE), P_SIZE)]
            weights = b_ref[leaf]
            value = dot_nt(x, jnp.concatenate([weights, weights], axis=0))
            high_ref[leaf], low_ref[leaf] = halves(value)
            both.append(value)
        coef[c] = jnp.where(low32, both[0], both[1])
        return carry

    lax.fori_loop(0, PAIRS, leaf_pair, 0, unroll=8)

    t_high, t_low = halves(doubled_transfer(t_ref))
    pairs = coef[...]
    for level in range(1, 7):
        pairs = pair_lanes(merge_up(pairs, t_high, t_low))
        lev_ref[pl.ds(PAIR_OFFSETS[level], pairs.shape[0])] = pairs
    root = merge_up(pairs, t_high, t_low)[0]

    for i in range(LD):
        for d in range(3):
            pts[d, i : i + 1, :] = p_ref[d : d + 1, i * P_SIZE : (i + 1) * P_SIZE]
    centers, squares = [], 0.0
    for d in range(3):
        coords = (pts[d] - origin if d == 2 else pts[d]) * SCALE
        center = jnp.sum(coords, axis=1, keepdims=True) * (1.0 / P_SIZE)
        centers.append(center)
        squares = squares + jnp.square(coords - center)
    radius = jnp.sqrt(jnp.max(squares, axis=1, keepdims=True))
    lane = lanes((LD, 128))
    shapes[0:LD, :] = jnp.where(
        lane == 0,
        centers[0],
        jnp.where(
            lane == 1,
            centers[1],
            jnp.where(lane == 2, centers[2], jnp.where(lane == 3, radius, 0.0)),
        ),
    )
    count = LD // 2
    for level in range(1, 8):
        source = LEVEL_OFFSETS[level - 1]
        joined = merge_shape_rows(
            shapes[pl.ds(source, count, stride=2), :],
            shapes[pl.ds(source + 1, count, stride=2), :],
        )
        shapes[pl.ds(LEVEL_OFFSETS[level], count), :] = joined
        count //= 2
    shape_rows = jnp.concatenate(
        [jnp.transpose(shapes[0:128, :])[0:8], jnp.transpose(shapes[128:256, :])[0:8]], axis=1
    )
    shape_ref[...] = shape_rows
    low = lanes((R // 2, 128)) < K
    block = jnp.concatenate(
        [
            jnp.where(low, root[0 : R // 2], root[R // 2 : R]),
            jnp.broadcast_to(shapes[254:255, :], (8, 128)),
        ],
        axis=0,
    )
    root_ref[...] = jnp.broadcast_to(block[None], root_ref.shape)

    p8[...] = jnp.zeros((8, 512), F32)
    for send, first_pair, group in ((send_next, PAIRS // 2, GROUPS - 1), (send_prev, 0, 0)):

        def copy_pair(m, carry):
            send[m], send[32 + m] = halves(coef[first_pair + m])
            return carry

        lax.fori_loop(0, PAIRS // 2, copy_pair, 0, unroll=8)
        parts = thirds(shape_rows[:, 0:128])
        send[68] = jnp.concatenate(list(parts) + [jnp.zeros((8, 128), F32)], axis=0).astype(BF16)
        p8[0:3, :] = p_ref[:, group * 512 : group * 512 + 512]
        parts = thirds(p8[...])
        for k in range(4):
            send[64 + k] = x_ref[:, group * 512 + k * P_SIZE : group * 512 + (k + 1) * P_SIZE]
        for part in range(3):
            send[69 + part] = jnp.concatenate(
                [parts[part][:, k * P_SIZE : (k + 1) * P_SIZE] for k in range(4)], axis=0
            ).astype(BF16)


def list_kernel(near_ref, coupling_ref, list_ref, count_ref, index_ref):
    first_leaf = device_index() * LD
    lane8 = lanes((8, 128))
    row8 = rows((8, 128))
    offset = jnp.where(near_ref[...] >= 0, near_ref[...] - first_leaf - lane8, 1000)

    def slots_at(delta):
        return jnp.sum(jnp.where(offset == delta, 1.0, 0.0), axis=0, keepdims=True)

    forward = jnp.concatenate([slots_at(delta) for delta in range(8)], axis=0)
    reverse = jnp.concatenate(
        [jnp.zeros((1, 128), F32)] + [slots_at(-delta) for delta in range(1, 8)], axis=0
    )
    count_ref[0:8, :] = forward
    count_ref[8:16, :] = reverse
    backward = jnp.concatenate(
        [jnp.zeros((1, 128), F32)]
        + [pltpu.roll(reverse[delta : delta + 1, :], 128 - delta, 1) for delta in range(1, 8)],
        axis=0,
    )
    turned = (row8 == 1) & ((lane8 & 3) == 2)
    leaf = lane8.astype(F32)
    other = leaf + row8.astype(F32)
    first = jnp.where(turned, other, leaf)
    second = jnp.where(turned, leaf, other)
    to_first = jnp.where(turned, backward, forward)
    to_second = jnp.where(turned, forward, backward)
    odd = jnp.where(turned, lane8, lane8 + row8) & 1
    wanted = (lane8 + row8 < LD) & (forward + backward > 0.0)
    earlier = jnp.where(rows((128, 128)) < lanes((128, 128)), 1.0, 0.0).astype(BF16)
    place = jnp.full((8, 128), -1.0, F32)
    most = jnp.zeros((1, 1), F32)
    for parity in range(2):
        flags = jnp.where(wanted & (odd == parity), 1.0, 0.0)
        rank = dot(flags.astype(BF16), earlier)
        totals = jnp.sum(flags, axis=1, keepdims=True)
        before = jnp.zeros((1, 1), F32)
        starts = []
        for delta in range(8):
            starts.append(before)
            before = before + totals[delta : delta + 1, :]
        rank = rank + jnp.concatenate(starts, axis=0)
        place = jnp.where(flags > 0.0, 2.0 * rank + (1.0 * BATCH + parity), place)
        most = jnp.maximum(most, before)
    task_rows = []
    for delta in range(8):
        pick = slice(delta, delta + 1)
        task_rows.append(
            jnp.where(
                row8 == 0,
                first[pick],
                jnp.where(
                    row8 == 1,
                    second[pick],
                    jnp.where(
                        row8 == 2, to_first[pick], jnp.where(row8 == 3, to_second[pick], 0.0)
                    ),
                ),
            ).astype(BF16)
        )
    tasks = jnp.concatenate(task_rows, axis=1)
    slot_row = rows((128, 128)).astype(F32)
    for m in range(LIST // 128):
        chosen = jnp.concatenate(
            [
                jnp.where(place[delta : delta + 1, :] == slot_row + 128.0 * m, 1.0, 0.0).astype(BF16)
                for delta in range(8)
            ],
            axis=1,
        )
        part = dot_nt(tasks, chosen)
        part = jnp.where(row8 == 4, 2.0 * most, part)
        list_ref[:, m * 128 : (m + 1) * 128] = part.astype(jnp.int32)

    target = coupling_ref[...]
    reach = target - first_leaf + HALF
    swap = ((reach ^ row8) & 1) * (PAIRS // 2)
    entry = jnp.where(
        reach < HALF,
        LD + (reach >> 1) + swap,
        jnp.where(reach < HALF + LD, reach - HALF, LD + HALF + ((reach - HALF - LD) >> 1) + swap),
    )
    index_ref[0:8, :] = jnp.where(target >= 0, entry, TABLE - 1)
    index_ref[8:16, :] = jnp.where(target >= 0, reach, 0)


def point_features(points8, origin_z):
    row = rows(points8.shape)
    center = jnp.where(row == 2, origin_z + 0.5, 1.0)
    v = jnp.where(row < 3, (points8 - center) * SCALE, 0.0)
    norm = jnp.sum(v * v, axis=0, keepdims=True)
    far = jnp.where(row == 3, norm, jnp.where(row == 4, 1.0, v))
    own = jnp.where(row == 3, 1.0, jnp.where(row == 4, norm, -2.0 * v))
    return far, own


def far_stack(value):
    first, second, third = thirds(value)
    none = jnp.zeros(value.shape, F32)
    return jnp.concatenate(
        [first, first, first, second, second, third, none, none], axis=0
    ).astype(BF16)


def own_stack(value):
    first, second, third = thirds(value)
    none = jnp.zeros(value.shape, F32)
    return jnp.concatenate(
        [first, second, third, first, second, first, none, none], axis=0
    ).astype(BF16)


def identity():
    return jnp.where(rows((128, 128)) == lanes((128, 128)), 1.0, 0.0).astype(BF16)


def near_kernel(
    list_ref, x_ref, p_ref, out_ref,
    p8, far_feat, own_feat, back, tile0, tile1,
):
    first_group = device_index() * GROUPS
    p8[...] = jnp.zeros(p8.shape, F32)
    eye = identity()

    def features(m, carry):
        for v in range(4):
            g = 4 * m + v
            p8[v, 0:3, :] = p_ref[:, pl.ds(pl.multiple_of(g * 512, 512), 512)]
            coords = p8[v]
            origin_z = (first_group + g).astype(F32)
            far, own = point_features(coords, origin_z)
            _, own_up = point_features(coords, origin_z + 1.0)
            far = far_stack(far)
            own = own_stack(own)
            own_up = own_stack(own_up)
            parts = [far[:, k * P_SIZE : (k + 1) * P_SIZE] for k in range(4)]
            turned = dot_nt(eye, jnp.concatenate(parts, axis=0)).astype(BF16)
            far_feat[2 * g] = turned[:, 0:128]
            far_feat[2 * g + 1] = turned[:, 128:256]
            for k in range(4):
                part = slice(k * P_SIZE, (k + 1) * P_SIZE)
                own_feat[4 * g + k] = own[:, part]
                own_feat[LD + 4 * g + k] = own_up[:, part]
        return carry

    lax.fori_loop(0, GROUPS // 4, features, 0)

    out_ref[...] = x_ref[...].astype(F32)
    for ref in (back, tile0, tile1):
        ref[...] = jnp.zeros(ref.shape, ref.dtype)

    total = list_ref[4, 0]
    steps = (total + BATCH - 1) // BATCH + 1
    low = lanes((128, 128)) < K

    def leaf_slice(i):
        return pl.ds(pl.multiple_of(i * P_SIZE, P_SIZE), P_SIZE)

    def phase(n, tile_new, tile_old):
        for u in range(BATCH // 2):
            far, own = [], []
            for h in range(2):
                k = (n + 1) * BATCH + 2 * u + h
                i, j = list_ref[0, k], list_ref[1, k]
                variant = ((j >> 2) - (i >> 2)) * LD
                far.append(far_feat[j >> 1])
                own.append(own_feat[variant + i])
            dist = dot(jnp.where(low, far[0], far[1]), block_diagonal(own[0], own[1]))
            tile_new[u] = decay(dist).astype(BF16)
            for h in range(2):
                k = n * BATCH + 2 * u + h
                i, j = list_ref[0, k], list_ref[1, k]
                tile = tile_old[u, :, h * 128 : h * 128 + 128]
                to_i = dot(x_ref[:, leaf_slice(j)], tile) * list_ref[2, k].astype(F32)
                to_j = dot_nt(x_ref[:, leaf_slice(i)], tile) * list_ref[3, k].astype(F32)
                out_ref[:, leaf_slice(i)] += to_i
                back[:, leaf_slice(j)] += to_j

    def two_phases(m, carry):
        phase(2 * m, tile0, tile1)
        phase(2 * m + 1, tile1, tile0)
        return carry

    lax.fori_loop(0, (steps + 1) // 2, two_phases, 0)
    out_ref[...] += back[...]


def down_kernel(
    shape_ref, lev_ref, t_ref, root_ref, down_ref, couple, pairs_scr, shapes,
):
    lane_u = lane_nodes()
    row_y, row_z = row_nodes()

    def sibling(pair, cluster):
        left = [shape_ref[d, cluster] for d in range(4)]
        right = [shape_ref[d, cluster + 1] for d in range(4)]
        tile = sibling_tile(left, right, lane_u, row_y, row_z)
        couple[pair] = sibling_apply(tile, lev_ref[pair])

    def siblings(m, carry):
        for u in range(21):
            pair = 21 * m + u
            sibling(pair, LD + 2 * pair)
        return carry

    lax.fori_loop(0, 3, siblings, 0)

    t_high, t_low = halves(doubled_transfer(t_ref))
    device = device_index()
    n = root_ref.shape[0]
    low = lanes((R, 128)) < K
    for k in range(n):
        shift = lanes((1, 128)) == 2
        shapes[k : k + 1, :] = (
            root_ref[k, R // 2 : R // 2 + 1, :] + jnp.where(shift, (k * GROUPS) * SCALE, 0.0)
        )
    for k in range(n // 2):
        left = root_ref[2 * k, 0 : R // 2, :]
        right = root_ref[2 * k + 1, 0 : R // 2, :]
        left = jnp.concatenate([left, pltpu.roll(left, K, 1)], axis=0)
        right = jnp.concatenate([pltpu.roll(right, K, 1), right], axis=0)
        pairs_scr[k] = jnp.where(low, left, right)
    source, count, pair_source = 0, n // 2, 0
    levels = []
    while count >= 1:
        levels.append((source, pair_source))
        if count > 1:
            pairs = pair_lanes(merge_up(pairs_scr[pl.ds(pair_source, count)], t_high, t_low))
            pairs_scr[pl.ds(pair_source + count, count // 2)] = pairs
            joined = merge_shape_rows(
                shapes[pl.ds(source, count, stride=2), :],
                shapes[pl.ds(source + 1, count, stride=2), :],
            )
            shapes[pl.ds(source + 2 * count, count), :] = joined
        source += 2 * count
        pair_source += count
        count //= 2
    couples = []
    for level, (source, pair_source) in enumerate(levels):
        pair = device >> (level + 1)
        left_row = shapes[pl.ds(source + 2 * pair, 1), :]
        right_row = shapes[pl.ds(source + 2 * pair + 1, 1), :]
        left = [jnp.broadcast_to(left_row[:, d : d + 1], (8, 128)) for d in range(4)]
        right = [jnp.broadcast_to(right_row[:, d : d + 1], (8, 128)) for d in range(4)]
        tile = sibling_tile(left, right, lane_u, row_y, row_z)
        couples.append(sibling_apply(tile, pairs_scr[pair_source + pair]))
    incoming = None
    for level in reversed(range(len(levels))):
        value = couples[level]
        if incoming is not None:
            value = value + push_down(incoming[None], t_high, t_low)[0]
        side = (device >> level) & 1
        keep_low = jnp.where(low, 1, 0) == (1 - side)
        incoming = jnp.where(keep_low, value, 0.0)
    value = couple[pl.ds(PAIR_OFFSETS[6], 1)] + push_down(incoming[None], t_high, t_low)
    for level in range(5, 0, -1):
        n = PAIRS >> level
        value = couple[pl.ds(PAIR_OFFSETS[level], n)] + push_down(
            children_of(value), t_high, t_low
        )
    down_ref[...] = push_down(children_of(value), t_high, t_low)


UNIT = 4


def couple_kernel(
    entries, shape_ref, prev_ref, next_ref, high_ref, low_ref,
    leaf_couple,
    shape_tab, high_tab, low_tab, halo_rows, halo_shape, sems,
    tile_h0, tile_l0, lhs0, tile_h1, tile_l1, lhs1,
):
    copies = [
        pltpu.make_async_copy(high_ref, high_tab.at[0:LD], sems.at[2]),
        pltpu.make_async_copy(low_ref, low_tab.at[0:LD], sems.at[3]),
    ]
    for k, ref in enumerate((prev_ref, next_ref)):
        parts = ref[68].astype(F32)
        halo_rows[k] = parts[0:8] + parts[8:16] + parts[16:24]
        copies.append(pltpu.make_async_copy(halo_rows.at[k], halo_shape.at[k], sems.at[k]))
    for copy in copies:
        copy.start()
    low32 = lanes((R, 128)) < K
    lane_u = lane_nodes()
    row8 = rows((8, 128))
    low8 = lanes((8, 128)) < K

    def shape_rows(read, k, shift):
        return jnp.where(
            row8 == 0,
            read(0, k),
            jnp.where(row8 == 1, read(1, k), jnp.where(row8 == 2, read(2, k) + shift, read(3, k))),
        )

    def own_nodes(m, carry):
        shape_tab[HALF + m] = shape_rows(lambda d, k: shape_ref[d, k], m, 0.0)
        return carry

    lax.fori_loop(0, LD, own_nodes, 0, unroll=8)
    for copy in copies[2:]:
        copy.wait()
    for side, ref in enumerate((prev_ref, next_ref)):
        first = LD + side * HALF

        def halo_pair(m, carry):
            def read(d, k):
                return halo_shape[side, d, k]

            source = HALF if side == 0 else 0
            place = 0 if side == 0 else HALF + LD
            shift = (2.0 * side - 1.0) * GROUPS * SCALE
            for h in range(2):
                shape_tab[place + 2 * m + h] = shape_rows(read, source + 2 * m + h, shift)
            for tab, place in ((high_tab, m), (low_tab, 32 + m)):
                pair = ref[place]
                tab[first + m] = pair
                tab[first + PAIRS // 2 + m] = pltpu.roll(pair.astype(F32), K, 1).astype(BF16)
            return carry

        lax.fori_loop(0, PAIRS // 2, halo_pair, 0, unroll=4)
    high_tab[TABLE - 1] = jnp.zeros((R, 128), BF16)
    low_tab[TABLE - 1] = jnp.zeros((R, 128), BF16)
    for copy in copies[:2]:
        copy.wait()

    row_y, row_z = row_nodes()

    def couple_tiles(pair, u, tile_h, tile_l, lhs):
        leaves = (2 * pair, 2 * pair + 1)
        own = jnp.where(low8, shape_tab[HALF + leaves[0]], shape_tab[HALF + leaves[1]])
        radius = jnp.broadcast_to(own[3:4], (8, 128))
        own = [jnp.broadcast_to(own[d : d + 1], (8, 128)) + radius * lane_u[d] for d in range(3)]
        for s in range(8):
            e0, e1 = entries[8 + s, leaves[0]], entries[8 + s, leaves[1]]
            far = jnp.where(low8, shape_tab[e0], shape_tab[e1])
            reach = jnp.broadcast_to(far[3:4], (8, 128))
            gap = [own[d] - jnp.broadcast_to(far[d : d + 1], (8, 128)) for d in range(3)]
            tile = tile_from_axes(
                [jnp.square(gap[0] - reach * NODE[b]) for b in range(4)],
                [jnp.square(gap[1] - reach * row_y[h]) for h in range(2)],
                jnp.square(gap[2] - reach * row_z),
            )
            high, low = halves(tile)
            tile_h[u, s * K : (s + 1) * K, :] = high
            tile_l[u, s * K : (s + 1) * K, :] = low
        for q in range(4):
            span = slice(q * 128, (q + 1) * 128)
            for h in range(2):
                e0, e1 = entries[2 * q, leaves[h]], entries[2 * q + 1, leaves[h]]
                lhs[u, h * R : (h + 1) * R, span] = jnp.where(low32, high_tab[e0], high_tab[e1])
                lhs[u, (2 + h) * R : (3 + h) * R, span] = jnp.where(
                    low32, low_tab[e0], low_tab[e1]
                )

    def couple_apply(u, tile_h, tile_l, lhs):
        both = dot(lhs[u], tile_h[u])
        both = both[0 : 2 * R] + both[2 * R : 4 * R] + dot(lhs[u, 0 : 2 * R], tile_l[u])
        return jnp.where(low32, both[0:R], both[R : 2 * R])

    def couple_phase(n, new, old):
        for u in range(UNIT):
            leaf_couple[(n - 1) * UNIT + u + UNIT] = couple_apply(u, *old)
            couple_tiles(jnp.minimum(n * UNIT + u, PAIRS - 1), u, *new)

    buffers = ((tile_h0, tile_l0, lhs0), (tile_h1, tile_l1, lhs1))
    for ref in buffers[1]:
        ref[...] = jnp.zeros(ref.shape, ref.dtype)

    def couple_two(m, carry):
        couple_phase(2 * m, buffers[0], buffers[1])
        couple_phase(2 * m + 1, buffers[1], buffers[0])
        return carry

    lax.fori_loop(0, PAIRS // UNIT // 2 + 1, couple_two, 0)


def finish_kernel(
    counts, near_ref, p_ref, b_ref, prev_ref, next_ref, down_ref, leaf_couple,
    out_ref,
    p8, coords,
):
    device = device_index()

    def finish(c, carry):
        value = (down_ref[c] + leaf_couple[c + UNIT]).astype(BF16)
        span = pl.ds(pl.multiple_of(c * 256, 256), 256)
        out_ref[:, span] = near_ref[:, span] + dot(
            value, block_diagonal(b_ref[2 * c], b_ref[2 * c + 1])
        )
        return carry

    lax.fori_loop(0, PAIRS, finish, 0, unroll=8)

    p8[...] = jnp.zeros(p8.shape, F32)
    eye = identity()
    sides = ((prev_ref, 0), (next_ref, GROUPS - 1))
    for side, (halo_ref, group) in enumerate(sides):
        p8[side, 0:3, :] = p_ref[:, group * 512 : group * 512 + 512]
        coords[side] = halo_ref[69].astype(F32) + halo_ref[70].astype(F32) + halo_ref[71].astype(F32)

    def edge(k, carry):
        for side, (halo_ref, group) in enumerate(sides):
            origin_z = (device * GROUPS + group).astype(F32)
            _, own = point_features(p8[side], origin_z)
            far, _ = point_features(coords[side, pl.ds(pl.multiple_of(8 * k, 8), 8), :], origin_z)
            far = dot_nt(eye, far_stack(far)).astype(BF16)
            tiles = decay(dot(far, own_stack(own))).astype(BF16)
            products = dot(halo_ref[64 + k], tiles)
            for i in range(4):
                delta = (4 + i - k) if side == 0 else (4 + k - i)
                weight = counts[8 * (1 - side) + jnp.clip(delta, 0, 7), 4 * group + i]
                place = slice((4 * group + i) * P_SIZE, (4 * group + i + 1) * P_SIZE)
                out_ref[:, place] += products[:, i * P_SIZE : (i + 1) * P_SIZE] * weight
        return carry

    lax.fori_loop(0, 4, edge, 0)


def shaped(*shape, dtype=F32):
    return jax.ShapeDtypeStruct(shape, dtype)


def vmem():
    return pl.BlockSpec(memory_space=pltpu.VMEM)


def smem():
    return pl.BlockSpec(memory_space=pltpu.SMEM)


PARAMS = pltpu.CompilerParams(vmem_limit_bytes=VMEM_LIMIT)


def per_device(charges, points, basis, transfer, near_list, coupling_list):
    near_rows = near_list.T
    coupling_rows = coupling_list.T
    devices = lax.axis_size("sub") * lax.axis_size("leaf")
    send_next, send_prev, high, low, lev, root, shapes = pl.pallas_call(
        leaf_kernel,
        name="leaf_up",
        out_shape=(
            shaped(SEND, R, 128, dtype=BF16),
            shaped(SEND, R, 128, dtype=BF16),
            shaped(LD, R, 128, dtype=BF16),
            shaped(LD, R, 128, dtype=BF16),
            shaped(PAIRS - 1, R, 128),
            shaped(devices, R // 2 + 8, 128),
            shaped(8, 256),
        ),
        in_specs=[vmem()] * 4,
        out_specs=[vmem()] * 7,
        scratch_shapes=[
            pltpu.VMEM((PAIRS, R, 128), F32),
            pltpu.VMEM((3, LD, 128), F32),
            pltpu.VMEM((256, 128), F32),
            pltpu.VMEM((8, 512), F32),
        ],
        compiler_params=PARAMS,
    )(charges, points, basis, transfer)

    roots = lax.all_to_all(root, AXES, 0, 0, tiled=True)
    forward = [(i, i + 1) for i in range(devices - 1)]
    backward = [(i + 1, i) for i in range(devices - 1)]
    from_prev = lax.ppermute(send_next, AXES, forward)
    from_next = lax.ppermute(send_prev, AXES, backward)

    tasks, counts, entries = pl.pallas_call(
        list_kernel,
        name="lists",
        out_shape=(
            shaped(8, LIST, dtype=jnp.int32),
            shaped(16, 128),
            shaped(16, 128, dtype=jnp.int32),
        ),
        in_specs=[vmem()] * 2,
        out_specs=[vmem()] * 3,
        compiler_params=PARAMS,
        cost_estimate=pl.CostEstimate(flops=1 << 24, bytes_accessed=1 << 16, transcendentals=0),
    )(near_rows, coupling_rows)
    near = pl.pallas_call(
        near_kernel,
        name="near_field",
        out_shape=shaped(R, LD * P_SIZE),
        in_specs=[smem(), vmem(), vmem()],
        out_specs=vmem(),
        scratch_shapes=[
            pltpu.VMEM((4, 8, 512), F32),
            pltpu.VMEM((PAIRS, P_SIZE, 2 * FEATS), BF16),
            pltpu.VMEM((2 * LD, FEATS, P_SIZE), BF16),
            pltpu.VMEM((R, LD * P_SIZE), F32),
            pltpu.VMEM((BATCH // 2, 128, 256), BF16),
            pltpu.VMEM((BATCH // 2, 128, 256), BF16),
        ],
        compiler_params=PARAMS,
        cost_estimate=pl.CostEstimate(
            flops=2 * 460 * 128 * 128 * 128, bytes_accessed=4 << 20, transcendentals=460 * 32768
        ),
    )(tasks, charges, points)

    down = pl.pallas_call(
        down_kernel,
        name="tree_down",
        out_shape=shaped(PAIRS, R, 128),
        in_specs=[smem()] + [vmem()] * 3,
        out_specs=vmem(),
        scratch_shapes=[
            pltpu.VMEM((PAIRS - 1, R, 128), F32),
            pltpu.VMEM((devices, R, 128), F32),
            pltpu.VMEM((2 * devices, 128), F32),
        ],
        compiler_params=PARAMS,
    )(shapes, lev, transfer, roots)

    stages = [
        pltpu.VMEM((UNIT, 512, 128), BF16),
        pltpu.VMEM((UNIT, 512, 128), BF16),
        pltpu.VMEM((UNIT, 4 * R, 512), BF16),
    ]
    leaf_couple = pl.pallas_call(
        couple_kernel,
        name="leaf_couple",
        out_shape=shaped(PAIRS + 2 * UNIT, R, 128),
        in_specs=[smem()] * 2 + [vmem()] * 2 + [pl.BlockSpec(memory_space=pl.ANY)] * 2,
        out_specs=vmem(),
        scratch_shapes=[
            pltpu.VMEM((2 * LD, 8, 128), F32),
            pltpu.VMEM((TABLE, R, 128), BF16),
            pltpu.VMEM((TABLE, R, 128), BF16),
            pltpu.VMEM((2, 8, 128), F32),
            pltpu.SMEM((2, 8, 128), F32),
            pltpu.SemaphoreType.DMA((4,)),
        ]
        + stages
        + stages,
        compiler_params=PARAMS,
    )(entries, shapes, from_prev, from_next, high, low)

    return pl.pallas_call(
        finish_kernel,
        name="finish",
        out_shape=shaped(R, LD * P_SIZE),
        in_specs=[smem()] + [vmem()] * 7,
        out_specs=vmem(),
        scratch_shapes=[pltpu.VMEM((2, 8, 512), F32), pltpu.VMEM((2, R, 128), F32)],
        compiler_params=PARAMS,
    )(counts, near, points, basis, from_prev, from_next, down, leaf_couple)


def solution(mesh):
    in_specs = (
        P(None, AXES),
        P(None, AXES),
        P(AXES, None, None),
        P(),
        P(AXES, None),
        P(AXES, None),
    )
    return jax.shard_map(
        per_device, mesh=mesh, in_specs=in_specs, out_specs=P(None, AXES), check_vma=False
    )
```

```python
import functools
import math

import jax
import jax.numpy as jnp
from jax import lax
from jax.experimental import pallas as pl
from jax.experimental.pallas import tpu as pltpu
from jax.sharding import PartitionSpec as P

P_SIZE = 128
K = 64
R = 32
LD = 128
PAIRS = LD // 2
GROUPS = LD // 4
TABLE = 257
HALF = LD // 2
NEAR_REACH = 8
FEATS = 64
BATCH = 16
LIST = 896
SEND = 72
SCALE = 0.5 * math.log2(math.e)
NODE = [math.cos((2 * a + 1) * math.pi / 8) for a in range(4)]
AXES = ("leaf", "sub")
F32 = jnp.float32
BF16 = jnp.bfloat16
NT = (((1,), (1,)), ((), ()))
TINY = 1e-30
VMEM_LIMIT = 56 * 1024 * 1024


def lanes(shape):
    return lax.broadcasted_iota(jnp.int32, shape, len(shape) - 1)


def rows(shape):
    return lax.broadcasted_iota(jnp.int32, shape, len(shape) - 2)


def dot(a, b):
    return jnp.dot(a, b, preferred_element_type=F32)


def dot_nt(a, b):
    return lax.dot_general(a, b, NT, preferred_element_type=F32)


def halves(value):
    high = value.astype(BF16)
    return high, (value - high.astype(F32)).astype(BF16)


def thirds(value):
    first = value.astype(BF16).astype(F32)
    rest = value - first
    second = rest.astype(BF16).astype(F32)
    return first, second, rest - second


def unit_node(index):
    return jnp.where(
        index == 0,
        NODE[0],
        jnp.where(index == 1, NODE[1], jnp.where(index == 2, NODE[2], NODE[3])),
    ).astype(F32)


def lane_nodes():
    b = lanes((8, 128)) & 63
    return [unit_node(b >> 4), unit_node((b >> 2) & 3), unit_node(b & 3)]


def row_nodes():
    r = rows((8, 128))
    return [unit_node(r >> 2), unit_node((r >> 2) + 2)], unit_node(r & 3)


def decay(t):
    t = jnp.maximum(t, TINY)
    return jnp.exp2(-(t * lax.rsqrt(t)))


def tile_from_axes(x_sq, y_sq, z_sq):
    yz = [y_sq[0] + z_sq, y_sq[1] + z_sq]
    return decay(jnp.concatenate([x_sq[k // 2] + yz[k % 2] for k in range(8)], axis=0))


def doubled_transfer(t_ref):
    flat = t_ref[...].reshape(2 * K, K)
    return jnp.concatenate([flat, flat], axis=1)


def device_index():
    return lax.axis_index("leaf") * lax.axis_size("sub") + lax.axis_index("sub")


def merge_up(pairs, t_high, t_low):
    n = pairs.shape[0]
    high, low = halves(pairs.reshape(n * R, 128))
    out = dot(high, t_high) + dot(high, t_low) + dot(low, t_high)
    return out.reshape(n, R, 128)


def pair_lanes(clusters):
    n = clusters.shape[0]
    split = clusters.reshape(n // 2, 2, R, 128)
    return jnp.where(lanes((1, R, 128)) < K, split[:, 0], split[:, 1])


def push_down(value, t_high, t_low):
    n = value.shape[0]
    high, low = halves(value.reshape(n * R, 128))
    out = dot_nt(high, t_high) + dot_nt(high, t_low) + dot_nt(low, t_high)
    return out.reshape(n, R, 128)


def children_of(pairs):
    lane = lanes((1, R, 128))
    left = jnp.where(lane < K, pairs, 0.0)
    right = jnp.where(lane < K, 0.0, pairs)
    return jnp.stack([left, right], axis=1).reshape(2 * pairs.shape[0], R, 128)


def merge_shape_rows(left, right):
    lane = lanes(left.shape)
    sep = left - right
    gap = jnp.sqrt(jnp.sum(jnp.where(lane < 3, sep * sep, 0.0), axis=1, keepdims=True))
    radius = jnp.maximum(left, right) + 0.5 * gap
    return jnp.where(lane == 3, radius, jnp.where(lane < 3, 0.5 * (left + right), 0.0))


def sibling_tile(left, right, lane_u, row_y, row_z):
    low = lanes((8, 128)) < K
    alpha = jnp.where(low, left[3], right[3])
    beta = jnp.where(low, right[3], left[3])
    base = [jnp.where(low, left[d] - right[d], right[d] - left[d]) - beta * lane_u[d] for d in range(3)]
    x_sq = [jnp.square(base[0] + alpha * NODE[a]) for a in range(4)]
    y_sq = [jnp.square(base[1] + alpha * row_y[h]) for h in range(2)]
    z_sq = jnp.square(base[2] + alpha * row_z)
    return tile_from_axes(x_sq, y_sq, z_sq)


def sibling_apply(tile, pair):
    low = lanes((R, 128)) < K
    swapped = pltpu.roll(pair, K, 1)
    stacked = jnp.concatenate(
        [jnp.where(low, swapped, 0.0), jnp.where(low, 0.0, swapped)], axis=0
    )
    high, low_part = halves(stacked)
    t_high, t_low = halves(tile)
    t_high = jnp.concatenate([t_high, t_high], axis=0)
    t_low = jnp.concatenate([t_low, t_low], axis=0)
    out = dot_nt(high, t_high) + dot_nt(high, t_low) + dot_nt(low_part, t_high)
    return jnp.where(low, out[:R], out[R:])


LEVEL_OFFSETS = [0, 128, 192, 224, 240, 248, 252, 254]
PAIR_OFFSETS = [0, 0, 32, 48, 56, 60, 62]


def block_diagonal(left, right):
    zero = jnp.zeros(left.shape, left.dtype)
    return jnp.concatenate(
        [jnp.concatenate([left, zero], axis=1), jnp.concatenate([zero, right], axis=1)], axis=0
    )


def leaf_kernel(
    x_ref, p_ref, b_ref, t_ref,
    send_next, send_prev, high_ref, low_ref, lev_ref, root_ref, shape_ref,
    coef, pts, shapes, p8,
):
    origin = (device_index() * GROUPS).astype(F32)
    low32 = lanes((R, 128)) < K

    def leaf_pairs(m, carry):
        values = []
        for v in range(16):
            leaf = 16 * m + v
            x = x_ref[:, pl.ds(pl.multiple_of(leaf * P_SIZE, P_SIZE), P_SIZE)]
            weights = b_ref[leaf]
            values.append(dot_nt(x, jnp.concatenate([weights, weights], axis=0)))
        for v in range(16):
            high_ref[16 * m + v], low_ref[16 * m + v] = halves(values[v])
        for v in range(8):
            coef[8 * m + v] = jnp.where(low32, values[2 * v], values[2 * v + 1])
        return carry

    lax.fori_loop(0, LD // 16, leaf_pairs, 0)

    t_high, t_low = halves(doubled_transfer(t_ref))
    pairs = coef[...]
    for level in range(1, 7):
        pairs = pair_lanes(merge_up(pairs, t_high, t_low))
        lev_ref[pl.ds(PAIR_OFFSETS[level], pairs.shape[0])] = pairs
    root = merge_up(pairs, t_high, t_low)[0]

    for i in range(LD):
        for d in range(3):
            pts[d, i : i + 1, :] = p_ref[d : d + 1, i * P_SIZE : (i + 1) * P_SIZE]
    centers, squares = [], 0.0
    for d in range(3):
        coords = (pts[d] - origin if d == 2 else pts[d]) * SCALE
        center = jnp.sum(coords, axis=1, keepdims=True) * (1.0 / P_SIZE)
        centers.append(center)
        squares = squares + jnp.square(coords - center)
    radius = jnp.sqrt(jnp.max(squares, axis=1, keepdims=True))
    lane = lanes((LD, 128))
    shapes[0:LD, :] = jnp.where(
        lane == 0,
        centers[0],
        jnp.where(
            lane == 1,
            centers[1],
            jnp.where(lane == 2, centers[2], jnp.where(lane == 3, radius, 0.0)),
        ),
    )
    count = LD // 2
    for level in range(1, 8):
        source = LEVEL_OFFSETS[level - 1]
        joined = merge_shape_rows(
            shapes[pl.ds(source, count, stride=2), :],
            shapes[pl.ds(source + 1, count, stride=2), :],
        )
        shapes[pl.ds(LEVEL_OFFSETS[level], count), :] = joined
        count //= 2
    shape_rows = jnp.concatenate(
        [jnp.transpose(shapes[0:128, :])[0:8], jnp.transpose(shapes[128:256, :])[0:8]], axis=1
    )
    shape_ref[...] = shape_rows
    low = lanes((R // 2, 128)) < K
    block = jnp.concatenate(
        [
            jnp.where(low, root[0 : R // 2], root[R // 2 : R]),
            jnp.broadcast_to(shapes[254:255, :], (8, 128)),
        ],
        axis=0,
    )
    root_ref[...] = jnp.broadcast_to(block[None], root_ref.shape)

    p8[...] = jnp.zeros((8, 512), F32)
    for send, first_pair, group in ((send_next, PAIRS // 2, GROUPS - 1), (send_prev, 0, 0)):

        def copy_pairs(m, carry):
            parts = [halves(coef[first_pair + 8 * m + v]) for v in range(8)]
            for v in range(8):
                send[8 * m + v], send[32 + 8 * m + v] = parts[v]
            return carry

        lax.fori_loop(0, PAIRS // 16, copy_pairs, 0)
        parts = thirds(shape_rows[:, 0:128])
        send[68] = jnp.concatenate(list(parts) + [jnp.zeros((8, 128), F32)], axis=0).astype(BF16)
        p8[0:3, :] = p_ref[:, group * 512 : group * 512 + 512]
        parts = thirds(p8[...])
        for k in range(4):
            send[64 + k] = x_ref[:, group * 512 + k * P_SIZE : group * 512 + (k + 1) * P_SIZE]
        for part in range(3):
            send[69 + part] = jnp.concatenate(
                [parts[part][:, k * P_SIZE : (k + 1) * P_SIZE] for k in range(4)], axis=0
            ).astype(BF16)


def list_kernel(near_ref, coupling_ref, list_ref, count_ref, index_ref):
    first_leaf = device_index() * LD
    lane8 = lanes((8, 128))
    row8 = rows((8, 128))
    offset = jnp.where(near_ref[...] >= 0, near_ref[...] - first_leaf - lane8, 1000)

    def slots_at(delta):
        return jnp.sum(jnp.where(offset == delta, 1.0, 0.0), axis=0, keepdims=True)

    forward = jnp.concatenate([slots_at(delta) for delta in range(8)], axis=0)
    reverse = jnp.concatenate(
        [jnp.zeros((1, 128), F32)] + [slots_at(-delta) for delta in range(1, 8)], axis=0
    )
    count_ref[0:8, :] = forward
    count_ref[8:16, :] = reverse
    backward = jnp.concatenate(
        [jnp.zeros((1, 128), F32)]
        + [pltpu.roll(reverse[delta : delta + 1, :], 128 - delta, 1) for delta in range(1, 8)],
        axis=0,
    )
    turned = (row8 == 1) & ((lane8 & 3) == 2)
    leaf = lane8.astype(F32)
    other = leaf + row8.astype(F32)
    first = jnp.where(turned, other, leaf)
    second = jnp.where(turned, leaf, other)
    to_first = jnp.where(turned, backward, forward)
    to_second = jnp.where(turned, forward, backward)
    odd = jnp.where(turned, lane8, lane8 + row8) & 1
    wanted = (lane8 + row8 < LD) & (forward + backward > 0.0)
    earlier = jnp.where(rows((128, 128)) < lanes((128, 128)), 1.0, 0.0).astype(BF16)
    place = jnp.full((8, 128), -1.0, F32)
    most = jnp.zeros((1, 1), F32)
    for parity in range(2):
        flags = jnp.where(wanted & (odd == parity), 1.0, 0.0)
        rank = dot(flags.astype(BF16), earlier)
        totals = jnp.sum(flags, axis=1, keepdims=True)
        before = jnp.zeros((1, 1), F32)
        starts = []
        for delta in range(8):
            starts.append(before)
            before = before + totals[delta : delta + 1, :]
        rank = rank + jnp.concatenate(starts, axis=0)
        place = jnp.where(flags > 0.0, 2.0 * rank + (1.0 * BATCH + parity), place)
        most = jnp.maximum(most, before)
    task_rows = []
    for delta in range(8):
        pick = slice(delta, delta + 1)
        task_rows.append(
            jnp.where(
                row8 == 0,
                first[pick],
                jnp.where(
                    row8 == 1,
                    second[pick],
                    jnp.where(
                        row8 == 2, to_first[pick], jnp.where(row8 == 3, to_second[pick], 0.0)
                    ),
                ),
            ).astype(BF16)
        )
    tasks = jnp.concatenate(task_rows, axis=1)
    slot_row = rows((128, 128)).astype(F32)
    for m in range(LIST // 128):
        chosen = jnp.concatenate(
            [
                jnp.where(place[delta : delta + 1, :] == slot_row + 128.0 * m, 1.0, 0.0).astype(BF16)
                for delta in range(8)
            ],
            axis=1,
        )
        part = dot_nt(tasks, chosen)
        part = jnp.where(row8 == 4, 2.0 * most, part)
        list_ref[:, m * 128 : (m + 1) * 128] = part.astype(jnp.int32)

    target = coupling_ref[...]
    reach = target - first_leaf + HALF
    swap = ((reach ^ row8) & 1) * (PAIRS // 2)
    entry = jnp.where(
        reach < HALF,
        LD + (reach >> 1) + swap,
        jnp.where(reach < HALF + LD, reach - HALF, LD + HALF + ((reach - HALF - LD) >> 1) + swap),
    )
    index_ref[0:8, :] = jnp.where(target >= 0, entry, TABLE - 1)
    index_ref[8:16, :] = jnp.where(target >= 0, reach, 0)


def point_features(points8, origin_z):
    row = rows(points8.shape)
    center = jnp.where(row == 2, origin_z + 0.5, 1.0)
    v = jnp.where(row < 3, (points8 - center) * SCALE, 0.0)
    norm = jnp.sum(v * v, axis=0, keepdims=True)
    far = jnp.where(row == 3, norm, jnp.where(row == 4, 1.0, v))
    own = jnp.where(row == 3, 1.0, jnp.where(row == 4, norm, -2.0 * v))
    return far, own


def far_stack(value):
    first, second, third = thirds(value)
    none = jnp.zeros(value.shape, F32)
    return jnp.concatenate(
        [first, first, first, second, second, third, none, none], axis=0
    ).astype(BF16)


def own_stack(value):
    first, second, third = thirds(value)
    none = jnp.zeros(value.shape, F32)
    return jnp.concatenate(
        [first, second, third, first, second, first, none, none], axis=0
    ).astype(BF16)


def identity():
    return jnp.where(rows((128, 128)) == lanes((128, 128)), 1.0, 0.0).astype(BF16)


def near_kernel(
    list_ref, x_ref, p_ref, out_ref,
    p8, far_feat, own_feat, part1, part2, part3, tile0, tile1,
):
    first_group = device_index() * GROUPS
    p8[...] = jnp.zeros(p8.shape, F32)
    eye = identity()

    def features(m, carry):
        loaded = [p_ref[:, pl.ds(pl.multiple_of((4 * m + v) * 512, 512), 512)] for v in range(4)]
        for v in range(4):
            p8[v, 0:3, :] = loaded[v]
        made = []
        for v in range(4):
            coords = p8[v]
            origin_z = (first_group + 4 * m + v).astype(F32)
            far, own = point_features(coords, origin_z)
            _, own_up = point_features(coords, origin_z + 1.0)
            far = far_stack(far)
            parts = [far[:, k * P_SIZE : (k + 1) * P_SIZE] for k in range(4)]
            turned = dot_nt(eye, jnp.concatenate(parts, axis=0)).astype(BF16)
            made.append((turned, own_stack(own), own_stack(own_up)))
        for v in range(4):
            g = 4 * m + v
            turned, own, own_up = made[v]
            far_feat[2 * g] = turned[:, 0:128]
            far_feat[2 * g + 1] = turned[:, 128:256]
            for k in range(4):
                part = slice(k * P_SIZE, (k + 1) * P_SIZE)
                own_feat[4 * g + k] = own[:, part]
                own_feat[LD + 4 * g + k] = own_up[:, part]
        return carry

    lax.fori_loop(0, GROUPS // 4, features, 0)

    out_ref[...] = x_ref[...].astype(F32)
    parts = (out_ref, part1, part2, part3)
    for ref in (part1, part2, part3, tile0, tile1):
        ref[...] = jnp.zeros(ref.shape, ref.dtype)

    total = list_ref[4, 0]
    steps = (total + BATCH - 1) // BATCH + 1
    low = lanes((128, 128)) < K

    def leaf_slice(i):
        return pl.ds(pl.multiple_of(i * P_SIZE, P_SIZE), P_SIZE)

    def phase(n, tile_new, tile_old):
        far, own, sources, updates = [], [], [], []
        for u in range(BATCH):
            k = (n + 1) * BATCH + u
            i, j = list_ref[0, k], list_ref[1, k]
            variant = ((j >> 2) - (i >> 2)) * LD
            far.append(far_feat[j >> 1])
            own.append(own_feat[variant + i])
        for u in range(BATCH):
            k = n * BATCH + u
            i, j = list_ref[0, k], list_ref[1, k]
            sources.append((x_ref[:, leaf_slice(j)], x_ref[:, leaf_slice(i)]))
        tiles = []
        for u in range(BATCH // 2):
            pick = jnp.where(low, far[2 * u], far[2 * u + 1])
            dist = dot(pick, block_diagonal(own[2 * u], own[2 * u + 1]))
            tiles.append(decay(dist).astype(BF16))
            for h in range(2):
                k = n * BATCH + 2 * u + h
                tile = tile_old[u, :, h * 128 : h * 128 + 128]
                x_j, x_i = sources[2 * u + h]
                updates.append(
                    (
                        dot(x_j, tile) * list_ref[2, k].astype(F32),
                        dot_nt(x_i, tile) * list_ref[3, k].astype(F32),
                    )
                )
        for u in range(BATCH // 2):
            tile_new[u] = tiles[u]
        for u in range(BATCH // 2):
            places, sums = [], []
            for h in range(2):
                k = n * BATCH + 2 * u + h
                for side in range(2):
                    place = leaf_slice(list_ref[side, k])
                    places.append(place)
                    sums.append(parts[2 * h + side][:, place] + updates[2 * u + h][side])
            for ref, place, value in zip(parts, places, sums):
                ref[:, place] = value

    def two_phases(m, carry):
        phase(2 * m, tile0, tile1)
        phase(2 * m + 1, tile1, tile0)
        return carry

    lax.fori_loop(0, (steps + 1) // 2, two_phases, 0)

    def total_up(m, carry):
        place = pl.ds(pl.multiple_of(m * 1024, 1024), 1024)
        out_ref[:, place] = (out_ref[:, place] + part1[:, place]) + (
            part2[:, place] + part3[:, place]
        )
        return carry

    lax.fori_loop(0, LD * P_SIZE // 1024, total_up, 0)


def down_kernel(
    shape_ref, lev_ref, t_ref, root_ref, down_ref, couple, pairs_scr, shapes,
):
    lane_u = lane_nodes()
    row_y, row_z = row_nodes()

    def siblings(m, carry):
        loaded = [lev_ref[9 * m + u] for u in range(9)]
        values = []
        for u in range(9):
            cluster = LD + 2 * (9 * m + u)
            left = [shape_ref[d, cluster] for d in range(4)]
            right = [shape_ref[d, cluster + 1] for d in range(4)]
            tile = sibling_tile(left, right, lane_u, row_y, row_z)
            values.append(sibling_apply(tile, loaded[u]))
        for u in range(9):
            couple[9 * m + u] = values[u]
        return carry

    lax.fori_loop(0, 7, siblings, 0)

    t_high, t_low = halves(doubled_transfer(t_ref))
    device = device_index()
    n = root_ref.shape[0]
    low = lanes((R, 128)) < K
    shift = lanes((1, 128)) == 2
    for k in range(n):
        shapes[k : k + 1, :] = root_ref[k, R // 2 : R // 2 + 1, :] + jnp.where(
            shift, (k * GROUPS) * SCALE, 0.0
        )
    for k in range(n // 2):
        left = root_ref[2 * k, 0 : R // 2, :]
        right = root_ref[2 * k + 1, 0 : R // 2, :]
        left = jnp.concatenate([left, pltpu.roll(left, K, 1)], axis=0)
        right = jnp.concatenate([pltpu.roll(right, K, 1), right], axis=0)
        pairs_scr[k] = jnp.where(low, left, right)
    source, count, pair_source = 0, n // 2, 0
    levels = []
    while count >= 1:
        levels.append((source, pair_source))
        if count > 1:
            pairs = pair_lanes(merge_up(pairs_scr[pl.ds(pair_source, count)], t_high, t_low))
            pairs_scr[pl.ds(pair_source + count, count // 2)] = pairs
            joined = merge_shape_rows(
                shapes[pl.ds(source, count, stride=2), :],
                shapes[pl.ds(source + 1, count, stride=2), :],
            )
            shapes[pl.ds(source + 2 * count, count), :] = joined
        source += 2 * count
        pair_source += count
        count //= 2
    couples = []
    for level, (source, pair_source) in enumerate(levels):
        pair = device >> (level + 1)
        left_row = shapes[pl.ds(source + 2 * pair, 1), :]
        right_row = shapes[pl.ds(source + 2 * pair + 1, 1), :]
        left = [jnp.broadcast_to(left_row[:, d : d + 1], (8, 128)) for d in range(4)]
        right = [jnp.broadcast_to(right_row[:, d : d + 1], (8, 128)) for d in range(4)]
        tile = sibling_tile(left, right, lane_u, row_y, row_z)
        couples.append(sibling_apply(tile, pairs_scr[pair_source + pair]))
    incoming = None
    for level in reversed(range(len(levels))):
        value = couples[level]
        if incoming is not None:
            value = value + push_down(incoming[None], t_high, t_low)[0]
        side = (device >> level) & 1
        keep_low = jnp.where(low, 1, 0) == (1 - side)
        incoming = jnp.where(keep_low, value, 0.0)
    value = couple[pl.ds(PAIR_OFFSETS[6], 1)] + push_down(incoming[None], t_high, t_low)
    for level in range(5, 0, -1):
        n = PAIRS >> level
        value = couple[pl.ds(PAIR_OFFSETS[level], n)] + push_down(
            children_of(value), t_high, t_low
        )
    down_ref[...] = push_down(children_of(value), t_high, t_low)


UNIT = 2


def couple_kernel(
    entries, shape_ref, prev_ref, next_ref, high_ref, low_ref,
    leaf_couple,
    shape_tab, high_tab, low_tab, halo_rows, halo_shape, sems,
    tile_h0, tile_l0, lhs0, tile_h1, tile_l1, lhs1,
):
    copies = [
        pltpu.make_async_copy(high_ref, high_tab.at[0:LD], sems.at[2]),
        pltpu.make_async_copy(low_ref, low_tab.at[0:LD], sems.at[3]),
    ]
    for k, ref in enumerate((prev_ref, next_ref)):
        parts = ref[68].astype(F32)
        halo_rows[k] = parts[0:8] + parts[8:16] + parts[16:24]
        copies.append(pltpu.make_async_copy(halo_rows.at[k], halo_shape.at[k], sems.at[k]))
    for copy in copies:
        copy.start()
    low32 = lanes((R, 128)) < K
    lane_u = lane_nodes()
    row8 = rows((8, 128))
    low8 = lanes((8, 128)) < K

    def shape_rows(read, k, shift):
        return jnp.where(
            row8 == 0,
            read(0, k),
            jnp.where(row8 == 1, read(1, k), jnp.where(row8 == 2, read(2, k) + shift, read(3, k))),
        )

    def own_nodes(m, carry):
        shape_tab[HALF + m] = shape_rows(lambda d, k: shape_ref[d, k], m, 0.0)
        return carry

    lax.fori_loop(0, LD, own_nodes, 0, unroll=8)
    for copy in copies[2:]:
        copy.wait()
    for side, ref in enumerate((prev_ref, next_ref)):
        first = LD + side * HALF

        def halo_pairs(m, carry):
            def read(d, k):
                return halo_shape[side, d, k]

            loaded = [
                (tab, 4 * m + v, ref[offset + 4 * m + v])
                for tab, offset in ((high_tab, 0), (low_tab, 32))
                for v in range(4)
            ]
            turned = [pltpu.roll(pair.astype(F32), K, 1).astype(BF16) for _, _, pair in loaded]
            source = HALF if side == 0 else 0
            place = 0 if side == 0 else HALF + LD
            shift = (2.0 * side - 1.0) * GROUPS * SCALE
            for v in range(8):
                shape_tab[place + 8 * m + v] = shape_rows(read, source + 8 * m + v, shift)
            for (tab, pair, value), other in zip(loaded, turned):
                tab[first + pair] = value
                tab[first + PAIRS // 2 + pair] = other
            return carry

        lax.fori_loop(0, PAIRS // 8, halo_pairs, 0)
    high_tab[TABLE - 1] = jnp.zeros((R, 128), BF16)
    low_tab[TABLE - 1] = jnp.zeros((R, 128), BF16)
    for copy in copies[:2]:
        copy.wait()

    row_y, row_z = row_nodes()

    def couple_load(pair):
        leaves = (2 * pair, 2 * pair + 1)
        own = jnp.where(low8, shape_tab[HALF + leaves[0]], shape_tab[HALF + leaves[1]])
        fars = []
        for s in range(8):
            e0, e1 = entries[8 + s, leaves[0]], entries[8 + s, leaves[1]]
            fars.append(jnp.where(low8, shape_tab[e0], shape_tab[e1]))
        sources = []
        for tab in (high_tab, low_tab):
            for h in range(2):
                for q in range(4):
                    e0, e1 = entries[2 * q, leaves[h]], entries[2 * q + 1, leaves[h]]
                    sources.append(jnp.where(low32, tab[e0], tab[e1]))
        return own, fars, sources

    def couple_tiles(own, fars):
        radius = jnp.broadcast_to(own[3:4], (8, 128))
        own = [jnp.broadcast_to(own[d : d + 1], (8, 128)) + radius * lane_u[d] for d in range(3)]
        tiles = []
        for far in fars:
            reach = jnp.broadcast_to(far[3:4], (8, 128))
            gap = [own[d] - jnp.broadcast_to(far[d : d + 1], (8, 128)) for d in range(3)]
            tile = tile_from_axes(
                [jnp.square(gap[0] - reach * NODE[b]) for b in range(4)],
                [jnp.square(gap[1] - reach * row_y[h]) for h in range(2)],
                jnp.square(gap[2] - reach * row_z),
            )
            tiles.append(halves(tile))
        return tiles

    def couple_apply(u, tile_h, tile_l, lhs):
        both = dot(lhs[u], tile_h[u])
        both = both[0 : 2 * R] + both[2 * R : 4 * R] + dot(lhs[u, 0 : 2 * R], tile_l[u])
        return jnp.where(low32, both[0:R], both[R : 2 * R])

    def couple_phase(n, new, old):
        tile_h, tile_l, lhs = new
        loaded = [couple_load(jnp.minimum(n * UNIT + u, PAIRS - 1)) for u in range(UNIT)]
        results, made = [], []
        for u in range(UNIT):
            results.append(couple_apply(u, *old))
            made.append(couple_tiles(loaded[u][0], loaded[u][1]))
        for u in range(UNIT):
            for k, value in enumerate(loaded[u][2]):
                r, q = k // 4, k % 4
                lhs[u, r * R : (r + 1) * R, q * 128 : (q + 1) * 128] = value
            for s, (high, low) in enumerate(made[u]):
                tile_h[u, s * K : (s + 1) * K, :] = high
                tile_l[u, s * K : (s + 1) * K, :] = low
        for u in range(UNIT):
            leaf_couple[n * UNIT + u] = results[u]

    buffers = ((tile_h0, tile_l0, lhs0), (tile_h1, tile_l1, lhs1))
    for ref in buffers[1]:
        ref[...] = jnp.zeros(ref.shape, ref.dtype)

    def couple_two(m, carry):
        couple_phase(2 * m, buffers[0], buffers[1])
        couple_phase(2 * m + 1, buffers[1], buffers[0])
        return carry

    lax.fori_loop(0, PAIRS // UNIT // 2 + 1, couple_two, 0)


def finish_kernel(
    counts, near_ref, p_ref, b_ref, prev_ref, next_ref, down_ref, leaf_couple,
    out_ref,
    p8, coords,
):
    device = device_index()

    def finish(m, carry):
        values = []
        for v in range(8):
            c = 8 * m + v
            value = (down_ref[c] + leaf_couple[c + UNIT]).astype(BF16)
            span = pl.ds(pl.multiple_of(c * 256, 256), 256)
            values.append(
                (
                    span,
                    near_ref[:, span]
                    + dot(value, block_diagonal(b_ref[2 * c], b_ref[2 * c + 1])),
                )
            )
        for span, value in values:
            out_ref[:, span] = value
        return carry

    lax.fori_loop(0, PAIRS // 8, finish, 0)

    p8[...] = jnp.zeros(p8.shape, F32)
    eye = identity()
    sides = ((prev_ref, 0), (next_ref, GROUPS - 1))
    for side, (halo_ref, group) in enumerate(sides):
        p8[side, 0:3, :] = p_ref[:, group * 512 : group * 512 + 512]
        coords[side] = halo_ref[69].astype(F32) + halo_ref[70].astype(F32) + halo_ref[71].astype(F32)

    def edge(k, carry):
        loaded = [
            (halo_ref[64 + k], coords[side, pl.ds(pl.multiple_of(8 * k, 8), 8), :], p8[side])
            for side, (halo_ref, _) in enumerate(sides)
        ]
        for side, (_, group) in enumerate(sides):
            x_far, far, own = loaded[side]
            origin_z = (device * GROUPS + group).astype(F32)
            _, own = point_features(own, origin_z)
            far, _ = point_features(far, origin_z)
            far = dot_nt(eye, far_stack(far)).astype(BF16)
            tiles = decay(dot(far, own_stack(own))).astype(BF16)
            products = dot(x_far, tiles)
            for i in range(4):
                delta = (4 + i - k) if side == 0 else (4 + k - i)
                weight = counts[8 * (1 - side) + jnp.clip(delta, 0, 7), 4 * group + i]
                place = slice((4 * group + i) * P_SIZE, (4 * group + i + 1) * P_SIZE)
                out_ref[:, place] += products[:, i * P_SIZE : (i + 1) * P_SIZE] * weight
        return carry

    lax.fori_loop(0, 4, edge, 0)


def shaped(*shape, dtype=F32):
    return jax.ShapeDtypeStruct(shape, dtype)


def vmem():
    return pl.BlockSpec(memory_space=pltpu.VMEM)


def smem():
    return pl.BlockSpec(memory_space=pltpu.SMEM)


PARAMS = pltpu.CompilerParams(vmem_limit_bytes=VMEM_LIMIT)


def per_device(charges, points, basis, transfer, near_list, coupling_list):
    near_rows = near_list.T
    coupling_rows = coupling_list.T
    devices = lax.axis_size("sub") * lax.axis_size("leaf")
    send_next, send_prev, high, low, lev, root, shapes = pl.pallas_call(
        leaf_kernel,
        name="leaf_up",
        out_shape=(
            shaped(SEND, R, 128, dtype=BF16),
            shaped(SEND, R, 128, dtype=BF16),
            shaped(LD, R, 128, dtype=BF16),
            shaped(LD, R, 128, dtype=BF16),
            shaped(PAIRS - 1, R, 128),
            shaped(devices, R // 2 + 8, 128),
            shaped(8, 256),
        ),
        in_specs=[vmem()] * 4,
        out_specs=[vmem()] * 7,
        scratch_shapes=[
            pltpu.VMEM((PAIRS, R, 128), F32),
            pltpu.VMEM((3, LD, 128), F32),
            pltpu.VMEM((256, 128), F32),
            pltpu.VMEM((8, 512), F32),
        ],
        compiler_params=PARAMS,
    )(charges, points, basis, transfer)

    roots = lax.all_to_all(root, AXES, 0, 0, tiled=True)
    forward = [(i, i + 1) for i in range(devices - 1)]
    backward = [(i + 1, i) for i in range(devices - 1)]
    from_prev = lax.ppermute(send_next, AXES, forward)
    from_next = lax.ppermute(send_prev, AXES, backward)

    tasks, counts, entries = pl.pallas_call(
        list_kernel,
        name="lists",
        out_shape=(
            shaped(8, LIST, dtype=jnp.int32),
            shaped(16, 128),
            shaped(16, 128, dtype=jnp.int32),
        ),
        in_specs=[vmem()] * 2,
        out_specs=[vmem()] * 3,
        compiler_params=PARAMS,
        cost_estimate=pl.CostEstimate(flops=1 << 24, bytes_accessed=1 << 16, transcendentals=0),
    )(near_rows, coupling_rows)
    near = pl.pallas_call(
        near_kernel,
        name="near_field",
        out_shape=shaped(R, LD * P_SIZE),
        in_specs=[smem(), vmem(), vmem()],
        out_specs=vmem(),
        scratch_shapes=[
            pltpu.VMEM((4, 8, 512), F32),
            pltpu.VMEM((PAIRS, P_SIZE, 2 * FEATS), BF16),
            pltpu.VMEM((2 * LD, FEATS, P_SIZE), BF16),
            pltpu.VMEM((R, LD * P_SIZE), F32),
            pltpu.VMEM((R, LD * P_SIZE), F32),
            pltpu.VMEM((R, LD * P_SIZE), F32),
            pltpu.VMEM((BATCH // 2, 128, 256), BF16),
            pltpu.VMEM((BATCH // 2, 128, 256), BF16),
        ],
        compiler_params=PARAMS,
        cost_estimate=pl.CostEstimate(
            flops=2 * 460 * 128 * 128 * 128, bytes_accessed=4 << 20, transcendentals=460 * 32768
        ),
    )(tasks, charges, points)

    down = pl.pallas_call(
        down_kernel,
        name="tree_down",
        out_shape=shaped(PAIRS, R, 128),
        in_specs=[smem()] + [vmem()] * 3,
        out_specs=vmem(),
        scratch_shapes=[
            pltpu.VMEM((PAIRS - 1, R, 128), F32),
            pltpu.VMEM((devices, R, 128), F32),
            pltpu.VMEM((2 * devices, 128), F32),
        ],
        compiler_params=PARAMS,
    )(shapes, lev, transfer, roots)

    stages = [
        pltpu.VMEM((UNIT, 512, 128), BF16),
        pltpu.VMEM((UNIT, 512, 128), BF16),
        pltpu.VMEM((UNIT, 4 * R, 512), BF16),
    ]
    leaf_couple = pl.pallas_call(
        couple_kernel,
        name="leaf_couple",
        out_shape=shaped(PAIRS + 2 * UNIT, R, 128),
        in_specs=[smem()] * 2 + [vmem()] * 2 + [pl.BlockSpec(memory_space=pl.ANY)] * 2,
        out_specs=vmem(),
        scratch_shapes=[
            pltpu.VMEM((2 * LD, 8, 128), F32),
            pltpu.VMEM((TABLE, R, 128), BF16),
            pltpu.VMEM((TABLE, R, 128), BF16),
            pltpu.VMEM((2, 8, 128), F32),
            pltpu.SMEM((2, 8, 128), F32),
            pltpu.SemaphoreType.DMA((4,)),
        ]
        + stages
        + stages,
        compiler_params=PARAMS,
    )(entries, shapes, from_prev, from_next, high, low)

    return pl.pallas_call(
        finish_kernel,
        name="finish",
        out_shape=shaped(R, LD * P_SIZE),
        in_specs=[smem()] + [vmem()] * 7,
        out_specs=vmem(),
        scratch_shapes=[pltpu.VMEM((2, 8, 512), F32), pltpu.VMEM((2, R, 128), F32)],
        compiler_params=PARAMS,
    )(counts, near, points, basis, from_prev, from_next, down, leaf_couple)


def solution(mesh):
    in_specs = (
        P(None, AXES),
        P(None, AXES),
        P(AXES, None, None),
        P(),
        P(AXES, None),
        P(AXES, None),
    )
    return jax.shard_map(
        per_device, mesh=mesh, in_specs=in_specs, out_specs=P(None, AXES), check_vma=False
    )
```

```python
import functools
import math

import jax
import jax.numpy as jnp
from jax import lax
from jax.experimental import pallas as pl
from jax.experimental.pallas import tpu as pltpu
from jax.sharding import PartitionSpec as P

P_SIZE = 128
K = 64
R = 32
LD = 128
PAIRS = LD // 2
GROUPS = LD // 4
TABLE = 257
HALF = LD // 2
NEAR_REACH = 8
FEATS = 64
BATCH = 8
LIST = 896
SEND = 72
SCALE = 0.25 * math.log2(math.e)
NODE = [math.cos((2 * a + 1) * math.pi / 8) for a in range(4)]
AXES = ("leaf", "sub")
F32 = jnp.float32
BF16 = jnp.bfloat16
NT = (((1,), (1,)), ((), ()))
TINY = 1e-30
VMEM_LIMIT = 56 * 1024 * 1024


def lanes(shape):
    return lax.broadcasted_iota(jnp.int32, shape, len(shape) - 1)


def rows(shape):
    return lax.broadcasted_iota(jnp.int32, shape, len(shape) - 2)


def dot(a, b):
    return jnp.dot(a, b, preferred_element_type=F32)


def dot_nt(a, b):
    return lax.dot_general(a, b, NT, preferred_element_type=F32)


def halves(value):
    high = value.astype(BF16)
    return high, (value - high.astype(F32)).astype(BF16)


def thirds(value):
    first = value.astype(BF16).astype(F32)
    rest = value - first
    second = rest.astype(BF16).astype(F32)
    return first, second, rest - second


def unit_node(index):
    return jnp.where(
        index == 0,
        NODE[0],
        jnp.where(index == 1, NODE[1], jnp.where(index == 2, NODE[2], NODE[3])),
    ).astype(F32)


def lane_nodes():
    b = lanes((8, 128)) & 63
    return [unit_node(b >> 4), unit_node((b >> 2) & 3), unit_node(b & 3)]


def row_nodes():
    r = rows((8, 128))
    return [unit_node(r >> 2), unit_node((r >> 2) + 2)], unit_node(r & 3)


def decay(t):
    t = jnp.maximum(t, TINY)
    r = lax.rsqrt(t.astype(BF16)).astype(F32)
    s = t * r
    return jnp.exp2(s * (s * r - 3.0))


def tile_from_axes(x_sq, y_sq, z_sq):
    yz = [y_sq[0] + z_sq, y_sq[1] + z_sq]
    return decay(jnp.concatenate([x_sq[k // 2] + yz[k % 2] for k in range(8)], axis=0))


def doubled_transfer(t_ref):
    flat = t_ref[...].reshape(2 * K, K)
    return jnp.concatenate([flat, flat], axis=1)


def device_index():
    return lax.axis_index("leaf") * lax.axis_size("sub") + lax.axis_index("sub")


def merge_up(pairs, t_high, t_low):
    n = pairs.shape[0]
    high, low = halves(pairs.reshape(n * R, 128))
    out = dot(high, jnp.concatenate([t_high, t_low], axis=1))
    out = out[:, 0:128] + out[:, 128:256] + dot(low, t_high)
    return out.reshape(n, R, 128)


def pair_lanes(clusters):
    n = clusters.shape[0]
    split = clusters.reshape(n // 2, 2, R, 128)
    return jnp.where(lanes((1, R, 128)) < K, split[:, 0], split[:, 1])


def push_down(value, t_high, t_low):
    n = value.shape[0]
    high, low = halves(value.reshape(n * R, 128))
    out = dot_nt(high, jnp.concatenate([t_high, t_low], axis=0))
    out = out[:, 0:128] + out[:, 128:256] + dot_nt(low, t_high)
    return out.reshape(n, R, 128)


def children_of(pairs):
    lane = lanes((1, R, 128))
    left = jnp.where(lane < K, pairs, 0.0)
    right = jnp.where(lane < K, 0.0, pairs)
    return jnp.stack([left, right], axis=1).reshape(2 * pairs.shape[0], R, 128)


def merge_shape_rows(left, right):
    lane = lanes(left.shape)
    sep = left - right
    gap = jnp.sqrt(jnp.sum(jnp.where(lane < 3, sep * sep, 0.0), axis=1, keepdims=True))
    radius = jnp.maximum(left, right) + 0.5 * gap
    return jnp.where(lane == 3, radius, jnp.where(lane < 3, 0.5 * (left + right), 0.0))


def sibling_tile(left, right, lane_u, row_y, row_z):
    low = lanes((8, 128)) < K
    alpha = jnp.where(low, left[3], right[3])
    beta = jnp.where(low, right[3], left[3])
    base = [jnp.where(low, left[d] - right[d], right[d] - left[d]) - beta * lane_u[d] for d in range(3)]
    x_sq = [jnp.square(base[0] + alpha * NODE[a]) for a in range(4)]
    y_sq = [jnp.square(base[1] + alpha * row_y[h]) for h in range(2)]
    z_sq = jnp.square(base[2] + alpha * row_z)
    return tile_from_axes(x_sq, y_sq, z_sq)


def sibling_apply(tile, pair):
    low = lanes((R, 128)) < K
    swapped = pltpu.roll(pair, K, 1)
    stacked = jnp.concatenate(
        [jnp.where(low, swapped, 0.0), jnp.where(low, 0.0, swapped)], axis=0
    )
    high, low_part = halves(stacked)
    t_high, t_low = halves(tile)
    t_high = jnp.concatenate([t_high, t_high], axis=0)
    t_low = jnp.concatenate([t_low, t_low], axis=0)
    out = dot_nt(high, jnp.concatenate([t_high, t_low], axis=0))
    out = out[:, 0:128] + out[:, 128:256] + dot_nt(low_part, t_high)
    return jnp.where(low, out[:R], out[R:])


LEVEL_OFFSETS = [0, 128, 192, 224, 240, 248, 252, 254]
PAIR_OFFSETS = [0, 0, 32, 48, 56, 60, 62]


def block_diagonal(left, right):
    zero = jnp.zeros(left.shape, left.dtype)
    return jnp.concatenate(
        [jnp.concatenate([left, zero], axis=1), jnp.concatenate([zero, right], axis=1)], axis=0
    )


def leaf_kernel(
    x_ref, p_ref, b_ref, t_ref,
    send_next, send_prev, high_ref, low_ref, lev_ref, root_ref, shape_ref,
    coef, pts, shapes, p8,
):
    origin = (device_index() * GROUPS).astype(F32)
    low32 = lanes((R, 128)) < K

    def leaf_pairs(m, carry):
        values = []
        for v in range(16):
            leaf = 16 * m + v
            x = x_ref[:, pl.ds(pl.multiple_of(leaf * P_SIZE, P_SIZE), P_SIZE)]
            weights = b_ref[leaf]
            values.append(dot_nt(x, jnp.concatenate([weights, weights], axis=0)))
        for v in range(16):
            high_ref[16 * m + v], low_ref[16 * m + v] = halves(values[v])
        for v in range(8):
            coef[8 * m + v] = jnp.where(low32, values[2 * v], values[2 * v + 1])
        return carry

    lax.fori_loop(0, LD // 16, leaf_pairs, 0)

    t_high, t_low = halves(doubled_transfer(t_ref))
    pairs = coef[...]
    for level in range(1, 7):
        pairs = pair_lanes(merge_up(pairs, t_high, t_low))
        lev_ref[pl.ds(PAIR_OFFSETS[level], pairs.shape[0])] = pairs
    root = merge_up(pairs, t_high, t_low)[0]

    for i in range(LD):
        for d in range(3):
            pts[d, i : i + 1, :] = p_ref[d : d + 1, i * P_SIZE : (i + 1) * P_SIZE]
    centers, squares = [], 0.0
    for d in range(3):
        coords = (pts[d] - origin if d == 2 else pts[d]) * SCALE
        center = jnp.sum(coords, axis=1, keepdims=True) * (1.0 / P_SIZE)
        centers.append(center)
        squares = squares + jnp.square(coords - center)
    radius = jnp.sqrt(jnp.max(squares, axis=1, keepdims=True))
    lane = lanes((LD, 128))
    shapes[0:LD, :] = jnp.where(
        lane == 0,
        centers[0],
        jnp.where(
            lane == 1,
            centers[1],
            jnp.where(lane == 2, centers[2], jnp.where(lane == 3, radius, 0.0)),
        ),
    )
    count = LD // 2
    for level in range(1, 8):
        source = LEVEL_OFFSETS[level - 1]
        joined = merge_shape_rows(
            shapes[pl.ds(source, count, stride=2), :],
            shapes[pl.ds(source + 1, count, stride=2), :],
        )
        shapes[pl.ds(LEVEL_OFFSETS[level], count), :] = joined
        count //= 2
    shape_rows = jnp.concatenate(
        [jnp.transpose(shapes[0:128, :])[0:8], jnp.transpose(shapes[128:256, :])[0:8]], axis=1
    )
    shape_ref[...] = shape_rows
    low = lanes((R // 2, 128)) < K
    block = jnp.concatenate(
        [
            jnp.where(low, root[0 : R // 2], root[R // 2 : R]),
            jnp.broadcast_to(shapes[254:255, :], (8, 128)),
        ],
        axis=0,
    )
    root_ref[...] = jnp.broadcast_to(block[None], root_ref.shape)

    p8[...] = jnp.zeros((8, 512), F32)
    for send, first_pair, group in ((send_next, PAIRS // 2, GROUPS - 1), (send_prev, 0, 0)):

        def copy_pairs(m, carry):
            parts = [halves(coef[first_pair + 8 * m + v]) for v in range(8)]
            for v in range(8):
                send[8 * m + v], send[32 + 8 * m + v] = parts[v]
            return carry

        lax.fori_loop(0, PAIRS // 16, copy_pairs, 0)
        parts = thirds(shape_rows[:, 0:128])
        send[68] = jnp.concatenate(list(parts) + [jnp.zeros((8, 128), F32)], axis=0).astype(BF16)
        p8[0:3, :] = p_ref[:, group * 512 : group * 512 + 512]
        parts = thirds(p8[...])
        for k in range(4):
            send[64 + k] = x_ref[:, group * 512 + k * P_SIZE : group * 512 + (k + 1) * P_SIZE]
        for part in range(3):
            send[69 + part] = jnp.concatenate(
                [parts[part][:, k * P_SIZE : (k + 1) * P_SIZE] for k in range(4)], axis=0
            ).astype(BF16)


def list_kernel(near_ref, coupling_ref, list_ref, count_ref, index_ref):
    first_leaf = device_index() * LD
    lane8 = lanes((8, 128))
    row8 = rows((8, 128))
    offset = jnp.where(near_ref[...] >= 0, near_ref[...] - first_leaf - lane8, 1000)

    def slots_at(delta):
        return jnp.sum(jnp.where(offset == delta, 1.0, 0.0), axis=0, keepdims=True)

    forward = jnp.concatenate([slots_at(delta) for delta in range(8)], axis=0)
    reverse = jnp.concatenate(
        [jnp.zeros((1, 128), F32)] + [slots_at(-delta) for delta in range(1, 8)], axis=0
    )
    count_ref[0:8, :] = forward
    count_ref[8:16, :] = reverse
    backward = jnp.concatenate(
        [jnp.zeros((1, 128), F32)]
        + [pltpu.roll(reverse[delta : delta + 1, :], 128 - delta, 1) for delta in range(1, 8)],
        axis=0,
    )
    turned = (row8 == 1) & ((lane8 & 3) == 2)
    leaf = lane8.astype(F32)
    other = leaf + row8.astype(F32)
    first = jnp.where(turned, other, leaf)
    second = jnp.where(turned, leaf, other)
    to_first = jnp.where(turned, backward, forward)
    to_second = jnp.where(turned, forward, backward)
    odd = jnp.where(turned, lane8, lane8 + row8) & 1
    wanted = (lane8 + row8 < LD) & (forward + backward > 0.0)
    earlier = jnp.where(rows((128, 128)) < lanes((128, 128)), 1.0, 0.0).astype(BF16)
    place = jnp.full((8, 128), -1.0, F32)
    most = jnp.zeros((1, 1), F32)
    for parity in range(2):
        flags = jnp.where(wanted & (odd == parity), 1.0, 0.0)
        rank = dot(flags.astype(BF16), earlier)
        totals = jnp.sum(flags, axis=1, keepdims=True)
        before = jnp.zeros((1, 1), F32)
        starts = []
        for delta in range(8):
            starts.append(before)
            before = before + totals[delta : delta + 1, :]
        rank = rank + jnp.concatenate(starts, axis=0)
        place = jnp.where(flags > 0.0, 2.0 * rank + (1.0 * BATCH + parity), place)
        most = jnp.maximum(most, before)
    task_rows = []
    for delta in range(8):
        pick = slice(delta, delta + 1)
        task_rows.append(
            jnp.where(
                row8 == 0,
                first[pick],
                jnp.where(
                    row8 == 1,
                    second[pick],
                    jnp.where(
                        row8 == 2, to_first[pick], jnp.where(row8 == 3, to_second[pick], 0.0)
                    ),
                ),
            ).astype(BF16)
        )
    tasks = jnp.concatenate(task_rows, axis=1)
    slot_row = rows((128, 128)).astype(F32)
    for m in range(LIST // 128):
        chosen = jnp.concatenate(
            [
                jnp.where(place[delta : delta + 1, :] == slot_row + 128.0 * m, 1.0, 0.0).astype(BF16)
                for delta in range(8)
            ],
            axis=1,
        )
        part = dot_nt(tasks, chosen)
        part = jnp.where(row8 == 4, 2.0 * most, part)
        list_ref[:, m * 128 : (m + 1) * 128] = part.astype(jnp.int32)

    target = coupling_ref[...]
    reach = target - first_leaf + HALF
    swap = ((reach ^ row8) & 1) * (PAIRS // 2)
    entry = jnp.where(
        reach < HALF,
        LD + (reach >> 1) + swap,
        jnp.where(reach < HALF + LD, reach - HALF, LD + HALF + ((reach - HALF - LD) >> 1) + swap),
    )
    index_ref[0:8, :] = jnp.where(target >= 0, entry, TABLE - 1)
    index_ref[8:16, :] = jnp.where(target >= 0, reach, 0)


def point_features(points8, origin_z):
    row = rows(points8.shape)
    center = jnp.where(row == 2, origin_z + 0.5, 1.0)
    v = jnp.where(row < 3, (points8 - center) * SCALE, 0.0)
    norm = jnp.sum(v * v, axis=0, keepdims=True)
    far = jnp.where(row == 3, norm, jnp.where(row == 4, 1.0, v))
    own = jnp.where(row == 3, 1.0, jnp.where(row == 4, norm, -2.0 * v))
    return far, own


def far_stack(value):
    first, second, third = thirds(value)
    none = jnp.zeros(value.shape, F32)
    return jnp.concatenate(
        [first, first, first, second, second, third, none, none], axis=0
    ).astype(BF16)


def own_stack(value):
    first, second, third = thirds(value)
    none = jnp.zeros(value.shape, F32)
    return jnp.concatenate(
        [first, second, third, first, second, first, none, none], axis=0
    ).astype(BF16)


def identity():
    return jnp.where(rows((128, 128)) == lanes((128, 128)), 1.0, 0.0).astype(BF16)


def near_kernel(
    list_ref, x_ref, p_ref, out_ref,
    p8, far_feat, own_feat, part1, part2, part3, tile0, tile1,
):
    first_group = device_index() * GROUPS
    p8[...] = jnp.zeros(p8.shape, F32)
    eye = identity()

    def features(m, carry):
        loaded = [p_ref[:, pl.ds(pl.multiple_of((4 * m + v) * 512, 512), 512)] for v in range(4)]
        for v in range(4):
            p8[v, 0:3, :] = loaded[v]
        made = []
        for v in range(4):
            coords = p8[v]
            origin_z = (first_group + 4 * m + v).astype(F32)
            far, own = point_features(coords, origin_z)
            _, own_up = point_features(coords, origin_z + 1.0)
            far = far_stack(far)
            parts = [far[:, k * P_SIZE : (k + 1) * P_SIZE] for k in range(4)]
            turned = dot_nt(eye, jnp.concatenate(parts, axis=0)).astype(BF16)
            made.append((turned, own_stack(own), own_stack(own_up)))
        for v in range(4):
            g = 4 * m + v
            turned, own, own_up = made[v]
            far_feat[2 * g] = turned[:, 0:128]
            far_feat[2 * g + 1] = turned[:, 128:256]
            for k in range(4):
                part = slice(k * P_SIZE, (k + 1) * P_SIZE)
                own_feat[4 * g + k] = own[:, part]
                own_feat[LD + 4 * g + k] = own_up[:, part]
        return carry

    lax.fori_loop(0, GROUPS // 4, features, 0)

    out_ref[...] = x_ref[...].astype(F32)
    parts = (out_ref, part1, part2, part3)
    for ref in (part1, part2, part3, tile0, tile1):
        ref[...] = jnp.zeros(ref.shape, ref.dtype)

    total = list_ref[4, 0]
    steps = (total + BATCH - 1) // BATCH + 1
    low = lanes((128, 128)) < K

    def leaf_slice(i):
        return pl.ds(pl.multiple_of(i * P_SIZE, P_SIZE), P_SIZE)

    def phase(n, tile_new, tile_old):
        far, own, sources, updates = [], [], [], []
        for u in range(BATCH):
            k = (n + 1) * BATCH + u
            i, j = list_ref[0, k], list_ref[1, k]
            variant = ((j >> 2) - (i >> 2)) * LD
            far.append(far_feat[j >> 1])
            own.append(own_feat[variant + i])
        for u in range(BATCH):
            k = n * BATCH + u
            i, j = list_ref[0, k], list_ref[1, k]
            sources.append((x_ref[:, leaf_slice(j)], x_ref[:, leaf_slice(i)]))
        tiles = []
        for u in range(BATCH // 2):
            pick = jnp.where(low, far[2 * u], far[2 * u + 1])
            dist = dot(pick, block_diagonal(own[2 * u], own[2 * u + 1]))
            tiles.append(decay(dist).astype(BF16))
            for h in range(2):
                k = n * BATCH + 2 * u + h
                tile = tile_old[u, :, h * 128 : h * 128 + 128]
                x_j, x_i = sources[2 * u + h]
                updates.append(
                    (
                        dot(x_j, tile) * list_ref[2, k].astype(F32),
                        dot_nt(x_i, tile) * list_ref[3, k].astype(F32),
                    )
                )
        for u in range(BATCH // 2):
            tile_new[u] = tiles[u]
        for u in range(BATCH // 2):
            places, sums = [], []
            for h in range(2):
                k = n * BATCH + 2 * u + h
                for side in range(2):
                    place = leaf_slice(list_ref[side, k])
                    places.append(place)
                    sums.append(parts[2 * h + side][:, place] + updates[2 * u + h][side])
            for ref, place, value in zip(parts, places, sums):
                ref[:, place] = value

    def two_phases(m, carry):
        phase(2 * m, tile0, tile1)
        phase(2 * m + 1, tile1, tile0)
        return carry

    lax.fori_loop(0, (steps + 1) // 2, two_phases, 0)

    def total_up(m, carry):
        place = pl.ds(pl.multiple_of(m * 1024, 1024), 1024)
        out_ref[:, place] = (out_ref[:, place] + part1[:, place]) + (
            part2[:, place] + part3[:, place]
        )
        return carry

    lax.fori_loop(0, LD * P_SIZE // 1024, total_up, 0)


def down_kernel(
    shape_ref, lev_ref, t_ref, root_ref, down_ref, couple, pairs_scr, shapes,
):
    lane_u = lane_nodes()
    row_y, row_z = row_nodes()

    def siblings(m, carry):
        loaded = [lev_ref[9 * m + u] for u in range(9)]
        values = []
        for u in range(9):
            cluster = LD + 2 * (9 * m + u)
            left = [shape_ref[d, cluster] for d in range(4)]
            right = [shape_ref[d, cluster + 1] for d in range(4)]
            tile = sibling_tile(left, right, lane_u, row_y, row_z)
            values.append(sibling_apply(tile, loaded[u]))
        for u in range(9):
            couple[9 * m + u] = values[u]
        return carry

    lax.fori_loop(0, 7, siblings, 0)

    t_high, t_low = halves(doubled_transfer(t_ref))
    device = device_index()
    n = root_ref.shape[0]
    low = lanes((R, 128)) < K
    shift = lanes((1, 128)) == 2
    for k in range(n):
        shapes[k : k + 1, :] = root_ref[k, R // 2 : R // 2 + 1, :] + jnp.where(
            shift, (k * GROUPS) * SCALE, 0.0
        )
    for k in range(n // 2):
        left = root_ref[2 * k, 0 : R // 2, :]
        right = root_ref[2 * k + 1, 0 : R // 2, :]
        left = jnp.concatenate([left, pltpu.roll(left, K, 1)], axis=0)
        right = jnp.concatenate([pltpu.roll(right, K, 1), right], axis=0)
        pairs_scr[k] = jnp.where(low, left, right)
    source, count, pair_source = 0, n // 2, 0
    levels = []
    while count >= 1:
        levels.append((source, pair_source))
        if count > 1:
            pairs = pair_lanes(merge_up(pairs_scr[pl.ds(pair_source, count)], t_high, t_low))
            pairs_scr[pl.ds(pair_source + count, count // 2)] = pairs
            joined = merge_shape_rows(
                shapes[pl.ds(source, count, stride=2), :],
                shapes[pl.ds(source + 1, count, stride=2), :],
            )
            shapes[pl.ds(source + 2 * count, count), :] = joined
        source += 2 * count
        pair_source += count
        count //= 2
    couples = []
    for level, (source, pair_source) in enumerate(levels):
        pair = device >> (level + 1)
        left_row = shapes[pl.ds(source + 2 * pair, 1), :]
        right_row = shapes[pl.ds(source + 2 * pair + 1, 1), :]
        left = [jnp.broadcast_to(left_row[:, d : d + 1], (8, 128)) for d in range(4)]
        right = [jnp.broadcast_to(right_row[:, d : d + 1], (8, 128)) for d in range(4)]
        tile = sibling_tile(left, right, lane_u, row_y, row_z)
        couples.append(sibling_apply(tile, pairs_scr[pair_source + pair]))
    incoming = None
    for level in reversed(range(len(levels))):
        value = couples[level]
        if incoming is not None:
            value = value + push_down(incoming[None], t_high, t_low)[0]
        side = (device >> level) & 1
        keep_low = jnp.where(low, 1, 0) == (1 - side)
        incoming = jnp.where(keep_low, value, 0.0)
    value = couple[pl.ds(PAIR_OFFSETS[6], 1)] + push_down(incoming[None], t_high, t_low)
    for level in range(5, 0, -1):
        n = PAIRS >> level
        value = couple[pl.ds(PAIR_OFFSETS[level], n)] + push_down(
            children_of(value), t_high, t_low
        )
    down_ref[...] = push_down(children_of(value), t_high, t_low)


UNIT = 2


def couple_kernel(
    entries, shape_ref, prev_ref, next_ref, high_ref, low_ref,
    leaf_couple,
    shape_tab, high_tab, low_tab, halo_rows, halo_shape, sems,
    tiles0, lhs0, tiles1, lhs1,
):
    copies = [
        pltpu.make_async_copy(high_ref, high_tab.at[0:LD], sems.at[2]),
        pltpu.make_async_copy(low_ref, low_tab.at[0:LD], sems.at[3]),
    ]
    for k, ref in enumerate((prev_ref, next_ref)):
        parts = ref[68].astype(F32)
        halo_rows[k] = parts[0:8] + parts[8:16] + parts[16:24]
        copies.append(pltpu.make_async_copy(halo_rows.at[k], halo_shape.at[k], sems.at[k]))
    for copy in copies:
        copy.start()
    low32 = lanes((R, 128)) < K
    lane_u = lane_nodes()
    row8 = rows((8, 128))
    low8 = lanes((8, 128)) < K

    def shape_rows(read, k, shift):
        return jnp.where(
            row8 == 0,
            read(0, k),
            jnp.where(row8 == 1, read(1, k), jnp.where(row8 == 2, read(2, k) + shift, read(3, k))),
        )

    def own_nodes(m, carry):
        shape_tab[HALF + m] = shape_rows(lambda d, k: shape_ref[d, k], m, 0.0)
        return carry

    lax.fori_loop(0, LD, own_nodes, 0, unroll=8)
    for copy in copies[2:]:
        copy.wait()
    for side, ref in enumerate((prev_ref, next_ref)):
        first = LD + side * HALF

        def halo_pairs(m, carry):
            def read(d, k):
                return halo_shape[side, d, k]

            loaded = [
                (tab, 4 * m + v, ref[offset + 4 * m + v])
                for tab, offset in ((high_tab, 0), (low_tab, 32))
                for v in range(4)
            ]
            turned = [pltpu.roll(pair.astype(F32), K, 1).astype(BF16) for _, _, pair in loaded]
            source = HALF if side == 0 else 0
            place = 0 if side == 0 else HALF + LD
            shift = (2.0 * side - 1.0) * GROUPS * SCALE
            for v in range(8):
                shape_tab[place + 8 * m + v] = shape_rows(read, source + 8 * m + v, shift)
            for (tab, pair, value), other in zip(loaded, turned):
                tab[first + pair] = value
                tab[first + PAIRS // 2 + pair] = other
            return carry

        lax.fori_loop(0, PAIRS // 8, halo_pairs, 0)
    high_tab[TABLE - 1] = jnp.zeros((R, 128), BF16)
    low_tab[TABLE - 1] = jnp.zeros((R, 128), BF16)
    for copy in copies[:2]:
        copy.wait()

    row_y, row_z = row_nodes()

    def couple_load(pair):
        leaves = (2 * pair, 2 * pair + 1)
        own = jnp.where(low8, shape_tab[HALF + leaves[0]], shape_tab[HALF + leaves[1]])
        fars = []
        for s in range(8):
            e0, e1 = entries[8 + s, leaves[0]], entries[8 + s, leaves[1]]
            fars.append(jnp.where(low8, shape_tab[e0], shape_tab[e1]))
        sources = []
        for tab in (high_tab, low_tab):
            for h in range(2):
                for q in range(4):
                    e0, e1 = entries[2 * q, leaves[h]], entries[2 * q + 1, leaves[h]]
                    sources.append(jnp.where(low32, tab[e0], tab[e1]))
        return own, fars, sources

    def couple_tiles(own, fars):
        radius = jnp.broadcast_to(own[3:4], (8, 128))
        own = [jnp.broadcast_to(own[d : d + 1], (8, 128)) + radius * lane_u[d] for d in range(3)]
        tiles = []
        for far in fars:
            reach = jnp.broadcast_to(far[3:4], (8, 128))
            gap = [own[d] - jnp.broadcast_to(far[d : d + 1], (8, 128)) for d in range(3)]
            tile = tile_from_axes(
                [jnp.square(gap[0] - reach * NODE[b]) for b in range(4)],
                [jnp.square(gap[1] - reach * row_y[h]) for h in range(2)],
                jnp.square(gap[2] - reach * row_z),
            )
            tiles.append(halves(tile))
        return tiles

    def couple_apply(u, tiles, lhs):
        both = dot(lhs[u], tiles[u])
        both = both[0 : 2 * R, 0:128] + (both[2 * R : 4 * R, 0:128] + both[0 : 2 * R, 128:256])
        return jnp.where(low32, both[0:R], both[R : 2 * R])

    def couple_phase(n, new, old):
        tiles, lhs = new
        loaded = [couple_load(jnp.minimum(n * UNIT + u, PAIRS - 1)) for u in range(UNIT)]
        results, made = [], []
        for u in range(UNIT):
            results.append(couple_apply(u, *old))
            made.append(couple_tiles(loaded[u][0], loaded[u][1]))
        for u in range(UNIT):
            for k, value in enumerate(loaded[u][2]):
                r, q = k // 4, k % 4
                lhs[u, r * R : (r + 1) * R, q * 128 : (q + 1) * 128] = value
            for s, (high, low) in enumerate(made[u]):
                tiles[u, s * K : (s + 1) * K, 0:128] = high
                tiles[u, s * K : (s + 1) * K, 128:256] = low
        for u in range(UNIT):
            leaf_couple[n * UNIT + u] = results[u]

    buffers = ((tiles0, lhs0), (tiles1, lhs1))
    for ref in buffers[1]:
        ref[...] = jnp.zeros(ref.shape, ref.dtype)

    def couple_two(m, carry):
        couple_phase(2 * m, buffers[0], buffers[1])
        couple_phase(2 * m + 1, buffers[1], buffers[0])
        return carry

    lax.fori_loop(0, PAIRS // UNIT // 2 + 1, couple_two, 0)


def finish_kernel(
    counts, near_ref, p_ref, b_ref, prev_ref, next_ref, down_ref, leaf_couple,
    out_ref,
    p8, coords,
):
    device = device_index()

    def finish(m, carry):
        values = []
        for v in range(8):
            c = 8 * m + v
            value = (down_ref[c] + leaf_couple[c + UNIT]).astype(BF16)
            span = pl.ds(pl.multiple_of(c * 256, 256), 256)
            values.append(
                (
                    span,
                    near_ref[:, span]
                    + dot(value, block_diagonal(b_ref[2 * c], b_ref[2 * c + 1])),
                )
            )
        for span, value in values:
            out_ref[:, span] = value
        return carry

    lax.fori_loop(0, PAIRS // 8, finish, 0)

    p8[...] = jnp.zeros(p8.shape, F32)
    eye = identity()
    sides = ((prev_ref, 0), (next_ref, GROUPS - 1))
    for side, (halo_ref, group) in enumerate(sides):
        p8[side, 0:3, :] = p_ref[:, group * 512 : group * 512 + 512]
        coords[side] = halo_ref[69].astype(F32) + halo_ref[70].astype(F32) + halo_ref[71].astype(F32)

    def edge(k, carry):
        loaded = [
            (halo_ref[64 + k], coords[side, pl.ds(pl.multiple_of(8 * k, 8), 8), :], p8[side])
            for side, (halo_ref, _) in enumerate(sides)
        ]
        for side, (_, group) in enumerate(sides):
            x_far, far, own = loaded[side]
            origin_z = (device * GROUPS + group).astype(F32)
            _, own = point_features(own, origin_z)
            far, _ = point_features(far, origin_z)
            far = dot_nt(eye, far_stack(far)).astype(BF16)
            tiles = decay(dot(far, own_stack(own))).astype(BF16)
            products = dot(x_far, tiles)
            for i in range(4):
                delta = (4 + i - k) if side == 0 else (4 + k - i)
                weight = counts[8 * (1 - side) + jnp.clip(delta, 0, 7), 4 * group + i]
                place = slice((4 * group + i) * P_SIZE, (4 * group + i + 1) * P_SIZE)
                out_ref[:, place] += products[:, i * P_SIZE : (i + 1) * P_SIZE] * weight
        return carry

    lax.fori_loop(0, 4, edge, 0)


def shaped(*shape, dtype=F32):
    return jax.ShapeDtypeStruct(shape, dtype)


def vmem():
    return pl.BlockSpec(memory_space=pltpu.VMEM)


def smem():
    return pl.BlockSpec(memory_space=pltpu.SMEM)


PARAMS = pltpu.CompilerParams(vmem_limit_bytes=VMEM_LIMIT)


def per_device(charges, points, basis, transfer, near_list, coupling_list):
    near_rows = near_list.T
    coupling_rows = coupling_list.T
    devices = lax.axis_size("sub") * lax.axis_size("leaf")
    send_next, send_prev, high, low, lev, root, shapes = pl.pallas_call(
        leaf_kernel,
        name="leaf_up",
        out_shape=(
            shaped(SEND, R, 128, dtype=BF16),
            shaped(SEND, R, 128, dtype=BF16),
            shaped(LD, R, 128, dtype=BF16),
            shaped(LD, R, 128, dtype=BF16),
            shaped(PAIRS - 1, R, 128),
            shaped(devices, R // 2 + 8, 128),
            shaped(8, 256),
        ),
        in_specs=[vmem()] * 4,
        out_specs=[vmem()] * 7,
        scratch_shapes=[
            pltpu.VMEM((PAIRS, R, 128), F32),
            pltpu.VMEM((3, LD, 128), F32),
            pltpu.VMEM((256, 128), F32),
            pltpu.VMEM((8, 512), F32),
        ],
        compiler_params=PARAMS,
    )(charges, points, basis, transfer)

    roots = lax.all_to_all(root, AXES, 0, 0, tiled=True)
    forward = [(i, i + 1) for i in range(devices - 1)]
    backward = [(i + 1, i) for i in range(devices - 1)]
    from_prev = lax.ppermute(send_next, AXES, forward)
    from_next = lax.ppermute(send_prev, AXES, backward)

    tasks, counts, entries = pl.pallas_call(
        list_kernel,
        name="lists",
        out_shape=(
            shaped(8, LIST, dtype=jnp.int32),
            shaped(16, 128),
            shaped(16, 128, dtype=jnp.int32),
        ),
        in_specs=[vmem()] * 2,
        out_specs=[vmem()] * 3,
        compiler_params=PARAMS,
        cost_estimate=pl.CostEstimate(flops=1 << 24, bytes_accessed=1 << 16, transcendentals=0),
    )(near_rows, coupling_rows)
    near = pl.pallas_call(
        near_kernel,
        name="near_field",
        out_shape=shaped(R, LD * P_SIZE),
        in_specs=[smem(), vmem(), vmem()],
        out_specs=vmem(),
        scratch_shapes=[
            pltpu.VMEM((4, 8, 512), F32),
            pltpu.VMEM((PAIRS, P_SIZE, 2 * FEATS), BF16),
            pltpu.VMEM((2 * LD, FEATS, P_SIZE), BF16),
            pltpu.VMEM((R, LD * P_SIZE), F32),
            pltpu.VMEM((R, LD * P_SIZE), F32),
            pltpu.VMEM((R, LD * P_SIZE), F32),
            pltpu.VMEM((BATCH // 2, 128, 256), BF16),
            pltpu.VMEM((BATCH // 2, 128, 256), BF16),
        ],
        compiler_params=PARAMS,
        cost_estimate=pl.CostEstimate(
            flops=2 * 460 * 128 * 128 * 128, bytes_accessed=4 << 20, transcendentals=460 * 32768
        ),
    )(tasks, charges, points)

    down = pl.pallas_call(
        down_kernel,
        name="tree_down",
        out_shape=shaped(PAIRS, R, 128),
        in_specs=[smem()] + [vmem()] * 3,
        out_specs=vmem(),
        scratch_shapes=[
            pltpu.VMEM((PAIRS - 1, R, 128), F32),
            pltpu.VMEM((devices, R, 128), F32),
            pltpu.VMEM((2 * devices, 128), F32),
        ],
        compiler_params=PARAMS,
    )(shapes, lev, transfer, roots)

    stages = [
        pltpu.VMEM((UNIT, 512, 256), BF16),
        pltpu.VMEM((UNIT, 4 * R, 512), BF16),
    ]
    leaf_couple = pl.pallas_call(
        couple_kernel,
        name="leaf_couple",
        out_shape=shaped(PAIRS + 2 * UNIT, R, 128),
        in_specs=[smem()] * 2 + [vmem()] * 2 + [pl.BlockSpec(memory_space=pl.ANY)] * 2,
        out_specs=vmem(),
        scratch_shapes=[
            pltpu.VMEM((2 * LD, 8, 128), F32),
            pltpu.VMEM((TABLE, R, 128), BF16),
            pltpu.VMEM((TABLE, R, 128), BF16),
            pltpu.VMEM((2, 8, 128), F32),
            pltpu.SMEM((2, 8, 128), F32),
            pltpu.SemaphoreType.DMA((4,)),
        ]
        + stages
        + stages,
        compiler_params=PARAMS,
    )(entries, shapes, from_prev, from_next, high, low)

    return pl.pallas_call(
        finish_kernel,
        name="finish",
        out_shape=shaped(R, LD * P_SIZE),
        in_specs=[smem()] + [vmem()] * 7,
        out_specs=vmem(),
        scratch_shapes=[pltpu.VMEM((2, 8, 512), F32), pltpu.VMEM((2, R, 128), F32)],
        compiler_params=PARAMS,
    )(counts, near, points, basis, from_prev, from_next, down, leaf_couple)


def solution(mesh):
    in_specs = (
        P(None, AXES),
        P(None, AXES),
        P(AXES, None, None),
        P(),
        P(AXES, None),
        P(AXES, None),
    )
    return jax.shard_map(
        per_device, mesh=mesh, in_specs=in_specs, out_specs=P(None, AXES), check_vma=False
    )
```

```python
import functools
import math

import jax
import jax.numpy as jnp
from jax import lax
from jax.experimental import pallas as pl
from jax.experimental.pallas import tpu as pltpu
from jax.sharding import PartitionSpec as P

P_SIZE = 128
K = 64
R = 32
LD = 128
PAIRS = LD // 2
GROUPS = LD // 4
TABLE = 257
HALF = LD // 2
NEAR_REACH = 8
FEATS = 64
BATCH = 8
LIST = 896
SEND = 72
SCALE = 0.5 * math.log2(math.e)
NODE = [math.cos((2 * a + 1) * math.pi / 8) for a in range(4)]
AXES = ("leaf", "sub")
F32 = jnp.float32
BF16 = jnp.bfloat16
NT = (((1,), (1,)), ((), ()))
TINY = 1e-30
EXP_FIT = [0.9999997512304358, 0.9999730886879146, 0.49952048226020057, 0.16360993458180054, 0.03348150378325188]
EXP_NEAR = [c * (-math.log(2.0) / 4.0) ** k for k, c in enumerate(EXP_FIT)]
VMEM_LIMIT = 56 * 1024 * 1024


def lanes(shape):
    return lax.broadcasted_iota(jnp.int32, shape, len(shape) - 1)


def rows(shape):
    return lax.broadcasted_iota(jnp.int32, shape, len(shape) - 2)


def dot(a, b):
    return jnp.dot(a, b, preferred_element_type=F32)


def dot_nt(a, b):
    return lax.dot_general(a, b, NT, preferred_element_type=F32)


def halves(value):
    high = value.astype(BF16)
    return high, (value - high.astype(F32)).astype(BF16)


def thirds(value):
    first = value.astype(BF16).astype(F32)
    rest = value - first
    second = rest.astype(BF16).astype(F32)
    return first, second, rest - second


def unit_node(index):
    return jnp.where(
        index == 0,
        NODE[0],
        jnp.where(index == 1, NODE[1], jnp.where(index == 2, NODE[2], NODE[3])),
    ).astype(F32)


def lane_nodes():
    b = lanes((8, 128)) & 63
    return [unit_node(b >> 4), unit_node((b >> 2) & 3), unit_node(b & 3)]


def row_nodes():
    r = rows((8, 128))
    return [unit_node(r >> 2), unit_node((r >> 2) + 2)], unit_node(r & 3)


def decay(t):
    t = jnp.maximum(t, TINY)
    return jnp.exp2(-(t * lax.rsqrt(t)))


def decay_near(t):
    t = jnp.maximum(t, TINY)
    s = t * lax.rsqrt(t)
    value = EXP_NEAR[4]
    for coefficient in EXP_NEAR[3::-1]:
        value = value * s + coefficient
    value = value * value
    return value * value


def tile_from_axes(x_sq, y_sq, z_sq):
    yz = [y_sq[0] + z_sq, y_sq[1] + z_sq]
    return decay(jnp.concatenate([x_sq[k // 2] + yz[k % 2] for k in range(8)], axis=0))


def doubled_transfer(t_ref):
    flat = t_ref[...].reshape(2 * K, K)
    return jnp.concatenate([flat, flat], axis=1)


def device_index():
    return lax.axis_index("leaf") * lax.axis_size("sub") + lax.axis_index("sub")


def merge_up(pairs, t_high, t_low):
    n = pairs.shape[0]
    high, low = halves(pairs.reshape(n * R, 128))
    out = dot(high, jnp.concatenate([t_high, t_low], axis=1))
    out = out[:, 0:128] + out[:, 128:256] + dot(low, t_high)
    return out.reshape(n, R, 128)


def pair_lanes(clusters):
    n = clusters.shape[0]
    split = clusters.reshape(n // 2, 2, R, 128)
    return jnp.where(lanes((1, R, 128)) < K, split[:, 0], split[:, 1])


def push_down(value, t_high, t_low):
    n = value.shape[0]
    high, low = halves(value.reshape(n * R, 128))
    out = dot_nt(high, jnp.concatenate([t_high, t_low], axis=0))
    out = out[:, 0:128] + out[:, 128:256] + dot_nt(low, t_high)
    return out.reshape(n, R, 128)


def children_of(pairs):
    lane = lanes((1, R, 128))
    left = jnp.where(lane < K, pairs, 0.0)
    right = jnp.where(lane < K, 0.0, pairs)
    return jnp.stack([left, right], axis=1).reshape(2 * pairs.shape[0], R, 128)


def merge_shape_rows(left, right):
    lane = lanes(left.shape)
    sep = left - right
    gap = jnp.sqrt(jnp.sum(jnp.where(lane < 3, sep * sep, 0.0), axis=1, keepdims=True))
    radius = jnp.maximum(left, right) + 0.5 * gap
    return jnp.where(lane == 3, radius, jnp.where(lane < 3, 0.5 * (left + right), 0.0))


def sibling_tile(left, right, lane_u, row_y, row_z):
    low = lanes((8, 128)) < K
    alpha = jnp.where(low, left[3], right[3])
    beta = jnp.where(low, right[3], left[3])
    base = [jnp.where(low, left[d] - right[d], right[d] - left[d]) - beta * lane_u[d] for d in range(3)]
    x_sq = [jnp.square(base[0] + alpha * NODE[a]) for a in range(4)]
    y_sq = [jnp.square(base[1] + alpha * row_y[h]) for h in range(2)]
    z_sq = jnp.square(base[2] + alpha * row_z)
    return tile_from_axes(x_sq, y_sq, z_sq)


def sibling_apply(tile, pair):
    low = lanes((R, 128)) < K
    swapped = pltpu.roll(pair, K, 1)
    stacked = jnp.concatenate(
        [jnp.where(low, swapped, 0.0), jnp.where(low, 0.0, swapped)], axis=0
    )
    high, low_part = halves(stacked)
    t_high, t_low = halves(tile)
    t_high = jnp.concatenate([t_high, t_high], axis=0)
    t_low = jnp.concatenate([t_low, t_low], axis=0)
    out = dot_nt(high, jnp.concatenate([t_high, t_low], axis=0))
    out = out[:, 0:128] + out[:, 128:256] + dot_nt(low_part, t_high)
    return jnp.where(low, out[:R], out[R:])


LEVEL_OFFSETS = [0, 128, 192, 224, 240, 248, 252, 254]
PAIR_OFFSETS = [0, 0, 32, 48, 56, 60, 62]


def block_diagonal(left, right):
    zero = jnp.zeros(left.shape, left.dtype)
    return jnp.concatenate(
        [jnp.concatenate([left, zero], axis=1), jnp.concatenate([zero, right], axis=1)], axis=0
    )


def leaf_kernel(
    x_ref, p_ref, b_ref, t_ref,
    send_next, send_prev, high_ref, low_ref, lev_ref, root_ref, shape_ref,
    coef, pts, shapes, p8,
):
    origin = (device_index() * GROUPS).astype(F32)
    low32 = lanes((R, 128)) < K

    def leaf_pairs(m, carry):
        values = []
        for v in range(16):
            leaf = 16 * m + v
            x = x_ref[:, pl.ds(pl.multiple_of(leaf * P_SIZE, P_SIZE), P_SIZE)]
            weights = b_ref[leaf]
            values.append(dot_nt(x, jnp.concatenate([weights, weights], axis=0)))
        for v in range(16):
            high_ref[16 * m + v], low_ref[16 * m + v] = halves(values[v])
        for v in range(8):
            coef[8 * m + v] = jnp.where(low32, values[2 * v], values[2 * v + 1])
        return carry

    lax.fori_loop(0, LD // 16, leaf_pairs, 0)

    t_high, t_low = halves(doubled_transfer(t_ref))
    pairs = coef[...]
    for level in range(1, 7):
        pairs = pair_lanes(merge_up(pairs, t_high, t_low))
        lev_ref[pl.ds(PAIR_OFFSETS[level], pairs.shape[0])] = pairs
    root = merge_up(pairs, t_high, t_low)[0]

    for i in range(LD):
        for d in range(3):
            pts[d, i : i + 1, :] = p_ref[d : d + 1, i * P_SIZE : (i + 1) * P_SIZE]
    centers, squares = [], 0.0
    for d in range(3):
        coords = (pts[d] - origin if d == 2 else pts[d]) * SCALE
        center = jnp.sum(coords, axis=1, keepdims=True) * (1.0 / P_SIZE)
        centers.append(center)
        squares = squares + jnp.square(coords - center)
    radius = jnp.sqrt(jnp.max(squares, axis=1, keepdims=True))
    lane = lanes((LD, 128))
    shapes[0:LD, :] = jnp.where(
        lane == 0,
        centers[0],
        jnp.where(
            lane == 1,
            centers[1],
            jnp.where(lane == 2, centers[2], jnp.where(lane == 3, radius, 0.0)),
        ),
    )
    count = LD // 2
    for level in range(1, 8):
        source = LEVEL_OFFSETS[level - 1]
        joined = merge_shape_rows(
            shapes[pl.ds(source, count, stride=2), :],
            shapes[pl.ds(source + 1, count, stride=2), :],
        )
        shapes[pl.ds(LEVEL_OFFSETS[level], count), :] = joined
        count //= 2
    shape_rows = jnp.concatenate(
        [jnp.transpose(shapes[0:128, :])[0:8], jnp.transpose(shapes[128:256, :])[0:8]], axis=1
    )
    shape_ref[...] = shape_rows
    low = lanes((R // 2, 128)) < K
    block = jnp.concatenate(
        [
            jnp.where(low, root[0 : R // 2], root[R // 2 : R]),
            jnp.broadcast_to(shapes[254:255, :], (8, 128)),
        ],
        axis=0,
    )
    root_ref[...] = jnp.broadcast_to(block[None], root_ref.shape)

    p8[...] = jnp.zeros((8, 512), F32)
    for send, first_pair, group in ((send_next, PAIRS // 2, GROUPS - 1), (send_prev, 0, 0)):

        def copy_pairs(m, carry):
            parts = [halves(coef[first_pair + 8 * m + v]) for v in range(8)]
            for v in range(8):
                send[8 * m + v], send[32 + 8 * m + v] = parts[v]
            return carry

        lax.fori_loop(0, PAIRS // 16, copy_pairs, 0)
        parts = thirds(shape_rows[:, 0:128])
        send[68] = jnp.concatenate(list(parts) + [jnp.zeros((8, 128), F32)], axis=0).astype(BF16)
        p8[0:3, :] = p_ref[:, group * 512 : group * 512 + 512]
        parts = thirds(p8[...])
        for k in range(4):
            send[64 + k] = x_ref[:, group * 512 + k * P_SIZE : group * 512 + (k + 1) * P_SIZE]
        for part in range(3):
            send[69 + part] = jnp.concatenate(
                [parts[part][:, k * P_SIZE : (k + 1) * P_SIZE] for k in range(4)], axis=0
            ).astype(BF16)


def list_kernel(near_ref, coupling_ref, list_ref, count_ref, index_ref):
    first_leaf = device_index() * LD
    lane8 = lanes((8, 128))
    row8 = rows((8, 128))
    offset = jnp.where(near_ref[...] >= 0, near_ref[...] - first_leaf - lane8, 1000)

    def slots_at(delta):
        return jnp.sum(jnp.where(offset == delta, 1.0, 0.0), axis=0, keepdims=True)

    forward = jnp.concatenate([slots_at(delta) for delta in range(8)], axis=0)
    reverse = jnp.concatenate(
        [jnp.zeros((1, 128), F32)] + [slots_at(-delta) for delta in range(1, 8)], axis=0
    )
    count_ref[0:8, :] = forward
    count_ref[8:16, :] = reverse
    backward = jnp.concatenate(
        [jnp.zeros((1, 128), F32)]
        + [pltpu.roll(reverse[delta : delta + 1, :], 128 - delta, 1) for delta in range(1, 8)],
        axis=0,
    )
    turned = (row8 == 1) & ((lane8 & 3) == 2)
    leaf = lane8.astype(F32)
    other = leaf + row8.astype(F32)
    first = jnp.where(turned, other, leaf)
    second = jnp.where(turned, leaf, other)
    to_first = jnp.where(turned, backward, forward)
    to_second = jnp.where(turned, forward, backward)
    odd = jnp.where(turned, lane8, lane8 + row8) & 1
    wanted = (lane8 + row8 < LD) & (forward + backward > 0.0)
    earlier = jnp.where(rows((128, 128)) < lanes((128, 128)), 1.0, 0.0).astype(BF16)
    place = jnp.full((8, 128), -1.0, F32)
    most = jnp.zeros((1, 1), F32)
    for parity in range(2):
        flags = jnp.where(wanted & (odd == parity), 1.0, 0.0)
        rank = dot(flags.astype(BF16), earlier)
        totals = jnp.sum(flags, axis=1, keepdims=True)
        before = jnp.zeros((1, 1), F32)
        starts = []
        for delta in range(8):
            starts.append(before)
            before = before + totals[delta : delta + 1, :]
        rank = rank + jnp.concatenate(starts, axis=0)
        place = jnp.where(flags > 0.0, 2.0 * rank + (1.0 * BATCH + parity), place)
        most = jnp.maximum(most, before)
    task_rows = []
    for delta in range(8):
        pick = slice(delta, delta + 1)
        task_rows.append(
            jnp.where(
                row8 == 0,
                first[pick],
                jnp.where(
                    row8 == 1,
                    second[pick],
                    jnp.where(
                        row8 == 2, to_first[pick], jnp.where(row8 == 3, to_second[pick], 0.0)
                    ),
                ),
            ).astype(BF16)
        )
    tasks = jnp.concatenate(task_rows, axis=1)
    slot_row = rows((128, 128)).astype(F32)
    for m in range(LIST // 128):
        chosen = jnp.concatenate(
            [
                jnp.where(place[delta : delta + 1, :] == slot_row + 128.0 * m, 1.0, 0.0).astype(BF16)
                for delta in range(8)
            ],
            axis=1,
        )
        part = dot_nt(tasks, chosen)
        part = jnp.where(row8 == 4, 2.0 * most, part)
        list_ref[:, m * 128 : (m + 1) * 128] = part.astype(jnp.int32)

    target = coupling_ref[...]
    reach = target - first_leaf + HALF
    swap = ((reach ^ row8) & 1) * (PAIRS // 2)
    entry = jnp.where(
        reach < HALF,
        LD + (reach >> 1) + swap,
        jnp.where(reach < HALF + LD, reach - HALF, LD + HALF + ((reach - HALF - LD) >> 1) + swap),
    )
    index_ref[0:8, :] = jnp.where(target >= 0, entry, TABLE - 1)
    index_ref[8:16, :] = jnp.where(target >= 0, reach, 0)


def point_features(points8, origin_z):
    row = rows(points8.shape)
    center = jnp.where(row == 2, origin_z + 0.5, 1.0)
    v = jnp.where(row < 3, (points8 - center) * SCALE, 0.0)
    norm = jnp.sum(v * v, axis=0, keepdims=True)
    far = jnp.where(row == 3, norm, jnp.where(row == 4, 1.0, v))
    own = jnp.where(row == 3, 1.0, jnp.where(row == 4, norm, -2.0 * v))
    return far, own


def far_stack(value):
    first, second, third = thirds(value)
    none = jnp.zeros(value.shape, F32)
    return jnp.concatenate(
        [first, first, first, second, second, third, none, none], axis=0
    ).astype(BF16)


def own_stack(value):
    first, second, third = thirds(value)
    none = jnp.zeros(value.shape, F32)
    return jnp.concatenate(
        [first, second, third, first, second, first, none, none], axis=0
    ).astype(BF16)


def identity():
    return jnp.where(rows((128, 128)) == lanes((128, 128)), 1.0, 0.0).astype(BF16)


def near_kernel(
    list_ref, x_ref, p_ref, out_ref,
    p8, far_feat, own_feat, back, tile0, tile1,
):
    first_group = device_index() * GROUPS
    p8[...] = jnp.zeros(p8.shape, F32)
    eye = identity()

    def features(m, carry):
        loaded = [p_ref[:, pl.ds(pl.multiple_of((4 * m + v) * 512, 512), 512)] for v in range(4)]
        for v in range(4):
            p8[v, 0:3, :] = loaded[v]
        made = []
        for v in range(4):
            coords = p8[v]
            origin_z = (first_group + 4 * m + v).astype(F32)
            far, own = point_features(coords, origin_z)
            _, own_up = point_features(coords, origin_z + 1.0)
            far = far_stack(far)
            parts = [far[:, k * P_SIZE : (k + 1) * P_SIZE] for k in range(4)]
            turned = dot_nt(eye, jnp.concatenate(parts, axis=0)).astype(BF16)
            made.append((turned, own_stack(own), own_stack(own_up)))
        for v in range(4):
            g = 4 * m + v
            turned, own, own_up = made[v]
            far_feat[2 * g] = turned[:, 0:128]
            far_feat[2 * g + 1] = turned[:, 128:256]
            for k in range(4):
                part = slice(k * P_SIZE, (k + 1) * P_SIZE)
                own_feat[4 * g + k] = own[:, part]
                own_feat[LD + 4 * g + k] = own_up[:, part]
        return carry

    lax.fori_loop(0, GROUPS // 4, features, 0)

    out_ref[...] = x_ref[...].astype(F32)
    for ref in (back, tile0, tile1):
        ref[...] = jnp.zeros(ref.shape, ref.dtype)

    total = list_ref[4, 0]
    steps = (total + BATCH - 1) // BATCH + 1
    low = lanes((128, 128)) < K

    def leaf_slice(i):
        return pl.ds(pl.multiple_of(i * P_SIZE, P_SIZE), P_SIZE)

    def phase(n, tile_new, tile_old):
        far, own, sources, updates = [], [], [], []
        for u in range(BATCH):
            k = (n + 1) * BATCH + u
            i, j = list_ref[0, k], list_ref[1, k]
            variant = ((j >> 2) - (i >> 2)) * LD
            far.append(far_feat[j >> 1])
            own.append(own_feat[variant + i])
        for u in range(BATCH):
            k = n * BATCH + u
            i, j = list_ref[0, k], list_ref[1, k]
            sources.append((x_ref[:, leaf_slice(j)], x_ref[:, leaf_slice(i)]))
        tiles = []
        for u in range(BATCH // 2):
            pick = jnp.where(low, far[2 * u], far[2 * u + 1])
            dist = dot(pick, block_diagonal(own[2 * u], own[2 * u + 1]))
            tiles.append(
                jnp.concatenate([decay(dist[:, 0:128]), decay_near(dist[:, 128:256])], axis=1).astype(BF16)
            )
            for h in range(2):
                k = n * BATCH + 2 * u + h
                tile = tile_old[u, :, h * 128 : h * 128 + 128]
                x_j, x_i = sources[2 * u + h]
                updates.append(
                    (
                        dot(x_j, tile) * list_ref[2, k].astype(F32),
                        dot_nt(x_i, tile) * list_ref[3, k].astype(F32),
                    )
                )
        for u in range(BATCH // 2):
            tile_new[u] = tiles[u]
        for u in range(BATCH):
            k = n * BATCH + u
            to_i = leaf_slice(list_ref[0, k])
            to_j = leaf_slice(list_ref[1, k])
            at_i = out_ref[:, to_i] + updates[u][0]
            at_j = back[:, to_j] + updates[u][1]
            out_ref[:, to_i] = at_i
            back[:, to_j] = at_j

    def two_phases(m, carry):
        phase(2 * m, tile0, tile1)
        phase(2 * m + 1, tile1, tile0)
        return carry

    lax.fori_loop(0, (steps + 1) // 2, two_phases, 0)

    def total_up(m, carry):
        place = pl.ds(pl.multiple_of(m * 1024, 1024), 1024)
        out_ref[:, place] += back[:, place]
        return carry

    lax.fori_loop(0, LD * P_SIZE // 1024, total_up, 0)


def down_kernel(
    shape_ref, lev_ref, t_ref, root_ref, down_ref, couple, pairs_scr, shapes,
):
    lane_u = lane_nodes()
    row_y, row_z = row_nodes()

    def siblings(m, carry):
        loaded = [lev_ref[9 * m + u] for u in range(9)]
        values = []
        for u in range(9):
            cluster = LD + 2 * (9 * m + u)
            left = [shape_ref[d, cluster] for d in range(4)]
            right = [shape_ref[d, cluster + 1] for d in range(4)]
            tile = sibling_tile(left, right, lane_u, row_y, row_z)
            values.append(sibling_apply(tile, loaded[u]))
        for u in range(9):
            couple[9 * m + u] = values[u]
        return carry

    lax.fori_loop(0, 7, siblings, 0)

    t_high, t_low = halves(doubled_transfer(t_ref))
    device = device_index()
    n = root_ref.shape[0]
    low = lanes((R, 128)) < K
    shift = lanes((1, 128)) == 2
    for k in range(n):
        shapes[k : k + 1, :] = root_ref[k, R // 2 : R // 2 + 1, :] + jnp.where(
            shift, (k * GROUPS) * SCALE, 0.0
        )
    for k in range(n // 2):
        left = root_ref[2 * k, 0 : R // 2, :]
        right = root_ref[2 * k + 1, 0 : R // 2, :]
        left = jnp.concatenate([left, pltpu.roll(left, K, 1)], axis=0)
        right = jnp.concatenate([pltpu.roll(right, K, 1), right], axis=0)
        pairs_scr[k] = jnp.where(low, left, right)
    source, count, pair_source = 0, n // 2, 0
    levels = []
    while count >= 1:
        levels.append((source, pair_source))
        if count > 1:
            pairs = pair_lanes(merge_up(pairs_scr[pl.ds(pair_source, count)], t_high, t_low))
            pairs_scr[pl.ds(pair_source + count, count // 2)] = pairs
            joined = merge_shape_rows(
                shapes[pl.ds(source, count, stride=2), :],
                shapes[pl.ds(source + 1, count, stride=2), :],
            )
            shapes[pl.ds(source + 2 * count, count), :] = joined
        source += 2 * count
        pair_source += count
        count //= 2
    couples = []
    for level, (source, pair_source) in enumerate(levels):
        pair = device >> (level + 1)
        left_row = shapes[pl.ds(source + 2 * pair, 1), :]
        right_row = shapes[pl.ds(source + 2 * pair + 1, 1), :]
        left = [jnp.broadcast_to(left_row[:, d : d + 1], (8, 128)) for d in range(4)]
        right = [jnp.broadcast_to(right_row[:, d : d + 1], (8, 128)) for d in range(4)]
        tile = sibling_tile(left, right, lane_u, row_y, row_z)
        couples.append(sibling_apply(tile, pairs_scr[pair_source + pair]))
    incoming = None
    for level in reversed(range(len(levels))):
        value = couples[level]
        if incoming is not None:
            value = value + push_down(incoming[None], t_high, t_low)[0]
        side = (device >> level) & 1
        keep_low = jnp.where(low, 1, 0) == (1 - side)
        incoming = jnp.where(keep_low, value, 0.0)
    value = couple[pl.ds(PAIR_OFFSETS[6], 1)] + push_down(incoming[None], t_high, t_low)
    for level in range(5, 0, -1):
        n = PAIRS >> level
        value = couple[pl.ds(PAIR_OFFSETS[level], n)] + push_down(
            children_of(value), t_high, t_low
        )
    down_ref[...] = push_down(children_of(value), t_high, t_low)


UNIT = 2


def couple_kernel(
    entries, shape_ref, prev_ref, next_ref, high_ref, low_ref,
    leaf_couple,
    shape_tab, high_tab, low_tab, halo_rows, halo_shape, sems,
    tiles0, lhs0, tiles1, lhs1,
):
    copies = [
        pltpu.make_async_copy(high_ref, high_tab.at[0:LD], sems.at[2]),
        pltpu.make_async_copy(low_ref, low_tab.at[0:LD], sems.at[3]),
    ]
    for k, ref in enumerate((prev_ref, next_ref)):
        parts = ref[68].astype(F32)
        halo_rows[k] = parts[0:8] + parts[8:16] + parts[16:24]
        copies.append(pltpu.make_async_copy(halo_rows.at[k], halo_shape.at[k], sems.at[k]))
    for copy in copies:
        copy.start()
    low32 = lanes((R, 128)) < K
    lane_u = lane_nodes()
    row8 = rows((8, 128))
    low8 = lanes((8, 128)) < K

    def shape_rows(read, k, shift):
        return jnp.where(
            row8 == 0,
            read(0, k),
            jnp.where(row8 == 1, read(1, k), jnp.where(row8 == 2, read(2, k) + shift, read(3, k))),
        )

    def own_nodes(m, carry):
        shape_tab[HALF + m] = shape_rows(lambda d, k: shape_ref[d, k], m, 0.0)
        return carry

    lax.fori_loop(0, LD, own_nodes, 0, unroll=8)
    for copy in copies[2:]:
        copy.wait()
    for side, ref in enumerate((prev_ref, next_ref)):
        first = LD + side * HALF

        def halo_pairs(m, carry):
            def read(d, k):
                return halo_shape[side, d, k]

            loaded = [
                (tab, 4 * m + v, ref[offset + 4 * m + v])
                for tab, offset in ((high_tab, 0), (low_tab, 32))
                for v in range(4)
            ]
            turned = [pltpu.roll(pair.astype(F32), K, 1).astype(BF16) for _, _, pair in loaded]
            source = HALF if side == 0 else 0
            place = 0 if side == 0 else HALF + LD
            shift = (2.0 * side - 1.0) * GROUPS * SCALE
            for v in range(8):
                shape_tab[place + 8 * m + v] = shape_rows(read, source + 8 * m + v, shift)
            for (tab, pair, value), other in zip(loaded, turned):
                tab[first + pair] = value
                tab[first + PAIRS // 2 + pair] = other
            return carry

        lax.fori_loop(0, PAIRS // 8, halo_pairs, 0)
    high_tab[TABLE - 1] = jnp.zeros((R, 128), BF16)
    low_tab[TABLE - 1] = jnp.zeros((R, 128), BF16)
    for copy in copies[:2]:
        copy.wait()

    row_y, row_z = row_nodes()

    def couple_load(pair):
        leaves = (2 * pair, 2 * pair + 1)
        own = jnp.where(low8, shape_tab[HALF + leaves[0]], shape_tab[HALF + leaves[1]])
        fars = []
        for s in range(8):
            e0, e1 = entries[8 + s, leaves[0]], entries[8 + s, leaves[1]]
            fars.append(jnp.where(low8, shape_tab[e0], shape_tab[e1]))
        sources = []
        for tab in (high_tab, low_tab):
            for h in range(2):
                for q in range(4):
                    e0, e1 = entries[2 * q, leaves[h]], entries[2 * q + 1, leaves[h]]
                    sources.append(jnp.where(low32, tab[e0], tab[e1]))
        return own, fars, sources

    def couple_tiles(own, fars):
        radius = jnp.broadcast_to(own[3:4], (8, 128))
        own = [jnp.broadcast_to(own[d : d + 1], (8, 128)) + radius * lane_u[d] for d in range(3)]
        tiles = []
        for far in fars:
            reach = jnp.broadcast_to(far[3:4], (8, 128))
            gap = [own[d] - jnp.broadcast_to(far[d : d + 1], (8, 128)) for d in range(3)]
            tile = tile_from_axes(
                [jnp.square(gap[0] - reach * NODE[b]) for b in range(4)],
                [jnp.square(gap[1] - reach * row_y[h]) for h in range(2)],
                jnp.square(gap[2] - reach * row_z),
            )
            tiles.append(halves(tile))
        return tiles

    def couple_apply(u, tiles, lhs):
        both = dot(lhs[u], tiles[u])
        both = both[0 : 2 * R, 0:128] + (both[2 * R : 4 * R, 0:128] + both[0 : 2 * R, 128:256])
        return jnp.where(low32, both[0:R], both[R : 2 * R])

    def couple_phase(n, new, old):
        tiles, lhs = new
        loaded = [couple_load(jnp.minimum(n * UNIT + u, PAIRS - 1)) for u in range(UNIT)]
        results, made = [], []
        for u in range(UNIT):
            results.append(couple_apply(u, *old))
            made.append(couple_tiles(loaded[u][0], loaded[u][1]))
        for u in range(UNIT):
            for k, value in enumerate(loaded[u][2]):
                r, q = k // 4, k % 4
                lhs[u, r * R : (r + 1) * R, q * 128 : (q + 1) * 128] = value
            for s, (high, low) in enumerate(made[u]):
                tiles[u, s * K : (s + 1) * K, 0:128] = high
                tiles[u, s * K : (s + 1) * K, 128:256] = low
        for u in range(UNIT):
            leaf_couple[n * UNIT + u] = results[u]

    buffers = ((tiles0, lhs0), (tiles1, lhs1))
    for ref in buffers[1]:
        ref[...] = jnp.zeros(ref.shape, ref.dtype)

    def couple_two(m, carry):
        couple_phase(2 * m, buffers[0], buffers[1])
        couple_phase(2 * m + 1, buffers[1], buffers[0])
        return carry

    lax.fori_loop(0, PAIRS // UNIT // 2 + 1, couple_two, 0)


def finish_kernel(
    counts, near_ref, p_ref, b_ref, prev_ref, next_ref, down_ref, leaf_couple,
    out_ref,
    p8, coords,
):
    device = device_index()

    def finish(m, carry):
        values = []
        for v in range(8):
            c = 8 * m + v
            value = (down_ref[c] + leaf_couple[c + UNIT]).astype(BF16)
            span = pl.ds(pl.multiple_of(c * 256, 256), 256)
            values.append(
                (
                    span,
                    near_ref[:, span]
                    + dot(value, block_diagonal(b_ref[2 * c], b_ref[2 * c + 1])),
                )
            )
        for span, value in values:
            out_ref[:, span] = value
        return carry

    lax.fori_loop(0, PAIRS // 8, finish, 0)

    p8[...] = jnp.zeros(p8.shape, F32)
    eye = identity()
    sides = ((prev_ref, 0), (next_ref, GROUPS - 1))
    for side, (halo_ref, group) in enumerate(sides):
        p8[side, 0:3, :] = p_ref[:, group * 512 : group * 512 + 512]
        coords[side] = halo_ref[69].astype(F32) + halo_ref[70].astype(F32) + halo_ref[71].astype(F32)

    def edge(k, carry):
        loaded = [
            (halo_ref[64 + k], coords[side, pl.ds(pl.multiple_of(8 * k, 8), 8), :], p8[side])
            for side, (halo_ref, _) in enumerate(sides)
        ]
        for side, (_, group) in enumerate(sides):
            x_far, far, own = loaded[side]
            origin_z = (device * GROUPS + group).astype(F32)
            _, own = point_features(own, origin_z)
            far, _ = point_features(far, origin_z)
            far = dot_nt(eye, far_stack(far)).astype(BF16)
            tiles = decay(dot(far, own_stack(own))).astype(BF16)
            products = dot(x_far, tiles)
            for i in range(4):
                delta = (4 + i - k) if side == 0 else (4 + k - i)
                weight = counts[8 * (1 - side) + jnp.clip(delta, 0, 7), 4 * group + i]
                place = slice((4 * group + i) * P_SIZE, (4 * group + i + 1) * P_SIZE)
                out_ref[:, place] += products[:, i * P_SIZE : (i + 1) * P_SIZE] * weight
        return carry

    lax.fori_loop(0, 4, edge, 0)


def shaped(*shape, dtype=F32):
    return jax.ShapeDtypeStruct(shape, dtype)


def vmem():
    return pl.BlockSpec(memory_space=pltpu.VMEM)


def smem():
    return pl.BlockSpec(memory_space=pltpu.SMEM)


PARAMS = pltpu.CompilerParams(vmem_limit_bytes=VMEM_LIMIT)


def per_device(charges, points, basis, transfer, near_list, coupling_list):
    near_rows = near_list.T
    coupling_rows = coupling_list.T
    devices = lax.axis_size("sub") * lax.axis_size("leaf")
    send_next, send_prev, high, low, lev, root, shapes = pl.pallas_call(
        leaf_kernel,
        name="leaf_up",
        out_shape=(
            shaped(SEND, R, 128, dtype=BF16),
            shaped(SEND, R, 128, dtype=BF16),
            shaped(LD, R, 128, dtype=BF16),
            shaped(LD, R, 128, dtype=BF16),
            shaped(PAIRS - 1, R, 128),
            shaped(devices, R // 2 + 8, 128),
            shaped(8, 256),
        ),
        in_specs=[vmem()] * 4,
        out_specs=[vmem()] * 7,
        scratch_shapes=[
            pltpu.VMEM((PAIRS, R, 128), F32),
            pltpu.VMEM((3, LD, 128), F32),
            pltpu.VMEM((256, 128), F32),
            pltpu.VMEM((8, 512), F32),
        ],
        compiler_params=PARAMS,
    )(charges, points, basis, transfer)

    roots = lax.all_to_all(root, AXES, 0, 0, tiled=True)
    forward = [(i, i + 1) for i in range(devices - 1)]
    backward = [(i + 1, i) for i in range(devices - 1)]
    from_prev = lax.ppermute(send_next, AXES, forward)
    from_next = lax.ppermute(send_prev, AXES, backward)

    tasks, counts, entries = pl.pallas_call(
        list_kernel,
        name="lists",
        out_shape=(
            shaped(8, LIST, dtype=jnp.int32),
            shaped(16, 128),
            shaped(16, 128, dtype=jnp.int32),
        ),
        in_specs=[vmem()] * 2,
        out_specs=[vmem()] * 3,
        compiler_params=PARAMS,
        cost_estimate=pl.CostEstimate(flops=1 << 24, bytes_accessed=1 << 16, transcendentals=0),
    )(near_rows, coupling_rows)
    near = pl.pallas_call(
        near_kernel,
        name="near_field",
        out_shape=shaped(R, LD * P_SIZE),
        in_specs=[smem(), vmem(), vmem()],
        out_specs=vmem(),
        scratch_shapes=[
            pltpu.VMEM((4, 8, 512), F32),
            pltpu.VMEM((PAIRS, P_SIZE, 2 * FEATS), BF16),
            pltpu.VMEM((2 * LD, FEATS, P_SIZE), BF16),
            pltpu.VMEM((R, LD * P_SIZE), F32),
            pltpu.VMEM((BATCH // 2, 128, 256), BF16),
            pltpu.VMEM((BATCH // 2, 128, 256), BF16),
        ],
        compiler_params=PARAMS,
        cost_estimate=pl.CostEstimate(
            flops=2 * 460 * 128 * 128 * 128, bytes_accessed=4 << 20, transcendentals=460 * 32768
        ),
    )(tasks, charges, points)

    down = pl.pallas_call(
        down_kernel,
        name="tree_down",
        out_shape=shaped(PAIRS, R, 128),
        in_specs=[smem()] + [vmem()] * 3,
        out_specs=vmem(),
        scratch_shapes=[
            pltpu.VMEM((PAIRS - 1, R, 128), F32),
            pltpu.VMEM((devices, R, 128), F32),
            pltpu.VMEM((2 * devices, 128), F32),
        ],
        compiler_params=PARAMS,
    )(shapes, lev, transfer, roots)

    stages = [
        pltpu.VMEM((UNIT, 512, 256), BF16),
        pltpu.VMEM((UNIT, 4 * R, 512), BF16),
    ]
    leaf_couple = pl.pallas_call(
        couple_kernel,
        name="leaf_couple",
        out_shape=shaped(PAIRS + 2 * UNIT, R, 128),
        in_specs=[smem()] * 2 + [vmem()] * 2 + [pl.BlockSpec(memory_space=pl.ANY)] * 2,
        out_specs=vmem(),
        scratch_shapes=[
            pltpu.VMEM((2 * LD, 8, 128), F32),
            pltpu.VMEM((TABLE, R, 128), BF16),
            pltpu.VMEM((TABLE, R, 128), BF16),
            pltpu.VMEM((2, 8, 128), F32),
            pltpu.SMEM((2, 8, 128), F32),
            pltpu.SemaphoreType.DMA((4,)),
        ]
        + stages
        + stages,
        compiler_params=PARAMS,
    )(entries, shapes, from_prev, from_next, high, low)

    return pl.pallas_call(
        finish_kernel,
        name="finish",
        out_shape=shaped(R, LD * P_SIZE),
        in_specs=[smem()] + [vmem()] * 7,
        out_specs=vmem(),
        scratch_shapes=[pltpu.VMEM((2, 8, 512), F32), pltpu.VMEM((2, R, 128), F32)],
        compiler_params=PARAMS,
    )(counts, near, points, basis, from_prev, from_next, down, leaf_couple)


def solution(mesh):
    in_specs = (
        P(None, AXES),
        P(None, AXES),
        P(AXES, None, None),
        P(),
        P(AXES, None),
        P(AXES, None),
    )
    return jax.shard_map(
        per_device, mesh=mesh, in_specs=in_specs, out_specs=P(None, AXES), check_vma=False
    )
```

```python
import functools
import math

import jax
import jax.numpy as jnp
from jax import lax
from jax.experimental import pallas as pl
from jax.experimental.pallas import tpu as pltpu
from jax.sharding import PartitionSpec as P

P_SIZE = 128
K = 64
R = 32
LD = 128
PAIRS = LD // 2
GROUPS = LD // 4
TABLE = 257
HALF = LD // 2
NEAR_REACH = 8
FEATS = 64
BATCH = 16
LIST = 896
SEND = 72
SCALE = 0.5 * math.log2(math.e)
NODE = [math.cos((2 * a + 1) * math.pi / 8) for a in range(4)]
AXES = ("leaf", "sub")
F32 = jnp.float32
BF16 = jnp.bfloat16
NT = (((1,), (1,)), ((), ()))
TINY = 1e-30
VMEM_LIMIT = 56 * 1024 * 1024


def lanes(shape):
    return lax.broadcasted_iota(jnp.int32, shape, len(shape) - 1)


def rows(shape):
    return lax.broadcasted_iota(jnp.int32, shape, len(shape) - 2)


def dot(a, b):
    return jnp.dot(a, b, preferred_element_type=F32)


def dot_nt(a, b):
    return lax.dot_general(a, b, NT, preferred_element_type=F32)


def halves(value):
    high = value.astype(BF16)
    return high, (value - high.astype(F32)).astype(BF16)


def thirds(value):
    first = value.astype(BF16).astype(F32)
    rest = value - first
    second = rest.astype(BF16).astype(F32)
    return first, second, rest - second


def unit_node(index):
    return jnp.where(
        index == 0,
        NODE[0],
        jnp.where(index == 1, NODE[1], jnp.where(index == 2, NODE[2], NODE[3])),
    ).astype(F32)


def lane_nodes():
    b = lanes((8, 128)) & 63
    return [unit_node(b >> 4), unit_node((b >> 2) & 3), unit_node(b & 3)]


def row_nodes():
    r = rows((8, 128))
    return [unit_node(r >> 2), unit_node((r >> 2) + 2)], unit_node(r & 3)


def decay(t):
    t = jnp.maximum(t, TINY)
    return jnp.exp2(-(t * lax.rsqrt(t)))


def tile_from_axes(x_sq, y_sq, z_sq):
    yz = [y_sq[0] + z_sq, y_sq[1] + z_sq]
    return decay(jnp.concatenate([x_sq[k // 2] + yz[k % 2] for k in range(8)], axis=0))


def doubled_transfer(t_ref):
    flat = t_ref[...].reshape(2 * K, K)
    return jnp.concatenate([flat, flat], axis=1)


def device_index():
    return lax.axis_index("leaf") * lax.axis_size("sub") + lax.axis_index("sub")


def merge_up(pairs, t_high, t_low):
    n = pairs.shape[0]
    high, low = halves(pairs.reshape(n * R, 128))
    out = dot(high, jnp.concatenate([t_high, t_low], axis=1))
    out = out[:, 0:128] + out[:, 128:256] + dot(low, t_high)
    return out.reshape(n, R, 128)


def pair_lanes(clusters):
    n = clusters.shape[0]
    split = clusters.reshape(n // 2, 2, R, 128)
    return jnp.where(lanes((1, R, 128)) < K, split[:, 0], split[:, 1])


def push_down(value, t_high, t_low):
    n = value.shape[0]
    high, low = halves(value.reshape(n * R, 128))
    out = dot_nt(high, jnp.concatenate([t_high, t_low], axis=0))
    out = out[:, 0:128] + out[:, 128:256] + dot_nt(low, t_high)
    return out.reshape(n, R, 128)


def children_of(pairs):
    lane = lanes((1, R, 128))
    left = jnp.where(lane < K, pairs, 0.0)
    right = jnp.where(lane < K, 0.0, pairs)
    return jnp.stack([left, right], axis=1).reshape(2 * pairs.shape[0], R, 128)


def merge_shape_rows(left, right):
    lane = lanes(left.shape)
    sep = left - right
    gap = jnp.sqrt(jnp.sum(jnp.where(lane < 3, sep * sep, 0.0), axis=1, keepdims=True))
    radius = jnp.maximum(left, right) + 0.5 * gap
    return jnp.where(lane == 3, radius, jnp.where(lane < 3, 0.5 * (left + right), 0.0))


def sibling_tile(left, right, lane_u, row_y, row_z):
    low = lanes((8, 128)) < K
    alpha = jnp.where(low, left[3], right[3])
    beta = jnp.where(low, right[3], left[3])
    base = [jnp.where(low, left[d] - right[d], right[d] - left[d]) - beta * lane_u[d] for d in range(3)]
    x_sq = [jnp.square(base[0] + alpha * NODE[a]) for a in range(4)]
    y_sq = [jnp.square(base[1] + alpha * row_y[h]) for h in range(2)]
    z_sq = jnp.square(base[2] + alpha * row_z)
    return tile_from_axes(x_sq, y_sq, z_sq)


def sibling_apply(tile, pair):
    low = lanes((R, 128)) < K
    swapped = pltpu.roll(pair, K, 1)
    stacked = jnp.concatenate(
        [jnp.where(low, swapped, 0.0), jnp.where(low, 0.0, swapped)], axis=0
    )
    high, low_part = halves(stacked)
    t_high, t_low = halves(tile)
    t_high = jnp.concatenate([t_high, t_high], axis=0)
    t_low = jnp.concatenate([t_low, t_low], axis=0)
    out = dot_nt(high, jnp.concatenate([t_high, t_low], axis=0))
    out = out[:, 0:128] + out[:, 128:256] + dot_nt(low_part, t_high)
    return jnp.where(low, out[:R], out[R:])


LEVEL_OFFSETS = [0, 128, 192, 224, 240, 248, 252, 254]
PAIR_OFFSETS = [0, 0, 32, 48, 56, 60, 62]


def block_diagonal(left, right):
    zero = jnp.zeros(left.shape, left.dtype)
    return jnp.concatenate(
        [jnp.concatenate([left, zero], axis=1), jnp.concatenate([zero, right], axis=1)], axis=0
    )


def make_lists(near_ref, coupling_ref, list_ref, count_ref, index_ref):
    first_leaf = device_index() * LD
    lane8 = lanes((8, 128))
    row8 = rows((8, 128))
    offset = jnp.where(near_ref[...] >= 0, near_ref[...] - first_leaf - lane8, 1000)

    def slots_at(delta):
        return jnp.sum(jnp.where(offset == delta, 1.0, 0.0), axis=0, keepdims=True)

    forward = jnp.concatenate([slots_at(delta) for delta in range(8)], axis=0)
    reverse = jnp.concatenate(
        [jnp.zeros((1, 128), F32)] + [slots_at(-delta) for delta in range(1, 8)], axis=0
    )
    count_ref[0:8, :] = forward
    count_ref[8:16, :] = reverse
    backward = jnp.concatenate(
        [jnp.zeros((1, 128), F32)]
        + [pltpu.roll(reverse[delta : delta + 1, :], 128 - delta, 1) for delta in range(1, 8)],
        axis=0,
    )
    turned = (row8 == 1) & ((lane8 & 3) == 2)
    leaf = lane8.astype(F32)
    other = leaf + row8.astype(F32)
    first = jnp.where(turned, other, leaf)
    second = jnp.where(turned, leaf, other)
    to_first = jnp.where(turned, backward, forward)
    to_second = jnp.where(turned, forward, backward)
    odd = jnp.where(turned, lane8, lane8 + row8) & 1
    wanted = (lane8 + row8 < LD) & (forward + backward > 0.0)
    earlier = jnp.where(rows((128, 128)) < lanes((128, 128)), 1.0, 0.0).astype(BF16)
    place = jnp.full((8, 128), -1.0, F32)
    most = jnp.zeros((1, 1), F32)
    for parity in range(2):
        flags = jnp.where(wanted & (odd == parity), 1.0, 0.0)
        rank = dot(flags.astype(BF16), earlier)
        totals = jnp.sum(flags, axis=1, keepdims=True)
        before = jnp.zeros((1, 1), F32)
        starts = []
        for delta in range(8):
            starts.append(before)
            before = before + totals[delta : delta + 1, :]
        rank = rank + jnp.concatenate(starts, axis=0)
        place = jnp.where(flags > 0.0, 2.0 * rank + (1.0 * BATCH + parity), place)
        most = jnp.maximum(most, before)
    task_rows = []
    for delta in range(8):
        pick = slice(delta, delta + 1)
        task_rows.append(
            jnp.where(
                row8 == 0,
                first[pick],
                jnp.where(
                    row8 == 1,
                    second[pick],
                    jnp.where(
                        row8 == 2, to_first[pick], jnp.where(row8 == 3, to_second[pick], 0.0)
                    ),
                ),
            ).astype(BF16)
        )
    tasks = jnp.concatenate(task_rows, axis=1)
    slot_row = rows((128, 128)).astype(F32)
    for m in range(LIST // 128):
        chosen = jnp.concatenate(
            [
                jnp.where(place[delta : delta + 1, :] == slot_row + 128.0 * m, 1.0, 0.0).astype(BF16)
                for delta in range(8)
            ],
            axis=1,
        )
        part = dot_nt(tasks, chosen)
        part = jnp.where(row8 == 4, 2.0 * most, part)
        list_ref[:, m * 128 : (m + 1) * 128] = part.astype(jnp.int32)

    target = coupling_ref[...]
    reach = target - first_leaf + HALF
    swap = ((reach ^ row8) & 1) * (PAIRS // 2)
    entry = jnp.where(
        reach < HALF,
        LD + (reach >> 1) + swap,
        jnp.where(reach < HALF + LD, reach - HALF, LD + HALF + ((reach - HALF - LD) >> 1) + swap),
    )
    index_ref[0:8, :] = jnp.where(target >= 0, entry, TABLE - 1)
    index_ref[8:16, :] = jnp.where(target >= 0, reach, 0)


CHUNKS = 4


def leaf_kernel(
    x_any, p_ref, b_any, t_ref, near_ref, coupling_ref,
    send_next, send_prev, high_any, low_any, lev_any, root_ref, shape_ref,
    list_ref, count_ref, index_ref,
    x_ref, b_ref, high_ref, low_ref, lev_ref, coef, pts, shapes, p8, sems,
):
    leaves = LD // CHUNKS
    copies = []
    for c in range(CHUNKS):
        span = slice(c * leaves * P_SIZE, (c + 1) * leaves * P_SIZE)
        part = slice(c * leaves, (c + 1) * leaves)
        copies.append(
            (
                pltpu.make_async_copy(x_any.at[:, span], x_ref.at[:, span], sems.at[c]),
                pltpu.make_async_copy(b_any.at[part], b_ref.at[part], sems.at[CHUNKS + c]),
            )
        )
    for pair in copies:
        for copy in pair:
            copy.start()
    origin = (device_index() * GROUPS).astype(F32)
    low32 = lanes((R, 128)) < K

    make_lists(near_ref, coupling_ref, list_ref, count_ref, index_ref)
    for i in range(LD):
        for d in range(3):
            pts[d, i : i + 1, :] = p_ref[d : d + 1, i * P_SIZE : (i + 1) * P_SIZE]
    centers, squares = [], 0.0
    for d in range(3):
        coords = (pts[d] - origin if d == 2 else pts[d]) * SCALE
        center = jnp.sum(coords, axis=1, keepdims=True) * (1.0 / P_SIZE)
        centers.append(center)
        squares = squares + jnp.square(coords - center)
    radius = jnp.sqrt(jnp.max(squares, axis=1, keepdims=True))
    lane = lanes((LD, 128))
    shapes[0:LD, :] = jnp.where(
        lane == 0,
        centers[0],
        jnp.where(
            lane == 1,
            centers[1],
            jnp.where(lane == 2, centers[2], jnp.where(lane == 3, radius, 0.0)),
        ),
    )
    count = LD // 2
    for level in range(1, 8):
        source = LEVEL_OFFSETS[level - 1]
        joined = merge_shape_rows(
            shapes[pl.ds(source, count, stride=2), :],
            shapes[pl.ds(source + 1, count, stride=2), :],
        )
        shapes[pl.ds(LEVEL_OFFSETS[level], count), :] = joined
        count //= 2
    shape_rows = jnp.concatenate(
        [jnp.transpose(shapes[0:128, :])[0:8], jnp.transpose(shapes[128:256, :])[0:8]], axis=1
    )
    shape_ref[...] = shape_rows

    def leaf_pairs(m, carry):
        values = []
        for v in range(16):
            leaf = 16 * m + v
            x = x_ref[:, pl.ds(pl.multiple_of(leaf * P_SIZE, P_SIZE), P_SIZE)]
            weights = b_ref[leaf]
            values.append(dot_nt(x, jnp.concatenate([weights, weights], axis=0)))
        for v in range(16):
            high_ref[16 * m + v], low_ref[16 * m + v] = halves(values[v])
        for v in range(8):
            coef[8 * m + v] = jnp.where(low32, values[2 * v], values[2 * v + 1])
        return carry

    for c in range(CHUNKS):
        for copy in copies[c]:
            copy.wait()
        steps = leaves // 16
        lax.fori_loop(c * steps, (c + 1) * steps, leaf_pairs, 0)
    leaving = [
        pltpu.make_async_copy(high_ref, high_any, sems.at[2 * CHUNKS]),
        pltpu.make_async_copy(low_ref, low_any, sems.at[2 * CHUNKS + 1]),
    ]
    for copy in leaving:
        copy.start()

    t_high, t_low = halves(doubled_transfer(t_ref))
    pairs = coef[...]
    for level in range(1, 7):
        pairs = pair_lanes(merge_up(pairs, t_high, t_low))
        lev_ref[pl.ds(PAIR_OFFSETS[level], pairs.shape[0])] = pairs
    leaving.append(pltpu.make_async_copy(lev_ref, lev_any, sems.at[2 * CHUNKS + 2]))
    leaving[2].start()
    root = merge_up(pairs, t_high, t_low)[0]

    low = lanes((R // 2, 128)) < K
    block = jnp.concatenate(
        [
            jnp.where(low, root[0 : R // 2], root[R // 2 : R]),
            jnp.broadcast_to(shapes[254:255, :], (8, 128)),
        ],
        axis=0,
    )
    root_ref[...] = jnp.broadcast_to(block[None], root_ref.shape)

    p8[...] = jnp.zeros((8, 512), F32)
    for send, first_pair, group in ((send_next, PAIRS // 2, GROUPS - 1), (send_prev, 0, 0)):

        def copy_pairs(m, carry):
            parts = [halves(coef[first_pair + 8 * m + v]) for v in range(8)]
            for v in range(8):
                send[8 * m + v], send[32 + 8 * m + v] = parts[v]
            return carry

        lax.fori_loop(0, PAIRS // 16, copy_pairs, 0)
        parts = thirds(shape_rows[:, 0:128])
        send[68] = jnp.concatenate(list(parts) + [jnp.zeros((8, 128), F32)], axis=0).astype(BF16)
        p8[0:3, :] = p_ref[:, group * 512 : group * 512 + 512]
        parts = thirds(p8[...])
        for k in range(4):
            send[64 + k] = x_ref[:, group * 512 + k * P_SIZE : group * 512 + (k + 1) * P_SIZE]
        for part in range(3):
            send[69 + part] = jnp.concatenate(
                [parts[part][:, k * P_SIZE : (k + 1) * P_SIZE] for k in range(4)], axis=0
            ).astype(BF16)
    for copy in leaving:
        copy.wait()


def point_features(points8, origin_z):
    row = rows(points8.shape)
    center = jnp.where(row == 2, origin_z + 0.5, 1.0)
    v = jnp.where(row < 3, (points8 - center) * SCALE, 0.0)
    norm = jnp.sum(v * v, axis=0, keepdims=True)
    far = jnp.where(row == 3, norm, jnp.where(row == 4, 1.0, v))
    own = jnp.where(row == 3, 1.0, jnp.where(row == 4, norm, -2.0 * v))
    return far, own


def far_stack(value):
    first, second, third = thirds(value)
    none = jnp.zeros(value.shape, F32)
    return jnp.concatenate(
        [first, first, first, second, second, third, none, none], axis=0
    ).astype(BF16)


def own_stack(value):
    first, second, third = thirds(value)
    none = jnp.zeros(value.shape, F32)
    return jnp.concatenate(
        [first, second, third, first, second, first, none, none], axis=0
    ).astype(BF16)


def identity():
    return jnp.where(rows((128, 128)) == lanes((128, 128)), 1.0, 0.0).astype(BF16)


def near_kernel(
    list_ref, x_ref, p_ref, out_ref,
    p8, far_feat, own_feat, tile0, tile1,
):
    first_group = device_index() * GROUPS
    p8[...] = jnp.zeros(p8.shape, F32)
    eye = identity()

    def features(m, carry):
        loaded = [p_ref[:, pl.ds(pl.multiple_of((4 * m + v) * 512, 512), 512)] for v in range(4)]
        for v in range(4):
            p8[v, 0:3, :] = loaded[v]
        made = []
        for v in range(4):
            coords = p8[v]
            origin_z = (first_group + 4 * m + v).astype(F32)
            far, own = point_features(coords, origin_z)
            _, own_up = point_features(coords, origin_z + 1.0)
            far = far_stack(far)
            parts = [far[:, k * P_SIZE : (k + 1) * P_SIZE] for k in range(4)]
            turned = dot_nt(eye, jnp.concatenate(parts, axis=0)).astype(BF16)
            made.append((turned, own_stack(own), own_stack(own_up)))
        for v in range(4):
            g = 4 * m + v
            turned, own, own_up = made[v]
            far_feat[2 * g] = turned[:, 0:128]
            far_feat[2 * g + 1] = turned[:, 128:256]
            for k in range(4):
                part = slice(k * P_SIZE, (k + 1) * P_SIZE)
                own_feat[4 * g + k] = own[:, part]
                own_feat[LD + 4 * g + k] = own_up[:, part]
        return carry

    lax.fori_loop(0, GROUPS // 4, features, 0)

    out_ref[...] = x_ref[...].astype(F32)
    for ref in (tile0, tile1):
        ref[...] = jnp.zeros(ref.shape, ref.dtype)

    total = list_ref[4, 0]
    steps = (total + BATCH - 1) // BATCH + 1
    low = lanes((128, 128)) < K

    def leaf_slice(i):
        return pl.ds(pl.multiple_of(i * P_SIZE, P_SIZE), P_SIZE)

    def phase(n, tile_new, tile_old):
        far, own, sources, updates = [], [], [], []
        for u in range(BATCH):
            k = (n + 1) * BATCH + u
            i, j = list_ref[0, k], list_ref[1, k]
            variant = ((j >> 2) - (i >> 2)) * LD
            far.append(far_feat[j >> 1])
            own.append(own_feat[variant + i])
        for u in range(BATCH):
            k = n * BATCH + u
            i, j = list_ref[0, k], list_ref[1, k]
            sources.append((x_ref[:, leaf_slice(j)], x_ref[:, leaf_slice(i)]))
        tiles = []
        for u in range(BATCH // 2):
            pick = jnp.where(low, far[2 * u], far[2 * u + 1])
            dist = dot(pick, block_diagonal(own[2 * u], own[2 * u + 1]))
            tiles.append(decay(dist).astype(BF16))
            for h in range(2):
                k = n * BATCH + 2 * u + h
                tile = tile_old[u, :, h * 128 : h * 128 + 128]
                x_j, x_i = sources[2 * u + h]
                updates.append(
                    (
                        dot(x_j, tile) * list_ref[2, k].astype(F32),
                        dot_nt(x_i, tile) * list_ref[3, k].astype(F32),
                    )
                )
        for u in range(BATCH // 2):
            tile_new[u] = tiles[u]
        for u in range(BATCH):
            k = n * BATCH + u
            to_i = leaf_slice(list_ref[0, k])
            to_j = leaf_slice(list_ref[1, k])
            out_ref[:, to_i] += updates[u][0]
            out_ref[:, to_j] += updates[u][1]

    def two_phases(m, carry):
        phase(2 * m, tile0, tile1)
        phase(2 * m + 1, tile1, tile0)
        return carry

    lax.fori_loop(0, (steps + 1) // 2, two_phases, 0)


def tree_down(shape_ref, lev_ref, t_ref, root_ref, down_ref, couple, pairs_scr, shapes):
    lane_u = lane_nodes()
    row_y, row_z = row_nodes()

    def siblings(m, carry):
        loaded = [lev_ref[9 * m + u] for u in range(9)]
        values = []
        for u in range(9):
            cluster = LD + 2 * (9 * m + u)
            left = [shape_ref[d, cluster] for d in range(4)]
            right = [shape_ref[d, cluster + 1] for d in range(4)]
            tile = sibling_tile(left, right, lane_u, row_y, row_z)
            values.append(sibling_apply(tile, loaded[u]))
        for u in range(9):
            couple[9 * m + u] = values[u]
        return carry

    lax.fori_loop(0, 7, siblings, 0)

    t_high, t_low = halves(doubled_transfer(t_ref))
    device = device_index()
    n = root_ref.shape[0]
    low = lanes((R, 128)) < K
    shift = lanes((1, 128)) == 2
    for k in range(n):
        shapes[k : k + 1, :] = root_ref[k, R // 2 : R // 2 + 1, :] + jnp.where(
            shift, (k * GROUPS) * SCALE, 0.0
        )
    for k in range(n // 2):
        left = root_ref[2 * k, 0 : R // 2, :]
        right = root_ref[2 * k + 1, 0 : R // 2, :]
        left = jnp.concatenate([left, pltpu.roll(left, K, 1)], axis=0)
        right = jnp.concatenate([pltpu.roll(right, K, 1), right], axis=0)
        pairs_scr[k] = jnp.where(low, left, right)
    source, count, pair_source = 0, n // 2, 0
    levels = []
    while count >= 1:
        levels.append((source, pair_source))
        if count > 1:
            pairs = pair_lanes(merge_up(pairs_scr[pl.ds(pair_source, count)], t_high, t_low))
            pairs_scr[pl.ds(pair_source + count, count // 2)] = pairs
            joined = merge_shape_rows(
                shapes[pl.ds(source, count, stride=2), :],
                shapes[pl.ds(source + 1, count, stride=2), :],
            )
            shapes[pl.ds(source + 2 * count, count), :] = joined
        source += 2 * count
        pair_source += count
        count //= 2
    couples = []
    for level, (source, pair_source) in enumerate(levels):
        pair = device >> (level + 1)
        left_row = shapes[pl.ds(source + 2 * pair, 1), :]
        right_row = shapes[pl.ds(source + 2 * pair + 1, 1), :]
        left = [jnp.broadcast_to(left_row[:, d : d + 1], (8, 128)) for d in range(4)]
        right = [jnp.broadcast_to(right_row[:, d : d + 1], (8, 128)) for d in range(4)]
        tile = sibling_tile(left, right, lane_u, row_y, row_z)
        couples.append(sibling_apply(tile, pairs_scr[pair_source + pair]))
    incoming = None
    for level in reversed(range(len(levels))):
        value = couples[level]
        if incoming is not None:
            value = value + push_down(incoming[None], t_high, t_low)[0]
        side = (device >> level) & 1
        keep_low = jnp.where(low, 1, 0) == (1 - side)
        incoming = jnp.where(keep_low, value, 0.0)
    value = couple[pl.ds(PAIR_OFFSETS[6], 1)] + push_down(incoming[None], t_high, t_low)
    for level in range(5, 0, -1):
        n = PAIRS >> level
        value = couple[pl.ds(PAIR_OFFSETS[level], n)] + push_down(
            children_of(value), t_high, t_low
        )
    down_ref[...] = push_down(children_of(value), t_high, t_low)


UNIT = 2


def couple_leaves(
    entries, shape_ref, prev_ref, next_ref, table_copies, leaf_couple,
    shape_tab, high_tab, low_tab, halo_rows, halo_shape, sems,
    tiles0, lhs0, tiles1, lhs1,
):
    copies = []
    for k, ref in enumerate((prev_ref, next_ref)):
        parts = ref[68].astype(F32)
        halo_rows[k] = parts[0:8] + parts[8:16] + parts[16:24]
        copies.append(pltpu.make_async_copy(halo_rows.at[k], halo_shape.at[k], sems.at[k]))
    for copy in copies:
        copy.start()
    low32 = lanes((R, 128)) < K
    lane_u = lane_nodes()
    row8 = rows((8, 128))
    low8 = lanes((8, 128)) < K

    def shape_rows(read, k, shift):
        return jnp.where(
            row8 == 0,
            read(0, k),
            jnp.where(row8 == 1, read(1, k), jnp.where(row8 == 2, read(2, k) + shift, read(3, k))),
        )

    def own_nodes(m, carry):
        shape_tab[HALF + m] = shape_rows(lambda d, k: shape_ref[d, k], m, 0.0)
        return carry

    lax.fori_loop(0, LD, own_nodes, 0, unroll=8)
    for copy in copies:
        copy.wait()
    for side, ref in enumerate((prev_ref, next_ref)):
        first = LD + side * HALF

        def halo_pairs(m, carry):
            def read(d, k):
                return halo_shape[side, d, k]

            loaded = [
                (tab, 4 * m + v, ref[offset + 4 * m + v])
                for tab, offset in ((high_tab, 0), (low_tab, 32))
                for v in range(4)
            ]
            turned = [pltpu.roll(pair.astype(F32), K, 1).astype(BF16) for _, _, pair in loaded]
            source = HALF if side == 0 else 0
            place = 0 if side == 0 else HALF + LD
            shift = (2.0 * side - 1.0) * GROUPS * SCALE
            for v in range(8):
                shape_tab[place + 8 * m + v] = shape_rows(read, source + 8 * m + v, shift)
            for (tab, pair, value), other in zip(loaded, turned):
                tab[first + pair] = value
                tab[first + PAIRS // 2 + pair] = other
            return carry

        lax.fori_loop(0, PAIRS // 8, halo_pairs, 0)
    high_tab[TABLE - 1] = jnp.zeros((R, 128), BF16)
    low_tab[TABLE - 1] = jnp.zeros((R, 128), BF16)
    for copy in table_copies:
        copy.wait()

    row_y, row_z = row_nodes()

    def couple_load(pair):
        leaves = (2 * pair, 2 * pair + 1)
        own = jnp.where(low8, shape_tab[HALF + leaves[0]], shape_tab[HALF + leaves[1]])
        fars = []
        for s in range(8):
            e0, e1 = entries[8 + s, leaves[0]], entries[8 + s, leaves[1]]
            fars.append(jnp.where(low8, shape_tab[e0], shape_tab[e1]))
        sources = []
        for tab in (high_tab, low_tab):
            for h in range(2):
                for q in range(4):
                    e0, e1 = entries[2 * q, leaves[h]], entries[2 * q + 1, leaves[h]]
                    sources.append(jnp.where(low32, tab[e0], tab[e1]))
        return own, fars, sources

    def couple_tiles(own, fars):
        radius = jnp.broadcast_to(own[3:4], (8, 128))
        own = [jnp.broadcast_to(own[d : d + 1], (8, 128)) + radius * lane_u[d] for d in range(3)]
        tiles = []
        for far in fars:
            reach = jnp.broadcast_to(far[3:4], (8, 128))
            gap = [own[d] - jnp.broadcast_to(far[d : d + 1], (8, 128)) for d in range(3)]
            tile = tile_from_axes(
                [jnp.square(gap[0] - reach * NODE[b]) for b in range(4)],
                [jnp.square(gap[1] - reach * row_y[h]) for h in range(2)],
                jnp.square(gap[2] - reach * row_z),
            )
            tiles.append(halves(tile))
        return tiles

    def couple_apply(u, tiles, lhs):
        both = dot(lhs[u], tiles[u])
        both = both[0 : 2 * R, 0:128] + (both[2 * R : 4 * R, 0:128] + both[0 : 2 * R, 128:256])
        return jnp.where(low32, both[0:R], both[R : 2 * R])

    def couple_phase(n, new, old):
        tiles, lhs = new
        loaded = [couple_load(jnp.minimum(n * UNIT + u, PAIRS - 1)) for u in range(UNIT)]
        results, made = [], []
        for u in range(UNIT):
            results.append(couple_apply(u, *old))
            made.append(couple_tiles(loaded[u][0], loaded[u][1]))
        for u in range(UNIT):
            for k, value in enumerate(loaded[u][2]):
                r, q = k // 4, k % 4
                lhs[u, r * R : (r + 1) * R, q * 128 : (q + 1) * 128] = value
            for s, (high, low) in enumerate(made[u]):
                tiles[u, s * K : (s + 1) * K, 0:128] = high
                tiles[u, s * K : (s + 1) * K, 128:256] = low
        for u in range(UNIT):
            leaf_couple[n * UNIT + u] = results[u]

    buffers = ((tiles0, lhs0), (tiles1, lhs1))
    for ref in buffers[1]:
        ref[...] = jnp.zeros(ref.shape, ref.dtype)

    def couple_two(m, carry):
        couple_phase(2 * m, buffers[0], buffers[1])
        couple_phase(2 * m + 1, buffers[1], buffers[0])
        return carry

    lax.fori_loop(0, PAIRS // UNIT // 2 + 1, couple_two, 0)


def finish_leaves(
    counts, p_ref, b_ref, prev_ref, next_ref, down_ref, leaf_couple, out_ref, p8, coords
):
    device = device_index()

    def finish(m, carry):
        values = []
        for v in range(8):
            c = 8 * m + v
            value = (down_ref[c] + leaf_couple[c + UNIT]).astype(BF16)
            span = pl.ds(pl.multiple_of(c * 256, 256), 256)
            values.append(
                (
                    span,
                    out_ref[:, span]
                    + dot(value, block_diagonal(b_ref[2 * c], b_ref[2 * c + 1])),
                )
            )
        for span, value in values:
            out_ref[:, span] = value
        return carry

    lax.fori_loop(0, PAIRS // 8, finish, 0)

    p8[...] = jnp.zeros(p8.shape, F32)
    eye = identity()
    sides = ((prev_ref, 0), (next_ref, GROUPS - 1))
    for side, (halo_ref, group) in enumerate(sides):
        p8[side, 0:3, :] = p_ref[:, group * 512 : group * 512 + 512]
        coords[side] = halo_ref[69].astype(F32) + halo_ref[70].astype(F32) + halo_ref[71].astype(F32)

    def edge(k, carry):
        loaded = [
            (halo_ref[64 + k], coords[side, pl.ds(pl.multiple_of(8 * k, 8), 8), :], p8[side])
            for side, (halo_ref, _) in enumerate(sides)
        ]
        for side, (_, group) in enumerate(sides):
            x_far, far, own = loaded[side]
            origin_z = (device * GROUPS + group).astype(F32)
            _, own = point_features(own, origin_z)
            far, _ = point_features(far, origin_z)
            far = dot_nt(eye, far_stack(far)).astype(BF16)
            tiles = decay(dot(far, own_stack(own))).astype(BF16)
            products = dot(x_far, tiles)
            for i in range(4):
                delta = (4 + i - k) if side == 0 else (4 + k - i)
                weight = counts[8 * (1 - side) + jnp.clip(delta, 0, 7), 4 * group + i]
                place = slice((4 * group + i) * P_SIZE, (4 * group + i + 1) * P_SIZE)
                out_ref[:, place] += products[:, i * P_SIZE : (i + 1) * P_SIZE] * weight
        return carry

    lax.fori_loop(0, 4, edge, 0)


def final_kernel(
    entries, shape_ref, counts,
    p_ref, t_ref,
    near_any, b_any, prev_any, next_any, high_any, low_any, lev_any, root_any,
    out_ref,
    b_ref, prev_ref, next_ref, lev_ref, root_ref, down, leaf_couple,
    couple, pairs_scr, shapes, shape_tab, high_tab, low_tab, halo_rows, halo_shape,
    tiles0, lhs0, tiles1, lhs1, p8, coords, sems, halo_sems,
):
    moves = (
        (lev_any, lev_ref),
        (root_any, root_ref),
        (prev_any, prev_ref),
        (next_any, next_ref),
        (high_any, high_tab.at[0:LD]),
        (low_any, low_tab.at[0:LD]),
        (b_any, b_ref),
        (near_any, out_ref),
    )
    copies = [pltpu.make_async_copy(a, b, sems.at[k]) for k, (a, b) in enumerate(moves)]
    for copy in copies:
        copy.start()
    copies[0].wait()
    copies[1].wait()
    tree_down(shape_ref, lev_ref, t_ref, root_ref, down, couple, pairs_scr, shapes)
    copies[2].wait()
    copies[3].wait()
    couple_leaves(
        entries, shape_ref, prev_ref, next_ref, copies[4:6], leaf_couple,
        shape_tab, high_tab, low_tab, halo_rows, halo_shape, halo_sems,
        tiles0, lhs0, tiles1, lhs1,
    )
    copies[6].wait()
    copies[7].wait()
    finish_leaves(
        counts, p_ref, b_ref, prev_ref, next_ref, down, leaf_couple, out_ref, p8, coords
    )


def shaped(*shape, dtype=F32):
    return jax.ShapeDtypeStruct(shape, dtype)


def vmem():
    return pl.BlockSpec(memory_space=pltpu.VMEM)


def smem():
    return pl.BlockSpec(memory_space=pltpu.SMEM)


def anywhere():
    return pl.BlockSpec(memory_space=pl.ANY)


PARAMS = pltpu.CompilerParams(vmem_limit_bytes=VMEM_LIMIT)


def per_device(charges, points, basis, transfer, near_list, coupling_list):
    near_rows = near_list.T
    coupling_rows = coupling_list.T
    devices = lax.axis_size("sub") * lax.axis_size("leaf")
    send_next, send_prev, high, low, lev, root, shapes, tasks, counts, entries = pl.pallas_call(
        leaf_kernel,
        name="leaf_up",
        out_shape=(
            shaped(SEND, R, 128, dtype=BF16),
            shaped(SEND, R, 128, dtype=BF16),
            shaped(LD, R, 128, dtype=BF16),
            shaped(LD, R, 128, dtype=BF16),
            shaped(PAIRS - 1, R, 128),
            shaped(devices, R // 2 + 8, 128),
            shaped(8, 256),
            shaped(8, LIST, dtype=jnp.int32),
            shaped(16, 128),
            shaped(16, 128, dtype=jnp.int32),
        ),
        in_specs=[anywhere(), vmem(), anywhere(), vmem(), vmem(), vmem()],
        out_specs=[vmem()] * 2 + [anywhere()] * 3 + [vmem()] * 5,
        scratch_shapes=[
            pltpu.VMEM((R, LD * P_SIZE), BF16),
            pltpu.VMEM((LD, K, P_SIZE), BF16),
            pltpu.VMEM((LD, R, 128), BF16),
            pltpu.VMEM((LD, R, 128), BF16),
            pltpu.VMEM((PAIRS - 1, R, 128), F32),
            pltpu.VMEM((PAIRS, R, 128), F32),
            pltpu.VMEM((3, LD, 128), F32),
            pltpu.VMEM((256, 128), F32),
            pltpu.VMEM((8, 512), F32),
            pltpu.SemaphoreType.DMA((2 * CHUNKS + 3,)),
        ],
        compiler_params=PARAMS,
    )(charges, points, basis, transfer, near_rows, coupling_rows)

    roots = lax.all_to_all(root, AXES, 0, 0, tiled=True)
    forward = [(i, i + 1) for i in range(devices - 1)]
    backward = [(i + 1, i) for i in range(devices - 1)]
    from_prev = lax.ppermute(send_next, AXES, forward)
    from_next = lax.ppermute(send_prev, AXES, backward)

    near = pl.pallas_call(
        near_kernel,
        name="near_field",
        out_shape=shaped(R, LD * P_SIZE),
        in_specs=[smem(), vmem(), vmem()],
        out_specs=vmem(),
        scratch_shapes=[
            pltpu.VMEM((4, 8, 512), F32),
            pltpu.VMEM((PAIRS, P_SIZE, 2 * FEATS), BF16),
            pltpu.VMEM((2 * LD, FEATS, P_SIZE), BF16),
            pltpu.VMEM((BATCH // 2, 128, 256), BF16),
            pltpu.VMEM((BATCH // 2, 128, 256), BF16),
        ],
        compiler_params=PARAMS,
        cost_estimate=pl.CostEstimate(
            flops=2 * 460 * 128 * 128 * 128, bytes_accessed=4 << 20, transcendentals=460 * 32768
        ),
    )(tasks, charges, points)

    stages = [
        pltpu.VMEM((UNIT, 512, 256), BF16),
        pltpu.VMEM((UNIT, 4 * R, 512), BF16),
    ]
    return pl.pallas_call(
        final_kernel,
        name="tree_couple_finish",
        out_shape=shaped(R, LD * P_SIZE),
        in_specs=[smem()] * 3 + [vmem()] * 2 + [anywhere()] * 8,
        out_specs=vmem(),
        scratch_shapes=[
            pltpu.VMEM((LD, K, P_SIZE), BF16),
            pltpu.VMEM((SEND, R, 128), BF16),
            pltpu.VMEM((SEND, R, 128), BF16),
            pltpu.VMEM((PAIRS - 1, R, 128), F32),
            pltpu.VMEM((devices, R // 2 + 8, 128), F32),
            pltpu.VMEM((PAIRS, R, 128), F32),
            pltpu.VMEM((PAIRS + 2 * UNIT, R, 128), F32),
            pltpu.VMEM((PAIRS - 1, R, 128), F32),
            pltpu.VMEM((devices, R, 128), F32),
            pltpu.VMEM((2 * devices, 128), F32),
            pltpu.VMEM((2 * LD, 8, 128), F32),
            pltpu.VMEM((TABLE, R, 128), BF16),
            pltpu.VMEM((TABLE, R, 128), BF16),
            pltpu.VMEM((2, 8, 128), F32),
            pltpu.SMEM((2, 8, 128), F32),
        ]
        + stages
        + stages
        + [
            pltpu.VMEM((2, 8, 512), F32),
            pltpu.VMEM((2, R, 128), F32),
            pltpu.SemaphoreType.DMA((8,)),
            pltpu.SemaphoreType.DMA((2,)),
        ],
        compiler_params=PARAMS,
    )(
        entries, shapes, counts, points, transfer,
        near, basis, from_prev, from_next, high, low, lev, roots,
    )


def solution(mesh):
    in_specs = (
        P(None, AXES),
        P(None, AXES),
        P(AXES, None, None),
        P(),
        P(AXES, None),
        P(AXES, None),
    )
    return jax.shard_map(
        per_device, mesh=mesh, in_specs=in_specs, out_specs=P(None, AXES), check_vma=False
    )
```

```python
import functools
import math

import jax
import jax.numpy as jnp
from jax import lax
from jax.experimental import pallas as pl
from jax.experimental.pallas import tpu as pltpu
from jax.sharding import PartitionSpec as P

P_SIZE = 128
K = 64
R = 32
LD = 128
PAIRS = LD // 2
GROUPS = LD // 4
TABLE = 257
HALF = LD // 2
NEAR_REACH = 8
FEATS = 64
BATCH = 16
LIST = 896
SEND = 72
SCALE = 0.5 * math.log2(math.e)
NODE = [math.cos((2 * a + 1) * math.pi / 8) for a in range(4)]
AXES = ("leaf", "sub")
F32 = jnp.float32
BF16 = jnp.bfloat16
NT = (((1,), (1,)), ((), ()))
TINY = 1e-30
VMEM_LIMIT = 56 * 1024 * 1024


def lanes(shape):
    return lax.broadcasted_iota(jnp.int32, shape, len(shape) - 1)


def rows(shape):
    return lax.broadcasted_iota(jnp.int32, shape, len(shape) - 2)


def dot(a, b):
    return jnp.dot(a, b, preferred_element_type=F32)


def dot_nt(a, b):
    return lax.dot_general(a, b, NT, preferred_element_type=F32)


def halves(value):
    high = value.astype(BF16)
    return high, (value - high.astype(F32)).astype(BF16)


def thirds(value):
    first = value.astype(BF16).astype(F32)
    rest = value - first
    second = rest.astype(BF16).astype(F32)
    return first, second, rest - second


def unit_node(index):
    return jnp.where(
        index == 0,
        NODE[0],
        jnp.where(index == 1, NODE[1], jnp.where(index == 2, NODE[2], NODE[3])),
    ).astype(F32)


def lane_nodes():
    b = lanes((8, 128)) & 63
    return [unit_node(b >> 4), unit_node((b >> 2) & 3), unit_node(b & 3)]


def row_nodes():
    r = rows((8, 128))
    return [unit_node(r >> 2), unit_node((r >> 2) + 2)], unit_node(r & 3)


def decay(t):
    t = jnp.maximum(t, TINY)
    return jnp.exp2(-(t * lax.rsqrt(t)))


def tile_from_axes(x_sq, y_sq, z_sq):
    yz = [y_sq[0] + z_sq, y_sq[1] + z_sq]
    return decay(jnp.concatenate([x_sq[k // 2] + yz[k % 2] for k in range(8)], axis=0))


def doubled_transfer(t_ref):
    flat = t_ref[...].reshape(2 * K, K)
    return jnp.concatenate([flat, flat], axis=1)


def device_index():
    return lax.axis_index("leaf") * lax.axis_size("sub") + lax.axis_index("sub")


def merge_up(pairs, t_high, t_low):
    n = pairs.shape[0]
    high, low = halves(pairs.reshape(n * R, 128))
    out = dot(high, jnp.concatenate([t_high, t_low], axis=1))
    out = out[:, 0:128] + out[:, 128:256] + dot(low, t_high)
    return out.reshape(n, R, 128)


def pair_lanes(clusters):
    n = clusters.shape[0]
    split = clusters.reshape(n // 2, 2, R, 128)
    return jnp.where(lanes((1, R, 128)) < K, split[:, 0], split[:, 1])


def push_down(value, t_high, t_low):
    n = value.shape[0]
    high, low = halves(value.reshape(n * R, 128))
    out = dot_nt(high, jnp.concatenate([t_high, t_low], axis=0))
    out = out[:, 0:128] + out[:, 128:256] + dot_nt(low, t_high)
    return out.reshape(n, R, 128)


def children_of(pairs):
    lane = lanes((1, R, 128))
    left = jnp.where(lane < K, pairs, 0.0)
    right = jnp.where(lane < K, 0.0, pairs)
    return jnp.stack([left, right], axis=1).reshape(2 * pairs.shape[0], R, 128)


def merge_shape_rows(left, right):
    lane = lanes(left.shape)
    sep = left - right
    gap = jnp.sqrt(jnp.sum(jnp.where(lane < 3, sep * sep, 0.0), axis=1, keepdims=True))
    radius = jnp.maximum(left, right) + 0.5 * gap
    return jnp.where(lane == 3, radius, jnp.where(lane < 3, 0.5 * (left + right), 0.0))


def sibling_tile(left, right, lane_u, row_y, row_z):
    low = lanes((8, 128)) < K
    alpha = jnp.where(low, left[3], right[3])
    beta = jnp.where(low, right[3], left[3])
    base = [jnp.where(low, left[d] - right[d], right[d] - left[d]) - beta * lane_u[d] for d in range(3)]
    x_sq = [jnp.square(base[0] + alpha * NODE[a]) for a in range(4)]
    y_sq = [jnp.square(base[1] + alpha * row_y[h]) for h in range(2)]
    z_sq = jnp.square(base[2] + alpha * row_z)
    return tile_from_axes(x_sq, y_sq, z_sq)


def sibling_apply(tile, pair):
    low = lanes((R, 128)) < K
    swapped = pltpu.roll(pair, K, 1)
    stacked = jnp.concatenate(
        [jnp.where(low, swapped, 0.0), jnp.where(low, 0.0, swapped)], axis=0
    )
    high, low_part = halves(stacked)
    t_high, t_low = halves(tile)
    t_high = jnp.concatenate([t_high, t_high], axis=0)
    t_low = jnp.concatenate([t_low, t_low], axis=0)
    out = dot_nt(high, jnp.concatenate([t_high, t_low], axis=0))
    out = out[:, 0:128] + out[:, 128:256] + dot_nt(low_part, t_high)
    return jnp.where(low, out[:R], out[R:])


LEVEL_OFFSETS = [0, 128, 192, 224, 240, 248, 252, 254]
PAIR_OFFSETS = [0, 0, 32, 48, 56, 60, 62]


def block_diagonal(left, right):
    zero = jnp.zeros(left.shape, left.dtype)
    return jnp.concatenate(
        [jnp.concatenate([left, zero], axis=1), jnp.concatenate([zero, right], axis=1)], axis=0
    )


def make_lists(near_ref, coupling_ref, list_ref, count_ref, index_ref):
    first_leaf = device_index() * LD
    lane8 = lanes((8, 128))
    row8 = rows((8, 128))
    offset = jnp.where(near_ref[...] >= 0, near_ref[...] - first_leaf - lane8, 1000)

    def slots_at(delta):
        return jnp.sum(jnp.where(offset == delta, 1.0, 0.0), axis=0, keepdims=True)

    forward = jnp.concatenate([slots_at(delta) for delta in range(8)], axis=0)
    reverse = jnp.concatenate(
        [jnp.zeros((1, 128), F32)] + [slots_at(-delta) for delta in range(1, 8)], axis=0
    )
    count_ref[0:8, :] = forward
    count_ref[8:16, :] = reverse
    backward = jnp.concatenate(
        [jnp.zeros((1, 128), F32)]
        + [pltpu.roll(reverse[delta : delta + 1, :], 128 - delta, 1) for delta in range(1, 8)],
        axis=0,
    )
    turned = (row8 == 1) & ((lane8 & 3) == 2)
    leaf = lane8.astype(F32)
    other = leaf + row8.astype(F32)
    first = jnp.where(turned, other, leaf)
    second = jnp.where(turned, leaf, other)
    to_first = jnp.where(turned, backward, forward)
    to_second = jnp.where(turned, forward, backward)
    odd = jnp.where(turned, lane8, lane8 + row8) & 1
    wanted = (lane8 + row8 < LD) & (forward + backward > 0.0)
    earlier = jnp.where(rows((128, 128)) < lanes((128, 128)), 1.0, 0.0).astype(BF16)
    place = jnp.full((8, 128), -1.0, F32)
    most = jnp.zeros((1, 1), F32)
    for parity in range(2):
        flags = jnp.where(wanted & (odd == parity), 1.0, 0.0)
        rank = dot(flags.astype(BF16), earlier)
        totals = jnp.sum(flags, axis=1, keepdims=True)
        before = jnp.zeros((1, 1), F32)
        starts = []
        for delta in range(8):
            starts.append(before)
            before = before + totals[delta : delta + 1, :]
        rank = rank + jnp.concatenate(starts, axis=0)
        place = jnp.where(flags > 0.0, 2.0 * rank + (1.0 * BATCH + parity), place)
        most = jnp.maximum(most, before)
    task_rows = []
    for delta in range(8):
        pick = slice(delta, delta + 1)
        task_rows.append(
            jnp.where(
                row8 == 0,
                first[pick],
                jnp.where(
                    row8 == 1,
                    second[pick],
                    jnp.where(
                        row8 == 2, to_first[pick], jnp.where(row8 == 3, to_second[pick], 0.0)
                    ),
                ),
            ).astype(BF16)
        )
    tasks = jnp.concatenate(task_rows, axis=1)
    slot_row = rows((128, 128)).astype(F32)
    for m in range(LIST // 128):
        chosen = jnp.concatenate(
            [
                jnp.where(place[delta : delta + 1, :] == slot_row + 128.0 * m, 1.0, 0.0).astype(BF16)
                for delta in range(8)
            ],
            axis=1,
        )
        part = dot_nt(tasks, chosen)
        part = jnp.where(row8 == 4, 2.0 * most, part)
        list_ref[:, m * 128 : (m + 1) * 128] = part.astype(jnp.int32)

    target = coupling_ref[...]
    reach = target - first_leaf + HALF
    swap = ((reach ^ row8) & 1) * (PAIRS // 2)
    entry = jnp.where(
        reach < HALF,
        LD + (reach >> 1) + swap,
        jnp.where(reach < HALF + LD, reach - HALF, LD + HALF + ((reach - HALF - LD) >> 1) + swap),
    )
    index_ref[0:8, :] = jnp.where(target >= 0, entry, TABLE - 1)
    index_ref[8:16, :] = jnp.where(target >= 0, reach, 0)


CHUNKS = 4


def leaf_kernel(
    x_any, p_ref, b_any, t_ref, near_ref, coupling_ref,
    send_next, send_prev, high_any, low_any, lev_any, root_ref, shape_ref,
    list_ref, count_ref, index_ref,
    x_ref, b_ref, high_ref, low_ref, lev_ref, coef, pts, shapes, p8, sems,
):
    leaves = LD // CHUNKS
    copies = []
    for c in range(CHUNKS):
        span = slice(c * leaves * P_SIZE, (c + 1) * leaves * P_SIZE)
        part = slice(c * leaves, (c + 1) * leaves)
        copies.append(
            (
                pltpu.make_async_copy(x_any.at[:, span], x_ref.at[:, span], sems.at[c]),
                pltpu.make_async_copy(b_any.at[part], b_ref.at[part], sems.at[CHUNKS + c]),
            )
        )
    for pair in copies:
        for copy in pair:
            copy.start()
    origin = (device_index() * GROUPS).astype(F32)
    low32 = lanes((R, 128)) < K

    make_lists(near_ref, coupling_ref, list_ref, count_ref, index_ref)
    for i in range(LD):
        for d in range(3):
            pts[d, i : i + 1, :] = p_ref[d : d + 1, i * P_SIZE : (i + 1) * P_SIZE]
    centers, squares = [], 0.0
    for d in range(3):
        coords = (pts[d] - origin if d == 2 else pts[d]) * SCALE
        center = jnp.sum(coords, axis=1, keepdims=True) * (1.0 / P_SIZE)
        centers.append(center)
        squares = squares + jnp.square(coords - center)
    radius = jnp.sqrt(jnp.max(squares, axis=1, keepdims=True))
    lane = lanes((LD, 128))
    shapes[0:LD, :] = jnp.where(
        lane == 0,
        centers[0],
        jnp.where(
            lane == 1,
            centers[1],
            jnp.where(lane == 2, centers[2], jnp.where(lane == 3, radius, 0.0)),
        ),
    )
    count = LD // 2
    for level in range(1, 8):
        source = LEVEL_OFFSETS[level - 1]
        joined = merge_shape_rows(
            shapes[pl.ds(source, count, stride=2), :],
            shapes[pl.ds(source + 1, count, stride=2), :],
        )
        shapes[pl.ds(LEVEL_OFFSETS[level], count), :] = joined
        count //= 2
    shape_rows = jnp.concatenate(
        [jnp.transpose(shapes[0:128, :])[0:8], jnp.transpose(shapes[128:256, :])[0:8]], axis=1
    )
    shape_ref[...] = shape_rows

    def leaf_pairs(m, carry):
        values = []
        for v in range(16):
            leaf = 16 * m + v
            x = x_ref[:, pl.ds(pl.multiple_of(leaf * P_SIZE, P_SIZE), P_SIZE)]
            weights = b_ref[leaf]
            values.append(dot_nt(x, jnp.concatenate([weights, weights], axis=0)))
        for v in range(16):
            high_ref[16 * m + v], low_ref[16 * m + v] = halves(values[v])
        for v in range(8):
            coef[8 * m + v] = jnp.where(low32, values[2 * v], values[2 * v + 1])
        return carry

    for c in range(CHUNKS):
        for copy in copies[c]:
            copy.wait()
        steps = leaves // 16
        lax.fori_loop(c * steps, (c + 1) * steps, leaf_pairs, 0)
    leaving = [
        pltpu.make_async_copy(high_ref, high_any, sems.at[2 * CHUNKS]),
        pltpu.make_async_copy(low_ref, low_any, sems.at[2 * CHUNKS + 1]),
    ]
    for copy in leaving:
        copy.start()

    t_high, t_low = halves(doubled_transfer(t_ref))
    pairs = coef[...]
    for level in range(1, 7):
        pairs = pair_lanes(merge_up(pairs, t_high, t_low))
        lev_ref[pl.ds(PAIR_OFFSETS[level], pairs.shape[0])] = pairs
    leaving.append(pltpu.make_async_copy(lev_ref, lev_any, sems.at[2 * CHUNKS + 2]))
    leaving[2].start()
    root = merge_up(pairs, t_high, t_low)[0]

    low = lanes((R // 2, 128)) < K
    block = jnp.concatenate(
        [
            jnp.where(low, root[0 : R // 2], root[R // 2 : R]),
            jnp.broadcast_to(shapes[254:255, :], (8, 128)),
        ],
        axis=0,
    )
    root_ref[...] = jnp.broadcast_to(block[None], root_ref.shape)

    p8[...] = jnp.zeros((8, 512), F32)
    for send, first_pair, group in ((send_next, PAIRS // 2, GROUPS - 1), (send_prev, 0, 0)):

        def copy_pairs(m, carry):
            parts = [halves(coef[first_pair + 8 * m + v]) for v in range(8)]
            for v in range(8):
                send[8 * m + v], send[32 + 8 * m + v] = parts[v]
            return carry

        lax.fori_loop(0, PAIRS // 16, copy_pairs, 0)
        parts = thirds(shape_rows[:, 0:128])
        send[68] = jnp.concatenate(list(parts) + [jnp.zeros((8, 128), F32)], axis=0).astype(BF16)
        p8[0:3, :] = p_ref[:, group * 512 : group * 512 + 512]
        parts = thirds(p8[...])
        for k in range(4):
            send[64 + k] = x_ref[:, group * 512 + k * P_SIZE : group * 512 + (k + 1) * P_SIZE]
        for part in range(3):
            send[69 + part] = jnp.concatenate(
                [parts[part][:, k * P_SIZE : (k + 1) * P_SIZE] for k in range(4)], axis=0
            ).astype(BF16)
    for copy in leaving:
        copy.wait()


def point_features(points8, origin_z):
    row = rows(points8.shape)
    center = jnp.where(row == 2, origin_z + 0.5, 1.0)
    v = jnp.where(row < 3, (points8 - center) * SCALE, 0.0)
    norm = jnp.sum(v * v, axis=0, keepdims=True)
    far = jnp.where(row == 3, norm, jnp.where(row == 4, 1.0, v))
    own = jnp.where(row == 3, 1.0, jnp.where(row == 4, norm, -2.0 * v))
    return far, own


def far_stack(value):
    first, second, third = thirds(value)
    none = jnp.zeros(value.shape, F32)
    return jnp.concatenate(
        [first, first, first, second, second, third, none, none], axis=0
    ).astype(BF16)


def own_stack(value):
    first, second, third = thirds(value)
    none = jnp.zeros(value.shape, F32)
    return jnp.concatenate(
        [first, second, third, first, second, first, none, none], axis=0
    ).astype(BF16)


def identity():
    return jnp.where(rows((128, 128)) == lanes((128, 128)), 1.0, 0.0).astype(BF16)


def near_kernel(
    list_ref, x_ref, p_ref, out_ref,
    p8, far_feat, own_feat, tile0, tile1,
):
    first_group = device_index() * GROUPS
    p8[...] = jnp.zeros(p8.shape, F32)
    eye = identity()

    def features(m, carry):
        loaded = [p_ref[:, pl.ds(pl.multiple_of((4 * m + v) * 512, 512), 512)] for v in range(4)]
        for v in range(4):
            p8[v, 0:3, :] = loaded[v]
        made = []
        for v in range(4):
            coords = p8[v]
            origin_z = (first_group + 4 * m + v).astype(F32)
            far, own = point_features(coords, origin_z)
            _, own_up = point_features(coords, origin_z + 1.0)
            far = far_stack(far)
            parts = [far[:, k * P_SIZE : (k + 1) * P_SIZE] for k in range(4)]
            turned = dot_nt(eye, jnp.concatenate(parts, axis=0)).astype(BF16)
            made.append((turned, own_stack(own), own_stack(own_up)))
        for v in range(4):
            g = 4 * m + v
            turned, own, own_up = made[v]
            far_feat[2 * g] = turned[:, 0:128]
            far_feat[2 * g + 1] = turned[:, 128:256]
            for k in range(4):
                part = slice(k * P_SIZE, (k + 1) * P_SIZE)
                own_feat[4 * g + k] = own[:, part]
                own_feat[LD + 4 * g + k] = own_up[:, part]
        return carry

    lax.fori_loop(0, GROUPS // 4, features, 0)

    out_ref[...] = x_ref[...].astype(F32)
    for ref in (tile0, tile1):
        ref[...] = jnp.zeros(ref.shape, ref.dtype)

    total = list_ref[4, 0]
    steps = (total + BATCH - 1) // BATCH + 1
    low = lanes((128, 128)) < K

    def leaf_slice(i):
        return pl.ds(pl.multiple_of(i * P_SIZE, P_SIZE), P_SIZE)

    def phase(n, tile_new, tile_old):
        far, own, sources, updates = [], [], [], []
        for u in range(BATCH):
            k = (n + 1) * BATCH + u
            i, j = list_ref[0, k], list_ref[1, k]
            variant = ((j >> 2) - (i >> 2)) * LD
            far.append(far_feat[j >> 1])
            own.append(own_feat[variant + i])
        for u in range(BATCH):
            k = n * BATCH + u
            i, j = list_ref[0, k], list_ref[1, k]
            sources.append((x_ref[:, leaf_slice(j)], x_ref[:, leaf_slice(i)]))
        tiles = []
        for u in range(BATCH // 2):
            pick = jnp.where(low, far[2 * u], far[2 * u + 1])
            dist = dot(pick, block_diagonal(own[2 * u], own[2 * u + 1]))
            tiles.append(decay(dist).astype(BF16))
            weights = block_diagonal(tile_old[u, :, 0:128], tile_old[u, :, 128:256])
            to_i = dot(jnp.concatenate([sources[2 * u][0], sources[2 * u + 1][0]], axis=1), weights)
            to_j = dot_nt(jnp.concatenate([sources[2 * u][1], sources[2 * u + 1][1]], axis=1), weights)
            for h in range(2):
                k = n * BATCH + 2 * u + h
                span = slice(h * 128, (h + 1) * 128)
                updates.append(
                    (
                        to_i[:, span] * list_ref[2, k].astype(F32),
                        to_j[:, span] * list_ref[3, k].astype(F32),
                    )
                )
        for u in range(BATCH // 2):
            tile_new[u] = tiles[u]
        for u in range(BATCH):
            k = n * BATCH + u
            to_i = leaf_slice(list_ref[0, k])
            to_j = leaf_slice(list_ref[1, k])
            out_ref[:, to_i] += updates[u][0]
            out_ref[:, to_j] += updates[u][1]

    def two_phases(m, carry):
        phase(2 * m, tile0, tile1)
        phase(2 * m + 1, tile1, tile0)
        return carry

    lax.fori_loop(0, (steps + 1) // 2, two_phases, 0)


def tree_down(shape_ref, lev_ref, t_ref, root_ref, down_ref, couple, pairs_scr, shapes):
    lane_u = lane_nodes()
    row_y, row_z = row_nodes()

    def siblings(m, carry):
        loaded = [lev_ref[9 * m + u] for u in range(9)]
        values = []
        for u in range(9):
            cluster = LD + 2 * (9 * m + u)
            left = [shape_ref[d, cluster] for d in range(4)]
            right = [shape_ref[d, cluster + 1] for d in range(4)]
            tile = sibling_tile(left, right, lane_u, row_y, row_z)
            values.append(sibling_apply(tile, loaded[u]))
        for u in range(9):
            couple[9 * m + u] = values[u]
        return carry

    lax.fori_loop(0, 7, siblings, 0)

    t_high, t_low = halves(doubled_transfer(t_ref))
    device = device_index()
    n = root_ref.shape[0]
    low = lanes((R, 128)) < K
    shift = lanes((1, 128)) == 2
    for k in range(n):
        shapes[k : k + 1, :] = root_ref[k, R // 2 : R // 2 + 1, :] + jnp.where(
            shift, (k * GROUPS) * SCALE, 0.0
        )
    for k in range(n // 2):
        left = root_ref[2 * k, 0 : R // 2, :]
        right = root_ref[2 * k + 1, 0 : R // 2, :]
        left = jnp.concatenate([left, pltpu.roll(left, K, 1)], axis=0)
        right = jnp.concatenate([pltpu.roll(right, K, 1), right], axis=0)
        pairs_scr[k] = jnp.where(low, left, right)
    source, count, pair_source = 0, n // 2, 0
    levels = []
    while count >= 1:
        levels.append((source, pair_source))
        if count > 1:
            pairs = pair_lanes(merge_up(pairs_scr[pl.ds(pair_source, count)], t_high, t_low))
            pairs_scr[pl.ds(pair_source + count, count // 2)] = pairs
            joined = merge_shape_rows(
                shapes[pl.ds(source, count, stride=2), :],
                shapes[pl.ds(source + 1, count, stride=2), :],
            )
            shapes[pl.ds(source + 2 * count, count), :] = joined
        source += 2 * count
        pair_source += count
        count //= 2
    couples = []
    for level, (source, pair_source) in enumerate(levels):
        pair = device >> (level + 1)
        left_row = shapes[pl.ds(source + 2 * pair, 1), :]
        right_row = shapes[pl.ds(source + 2 * pair + 1, 1), :]
        left = [jnp.broadcast_to(left_row[:, d : d + 1], (8, 128)) for d in range(4)]
        right = [jnp.broadcast_to(right_row[:, d : d + 1], (8, 128)) for d in range(4)]
        tile = sibling_tile(left, right, lane_u, row_y, row_z)
        couples.append(sibling_apply(tile, pairs_scr[pair_source + pair]))
    incoming = None
    for level in reversed(range(len(levels))):
        value = couples[level]
        if incoming is not None:
            value = value + push_down(incoming[None], t_high, t_low)[0]
        side = (device >> level) & 1
        keep_low = jnp.where(low, 1, 0) == (1 - side)
        incoming = jnp.where(keep_low, value, 0.0)
    value = couple[pl.ds(PAIR_OFFSETS[6], 1)] + push_down(incoming[None], t_high, t_low)
    for level in range(5, 0, -1):
        n = PAIRS >> level
        value = couple[pl.ds(PAIR_OFFSETS[level], n)] + push_down(
            children_of(value), t_high, t_low
        )
    down_ref[...] = push_down(children_of(value), t_high, t_low)


UNIT = 4


def couple_leaves(
    entries, shape_ref, prev_ref, next_ref, table_copies, leaf_couple,
    shape_tab, high_tab, low_tab, halo_rows, halo_shape, sems,
    tiles0, lhs0, tiles1, lhs1,
):
    copies = []
    for k, ref in enumerate((prev_ref, next_ref)):
        parts = ref[68].astype(F32)
        halo_rows[k] = parts[0:8] + parts[8:16] + parts[16:24]
        copies.append(pltpu.make_async_copy(halo_rows.at[k], halo_shape.at[k], sems.at[k]))
    for copy in copies:
        copy.start()
    low32 = lanes((R, 128)) < K
    lane_u = lane_nodes()
    row8 = rows((8, 128))
    low8 = lanes((8, 128)) < K

    def shape_rows(read, k, shift):
        return jnp.where(
            row8 == 0,
            read(0, k),
            jnp.where(row8 == 1, read(1, k), jnp.where(row8 == 2, read(2, k) + shift, read(3, k))),
        )

    def own_nodes(m, carry):
        shape_tab[HALF + m] = shape_rows(lambda d, k: shape_ref[d, k], m, 0.0)
        return carry

    lax.fori_loop(0, LD, own_nodes, 0, unroll=8)
    for copy in copies:
        copy.wait()
    for side, ref in enumerate((prev_ref, next_ref)):
        first = LD + side * HALF

        def halo_pairs(m, carry):
            def read(d, k):
                return halo_shape[side, d, k]

            loaded = [
                (tab, 4 * m + v, ref[offset + 4 * m + v])
                for tab, offset in ((high_tab, 0), (low_tab, 32))
                for v in range(4)
            ]
            turned = [pltpu.roll(pair.astype(F32), K, 1).astype(BF16) for _, _, pair in loaded]
            source = HALF if side == 0 else 0
            place = 0 if side == 0 else HALF + LD
            shift = (2.0 * side - 1.0) * GROUPS * SCALE
            for v in range(8):
                shape_tab[place + 8 * m + v] = shape_rows(read, source + 8 * m + v, shift)
            for (tab, pair, value), other in zip(loaded, turned):
                tab[first + pair] = value
                tab[first + PAIRS // 2 + pair] = other
            return carry

        lax.fori_loop(0, PAIRS // 8, halo_pairs, 0)
    high_tab[TABLE - 1] = jnp.zeros((R, 128), BF16)
    low_tab[TABLE - 1] = jnp.zeros((R, 128), BF16)
    for copy in table_copies:
        copy.wait()

    row_y, row_z = row_nodes()

    def couple_tiles(pair, u, tiles, lhs):
        leaves = (2 * pair, 2 * pair + 1)
        for q in range(4):
            span = slice(q * 128, (q + 1) * 128)
            for h in range(2):
                e0, e1 = entries[2 * q, leaves[h]], entries[2 * q + 1, leaves[h]]
                lhs[u, h * R : (h + 1) * R, span] = jnp.where(low32, high_tab[e0], high_tab[e1])
                lhs[u, (2 + h) * R : (3 + h) * R, span] = jnp.where(
                    low32, low_tab[e0], low_tab[e1]
                )
        own = jnp.where(low8, shape_tab[HALF + leaves[0]], shape_tab[HALF + leaves[1]])
        radius = jnp.broadcast_to(own[3:4], (8, 128))
        own = [jnp.broadcast_to(own[d : d + 1], (8, 128)) + radius * lane_u[d] for d in range(3)]
        fars = []
        for s in range(8):
            e0, e1 = entries[8 + s, leaves[0]], entries[8 + s, leaves[1]]
            fars.append(jnp.where(low8, shape_tab[e0], shape_tab[e1]))
        for s, far in enumerate(fars):
            reach = jnp.broadcast_to(far[3:4], (8, 128))
            gap = [own[d] - jnp.broadcast_to(far[d : d + 1], (8, 128)) for d in range(3)]
            tile = tile_from_axes(
                [jnp.square(gap[0] - reach * NODE[b]) for b in range(4)],
                [jnp.square(gap[1] - reach * row_y[h]) for h in range(2)],
                jnp.square(gap[2] - reach * row_z),
            )
            high, low = halves(tile)
            tiles[u, s * K : (s + 1) * K, 0:128] = high
            tiles[u, s * K : (s + 1) * K, 128:256] = low

    def couple_apply(u, tiles, lhs):
        both = dot(lhs[u], tiles[u])
        both = both[0 : 2 * R, 0:128] + (both[2 * R : 4 * R, 0:128] + both[0 : 2 * R, 128:256])
        return jnp.where(low32, both[0:R], both[R : 2 * R])

    def couple_phase(n, new, old):
        for u in range(UNIT):
            couple_tiles(jnp.minimum(n * UNIT + u, PAIRS - 1), u, *new)
            leaf_couple[n * UNIT + u] = couple_apply(u, *old)

    buffers = ((tiles0, lhs0), (tiles1, lhs1))
    for ref in buffers[1]:
        ref[...] = jnp.zeros(ref.shape, ref.dtype)

    def couple_two(m, carry):
        couple_phase(2 * m, buffers[0], buffers[1])
        couple_phase(2 * m + 1, buffers[1], buffers[0])
        return carry

    lax.fori_loop(0, PAIRS // UNIT // 2 + 1, couple_two, 0)


def finish_leaves(
    counts, p_ref, b_ref, prev_ref, next_ref, down_ref, leaf_couple, out_ref, p8, coords
):
    device = device_index()

    def finish(m, carry):
        values = []
        for v in range(8):
            c = 8 * m + v
            value = (down_ref[c] + leaf_couple[c + UNIT]).astype(BF16)
            span = pl.ds(pl.multiple_of(c * 256, 256), 256)
            values.append(
                (
                    span,
                    out_ref[:, span]
                    + dot(value, block_diagonal(b_ref[2 * c], b_ref[2 * c + 1])),
                )
            )
        for span, value in values:
            out_ref[:, span] = value
        return carry

    lax.fori_loop(0, PAIRS // 8, finish, 0)

    p8[...] = jnp.zeros(p8.shape, F32)
    eye = identity()
    sides = ((prev_ref, 0), (next_ref, GROUPS - 1))
    for side, (halo_ref, group) in enumerate(sides):
        p8[side, 0:3, :] = p_ref[:, group * 512 : group * 512 + 512]
        coords[side] = halo_ref[69].astype(F32) + halo_ref[70].astype(F32) + halo_ref[71].astype(F32)

    def edge(k, carry):
        loaded = [
            (halo_ref[64 + k], coords[side, pl.ds(pl.multiple_of(8 * k, 8), 8), :], p8[side])
            for side, (halo_ref, _) in enumerate(sides)
        ]
        for side, (_, group) in enumerate(sides):
            x_far, far, own = loaded[side]
            origin_z = (device * GROUPS + group).astype(F32)
            _, own = point_features(own, origin_z)
            far, _ = point_features(far, origin_z)
            far = dot_nt(eye, far_stack(far)).astype(BF16)
            tiles = decay(dot(far, own_stack(own))).astype(BF16)
            products = dot(x_far, tiles)
            for i in range(4):
                delta = (4 + i - k) if side == 0 else (4 + k - i)
                weight = counts[8 * (1 - side) + jnp.clip(delta, 0, 7), 4 * group + i]
                place = slice((4 * group + i) * P_SIZE, (4 * group + i + 1) * P_SIZE)
                out_ref[:, place] += products[:, i * P_SIZE : (i + 1) * P_SIZE] * weight
        return carry

    lax.fori_loop(0, 4, edge, 0)


def tree_kernel(
    shape_ref, t_ref, lev_ref, root_any, down_ref, root_ref, couple, pairs_scr, shapes, sems
):
    copy = pltpu.make_async_copy(root_any, root_ref, sems.at[0])
    copy.start()
    copy.wait()
    tree_down(shape_ref, lev_ref, t_ref, root_ref, down_ref, couple, pairs_scr, shapes)


def final_kernel(
    entries, shape_ref, counts,
    p_ref,
    near_any, b_any, prev_any, next_any, high_any, low_any, down_any,
    out_ref,
    b_ref, prev_ref, next_ref, down, leaf_couple,
    shape_tab, high_tab, low_tab, halo_rows, halo_shape,
    tiles0, lhs0, tiles1, lhs1, p8, coords, sems, halo_sems,
):
    moves = (
        (prev_any, prev_ref),
        (next_any, next_ref),
        (high_any, high_tab.at[0:LD]),
        (low_any, low_tab.at[0:LD]),
        (b_any, b_ref),
        (near_any, out_ref),
        (down_any, down),
    )
    copies = [pltpu.make_async_copy(a, b, sems.at[k]) for k, (a, b) in enumerate(moves)]
    for copy in copies:
        copy.start()
    copies[0].wait()
    copies[1].wait()
    couple_leaves(
        entries, shape_ref, prev_ref, next_ref, copies[2:4], leaf_couple,
        shape_tab, high_tab, low_tab, halo_rows, halo_shape, halo_sems,
        tiles0, lhs0, tiles1, lhs1,
    )
    for copy in copies[4:]:
        copy.wait()
    finish_leaves(
        counts, p_ref, b_ref, prev_ref, next_ref, down, leaf_couple, out_ref, p8, coords
    )


def shaped(*shape, dtype=F32):
    return jax.ShapeDtypeStruct(shape, dtype)


def vmem():
    return pl.BlockSpec(memory_space=pltpu.VMEM)


def smem():
    return pl.BlockSpec(memory_space=pltpu.SMEM)


def anywhere():
    return pl.BlockSpec(memory_space=pl.ANY)


PARAMS = pltpu.CompilerParams(vmem_limit_bytes=VMEM_LIMIT)


def per_device(charges, points, basis, transfer, near_list, coupling_list):
    near_rows = near_list.T
    coupling_rows = coupling_list.T
    devices = lax.axis_size("sub") * lax.axis_size("leaf")
    send_next, send_prev, high, low, lev, root, shapes, tasks, counts, entries = pl.pallas_call(
        leaf_kernel,
        name="leaf_up",
        out_shape=(
            shaped(SEND, R, 128, dtype=BF16),
            shaped(SEND, R, 128, dtype=BF16),
            shaped(LD, R, 128, dtype=BF16),
            shaped(LD, R, 128, dtype=BF16),
            shaped(PAIRS - 1, R, 128),
            shaped(devices, R // 2 + 8, 128),
            shaped(8, 256),
            shaped(8, LIST, dtype=jnp.int32),
            shaped(16, 128),
            shaped(16, 128, dtype=jnp.int32),
        ),
        in_specs=[anywhere(), vmem(), anywhere(), vmem(), vmem(), vmem()],
        out_specs=[vmem()] * 2 + [anywhere()] * 3 + [vmem()] * 5,
        scratch_shapes=[
            pltpu.VMEM((R, LD * P_SIZE), BF16),
            pltpu.VMEM((LD, K, P_SIZE), BF16),
            pltpu.VMEM((LD, R, 128), BF16),
            pltpu.VMEM((LD, R, 128), BF16),
            pltpu.VMEM((PAIRS - 1, R, 128), F32),
            pltpu.VMEM((PAIRS, R, 128), F32),
            pltpu.VMEM((3, LD, 128), F32),
            pltpu.VMEM((256, 128), F32),
            pltpu.VMEM((8, 512), F32),
            pltpu.SemaphoreType.DMA((2 * CHUNKS + 3,)),
        ],
        compiler_params=PARAMS,
    )(charges, points, basis, transfer, near_rows, coupling_rows)

    roots = lax.all_to_all(root, AXES, 0, 0, tiled=True)
    forward = [(i, i + 1) for i in range(devices - 1)]
    backward = [(i + 1, i) for i in range(devices - 1)]
    from_prev = lax.ppermute(send_next, AXES, forward)
    from_next = lax.ppermute(send_prev, AXES, backward)

    near = pl.pallas_call(
        near_kernel,
        name="near_field",
        out_shape=shaped(R, LD * P_SIZE),
        in_specs=[smem(), vmem(), vmem()],
        out_specs=vmem(),
        scratch_shapes=[
            pltpu.VMEM((4, 8, 512), F32),
            pltpu.VMEM((PAIRS, P_SIZE, 2 * FEATS), BF16),
            pltpu.VMEM((2 * LD, FEATS, P_SIZE), BF16),
            pltpu.VMEM((BATCH // 2, 128, 256), BF16),
            pltpu.VMEM((BATCH // 2, 128, 256), BF16),
        ],
        compiler_params=PARAMS,
        cost_estimate=pl.CostEstimate(
            flops=2 * 460 * 128 * 128 * 128, bytes_accessed=4 << 20, transcendentals=460 * 32768
        ),
    )(tasks, charges, points)

    near, roots = lax.optimization_barrier((near, roots))
    stages = [
        pltpu.VMEM((UNIT, 512, 256), BF16),
        pltpu.VMEM((UNIT, 4 * R, 512), BF16),
    ]
    down = pl.pallas_call(
        tree_kernel,
        name="tree_down",
        out_shape=shaped(PAIRS, R, 128),
        in_specs=[smem(), vmem(), vmem(), anywhere()],
        out_specs=vmem(),
        scratch_shapes=[
            pltpu.VMEM((devices, R // 2 + 8, 128), F32),
            pltpu.VMEM((PAIRS - 1, R, 128), F32),
            pltpu.VMEM((devices, R, 128), F32),
            pltpu.VMEM((2 * devices, 128), F32),
            pltpu.SemaphoreType.DMA((1,)),
        ],
        compiler_params=PARAMS,
    )(shapes, transfer, lev, roots)
    from_prev, from_next, down = lax.optimization_barrier((from_prev, from_next, down))

    return pl.pallas_call(
        final_kernel,
        name="couple_finish",
        out_shape=shaped(R, LD * P_SIZE),
        in_specs=[smem()] * 3 + [vmem()] + [anywhere()] * 7,
        out_specs=vmem(),
        scratch_shapes=[
            pltpu.VMEM((LD, K, P_SIZE), BF16),
            pltpu.VMEM((SEND, R, 128), BF16),
            pltpu.VMEM((SEND, R, 128), BF16),
            pltpu.VMEM((PAIRS, R, 128), F32),
            pltpu.VMEM((PAIRS + 2 * UNIT, R, 128), F32),
            pltpu.VMEM((2 * LD, 8, 128), F32),
            pltpu.VMEM((TABLE, R, 128), BF16),
            pltpu.VMEM((TABLE, R, 128), BF16),
            pltpu.VMEM((2, 8, 128), F32),
            pltpu.SMEM((2, 8, 128), F32),
        ]
        + stages
        + stages
        + [
            pltpu.VMEM((2, 8, 512), F32),
            pltpu.VMEM((2, R, 128), F32),
            pltpu.SemaphoreType.DMA((7,)),
            pltpu.SemaphoreType.DMA((2,)),
        ],
        compiler_params=PARAMS,
    )(
        entries, shapes, counts, points,
        near, basis, from_prev, from_next, high, low, down,
    )


def solution(mesh):
    in_specs = (
        P(None, AXES),
        P(None, AXES),
        P(AXES, None, None),
        P(),
        P(AXES, None),
        P(AXES, None),
    )
    return jax.shard_map(
        per_device, mesh=mesh, in_specs=in_specs, out_specs=P(None, AXES), check_vma=False
    )
```

```python
import functools
import math

import jax
import jax.numpy as jnp
from jax import lax
from jax.experimental import pallas as pl
from jax.experimental.pallas import tpu as pltpu
from jax.sharding import PartitionSpec as P

P_SIZE = 128
K = 64
R = 32
LD = 128
PAIRS = LD // 2
GROUPS = LD // 4
TABLE = 257
HALF = LD // 2
NEAR_REACH = 8
FEATS = 64
BATCH = 16
LIST = 896
SEND = 72
SCALE = 0.5 * math.log2(math.e)
NODE = [math.cos((2 * a + 1) * math.pi / 8) for a in range(4)]
AXES = ("leaf", "sub")
F32 = jnp.float32
BF16 = jnp.bfloat16
NT = (((1,), (1,)), ((), ()))
TINY = 1e-30
VMEM_LIMIT = 56 * 1024 * 1024
SMALL_LIMIT = 40 * 1024 * 1024


def lanes(shape):
    return lax.broadcasted_iota(jnp.int32, shape, len(shape) - 1)


def rows(shape):
    return lax.broadcasted_iota(jnp.int32, shape, len(shape) - 2)


def dot(a, b):
    return jnp.dot(a, b, preferred_element_type=F32)


def dot_nt(a, b):
    return lax.dot_general(a, b, NT, preferred_element_type=F32)


def halves(value):
    high = value.astype(BF16)
    return high, (value - high.astype(F32)).astype(BF16)


def thirds(value):
    first = value.astype(BF16).astype(F32)
    rest = value - first
    second = rest.astype(BF16).astype(F32)
    return first, second, rest - second


def unit_node(index):
    return jnp.where(
        index == 0,
        NODE[0],
        jnp.where(index == 1, NODE[1], jnp.where(index == 2, NODE[2], NODE[3])),
    ).astype(F32)


def lane_nodes():
    b = lanes((8, 128)) & 63
    return [unit_node(b >> 4), unit_node((b >> 2) & 3), unit_node(b & 3)]


def row_nodes():
    r = rows((8, 128))
    return [unit_node(r >> 2), unit_node((r >> 2) + 2)], unit_node(r & 3)


def decay(t):
    return decay_positive(jnp.maximum(t, TINY))


def decay_positive(t):
    return jnp.exp2(-(t * lax.rsqrt(t)))


def tile_from_axes(x_sq, y_sq, z_sq):
    z_sq = z_sq + TINY
    yz = [y_sq[0] + z_sq, y_sq[1] + z_sq]
    return decay_positive(jnp.concatenate([x_sq[k // 2] + yz[k % 2] for k in range(8)], axis=0))


def doubled_transfer(t_ref):
    flat = t_ref[...].reshape(2 * K, K)
    return jnp.concatenate([flat, flat], axis=1)


def device_index():
    return lax.axis_index("leaf") * lax.axis_size("sub") + lax.axis_index("sub")


def merge_up(pairs, t_high, t_low):
    n = pairs.shape[0]
    high, low = halves(pairs.reshape(n * R, 128))
    out = dot(high, jnp.concatenate([t_high, t_low], axis=1))
    out = out[:, 0:128] + out[:, 128:256] + dot(low, t_high)
    return out.reshape(n, R, 128)


def pair_lanes(clusters):
    n = clusters.shape[0]
    split = clusters.reshape(n // 2, 2, R, 128)
    return jnp.where(lanes((1, R, 128)) < K, split[:, 0], split[:, 1])


def down_weights(doubled):
    low = lanes(doubled.shape) < K
    both = jnp.concatenate(
        [jnp.where(low, doubled, 0.0), jnp.where(low, 0.0, doubled)], axis=0
    )
    return halves(both)


def push_down(value, w_high, w_low):
    n = value.shape[0]
    high, low = halves(value.reshape(n * R, 128))
    out = dot_nt(high, w_high) + dot_nt(high, w_low) + dot_nt(low, w_high)
    out = out.reshape(n, R, 256)
    return jnp.stack([out[:, :, 0:128], out[:, :, 128:256]], axis=1).reshape(2 * n, R, 128)


def merge_shape_rows(left, right):
    lane = lanes(left.shape)
    sep = left - right
    gap = jnp.sqrt(jnp.sum(jnp.where(lane < 3, sep * sep, 0.0), axis=1, keepdims=True))
    radius = jnp.maximum(left, right) + 0.5 * gap
    return jnp.where(lane == 3, radius, jnp.where(lane < 3, 0.5 * (left + right), 0.0))


def sibling_tile(left, right, lane_u, row_y, row_z):
    low = lanes((8, 128)) < K
    alpha = jnp.where(low, left[3], right[3])
    beta = jnp.where(low, right[3], left[3])
    base = [jnp.where(low, left[d] - right[d], right[d] - left[d]) - beta * lane_u[d] for d in range(3)]
    x_sq = [jnp.square(base[0] + alpha * NODE[a]) for a in range(4)]
    y_sq = [jnp.square(base[1] + alpha * row_y[h]) for h in range(2)]
    z_sq = jnp.square(base[2] + alpha * row_z)
    return tile_from_axes(x_sq, y_sq, z_sq)


def sibling_apply(tile, pair):
    low = lanes((K, 128)) < K
    zero = jnp.zeros((K, 128), BF16)
    weights = []
    for part in halves(tile):
        weights.append(
            jnp.concatenate([jnp.where(low, part, zero), jnp.where(low, zero, part)], axis=0)
        )
    high, low_part = halves(pltpu.roll(pair, K, 1))
    out = dot_nt(high, jnp.concatenate(weights, axis=0))
    return out[:, 0:128] + out[:, 128:256] + dot_nt(low_part, weights[0])


LEVEL_OFFSETS = [0, 128, 192, 224, 240, 248, 252, 254]
PAIR_OFFSETS = [0, 0, 32, 48, 56, 60, 62]


def block_diagonal(left, right):
    zero = jnp.zeros(left.shape, left.dtype)
    return jnp.concatenate(
        [jnp.concatenate([left, zero], axis=1), jnp.concatenate([zero, right], axis=1)], axis=0
    )


def make_lists(near_ref, coupling_ref, list_ref, count_ref, index_ref):
    first_leaf = device_index() * LD
    lane8 = lanes((8, 128))
    row8 = rows((8, 128))
    offset = jnp.where(near_ref[...] >= 0, near_ref[...] - first_leaf - lane8, 1000)

    def slots_at(delta):
        return jnp.sum(jnp.where(offset == delta, 1.0, 0.0), axis=0, keepdims=True)

    forward = jnp.concatenate([slots_at(delta) for delta in range(8)], axis=0)
    reverse = jnp.concatenate(
        [jnp.zeros((1, 128), F32)] + [slots_at(-delta) for delta in range(1, 8)], axis=0
    )
    count_ref[0:8, :] = forward
    count_ref[8:16, :] = reverse
    backward = jnp.concatenate(
        [jnp.zeros((1, 128), F32)]
        + [pltpu.roll(reverse[delta : delta + 1, :], 128 - delta, 1) for delta in range(1, 8)],
        axis=0,
    )
    turned = (row8 == 1) & ((lane8 & 3) == 2)
    leaf = lane8.astype(F32)
    other = leaf + row8.astype(F32)
    first = jnp.where(turned, other, leaf)
    second = jnp.where(turned, leaf, other)
    to_first = jnp.where(turned, backward, forward)
    to_second = jnp.where(turned, forward, backward)
    odd = jnp.where(turned, lane8, lane8 + row8) & 1
    wanted = (lane8 + row8 < LD) & (forward + backward > 0.0)
    earlier = jnp.where(rows((128, 128)) < lanes((128, 128)), 1.0, 0.0).astype(BF16)
    place = jnp.full((8, 128), -1.0, F32)
    most = jnp.zeros((1, 1), F32)
    for parity in range(2):
        flags = jnp.where(wanted & (odd == parity), 1.0, 0.0)
        rank = dot(flags.astype(BF16), earlier)
        totals = jnp.sum(flags, axis=1, keepdims=True)
        before = jnp.zeros((1, 1), F32)
        starts = []
        for delta in range(8):
            starts.append(before)
            before = before + totals[delta : delta + 1, :]
        rank = rank + jnp.concatenate(starts, axis=0)
        place = jnp.where(flags > 0.0, 2.0 * rank + (1.0 * BATCH + parity), place)
        most = jnp.maximum(most, before)
    task_rows = []
    for delta in range(8):
        pick = slice(delta, delta + 1)
        task_rows.append(
            jnp.where(
                row8 == 0,
                first[pick],
                jnp.where(
                    row8 == 1,
                    second[pick],
                    jnp.where(
                        row8 == 2, to_first[pick], jnp.where(row8 == 3, to_second[pick], 0.0)
                    ),
                ),
            ).astype(BF16)
        )
    tasks = jnp.concatenate(task_rows, axis=1)
    slot_row = rows((128, 128)).astype(F32)
    for m in range(LIST // 128):
        chosen = jnp.concatenate(
            [
                jnp.where(place[delta : delta + 1, :] == slot_row + 128.0 * m, 1.0, 0.0).astype(BF16)
                for delta in range(8)
            ],
            axis=1,
        )
        part = dot_nt(tasks, chosen)
        part = jnp.where(row8 == 4, 2.0 * most, part)
        list_ref[:, m * 128 : (m + 1) * 128] = part.astype(jnp.int32)

    target = coupling_ref[...]
    reach = target - first_leaf + HALF
    swap = ((reach ^ row8) & 1) * (PAIRS // 2)
    entry = jnp.where(
        reach < HALF,
        LD + (reach >> 1) + swap,
        jnp.where(reach < HALF + LD, reach - HALF, LD + HALF + ((reach - HALF - LD) >> 1) + swap),
    )
    index_ref[0:8, :] = jnp.where(target >= 0, entry, TABLE - 1)
    index_ref[8:16, :] = jnp.where(target >= 0, reach, 0)


CHUNKS = 4


def leaf_kernel(
    x_any, p_ref, b_any, t_ref, near_ref, coupling_ref,
    send_next, send_prev, high_any, low_any, lev_any, root_ref, shape_ref,
    list_ref, count_ref, index_ref,
    x_ref, b_ref, high_ref, low_ref, lev_ref, coef, pts, shapes, p8, sems,
):
    leaves = LD // CHUNKS
    copies = []
    for c in range(CHUNKS):
        span = slice(c * leaves * P_SIZE, (c + 1) * leaves * P_SIZE)
        part = slice(c * leaves, (c + 1) * leaves)
        copies.append(
            (
                pltpu.make_async_copy(x_any.at[:, span], x_ref.at[:, span], sems.at[c]),
                pltpu.make_async_copy(b_any.at[part], b_ref.at[part], sems.at[CHUNKS + c]),
            )
        )
    for pair in copies:
        for copy in pair:
            copy.start()
    origin = (device_index() * GROUPS).astype(F32)
    low32 = lanes((R, 128)) < K

    make_lists(near_ref, coupling_ref, list_ref, count_ref, index_ref)
    for i in range(LD):
        for d in range(3):
            pts[d, i : i + 1, :] = p_ref[d : d + 1, i * P_SIZE : (i + 1) * P_SIZE]
    centers, squares = [], 0.0
    for d in range(3):
        coords = (pts[d] - origin if d == 2 else pts[d]) * SCALE
        center = jnp.sum(coords, axis=1, keepdims=True) * (1.0 / P_SIZE)
        centers.append(center)
        squares = squares + jnp.square(coords - center)
    radius = jnp.sqrt(jnp.max(squares, axis=1, keepdims=True))
    lane = lanes((LD, 128))
    shapes[0:LD, :] = jnp.where(
        lane == 0,
        centers[0],
        jnp.where(
            lane == 1,
            centers[1],
            jnp.where(lane == 2, centers[2], jnp.where(lane == 3, radius, 0.0)),
        ),
    )
    count = LD // 2
    for level in range(1, 8):
        source = LEVEL_OFFSETS[level - 1]
        joined = merge_shape_rows(
            shapes[pl.ds(source, count, stride=2), :],
            shapes[pl.ds(source + 1, count, stride=2), :],
        )
        shapes[pl.ds(LEVEL_OFFSETS[level], count), :] = joined
        count //= 2
    shape_rows = jnp.concatenate(
        [jnp.transpose(shapes[0:128, :])[0:8], jnp.transpose(shapes[128:256, :])[0:8]], axis=1
    )
    shape_ref[...] = shape_rows

    def leaf_pairs(m, carry):
        values = []
        for v in range(16):
            leaf = 16 * m + v
            x = x_ref[:, pl.ds(pl.multiple_of(leaf * P_SIZE, P_SIZE), P_SIZE)]
            weights = b_ref[leaf]
            values.append(dot_nt(x, jnp.concatenate([weights, weights], axis=0)))
        for v in range(16):
            high_ref[16 * m + v], low_ref[16 * m + v] = halves(values[v])
        for v in range(8):
            coef[8 * m + v] = jnp.where(low32, values[2 * v], values[2 * v + 1])
        return carry

    for c in range(CHUNKS):
        for copy in copies[c]:
            copy.wait()
        steps = leaves // 16
        lax.fori_loop(c * steps, (c + 1) * steps, leaf_pairs, 0)
    leaving = [
        pltpu.make_async_copy(high_ref, high_any, sems.at[2 * CHUNKS]),
        pltpu.make_async_copy(low_ref, low_any, sems.at[2 * CHUNKS + 1]),
    ]
    for copy in leaving:
        copy.start()

    t_high, t_low = halves(doubled_transfer(t_ref))
    pairs = coef[...]
    for level in range(1, 7):
        pairs = pair_lanes(merge_up(pairs, t_high, t_low))
        lev_ref[pl.ds(PAIR_OFFSETS[level], pairs.shape[0])] = pairs
    leaving.append(pltpu.make_async_copy(lev_ref, lev_any, sems.at[2 * CHUNKS + 2]))
    leaving[2].start()
    root = merge_up(pairs, t_high, t_low)[0]

    low = lanes((R // 2, 128)) < K
    block = jnp.concatenate(
        [
            jnp.where(low, root[0 : R // 2], root[R // 2 : R]),
            jnp.broadcast_to(shapes[254:255, :], (8, 128)),
        ],
        axis=0,
    )
    root_ref[...] = jnp.broadcast_to(block[None], root_ref.shape)

    p8[...] = jnp.zeros((8, 512), F32)
    for send, first_pair, group in ((send_next, PAIRS // 2, GROUPS - 1), (send_prev, 0, 0)):

        def copy_pairs(m, carry):
            parts = [halves(coef[first_pair + 8 * m + v]) for v in range(8)]
            for v in range(8):
                send[8 * m + v], send[32 + 8 * m + v] = parts[v]
            return carry

        lax.fori_loop(0, PAIRS // 16, copy_pairs, 0)
        parts = thirds(shape_rows[:, 0:128])
        send[68] = jnp.concatenate(list(parts) + [jnp.zeros((8, 128), F32)], axis=0).astype(BF16)
        p8[0:3, :] = p_ref[:, group * 512 : group * 512 + 512]
        parts = thirds(p8[...])
        for k in range(4):
            send[64 + k] = x_ref[:, group * 512 + k * P_SIZE : group * 512 + (k + 1) * P_SIZE]
        for part in range(3):
            send[69 + part] = jnp.concatenate(
                [parts[part][:, k * P_SIZE : (k + 1) * P_SIZE] for k in range(4)], axis=0
            ).astype(BF16)
    for copy in leaving:
        copy.wait()


def point_features(points8, origin_z):
    row = rows(points8.shape)
    center = jnp.where(row == 2, origin_z + 0.5, 1.0)
    v = jnp.where(row < 3, (points8 - center) * SCALE, 0.0)
    norm = jnp.sum(v * v, axis=0, keepdims=True)
    far = jnp.where(row == 3, norm, jnp.where(row == 4, 1.0, v))
    own = jnp.where(row == 3, 1.0, jnp.where(row == 4, norm, -2.0 * v))
    return far, own


def far_stack(value):
    first, second, third = thirds(value)
    none = jnp.zeros(value.shape, F32)
    return jnp.concatenate(
        [first, first, first, second, second, third, none, none], axis=0
    ).astype(BF16)


def own_stack(value):
    first, second, third = thirds(value)
    none = jnp.zeros(value.shape, F32)
    return jnp.concatenate(
        [first, second, third, first, second, first, none, none], axis=0
    ).astype(BF16)


def identity():
    return jnp.where(rows((128, 128)) == lanes((128, 128)), 1.0, 0.0).astype(BF16)


def near_kernel(
    list_ref, x_any, p_ref, out_ref,
    x_ref, sems, p8, far_feat, own_feat, tile0, tile1,
):
    copy = pltpu.make_async_copy(x_any, x_ref, sems.at[0])
    copy.start()
    first_group = device_index() * GROUPS
    p8[...] = jnp.zeros(p8.shape, F32)
    eye = identity()

    def features(m, carry):
        loaded = [p_ref[:, pl.ds(pl.multiple_of((4 * m + v) * 512, 512), 512)] for v in range(4)]
        for v in range(4):
            p8[v, 0:3, :] = loaded[v]
        made = []
        for v in range(4):
            coords = p8[v]
            origin_z = (first_group + 4 * m + v).astype(F32)
            far, own = point_features(coords, origin_z)
            _, own_up = point_features(coords, origin_z + 1.0)
            far = far_stack(far)
            parts = [far[:, k * P_SIZE : (k + 1) * P_SIZE] for k in range(4)]
            turned = dot_nt(eye, jnp.concatenate(parts, axis=0)).astype(BF16)
            made.append((turned, own_stack(own), own_stack(own_up)))
        for v in range(4):
            g = 4 * m + v
            turned, own, own_up = made[v]
            far_feat[2 * g] = turned[:, 0:128]
            far_feat[2 * g + 1] = turned[:, 128:256]
            for k in range(4):
                part = slice(k * P_SIZE, (k + 1) * P_SIZE)
                own_feat[4 * g + k] = own[:, part]
                own_feat[LD + 4 * g + k] = own_up[:, part]
        return carry

    lax.fori_loop(0, GROUPS // 4, features, 0)

    copy.wait()
    out_ref[...] = x_ref[...].astype(F32)
    for ref in (tile0, tile1):
        ref[...] = jnp.zeros(ref.shape, ref.dtype)

    total = list_ref[4, 0]
    steps = (total + BATCH - 1) // BATCH + 1
    low = lanes((128, 128)) < K

    def leaf_slice(i):
        return pl.ds(pl.multiple_of(i * P_SIZE, P_SIZE), P_SIZE)

    def phase(n, tile_new, tile_old):
        far, own, sources, updates = [], [], [], []
        for u in range(BATCH):
            k = (n + 1) * BATCH + u
            i, j = list_ref[0, k], list_ref[1, k]
            variant = ((j >> 2) - (i >> 2)) * LD
            far.append(far_feat[j >> 1])
            own.append(own_feat[variant + i])
        for u in range(BATCH):
            k = n * BATCH + u
            i, j = list_ref[0, k], list_ref[1, k]
            sources.append((x_ref[:, leaf_slice(j)], x_ref[:, leaf_slice(i)]))
        tiles = []
        for u in range(BATCH // 2):
            pick = jnp.where(low, far[2 * u], far[2 * u + 1])
            dist = dot(pick, block_diagonal(own[2 * u], own[2 * u + 1]))
            tiles.append(decay(dist).astype(BF16))
            weights = block_diagonal(tile_old[u, :, 0:128], tile_old[u, :, 128:256])
            to_i = dot(jnp.concatenate([sources[2 * u][0], sources[2 * u + 1][0]], axis=1), weights)
            to_j = dot_nt(jnp.concatenate([sources[2 * u][1], sources[2 * u + 1][1]], axis=1), weights)
            for h in range(2):
                k = n * BATCH + 2 * u + h
                span = slice(h * 128, (h + 1) * 128)
                updates.append(
                    (
                        to_i[:, span] * list_ref[2, k].astype(F32),
                        to_j[:, span] * list_ref[3, k].astype(F32),
                    )
                )
        for u in range(BATCH // 2):
            tile_new[u] = tiles[u]
        for u in range(BATCH):
            k = n * BATCH + u
            to_i = leaf_slice(list_ref[0, k])
            to_j = leaf_slice(list_ref[1, k])
            out_ref[:, to_i] += updates[u][0]
            out_ref[:, to_j] += updates[u][1]

    def two_phases(m, carry):
        phase(2 * m, tile0, tile1)
        phase(2 * m + 1, tile1, tile0)
        return carry

    lax.fori_loop(0, (steps + 1) // 2, two_phases, 0)


def tree_down(shape_ref, lev_ref, t_ref, root_ref, down_ref, couple, pairs_scr, shapes):
    lane_u = lane_nodes()
    row_y, row_z = row_nodes()

    def siblings(m, carry):
        loaded = [lev_ref[9 * m + u] for u in range(9)]
        values = []
        for u in range(9):
            cluster = LD + 2 * (9 * m + u)
            left = [shape_ref[d, cluster] for d in range(4)]
            right = [shape_ref[d, cluster + 1] for d in range(4)]
            tile = sibling_tile(left, right, lane_u, row_y, row_z)
            values.append(sibling_apply(tile, loaded[u]))
        for u in range(9):
            couple[9 * m + u] = values[u]
        return carry

    lax.fori_loop(0, 7, siblings, 0)

    doubled = doubled_transfer(t_ref)
    t_high, t_low = halves(doubled)
    w_high, w_low = down_weights(doubled)
    device = device_index()
    n = root_ref.shape[0]
    low = lanes((R, 128)) < K
    shift = lanes((1, 128)) == 2
    for k in range(n):
        shapes[k : k + 1, :] = root_ref[k, R // 2 : R // 2 + 1, :] + jnp.where(
            shift, (k * GROUPS) * SCALE, 0.0
        )
    for k in range(n // 2):
        left = root_ref[2 * k, 0 : R // 2, :]
        right = root_ref[2 * k + 1, 0 : R // 2, :]
        left = jnp.concatenate([left, pltpu.roll(left, K, 1)], axis=0)
        right = jnp.concatenate([pltpu.roll(right, K, 1), right], axis=0)
        pairs_scr[k] = jnp.where(low, left, right)
    source, count, pair_source = 0, n // 2, 0
    levels = []
    while count >= 1:
        levels.append((source, pair_source))
        if count > 1:
            pairs = pair_lanes(merge_up(pairs_scr[pl.ds(pair_source, count)], t_high, t_low))
            pairs_scr[pl.ds(pair_source + count, count // 2)] = pairs
            joined = merge_shape_rows(
                shapes[pl.ds(source, count, stride=2), :],
                shapes[pl.ds(source + 1, count, stride=2), :],
            )
            shapes[pl.ds(source + 2 * count, count), :] = joined
        source += 2 * count
        pair_source += count
        count //= 2
    couples = []
    for level, (source, pair_source) in enumerate(levels):
        pair = device >> (level + 1)
        left_row = shapes[pl.ds(source + 2 * pair, 1), :]
        right_row = shapes[pl.ds(source + 2 * pair + 1, 1), :]
        left = [jnp.broadcast_to(left_row[:, d : d + 1], (8, 128)) for d in range(4)]
        right = [jnp.broadcast_to(right_row[:, d : d + 1], (8, 128)) for d in range(4)]
        tile = sibling_tile(left, right, lane_u, row_y, row_z)
        couples.append(sibling_apply(tile, pairs_scr[pair_source + pair]))
    incoming = None
    for level in reversed(range(len(levels))):
        value = couples[level]
        if incoming is not None:
            pushed = push_down(incoming[None], w_high, w_low)
            value = value + (pushed[0] + pushed[1])
        side = (device >> level) & 1
        keep_low = jnp.where(low, 1, 0) == (1 - side)
        incoming = jnp.where(keep_low, value, 0.0)
    pushed = push_down(incoming[None], w_high, w_low)
    value = couple[pl.ds(PAIR_OFFSETS[6], 1)] + (pushed[0:1] + pushed[1:2])
    for level in range(5, 0, -1):
        n = PAIRS >> level
        value = couple[pl.ds(PAIR_OFFSETS[level], n)] + push_down(value, w_high, w_low)
    down_ref[...] = push_down(value, w_high, w_low)


UNIT = 4


def couple_leaves(
    entries, shape_ref, prev_ref, next_ref, table_copies, leaf_couple,
    shape_tab, high_tab, low_tab, halo_rows, halo_shape, sems,
    tiles0, lhs0, tiles1, lhs1,
):
    copies = []
    for k, ref in enumerate((prev_ref, next_ref)):
        parts = ref[68].astype(F32)
        halo_rows[k] = parts[0:8] + parts[8:16] + parts[16:24]
        copies.append(pltpu.make_async_copy(halo_rows.at[k], halo_shape.at[k], sems.at[k]))
    for copy in copies:
        copy.start()
    low32 = lanes((R, 128)) < K
    lane_u = lane_nodes()
    row8 = rows((8, 128))
    low8 = lanes((8, 128)) < K

    def shape_rows(read, k, shift):
        return jnp.where(
            row8 == 0,
            read(0, k),
            jnp.where(row8 == 1, read(1, k), jnp.where(row8 == 2, read(2, k) + shift, read(3, k))),
        )

    def own_nodes(m, carry):
        shape_tab[HALF + m] = shape_rows(lambda d, k: shape_ref[d, k], m, 0.0)
        return carry

    lax.fori_loop(0, LD, own_nodes, 0, unroll=8)
    for copy in copies:
        copy.wait()
    for side, ref in enumerate((prev_ref, next_ref)):
        first = LD + side * HALF

        def halo_pairs(m, carry):
            def read(d, k):
                return halo_shape[side, d, k]

            loaded = [
                (tab, 4 * m + v, ref[offset + 4 * m + v])
                for tab, offset in ((high_tab, 0), (low_tab, 32))
                for v in range(4)
            ]
            turned = [pltpu.roll(pair.astype(F32), K, 1).astype(BF16) for _, _, pair in loaded]
            source = HALF if side == 0 else 0
            place = 0 if side == 0 else HALF + LD
            shift = (2.0 * side - 1.0) * GROUPS * SCALE
            for v in range(8):
                shape_tab[place + 8 * m + v] = shape_rows(read, source + 8 * m + v, shift)
            for (tab, pair, value), other in zip(loaded, turned):
                tab[first + pair] = value
                tab[first + PAIRS // 2 + pair] = other
            return carry

        lax.fori_loop(0, PAIRS // 8, halo_pairs, 0)
    high_tab[TABLE - 1] = jnp.zeros((R, 128), BF16)
    low_tab[TABLE - 1] = jnp.zeros((R, 128), BF16)
    for copy in table_copies:
        copy.wait()

    row_y, row_z = row_nodes()

    def couple_tiles(pair, u, tiles, lhs):
        leaves = (2 * pair, 2 * pair + 1)
        for q in range(4):
            span = slice(q * 128, (q + 1) * 128)
            for h in range(2):
                e0, e1 = entries[2 * q, leaves[h]], entries[2 * q + 1, leaves[h]]
                lhs[u, h * R : (h + 1) * R, span] = jnp.where(low32, high_tab[e0], high_tab[e1])
                lhs[u, (2 + h) * R : (3 + h) * R, span] = jnp.where(
                    low32, low_tab[e0], low_tab[e1]
                )
        own = jnp.where(low8, shape_tab[HALF + leaves[0]], shape_tab[HALF + leaves[1]])
        radius = jnp.broadcast_to(own[3:4], (8, 128))
        own = [jnp.broadcast_to(own[d : d + 1], (8, 128)) + radius * lane_u[d] for d in range(3)]
        fars = []
        for s in range(8):
            e0, e1 = entries[8 + s, leaves[0]], entries[8 + s, leaves[1]]
            fars.append(jnp.where(low8, shape_tab[e0], shape_tab[e1]))
        for s, far in enumerate(fars):
            reach = jnp.broadcast_to(far[3:4], (8, 128))
            gap = [own[d] - jnp.broadcast_to(far[d : d + 1], (8, 128)) for d in range(3)]
            tile = tile_from_axes(
                [jnp.square(gap[0] - reach * NODE[b]) for b in range(4)],
                [jnp.square(gap[1] - reach * row_y[h]) for h in range(2)],
                jnp.square(gap[2] - reach * row_z),
            )
            high, low = halves(tile)
            tiles[u, s * K : (s + 1) * K, 0:128] = high
            tiles[u, s * K : (s + 1) * K, 128:256] = low

    def couple_apply(u, tiles, lhs):
        both = dot(lhs[u], tiles[u])
        both = both[0 : 2 * R, 0:128] + (both[2 * R : 4 * R, 0:128] + both[0 : 2 * R, 128:256])
        return jnp.where(low32, both[0:R], both[R : 2 * R])

    def couple_phase(n, new, old):
        for u in range(UNIT):
            couple_tiles(jnp.minimum(n * UNIT + u, PAIRS - 1), u, *new)
            leaf_couple[n * UNIT + u] = couple_apply(u, *old)

    buffers = ((tiles0, lhs0), (tiles1, lhs1))
    for ref in buffers[1]:
        ref[...] = jnp.zeros(ref.shape, ref.dtype)

    def couple_two(m, carry):
        couple_phase(2 * m, buffers[0], buffers[1])
        couple_phase(2 * m + 1, buffers[1], buffers[0])
        return carry

    lax.fori_loop(0, PAIRS // UNIT // 2 + 1, couple_two, 0)


def finish_leaves(
    counts, p_ref, b_ref, prev_ref, next_ref, down_ref, leaf_couple, out_ref, p8, coords
):
    device = device_index()

    def finish(m, carry):
        values = []
        for v in range(8):
            c = 8 * m + v
            value = (down_ref[c] + leaf_couple[c + UNIT]).astype(BF16)
            span = pl.ds(pl.multiple_of(c * 256, 256), 256)
            values.append(
                (
                    span,
                    out_ref[:, span]
                    + dot(value, block_diagonal(b_ref[2 * c], b_ref[2 * c + 1])),
                )
            )
        for span, value in values:
            out_ref[:, span] = value
        return carry

    lax.fori_loop(0, PAIRS // 8, finish, 0)

    p8[...] = jnp.zeros(p8.shape, F32)
    eye = identity()
    sides = ((prev_ref, 0), (next_ref, GROUPS - 1))
    for side, (halo_ref, group) in enumerate(sides):
        p8[side, 0:3, :] = p_ref[:, group * 512 : group * 512 + 512]
        coords[side] = halo_ref[69].astype(F32) + halo_ref[70].astype(F32) + halo_ref[71].astype(F32)

    def edge(k, carry):
        loaded = [
            (halo_ref[64 + k], coords[side, 8 * k : 8 * k + 8, :], p8[side])
            for side, (halo_ref, _) in enumerate(sides)
        ]
        for side, (_, group) in enumerate(sides):
            x_far, far, own = loaded[side]
            origin_z = (device * GROUPS + group).astype(F32)
            _, own = point_features(own, origin_z)
            far, _ = point_features(far, origin_z)
            far = dot_nt(eye, far_stack(far)).astype(BF16)
            tiles = decay(dot(far, own_stack(own))).astype(BF16)
            products = dot(x_far, tiles)
            for i in range(4):
                delta = (4 + i - k) if side == 0 else (4 + k - i)
                weight = counts[8 * (1 - side) + delta, 4 * group + i]
                place = slice((4 * group + i) * P_SIZE, (4 * group + i + 1) * P_SIZE)
                out_ref[:, place] += products[:, i * P_SIZE : (i + 1) * P_SIZE] * weight
        return carry

    for k in range(4):
        edge(k, 0)


def tree_kernel(
    shape_ref, t_any, lev_any, root_any, down_ref,
    t_ref, lev_ref, root_ref, couple, pairs_scr, shapes, sems,
):
    copies = [
        pltpu.make_async_copy(lev_any, lev_ref, sems.at[0]),
        pltpu.make_async_copy(root_any, root_ref, sems.at[1]),
        pltpu.make_async_copy(t_any, t_ref, sems.at[2]),
    ]
    for copy in copies:
        copy.start()
    for copy in copies:
        copy.wait()
    tree_down(shape_ref, lev_ref, t_ref, root_ref, down_ref, couple, pairs_scr, shapes)


def final_kernel(
    entries, shape_ref, counts,
    p_any,
    near_any, b_any, prev_any, next_any, high_any, low_any, down_any,
    out_ref,
    p_ref, b_ref, prev_ref, next_ref, down, leaf_couple,
    shape_tab, high_tab, low_tab, halo_rows, halo_shape,
    tiles0, lhs0, tiles1, lhs1, p8, coords, sems, halo_sems,
):
    moves = (
        (prev_any, prev_ref),
        (next_any, next_ref),
        (high_any, high_tab.at[0:LD]),
        (low_any, low_tab.at[0:LD]),
        (b_any, b_ref),
        (near_any, out_ref),
        (down_any, down),
        (p_any, p_ref),
    )
    copies = [pltpu.make_async_copy(a, b, sems.at[k]) for k, (a, b) in enumerate(moves)]
    for copy in copies:
        copy.start()
    copies[0].wait()
    copies[1].wait()
    couple_leaves(
        entries, shape_ref, prev_ref, next_ref, copies[2:4], leaf_couple,
        shape_tab, high_tab, low_tab, halo_rows, halo_shape, halo_sems,
        tiles0, lhs0, tiles1, lhs1,
    )
    for copy in copies[4:]:
        copy.wait()
    finish_leaves(
        counts, p_ref, b_ref, prev_ref, next_ref, down, leaf_couple, out_ref, p8, coords
    )


def shaped(*shape, dtype=F32):
    return jax.ShapeDtypeStruct(shape, dtype)


def vmem():
    return pl.BlockSpec(memory_space=pltpu.VMEM)


def smem():
    return pl.BlockSpec(memory_space=pltpu.SMEM)


def anywhere():
    return pl.BlockSpec(memory_space=pl.ANY)


def pinned():
    return pl.BlockSpec(memory_space=pltpu.HBM)


PARAMS = pltpu.CompilerParams(vmem_limit_bytes=VMEM_LIMIT)
SMALL = pltpu.CompilerParams(vmem_limit_bytes=SMALL_LIMIT)


def per_device(charges, points, basis, transfer, near_list, coupling_list):
    near_rows = near_list.T
    coupling_rows = coupling_list.T
    devices = lax.axis_size("sub") * lax.axis_size("leaf")
    send_next, send_prev, high, low, lev, root, shapes, tasks, counts, entries = pl.pallas_call(
        leaf_kernel,
        name="leaf_up",
        out_shape=(
            shaped(SEND, R, 128, dtype=BF16),
            shaped(SEND, R, 128, dtype=BF16),
            shaped(LD, R, 128, dtype=BF16),
            shaped(LD, R, 128, dtype=BF16),
            shaped(PAIRS - 1, R, 128),
            shaped(devices, R // 2 + 8, 128),
            shaped(8, 256),
            shaped(8, LIST, dtype=jnp.int32),
            shaped(16, 128),
            shaped(16, 128, dtype=jnp.int32),
        ),
        in_specs=[pinned(), vmem(), pinned(), vmem(), vmem(), vmem()],
        out_specs=[vmem()] * 2 + [pinned()] * 3 + [vmem()] * 5,
        scratch_shapes=[
            pltpu.VMEM((R, LD * P_SIZE), BF16),
            pltpu.VMEM((LD, K, P_SIZE), BF16),
            pltpu.VMEM((LD, R, 128), BF16),
            pltpu.VMEM((LD, R, 128), BF16),
            pltpu.VMEM((PAIRS - 1, R, 128), F32),
            pltpu.VMEM((PAIRS, R, 128), F32),
            pltpu.VMEM((3, LD, 128), F32),
            pltpu.VMEM((256, 128), F32),
            pltpu.VMEM((8, 512), F32),
            pltpu.SemaphoreType.DMA((2 * CHUNKS + 3,)),
        ],
        compiler_params=PARAMS,
    )(charges, points, basis, transfer, near_rows, coupling_rows)

    roots = lax.all_to_all(root, AXES, 0, 0, tiled=True)
    forward = [(i, i + 1) for i in range(devices - 1)]
    backward = [(i + 1, i) for i in range(devices - 1)]
    from_prev = lax.ppermute(send_next, AXES, forward)
    from_next = lax.ppermute(send_prev, AXES, backward)

    near = pl.pallas_call(
        near_kernel,
        name="near_field",
        out_shape=shaped(R, LD * P_SIZE),
        in_specs=[smem(), pinned(), vmem()],
        out_specs=vmem(),
        scratch_shapes=[
            pltpu.VMEM((R, LD * P_SIZE), BF16),
            pltpu.SemaphoreType.DMA((1,)),
            pltpu.VMEM((4, 8, 512), F32),
            pltpu.VMEM((PAIRS, P_SIZE, 2 * FEATS), BF16),
            pltpu.VMEM((2 * LD, FEATS, P_SIZE), BF16),
            pltpu.VMEM((BATCH // 2, 128, 256), BF16),
            pltpu.VMEM((BATCH // 2, 128, 256), BF16),
        ],
        compiler_params=PARAMS,
        cost_estimate=pl.CostEstimate(
            flops=2 * 460 * 128 * 128 * 128, bytes_accessed=4 << 20, transcendentals=460 * 32768
        ),
    )(tasks, charges, points)

    near, roots = lax.optimization_barrier((near, roots))
    stages = [
        pltpu.VMEM((UNIT, 512, 256), BF16),
        pltpu.VMEM((UNIT, 4 * R, 512), BF16),
    ]
    down = pl.pallas_call(
        tree_kernel,
        name="tree_down",
        out_shape=shaped(PAIRS, R, 128),
        in_specs=[smem(), pinned(), pinned(), anywhere()],
        out_specs=vmem(),
        scratch_shapes=[
            pltpu.VMEM((2, K, K), F32),
            pltpu.VMEM((PAIRS - 1, R, 128), F32),
            pltpu.VMEM((devices, R // 2 + 8, 128), F32),
            pltpu.VMEM((PAIRS - 1, R, 128), F32),
            pltpu.VMEM((devices, R, 128), F32),
            pltpu.VMEM((2 * devices, 128), F32),
            pltpu.SemaphoreType.DMA((3,)),
        ],
        compiler_params=SMALL,
    )(shapes, transfer, lev, roots)
    from_prev, from_next, down = lax.optimization_barrier((from_prev, from_next, down))

    return pl.pallas_call(
        final_kernel,
        name="couple_finish",
        out_shape=shaped(R, LD * P_SIZE),
        in_specs=[smem()] * 3 + [pinned()] * 3 + [anywhere()] * 2 + [pinned()] * 3,
        out_specs=vmem(),
        scratch_shapes=[
            pltpu.VMEM((3, LD * P_SIZE), F32),
            pltpu.VMEM((LD, K, P_SIZE), BF16),
            pltpu.VMEM((SEND, R, 128), BF16),
            pltpu.VMEM((SEND, R, 128), BF16),
            pltpu.VMEM((PAIRS, R, 128), F32),
            pltpu.VMEM((PAIRS + 2 * UNIT, R, 128), F32),
            pltpu.VMEM((2 * LD, 8, 128), F32),
            pltpu.VMEM((TABLE, R, 128), BF16),
            pltpu.VMEM((TABLE, R, 128), BF16),
            pltpu.VMEM((2, 8, 128), F32),
            pltpu.SMEM((2, 8, 128), F32),
        ]
        + stages
        + stages
        + [
            pltpu.VMEM((2, 8, 512), F32),
            pltpu.VMEM((2, R, 128), F32),
            pltpu.SemaphoreType.DMA((8,)),
            pltpu.SemaphoreType.DMA((2,)),
        ],
        compiler_params=SMALL,
    )(
        entries, shapes, counts, points,
        near, basis, from_prev, from_next, high, low, down,
    )


def solution(mesh):
    in_specs = (
        P(None, AXES),
        P(None, AXES),
        P(AXES, None, None),
        P(),
        P(AXES, None),
        P(AXES, None),
    )
    return jax.shard_map(
        per_device, mesh=mesh, in_specs=in_specs, out_specs=P(None, AXES), check_vma=False
    )
```

```python
import functools
import math

import jax
import jax.numpy as jnp
from jax import lax
from jax.experimental import pallas as pl
from jax.experimental.pallas import tpu as pltpu
from jax.sharding import PartitionSpec as P

P_SIZE = 128
K = 64
R = 32
LD = 128
PAIRS = LD // 2
GROUPS = LD // 4
TABLE = 257
HALF = LD // 2
NEAR_REACH = 8
FEATS = 64
BATCH = 16
SIBLINGS = 4
LIST = 896
SEND = 72
SCALE = 0.5 * math.log2(math.e)
NODE = [math.cos((2 * a + 1) * math.pi / 8) for a in range(4)]
AXES = ("leaf", "sub")
F32 = jnp.float32
BF16 = jnp.bfloat16
NT = (((1,), (1,)), ((), ()))
TINY = 1e-30
VMEM_LIMIT = 64 * 1024 * 1024


def lanes(shape):
    return lax.broadcasted_iota(jnp.int32, shape, len(shape) - 1)


def rows(shape):
    return lax.broadcasted_iota(jnp.int32, shape, len(shape) - 2)


def dot(a, b):
    return jnp.dot(a, b, preferred_element_type=F32)


def dot_nt(a, b):
    return lax.dot_general(a, b, NT, preferred_element_type=F32)


def halves(value):
    high = value.astype(BF16)
    return high, (value - high.astype(F32)).astype(BF16)


def thirds(value):
    first = value.astype(BF16).astype(F32)
    rest = value - first
    second = rest.astype(BF16).astype(F32)
    return first, second, rest - second


def unit_node(index):
    return jnp.where(
        index == 0,
        NODE[0],
        jnp.where(index == 1, NODE[1], jnp.where(index == 2, NODE[2], NODE[3])),
    ).astype(F32)


def lane_nodes():
    b = lanes((8, 128)) & 63
    return [unit_node(b >> 4), unit_node((b >> 2) & 3), unit_node(b & 3)]


def row_nodes():
    r = rows((8, 128))
    return [unit_node(r >> 2), unit_node((r >> 2) + 2)], unit_node(r & 3)


def decay(t):
    return decay_positive(jnp.maximum(t, TINY))


def decay_positive(t):
    return jnp.exp2(-(t * lax.rsqrt(t)))


def tile_from_axes(x_sq, y_sq, z_sq):
    z_sq = z_sq + TINY
    yz = [y_sq[0] + z_sq, y_sq[1] + z_sq]
    return decay_positive(jnp.concatenate([x_sq[k // 2] + yz[k % 2] for k in range(8)], axis=0))


def doubled_transfer(t_ref):
    flat = t_ref[...].reshape(2 * K, K)
    return jnp.concatenate([flat, flat], axis=1)


def device_index():
    return lax.axis_index("leaf") * lax.axis_size("sub") + lax.axis_index("sub")


def merge_up(pairs, t_high, t_low):
    n = pairs.shape[0]
    high, low = halves(pairs.reshape(n * R, 128))
    out = dot(high, jnp.concatenate([t_high, t_low], axis=1))
    out = out[:, 0:128] + out[:, 128:256] + dot(low, t_high)
    return out.reshape(n, R, 128)


def pair_lanes(clusters):
    n = clusters.shape[0]
    split = clusters.reshape(n // 2, 2, R, 128)
    return jnp.where(lanes((1, R, 128)) < K, split[:, 0], split[:, 1])


def down_weights(doubled):
    low = lanes(doubled.shape) < K
    both = jnp.concatenate(
        [jnp.where(low, doubled, 0.0), jnp.where(low, 0.0, doubled)], axis=0
    )
    return halves(both)


def push_down(value, w_high, w_low):
    n = value.shape[0]
    high, low = halves(value.reshape(n * R, 128))
    out = dot_nt(high, w_high) + dot_nt(high, w_low) + dot_nt(low, w_high)
    out = out.reshape(n, R, 256)
    return jnp.stack([out[:, :, 0:128], out[:, :, 128:256]], axis=1).reshape(2 * n, R, 128)


def merge_shape_rows(left, right):
    lane = lanes(left.shape)
    sep = left - right
    gap = jnp.sqrt(jnp.sum(jnp.where(lane < 3, sep * sep, 0.0), axis=1, keepdims=True))
    radius = jnp.maximum(left, right) + 0.5 * gap
    return jnp.where(lane == 3, radius, jnp.where(lane < 3, 0.5 * (left + right), 0.0))


def sibling_tile(left, right, lane_u, row_y, row_z):
    low = lanes((8, 128)) < K
    alpha = jnp.where(low, left[3], right[3])
    beta = jnp.where(low, right[3], left[3])
    base = [jnp.where(low, left[d] - right[d], right[d] - left[d]) - beta * lane_u[d] for d in range(3)]
    x_sq = [jnp.square(base[0] + alpha * NODE[a]) for a in range(4)]
    y_sq = [jnp.square(base[1] + alpha * row_y[h]) for h in range(2)]
    z_sq = jnp.square(base[2] + alpha * row_z)
    return tile_from_axes(x_sq, y_sq, z_sq)


def sibling_apply(tile, pair):
    low = lanes((K, 128)) < K
    zero = jnp.zeros((K, 128), BF16)
    weights = []
    for part in halves(tile):
        weights.append(
            jnp.concatenate([jnp.where(low, part, zero), jnp.where(low, zero, part)], axis=0)
        )
    high, low_part = halves(pltpu.roll(pair, K, 1))
    out = dot_nt(high, jnp.concatenate(weights, axis=0))
    return out[:, 0:128] + out[:, 128:256] + dot_nt(low_part, weights[0])


LEVEL_OFFSETS = [0, 128, 192, 224, 240, 248, 252, 254]
PAIR_OFFSETS = [0, 0, 32, 48, 56, 60, 62]


def block_diagonal(left, right):
    zero = jnp.zeros(left.shape, left.dtype)
    return jnp.concatenate(
        [jnp.concatenate([left, zero], axis=1), jnp.concatenate([zero, right], axis=1)], axis=0
    )


def make_lists(near_ref, coupling_ref, list_ref, count_ref, index_ref):
    first_leaf = device_index() * LD
    lane8 = lanes((8, 128))
    row8 = rows((8, 128))
    offset = jnp.where(near_ref[...] >= 0, near_ref[...] - first_leaf - lane8, 1000)

    def slots_at(delta):
        return jnp.sum(jnp.where(offset == delta, 1.0, 0.0), axis=0, keepdims=True)

    forward = jnp.concatenate([slots_at(delta) for delta in range(8)], axis=0)
    reverse = jnp.concatenate(
        [jnp.zeros((1, 128), F32)] + [slots_at(-delta) for delta in range(1, 8)], axis=0
    )
    count_ref[0:8, :] = forward
    count_ref[8:16, :] = reverse
    backward = jnp.concatenate(
        [jnp.zeros((1, 128), F32)]
        + [pltpu.roll(reverse[delta : delta + 1, :], 128 - delta, 1) for delta in range(1, 8)],
        axis=0,
    )
    turned = (row8 == 1) & ((lane8 & 3) == 2)
    leaf = lane8.astype(F32)
    other = leaf + row8.astype(F32)
    first = jnp.where(turned, other, leaf)
    second = jnp.where(turned, leaf, other)
    to_first = jnp.where(turned, backward, forward)
    to_second = jnp.where(turned, forward, backward)
    odd = jnp.where(turned, lane8, lane8 + row8) & 1
    wanted = (lane8 + row8 < LD) & (forward + backward > 0.0)
    earlier = jnp.where(rows((128, 128)) < lanes((128, 128)), 1.0, 0.0).astype(BF16)
    place = jnp.full((8, 128), -1.0, F32)
    most = jnp.zeros((1, 1), F32)
    for parity in range(2):
        flags = jnp.where(wanted & (odd == parity), 1.0, 0.0)
        rank = dot(flags.astype(BF16), earlier)
        totals = jnp.sum(flags, axis=1, keepdims=True)
        before = jnp.zeros((1, 1), F32)
        starts = []
        for delta in range(8):
            starts.append(before)
            before = before + totals[delta : delta + 1, :]
        rank = rank + jnp.concatenate(starts, axis=0)
        place = jnp.where(flags > 0.0, 2.0 * rank + (1.0 * BATCH + parity), place)
        most = jnp.maximum(most, before)
    task_rows = []
    for delta in range(8):
        pick = slice(delta, delta + 1)
        task_rows.append(
            jnp.where(
                row8 == 0,
                first[pick],
                jnp.where(
                    row8 == 1,
                    second[pick],
                    jnp.where(
                        row8 == 2, to_first[pick], jnp.where(row8 == 3, to_second[pick], 0.0)
                    ),
                ),
            ).astype(BF16)
        )
    tasks = jnp.concatenate(task_rows, axis=1)
    slot_row = rows((128, 128)).astype(F32)
    for m in range(LIST // 128):
        chosen = jnp.concatenate(
            [
                jnp.where(place[delta : delta + 1, :] == slot_row + 128.0 * m, 1.0, 0.0).astype(BF16)
                for delta in range(8)
            ],
            axis=1,
        )
        part = dot_nt(tasks, chosen)
        part = jnp.where(row8 == 4, 2.0 * most, part)
        list_ref[:, m * 128 : (m + 1) * 128] = part.astype(jnp.int32)

    target = coupling_ref[...]
    reach = target - first_leaf + HALF
    swap = ((reach ^ row8) & 1) * (PAIRS // 2)
    entry = jnp.where(
        reach < HALF,
        LD + (reach >> 1) + swap,
        jnp.where(reach < HALF + LD, reach - HALF, LD + HALF + ((reach - HALF - LD) >> 1) + swap),
    )
    index_ref[0:8, :] = jnp.where(target >= 0, entry, TABLE - 1)
    index_ref[8:16, :] = jnp.where(target >= 0, reach, 0)


CHUNKS = 4


def leaf_kernel(
    x_any, p_ref, b_any, t_ref, near_ref, coupling_ref,
    send_next, send_prev, high_any, low_any, lev_any, root_ref, shape_ref,
    list_ref, count_ref, index_ref,
    x_ref, b_ref, high_ref, low_ref, lev_ref, coef, pts, shapes, p8, sems,
):
    leaves = LD // CHUNKS
    copies = []
    for c in range(CHUNKS):
        span = slice(c * leaves * P_SIZE, (c + 1) * leaves * P_SIZE)
        part = slice(c * leaves, (c + 1) * leaves)
        copies.append(
            (
                pltpu.make_async_copy(x_any.at[:, span], x_ref.at[:, span], sems.at[c]),
                pltpu.make_async_copy(b_any.at[part], b_ref.at[part], sems.at[CHUNKS + c]),
            )
        )
    for pair in copies:
        for copy in pair:
            copy.start()
    origin = (device_index() * GROUPS).astype(F32)
    low32 = lanes((R, 128)) < K

    make_lists(near_ref, coupling_ref, list_ref, count_ref, index_ref)
    for i in range(LD):
        for d in range(3):
            pts[d, i : i + 1, :] = p_ref[d : d + 1, i * P_SIZE : (i + 1) * P_SIZE]
    centers, squares = [], 0.0
    for d in range(3):
        coords = (pts[d] - origin if d == 2 else pts[d]) * SCALE
        center = jnp.sum(coords, axis=1, keepdims=True) * (1.0 / P_SIZE)
        centers.append(center)
        squares = squares + jnp.square(coords - center)
    radius = jnp.sqrt(jnp.max(squares, axis=1, keepdims=True))
    lane = lanes((LD, 128))
    shapes[0:LD, :] = jnp.where(
        lane == 0,
        centers[0],
        jnp.where(
            lane == 1,
            centers[1],
            jnp.where(lane == 2, centers[2], jnp.where(lane == 3, radius, 0.0)),
        ),
    )
    count = LD // 2
    for level in range(1, 8):
        source = LEVEL_OFFSETS[level - 1]
        joined = merge_shape_rows(
            shapes[pl.ds(source, count, stride=2), :],
            shapes[pl.ds(source + 1, count, stride=2), :],
        )
        shapes[pl.ds(LEVEL_OFFSETS[level], count), :] = joined
        count //= 2
    shape_rows = jnp.concatenate(
        [jnp.transpose(shapes[0:128, :])[0:8], jnp.transpose(shapes[128:256, :])[0:8]], axis=1
    )
    shape_ref[...] = shape_rows

    def leaf_pairs(m, carry):
        values = []
        for v in range(16):
            leaf = 16 * m + v
            x = x_ref[:, pl.ds(pl.multiple_of(leaf * P_SIZE, P_SIZE), P_SIZE)]
            weights = b_ref[leaf]
            values.append(dot_nt(x, jnp.concatenate([weights, weights], axis=0)))
        for v in range(16):
            high_ref[16 * m + v], low_ref[16 * m + v] = halves(values[v])
        for v in range(8):
            coef[8 * m + v] = jnp.where(low32, values[2 * v], values[2 * v + 1])
        return carry

    for c in range(CHUNKS):
        for copy in copies[c]:
            copy.wait()
        steps = leaves // 16
        lax.fori_loop(c * steps, (c + 1) * steps, leaf_pairs, 0)
    leaving = [
        pltpu.make_async_copy(high_ref, high_any, sems.at[2 * CHUNKS]),
        pltpu.make_async_copy(low_ref, low_any, sems.at[2 * CHUNKS + 1]),
    ]
    for copy in leaving:
        copy.start()

    t_high, t_low = halves(doubled_transfer(t_ref))
    pairs = coef[...]
    for level in range(1, 7):
        pairs = pair_lanes(merge_up(pairs, t_high, t_low))
        lev_ref[pl.ds(PAIR_OFFSETS[level], pairs.shape[0])] = pairs
    leaving.append(pltpu.make_async_copy(lev_ref, lev_any, sems.at[2 * CHUNKS + 2]))
    leaving[2].start()
    root = merge_up(pairs, t_high, t_low)[0]

    low = lanes((R // 2, 128)) < K
    block = jnp.concatenate(
        [
            jnp.where(low, root[0 : R // 2], root[R // 2 : R]),
            jnp.broadcast_to(shapes[254:255, :], (8, 128)),
        ],
        axis=0,
    )
    root_ref[...] = block

    p8[...] = jnp.zeros((8, 512), F32)
    for send, first_pair, group in ((send_next, PAIRS // 2, GROUPS - 1), (send_prev, 0, 0)):

        def copy_pairs(m, carry):
            parts = [halves(coef[first_pair + 8 * m + v]) for v in range(8)]
            for v in range(8):
                send[8 * m + v], send[32 + 8 * m + v] = parts[v]
            return carry

        lax.fori_loop(0, PAIRS // 16, copy_pairs, 0)
        parts = thirds(shape_rows[:, 0:128])
        send[68] = jnp.concatenate(list(parts) + [jnp.zeros((8, 128), F32)], axis=0).astype(BF16)
        p8[0:3, :] = p_ref[:, group * 512 : group * 512 + 512]
        parts = thirds(p8[...])
        for k in range(4):
            send[64 + k] = x_ref[:, group * 512 + k * P_SIZE : group * 512 + (k + 1) * P_SIZE]
        for part in range(3):
            send[69 + part] = jnp.concatenate(
                [parts[part][:, k * P_SIZE : (k + 1) * P_SIZE] for k in range(4)], axis=0
            ).astype(BF16)
    for copy in leaving:
        copy.wait()


def point_features(points8, origin_z):
    row = rows(points8.shape)
    center = jnp.where(row == 2, origin_z + 0.5, 1.0)
    v = jnp.where(row < 3, (points8 - center) * SCALE, 0.0)
    norm = jnp.sum(v * v, axis=0, keepdims=True)
    far = jnp.where(row == 3, norm, jnp.where(row == 4, 1.0, v))
    own = jnp.where(row == 3, 1.0, jnp.where(row == 4, norm, -2.0 * v))
    return far, own


def far_stack(value):
    first, second, third = thirds(value)
    none = jnp.zeros(value.shape, F32)
    return jnp.concatenate(
        [first, first, first, second, second, third, none, none], axis=0
    ).astype(BF16)


def own_stack(value):
    first, second, third = thirds(value)
    none = jnp.zeros(value.shape, F32)
    return jnp.concatenate(
        [first, second, third, first, second, first, none, none], axis=0
    ).astype(BF16)


def identity():
    return jnp.where(rows((128, 128)) == lanes((128, 128)), 1.0, 0.0).astype(BF16)


def near_kernel(
    list_ref, shape_ref, x_any, p_ref, lev_any,
    out_ref, couple_ref,
    x_ref, lev_ref, sems, p8, far_feat, own_feat, tile0, tile1,
):
    copies = [
        pltpu.make_async_copy(x_any, x_ref, sems.at[0]),
        pltpu.make_async_copy(lev_any, lev_ref, sems.at[1]),
    ]
    for copy in copies:
        copy.start()
    first_group = device_index() * GROUPS
    p8[...] = jnp.zeros(p8.shape, F32)
    eye = identity()

    def features(m, carry):
        loaded = [p_ref[:, pl.ds(pl.multiple_of((4 * m + v) * 512, 512), 512)] for v in range(4)]
        for v in range(4):
            p8[v, 0:3, :] = loaded[v]
        made = []
        for v in range(4):
            coords = p8[v]
            origin_z = (first_group + 4 * m + v).astype(F32)
            far, own = point_features(coords, origin_z)
            _, own_up = point_features(coords, origin_z + 1.0)
            far = far_stack(far)
            parts = [far[:, k * P_SIZE : (k + 1) * P_SIZE] for k in range(4)]
            turned = dot_nt(eye, jnp.concatenate(parts, axis=0)).astype(BF16)
            made.append((turned, own_stack(own), own_stack(own_up)))
        for v in range(4):
            g = 4 * m + v
            turned, own, own_up = made[v]
            far_feat[2 * g] = turned[:, 0:128]
            far_feat[2 * g + 1] = turned[:, 128:256]
            for k in range(4):
                part = slice(k * P_SIZE, (k + 1) * P_SIZE)
                own_feat[4 * g + k] = own[:, part]
                own_feat[LD + 4 * g + k] = own_up[:, part]
        return carry

    lax.fori_loop(0, GROUPS // 4, features, 0)

    for copy in copies:
        copy.wait()
    out_ref[...] = x_ref[...].astype(F32)
    for ref in (tile0, tile1):
        ref[...] = jnp.zeros(ref.shape, ref.dtype)

    total = list_ref[4, 0]
    steps = (total + BATCH - 1) // BATCH + 1
    low = lanes((128, 128)) < K

    def leaf_slice(i):
        return pl.ds(pl.multiple_of(i * P_SIZE, P_SIZE), P_SIZE)

    lane_u = lane_nodes()
    row_y, row_z = row_nodes()

    def phase(n, tile_new, tile_old, pairs):
        far, own, sources, updates = [], [], [], []
        siblings = [jnp.minimum(pairs * n + v, PAIRS - 2) for v in range(pairs)]
        levels = [lev_ref[pair] for pair in siblings]
        for u in range(BATCH):
            k = (n + 1) * BATCH + u
            i, j = list_ref[0, k], list_ref[1, k]
            variant = ((j >> 2) - (i >> 2)) * LD
            far.append(far_feat[j >> 1])
            own.append(own_feat[variant + i])
        for u in range(BATCH):
            k = n * BATCH + u
            i, j = list_ref[0, k], list_ref[1, k]
            sources.append((x_ref[:, leaf_slice(j)], x_ref[:, leaf_slice(i)]))
        tiles = []
        for u in range(BATCH // 2):
            pick = jnp.where(low, far[2 * u], far[2 * u + 1])
            dist = dot(pick, block_diagonal(own[2 * u], own[2 * u + 1]))
            tiles.append(decay(dist).astype(BF16))
            weights = block_diagonal(tile_old[u, :, 0:128], tile_old[u, :, 128:256])
            to_i = dot(jnp.concatenate([sources[2 * u][0], sources[2 * u + 1][0]], axis=1), weights)
            to_j = dot_nt(jnp.concatenate([sources[2 * u][1], sources[2 * u + 1][1]], axis=1), weights)
            for h in range(2):
                k = n * BATCH + 2 * u + h
                span = slice(h * 128, (h + 1) * 128)
                updates.append(
                    (
                        to_i[:, span] * list_ref[2, k].astype(F32),
                        to_j[:, span] * list_ref[3, k].astype(F32),
                    )
                )
        for pair, level in zip(siblings, levels):
            cluster = LD + 2 * pair
            left = [shape_ref[d, cluster] for d in range(4)]
            right = [shape_ref[d, cluster + 1] for d in range(4)]
            couple_ref[pair] = sibling_apply(
                sibling_tile(left, right, lane_u, row_y, row_z), level
            )
        for u in range(BATCH // 2):
            tile_new[u] = tiles[u]
        for u in range(BATCH):
            k = n * BATCH + u
            to_i = leaf_slice(list_ref[0, k])
            to_j = leaf_slice(list_ref[1, k])
            out_ref[:, to_i] += updates[u][0]
            out_ref[:, to_j] += updates[u][1]

    def two_phases(pairs, m, carry):
        phase(2 * m, tile0, tile1, pairs)
        phase(2 * m + 1, tile1, tile0, pairs)
        return carry

    rides = PAIRS // (2 * SIBLINGS)
    lax.fori_loop(0, rides, functools.partial(two_phases, SIBLINGS), 0)
    lax.fori_loop(rides, (steps + 1) // 2, functools.partial(two_phases, 0), 0)


def tree_down(t_ref, root_ref, down_ref, couple, pairs_scr, shapes):
    lane_u = lane_nodes()
    row_y, row_z = row_nodes()

    doubled = doubled_transfer(t_ref)
    t_high, t_low = halves(doubled)
    w_high, w_low = down_weights(doubled)
    device = device_index()
    n = root_ref.shape[0]
    low = lanes((R, 128)) < K
    shift = lanes((1, 128)) == 2
    for k in range(n):
        shapes[k : k + 1, :] = root_ref[k, R // 2 : R // 2 + 1, :] + jnp.where(
            shift, (k * GROUPS) * SCALE, 0.0
        )
    for k in range(n // 2):
        left = root_ref[2 * k, 0 : R // 2, :]
        right = root_ref[2 * k + 1, 0 : R // 2, :]
        left = jnp.concatenate([left, pltpu.roll(left, K, 1)], axis=0)
        right = jnp.concatenate([pltpu.roll(right, K, 1), right], axis=0)
        pairs_scr[k] = jnp.where(low, left, right)
    source, count, pair_source = 0, n // 2, 0
    levels = []
    while count >= 1:
        levels.append((source, pair_source))
        if count > 1:
            pairs = pair_lanes(merge_up(pairs_scr[pl.ds(pair_source, count)], t_high, t_low))
            pairs_scr[pl.ds(pair_source + count, count // 2)] = pairs
            joined = merge_shape_rows(
                shapes[pl.ds(source, count, stride=2), :],
                shapes[pl.ds(source + 1, count, stride=2), :],
            )
            shapes[pl.ds(source + 2 * count, count), :] = joined
        source += 2 * count
        pair_source += count
        count //= 2
    couples = []
    for level, (source, pair_source) in enumerate(levels):
        pair = device >> (level + 1)
        left_row = shapes[pl.ds(source + 2 * pair, 1), :]
        right_row = shapes[pl.ds(source + 2 * pair + 1, 1), :]
        left = [jnp.broadcast_to(left_row[:, d : d + 1], (8, 128)) for d in range(4)]
        right = [jnp.broadcast_to(right_row[:, d : d + 1], (8, 128)) for d in range(4)]
        tile = sibling_tile(left, right, lane_u, row_y, row_z)
        couples.append(sibling_apply(tile, pairs_scr[pair_source + pair]))
    incoming = None
    for level in reversed(range(len(levels))):
        value = couples[level]
        if incoming is not None:
            pushed = push_down(incoming[None], w_high, w_low)
            value = value + (pushed[0] + pushed[1])
        side = (device >> level) & 1
        keep_low = jnp.where(low, 1, 0) == (1 - side)
        incoming = jnp.where(keep_low, value, 0.0)
    pushed = push_down(incoming[None], w_high, w_low)
    value = couple[pl.ds(PAIR_OFFSETS[6], 1)] + (pushed[0:1] + pushed[1:2])
    for level in range(5, 0, -1):
        n = PAIRS >> level
        value = couple[pl.ds(PAIR_OFFSETS[level], n)] + push_down(value, w_high, w_low)
    down_ref[...] = push_down(value, w_high, w_low)


UNIT = 4


def couple_leaves(
    entries, shape_ref, prev_ref, next_ref, table_copies, leaf_couple,
    shape_tab, high_tab, low_tab, halo_rows, halo_shape, sems,
    tiles0, lhs0, tiles1, lhs1,
):
    copies = []
    for k, ref in enumerate((prev_ref, next_ref)):
        parts = ref[68].astype(F32)
        halo_rows[k] = parts[0:8] + parts[8:16] + parts[16:24]
        copies.append(pltpu.make_async_copy(halo_rows.at[k], halo_shape.at[k], sems.at[k]))
    for copy in copies:
        copy.start()
    low32 = lanes((R, 128)) < K
    lane_u = lane_nodes()
    row8 = rows((8, 128))
    low8 = lanes((8, 128)) < K

    def shape_rows(read, k, shift):
        return jnp.where(
            row8 == 0,
            read(0, k),
            jnp.where(row8 == 1, read(1, k), jnp.where(row8 == 2, read(2, k) + shift, read(3, k))),
        )

    def own_nodes(m, carry):
        shape_tab[HALF + m] = shape_rows(lambda d, k: shape_ref[d, k], m, 0.0)
        return carry

    lax.fori_loop(0, LD, own_nodes, 0, unroll=8)
    for copy in copies:
        copy.wait()
    for side, ref in enumerate((prev_ref, next_ref)):
        first = LD + side * HALF

        def halo_pairs(m, carry):
            def read(d, k):
                return halo_shape[side, d, k]

            loaded = [
                (tab, 4 * m + v, ref[offset + 4 * m + v])
                for tab, offset in ((high_tab, 0), (low_tab, 32))
                for v in range(4)
            ]
            turned = [pltpu.roll(pair.astype(F32), K, 1).astype(BF16) for _, _, pair in loaded]
            source = HALF if side == 0 else 0
            place = 0 if side == 0 else HALF + LD
            shift = (2.0 * side - 1.0) * GROUPS * SCALE
            for v in range(8):
                shape_tab[place + 8 * m + v] = shape_rows(read, source + 8 * m + v, shift)
            for (tab, pair, value), other in zip(loaded, turned):
                tab[first + pair] = value
                tab[first + PAIRS // 2 + pair] = other
            return carry

        lax.fori_loop(0, PAIRS // 8, halo_pairs, 0)
    high_tab[TABLE - 1] = jnp.zeros((R, 128), BF16)
    low_tab[TABLE - 1] = jnp.zeros((R, 128), BF16)
    for copy in table_copies:
        copy.wait()

    row_y, row_z = row_nodes()

    def couple_tiles(pair, u, tiles, lhs):
        leaves = (2 * pair, 2 * pair + 1)
        for q in range(4):
            span = slice(q * 128, (q + 1) * 128)
            for h in range(2):
                e0, e1 = entries[2 * q, leaves[h]], entries[2 * q + 1, leaves[h]]
                lhs[u, h * R : (h + 1) * R, span] = jnp.where(low32, high_tab[e0], high_tab[e1])
                lhs[u, (2 + h) * R : (3 + h) * R, span] = jnp.where(
                    low32, low_tab[e0], low_tab[e1]
                )
        own = jnp.where(low8, shape_tab[HALF + leaves[0]], shape_tab[HALF + leaves[1]])
        radius = jnp.broadcast_to(own[3:4], (8, 128))
        own = [jnp.broadcast_to(own[d : d + 1], (8, 128)) + radius * lane_u[d] for d in range(3)]
        fars = []
        for s in range(8):
            e0, e1 = entries[8 + s, leaves[0]], entries[8 + s, leaves[1]]
            fars.append(jnp.where(low8, shape_tab[e0], shape_tab[e1]))
        for s, far in enumerate(fars):
            reach = jnp.broadcast_to(far[3:4], (8, 128))
            gap = [own[d] - jnp.broadcast_to(far[d : d + 1], (8, 128)) for d in range(3)]
            tile = tile_from_axes(
                [jnp.square(gap[0] - reach * NODE[b]) for b in range(4)],
                [jnp.square(gap[1] - reach * row_y[h]) for h in range(2)],
                jnp.square(gap[2] - reach * row_z),
            )
            high, low = halves(tile)
            tiles[u, s * K : (s + 1) * K, 0:128] = high
            tiles[u, s * K : (s + 1) * K, 128:256] = low

    def couple_apply(u, tiles, lhs):
        both = dot(lhs[u], tiles[u])
        both = both[0 : 2 * R, 0:128] + (both[2 * R : 4 * R, 0:128] + both[0 : 2 * R, 128:256])
        return jnp.where(low32, both[0:R], both[R : 2 * R])

    def couple_phase(n, new, old):
        for u in range(UNIT):
            couple_tiles(jnp.minimum(n * UNIT + u, PAIRS - 1), u, *new)
            leaf_couple[n * UNIT + u] = couple_apply(u, *old)

    buffers = ((tiles0, lhs0), (tiles1, lhs1))
    for ref in buffers[1]:
        ref[...] = jnp.zeros(ref.shape, ref.dtype)

    def couple_two(m, carry):
        couple_phase(2 * m, buffers[0], buffers[1])
        couple_phase(2 * m + 1, buffers[1], buffers[0])
        return carry

    lax.fori_loop(0, PAIRS // UNIT // 2 + 1, couple_two, 0)


def finish_leaves(
    counts, p_ref, b_ref, prev_ref, next_ref, down_ref, leaf_couple, out_ref, p8, coords
):
    device = device_index()

    def finish(m, carry):
        values = []
        for v in range(8):
            c = 8 * m + v
            value = (down_ref[c] + leaf_couple[c + UNIT]).astype(BF16)
            span = pl.ds(pl.multiple_of(c * 256, 256), 256)
            values.append(
                (
                    span,
                    out_ref[:, span]
                    + dot(value, block_diagonal(b_ref[2 * c], b_ref[2 * c + 1])),
                )
            )
        for span, value in values:
            out_ref[:, span] = value
        return carry

    lax.fori_loop(0, PAIRS // 8, finish, 0)

    p8[...] = jnp.zeros(p8.shape, F32)
    eye = identity()
    sides = ((prev_ref, 0), (next_ref, GROUPS - 1))
    for side, (halo_ref, group) in enumerate(sides):
        p8[side, 0:3, :] = p_ref[:, group * 512 : group * 512 + 512]
        coords[side] = halo_ref[69].astype(F32) + halo_ref[70].astype(F32) + halo_ref[71].astype(F32)

    def edge(k, carry):
        loaded = [
            (halo_ref[64 + k], coords[side, 8 * k : 8 * k + 8, :], p8[side])
            for side, (halo_ref, _) in enumerate(sides)
        ]
        for side, (_, group) in enumerate(sides):
            x_far, far, own = loaded[side]
            origin_z = (device * GROUPS + group).astype(F32)
            _, own = point_features(own, origin_z)
            far, _ = point_features(far, origin_z)
            far = dot_nt(eye, far_stack(far)).astype(BF16)
            tiles = decay(dot(far, own_stack(own))).astype(BF16)
            products = dot(x_far, tiles)
            for i in range(4):
                delta = (4 + i - k) if side == 0 else (4 + k - i)
                weight = counts[8 * (1 - side) + delta, 4 * group + i]
                place = slice((4 * group + i) * P_SIZE, (4 * group + i + 1) * P_SIZE)
                out_ref[:, place] += products[:, i * P_SIZE : (i + 1) * P_SIZE] * weight
        return carry

    for k in range(4):
        edge(k, 0)


def couple_kernel(
    entries, shape_ref,
    prev_any, next_any, high_any, low_any,
    leaf_couple,
    prev_ref, next_ref,
    shape_tab, high_tab, low_tab, halo_rows, halo_shape,
    tiles0, lhs0, tiles1, lhs1, sems, halo_sems,
):
    moves = (
        (prev_any, prev_ref),
        (next_any, next_ref),
        (high_any, high_tab.at[0:LD]),
        (low_any, low_tab.at[0:LD]),
    )
    copies = [pltpu.make_async_copy(a, b, sems.at[k]) for k, (a, b) in enumerate(moves)]
    for copy in copies:
        copy.start()
    copies[0].wait()
    copies[1].wait()
    couple_leaves(
        entries, shape_ref, prev_ref, next_ref, copies[2:4], leaf_couple,
        shape_tab, high_tab, low_tab, halo_rows, halo_shape, halo_sems,
        tiles0, lhs0, tiles1, lhs1,
    )


def final_kernel(
    counts,
    t_any, root_any, couple_any, b_any, couple_leaf_any, near_any, prev_any, next_any, p_any,
    out_ref,
    t_ref, root_ref, couple, b_ref, leaf_couple, prev_ref, next_ref, p_ref,
    down, pairs_scr, shapes, p8, coords, sems,
):
    moves = (
        (t_any, t_ref),
        (root_any, root_ref),
        (couple_any, couple),
        (b_any, b_ref),
        (couple_leaf_any, leaf_couple),
        (near_any, out_ref),
        (prev_any, prev_ref),
        (next_any, next_ref),
        (p_any, p_ref),
    )
    copies = [pltpu.make_async_copy(a, b, sems.at[k]) for k, (a, b) in enumerate(moves)]
    for copy in copies:
        copy.start()
    for copy in copies[0:3]:
        copy.wait()
    tree_down(t_ref, root_ref, down, couple, pairs_scr, shapes)
    for copy in copies[3:]:
        copy.wait()
    finish_leaves(
        counts, p_ref, b_ref, prev_ref, next_ref, down, leaf_couple, out_ref, p8, coords
    )


def shaped(*shape, dtype=F32):
    return jax.ShapeDtypeStruct(shape, dtype)


def vmem():
    return pl.BlockSpec(memory_space=pltpu.VMEM)


def smem():
    return pl.BlockSpec(memory_space=pltpu.SMEM)


def anywhere():
    return pl.BlockSpec(memory_space=pl.ANY)


PARAMS = pltpu.CompilerParams(vmem_limit_bytes=VMEM_LIMIT)


def per_device(charges, points, basis, transfer, near_list, coupling_list):
    near_rows = near_list.T
    coupling_rows = coupling_list.T
    devices = lax.axis_size("sub") * lax.axis_size("leaf")
    send_next, send_prev, high, low, lev, root, shapes, tasks, counts, entries = pl.pallas_call(
        leaf_kernel,
        name="leaf_up",
        out_shape=(
            shaped(SEND, R, 128, dtype=BF16),
            shaped(SEND, R, 128, dtype=BF16),
            shaped(LD, R, 128, dtype=BF16),
            shaped(LD, R, 128, dtype=BF16),
            shaped(PAIRS - 1, R, 128),
            shaped(R // 2 + 8, 128),
            shaped(8, 256),
            shaped(8, LIST, dtype=jnp.int32),
            shaped(16, 128),
            shaped(16, 128, dtype=jnp.int32),
        ),
        in_specs=[anywhere(), vmem(), anywhere(), vmem(), vmem(), vmem()],
        out_specs=[vmem()] * 2 + [anywhere()] * 3 + [vmem()] * 5,
        scratch_shapes=[
            pltpu.VMEM((R, LD * P_SIZE), BF16),
            pltpu.VMEM((LD, K, P_SIZE), BF16),
            pltpu.VMEM((LD, R, 128), BF16),
            pltpu.VMEM((LD, R, 128), BF16),
            pltpu.VMEM((PAIRS - 1, R, 128), F32),
            pltpu.VMEM((PAIRS, R, 128), F32),
            pltpu.VMEM((3, LD, 128), F32),
            pltpu.VMEM((256, 128), F32),
            pltpu.VMEM((8, 512), F32),
            pltpu.SemaphoreType.DMA((2 * CHUNKS + 3,)),
        ],
        compiler_params=PARAMS,
    )(charges, points, basis, transfer, near_rows, coupling_rows)

    roots = lax.all_gather(root, AXES, axis=0)
    forward = [(i, i + 1) for i in range(devices - 1)]
    backward = [(i + 1, i) for i in range(devices - 1)]
    from_prev = lax.ppermute(send_next, AXES, forward)
    from_next = lax.ppermute(send_prev, AXES, backward)

    near, couple = pl.pallas_call(
        near_kernel,
        name="near_field",
        out_shape=(shaped(R, LD * P_SIZE), shaped(PAIRS - 1, R, 128)),
        in_specs=[smem(), smem(), anywhere(), vmem(), anywhere()],
        out_specs=[vmem()] * 2,
        scratch_shapes=[
            pltpu.VMEM((R, LD * P_SIZE), BF16),
            pltpu.VMEM((PAIRS - 1, R, 128), F32),
            pltpu.SemaphoreType.DMA((2,)),
            pltpu.VMEM((4, 8, 512), F32),
            pltpu.VMEM((PAIRS, P_SIZE, 2 * FEATS), BF16),
            pltpu.VMEM((2 * LD, FEATS, P_SIZE), BF16),
            pltpu.VMEM((BATCH // 2, 128, 256), BF16),
            pltpu.VMEM((BATCH // 2, 128, 256), BF16),
        ],
        compiler_params=PARAMS,
        cost_estimate=pl.CostEstimate(
            flops=2 * 460 * 128 * 128 * 128, bytes_accessed=4 << 20, transcendentals=460 * 32768
        ),
    )(tasks, shapes, charges, points, lev)

    near, from_prev, from_next = lax.optimization_barrier((near, from_prev, from_next))
    stages = [
        pltpu.VMEM((UNIT, 512, 256), BF16),
        pltpu.VMEM((UNIT, 4 * R, 512), BF16),
    ]
    leaf_couple = pl.pallas_call(
        couple_kernel,
        name="leaf_couple",
        out_shape=shaped(PAIRS + 2 * UNIT, R, 128),
        in_specs=[smem()] * 2 + [anywhere()] * 4,
        out_specs=vmem(),
        scratch_shapes=[
            pltpu.VMEM((SEND, R, 128), BF16),
            pltpu.VMEM((SEND, R, 128), BF16),
            pltpu.VMEM((2 * LD, 8, 128), F32),
            pltpu.VMEM((TABLE, R, 128), BF16),
            pltpu.VMEM((TABLE, R, 128), BF16),
            pltpu.VMEM((2, 8, 128), F32),
            pltpu.SMEM((2, 8, 128), F32),
        ]
        + stages
        + stages
        + [pltpu.SemaphoreType.DMA((4,)), pltpu.SemaphoreType.DMA((2,))],
        compiler_params=PARAMS,
        cost_estimate=pl.CostEstimate(
            flops=2 * 1024 * 64 * 64 * 32 * 3, bytes_accessed=6 << 20, transcendentals=1024 * 8192
        ),
    )(entries, shapes, from_prev, from_next, high, low)

    leaf_couple, roots = lax.optimization_barrier((leaf_couple, roots))
    return pl.pallas_call(
        final_kernel,
        name="tree_finish",
        out_shape=shaped(R, LD * P_SIZE),
        in_specs=[smem()] + [anywhere()] * 9,
        out_specs=vmem(),
        scratch_shapes=[
            pltpu.VMEM((2, K, K), F32),
            pltpu.VMEM((devices, R // 2 + 8, 128), F32),
            pltpu.VMEM((PAIRS - 1, R, 128), F32),
            pltpu.VMEM((LD, K, P_SIZE), BF16),
            pltpu.VMEM((PAIRS + 2 * UNIT, R, 128), F32),
            pltpu.VMEM((SEND, R, 128), BF16),
            pltpu.VMEM((SEND, R, 128), BF16),
            pltpu.VMEM((3, LD * P_SIZE), F32),
            pltpu.VMEM((PAIRS, R, 128), F32),
            pltpu.VMEM((devices, R, 128), F32),
            pltpu.VMEM((2 * devices, 128), F32),
            pltpu.VMEM((2, 8, 512), F32),
            pltpu.VMEM((2, R, 128), F32),
            pltpu.SemaphoreType.DMA((9,)),
        ],
        compiler_params=PARAMS,
    )(counts, transfer, roots, couple, basis, leaf_couple, near, from_prev, from_next, points)


def solution(mesh):
    in_specs = (
        P(None, AXES),
        P(None, AXES),
        P(AXES, None, None),
        P(),
        P(AXES, None),
        P(AXES, None),
    )
    return jax.shard_map(
        per_device, mesh=mesh, in_specs=in_specs, out_specs=P(None, AXES), check_vma=False
    )
```

```python
import functools
import math

import jax
import jax.numpy as jnp
from jax import lax
from jax.experimental import pallas as pl
from jax.experimental.pallas import tpu as pltpu
from jax.sharding import PartitionSpec as P

P_SIZE = 128
K = 64
R = 32
LD = 128
PAIRS = LD // 2
GROUPS = LD // 4
TABLE = 257
HALF = LD // 2
NEAR_REACH = 8
FEATS = 64
BATCH = 16
SIBLINGS = 4
LIST = 896
SEND = 72
SCALE = 0.5 * math.log2(math.e)
NODE = [math.cos((2 * a + 1) * math.pi / 8) for a in range(4)]
AXES = ("leaf", "sub")
F32 = jnp.float32
BF16 = jnp.bfloat16
NT = (((1,), (1,)), ((), ()))
TINY = 1e-30
VMEM_LIMIT = 64 * 1024 * 1024


def lanes(shape):
    return lax.broadcasted_iota(jnp.int32, shape, len(shape) - 1)


def rows(shape):
    return lax.broadcasted_iota(jnp.int32, shape, len(shape) - 2)


def dot(a, b):
    return jnp.dot(a, b, preferred_element_type=F32)


def dot_nt(a, b):
    return lax.dot_general(a, b, NT, preferred_element_type=F32)


def halves(value):
    high = value.astype(BF16)
    return high, (value - high.astype(F32)).astype(BF16)


def thirds(value):
    first = value.astype(BF16).astype(F32)
    rest = value - first
    second = rest.astype(BF16).astype(F32)
    return first, second, rest - second


def unit_node(index):
    return jnp.where(
        index == 0,
        NODE[0],
        jnp.where(index == 1, NODE[1], jnp.where(index == 2, NODE[2], NODE[3])),
    ).astype(F32)


def lane_nodes():
    b = lanes((8, 128)) & 63
    return [unit_node(b >> 4), unit_node((b >> 2) & 3), unit_node(b & 3)]


def row_nodes():
    r = rows((8, 128))
    return [unit_node(r >> 2), unit_node((r >> 2) + 2)], unit_node(r & 3)


def decay(t):
    return decay_positive(jnp.maximum(t, TINY))


def decay_positive(t):
    return jnp.exp2(-(t * lax.rsqrt(t)))


def tile_from_axes(x_sq, y_sq, z_sq):
    z_sq = z_sq + TINY
    yz = [y_sq[0] + z_sq, y_sq[1] + z_sq]
    return decay_positive(jnp.concatenate([x_sq[k // 2] + yz[k % 2] for k in range(8)], axis=0))


def doubled_transfer(t_ref):
    flat = t_ref[...].reshape(2 * K, K)
    return jnp.concatenate([flat, flat], axis=1)


def device_index():
    return lax.axis_index("leaf") * lax.axis_size("sub") + lax.axis_index("sub")


def merge_up(pairs, t_high, t_low):
    n = pairs.shape[0]
    high, low = halves(pairs.reshape(n * R, 128))
    out = dot(high, jnp.concatenate([t_high, t_low], axis=1))
    out = out[:, 0:128] + out[:, 128:256] + dot(low, t_high)
    return out.reshape(n, R, 128)


def pair_lanes(clusters):
    n = clusters.shape[0]
    split = clusters.reshape(n // 2, 2, R, 128)
    return jnp.where(lanes((1, R, 128)) < K, split[:, 0], split[:, 1])


def down_weights(doubled):
    low = lanes(doubled.shape) < K
    both = jnp.concatenate(
        [jnp.where(low, doubled, 0.0), jnp.where(low, 0.0, doubled)], axis=0
    )
    return halves(both)


def push_down(value, w_high, w_low):
    n = value.shape[0]
    high, low = halves(value.reshape(n * R, 128))
    out = dot_nt(high, w_high) + dot_nt(high, w_low) + dot_nt(low, w_high)
    out = out.reshape(n, R, 256)
    return jnp.stack([out[:, :, 0:128], out[:, :, 128:256]], axis=1).reshape(2 * n, R, 128)


def merge_shape_rows(left, right):
    lane = lanes(left.shape)
    sep = left - right
    gap = jnp.sqrt(jnp.sum(jnp.where(lane < 3, sep * sep, 0.0), axis=1, keepdims=True))
    radius = jnp.maximum(left, right) + 0.5 * gap
    return jnp.where(lane == 3, radius, jnp.where(lane < 3, 0.5 * (left + right), 0.0))


def sibling_tile(left, right, lane_u, row_y, row_z):
    low = lanes((8, 128)) < K
    alpha = jnp.where(low, left[3], right[3])
    beta = jnp.where(low, right[3], left[3])
    base = [jnp.where(low, left[d] - right[d], right[d] - left[d]) - beta * lane_u[d] for d in range(3)]
    x_sq = [jnp.square(base[0] + alpha * NODE[a]) for a in range(4)]
    y_sq = [jnp.square(base[1] + alpha * row_y[h]) for h in range(2)]
    z_sq = jnp.square(base[2] + alpha * row_z)
    return tile_from_axes(x_sq, y_sq, z_sq)


def sibling_apply(tile, pair):
    low = lanes((K, 128)) < K
    zero = jnp.zeros((K, 128), BF16)
    weights = []
    for part in halves(tile):
        weights.append(
            jnp.concatenate([jnp.where(low, part, zero), jnp.where(low, zero, part)], axis=0)
        )
    high, low_part = halves(pltpu.roll(pair, K, 1))
    out = dot_nt(high, jnp.concatenate(weights, axis=0))
    return out[:, 0:128] + out[:, 128:256] + dot_nt(low_part, weights[0])


LEVEL_OFFSETS = [0, 128, 192, 224, 240, 248, 252, 254]
PAIR_OFFSETS = [0, 0, 32, 48, 56, 60, 62]


def block_diagonal(left, right):
    zero = jnp.zeros(left.shape, left.dtype)
    return jnp.concatenate(
        [jnp.concatenate([left, zero], axis=1), jnp.concatenate([zero, right], axis=1)], axis=0
    )


def make_lists(near_ref, coupling_ref, list_ref, count_ref, index_ref):
    first_leaf = device_index() * LD
    lane8 = lanes((8, 128))
    row8 = rows((8, 128))
    offset = jnp.where(near_ref[...] >= 0, near_ref[...] - first_leaf - lane8, 1000)

    def slots_at(delta):
        return jnp.sum(jnp.where(offset == delta, 1.0, 0.0), axis=0, keepdims=True)

    forward = jnp.concatenate([slots_at(delta) for delta in range(8)], axis=0)
    reverse = jnp.concatenate(
        [jnp.zeros((1, 128), F32)] + [slots_at(-delta) for delta in range(1, 8)], axis=0
    )
    count_ref[0:8, :] = forward
    count_ref[8:16, :] = reverse
    backward = jnp.concatenate(
        [jnp.zeros((1, 128), F32)]
        + [pltpu.roll(reverse[delta : delta + 1, :], 128 - delta, 1) for delta in range(1, 8)],
        axis=0,
    )
    turned = (row8 == 1) & ((lane8 & 3) == 2)
    leaf = lane8.astype(F32)
    other = leaf + row8.astype(F32)
    first = jnp.where(turned, other, leaf)
    second = jnp.where(turned, leaf, other)
    to_first = jnp.where(turned, backward, forward)
    to_second = jnp.where(turned, forward, backward)
    odd = jnp.where(turned, lane8, lane8 + row8) & 1
    wanted = (lane8 + row8 < LD) & (forward + backward > 0.0)
    earlier = jnp.where(rows((128, 128)) < lanes((128, 128)), 1.0, 0.0).astype(BF16)
    place = jnp.full((8, 128), -1.0, F32)
    most = jnp.zeros((1, 1), F32)
    for parity in range(2):
        flags = jnp.where(wanted & (odd == parity), 1.0, 0.0)
        rank = dot(flags.astype(BF16), earlier)
        totals = jnp.sum(flags, axis=1, keepdims=True)
        before = jnp.zeros((1, 1), F32)
        starts = []
        for delta in range(8):
            starts.append(before)
            before = before + totals[delta : delta + 1, :]
        rank = rank + jnp.concatenate(starts, axis=0)
        place = jnp.where(flags > 0.0, 2.0 * rank + (1.0 * BATCH + parity), place)
        most = jnp.maximum(most, before)
    task_rows = []
    for delta in range(8):
        pick = slice(delta, delta + 1)
        task_rows.append(
            jnp.where(
                row8 == 0,
                first[pick],
                jnp.where(
                    row8 == 1,
                    second[pick],
                    jnp.where(
                        row8 == 2, to_first[pick], jnp.where(row8 == 3, to_second[pick], 0.0)
                    ),
                ),
            ).astype(BF16)
        )
    tasks = jnp.concatenate(task_rows, axis=1)
    slot_row = rows((128, 128)).astype(F32)
    for m in range(LIST // 128):
        chosen = jnp.concatenate(
            [
                jnp.where(place[delta : delta + 1, :] == slot_row + 128.0 * m, 1.0, 0.0).astype(BF16)
                for delta in range(8)
            ],
            axis=1,
        )
        part = dot_nt(tasks, chosen)
        part = jnp.where(row8 == 4, 2.0 * most, part)
        list_ref[:, m * 128 : (m + 1) * 128] = part.astype(jnp.int32)

    target = coupling_ref[...]
    reach = target - first_leaf + HALF
    swap = ((reach ^ row8) & 1) * (PAIRS // 2)
    entry = jnp.where(
        reach < HALF,
        LD + (reach >> 1) + swap,
        jnp.where(reach < HALF + LD, reach - HALF, LD + HALF + ((reach - HALF - LD) >> 1) + swap),
    )
    index_ref[0:8, :] = jnp.where(target >= 0, entry, TABLE - 1)
    index_ref[8:16, :] = jnp.where(target >= 0, reach, 0)


CHUNKS = 4


def leaf_kernel(
    x_any, p_ref, b_any, t_ref, near_ref, coupling_ref,
    send_next, send_prev, high_any, low_any, lev_any, root_ref, shape_ref,
    list_ref, count_ref, index_ref,
    x_ref, b_ref, high_ref, low_ref, lev_ref, coef, pts, shapes, p8, sems,
):
    leaves = LD // CHUNKS
    copies = []
    for c in range(CHUNKS):
        span = slice(c * leaves * P_SIZE, (c + 1) * leaves * P_SIZE)
        part = slice(c * leaves, (c + 1) * leaves)
        copies.append(
            (
                pltpu.make_async_copy(x_any.at[:, span], x_ref.at[:, span], sems.at[c]),
                pltpu.make_async_copy(b_any.at[part], b_ref.at[part], sems.at[CHUNKS + c]),
            )
        )
    for pair in copies:
        for copy in pair:
            copy.start()
    origin = (device_index() * GROUPS).astype(F32)
    low32 = lanes((R, 128)) < K

    make_lists(near_ref, coupling_ref, list_ref, count_ref, index_ref)
    def leaf_pairs(m, carry):
        values = []
        for v in range(16):
            leaf = 16 * m + v
            x = x_ref[:, pl.ds(pl.multiple_of(leaf * P_SIZE, P_SIZE), P_SIZE)]
            weights = b_ref[leaf]
            values.append(dot_nt(x, jnp.concatenate([weights, weights], axis=0)))
        for v in range(16):
            high_ref[16 * m + v], low_ref[16 * m + v] = halves(values[v])
        for v in range(8):
            coef[8 * m + v] = jnp.where(low32, values[2 * v], values[2 * v + 1])
        return carry

    for c in range(CHUNKS):
        for copy in copies[c]:
            copy.wait()
        steps = leaves // 16
        lax.fori_loop(c * steps, (c + 1) * steps, leaf_pairs, 0)
    leaving = [
        pltpu.make_async_copy(high_ref, high_any, sems.at[2 * CHUNKS]),
        pltpu.make_async_copy(low_ref, low_any, sems.at[2 * CHUNKS + 1]),
    ]
    for copy in leaving:
        copy.start()

    for i in range(LD):
        for d in range(3):
            pts[d, i : i + 1, :] = p_ref[d : d + 1, i * P_SIZE : (i + 1) * P_SIZE]
    centers, squares = [], 0.0
    for d in range(3):
        coords = (pts[d] - origin if d == 2 else pts[d]) * SCALE
        center = jnp.sum(coords, axis=1, keepdims=True) * (1.0 / P_SIZE)
        centers.append(center)
        squares = squares + jnp.square(coords - center)
    radius = jnp.sqrt(jnp.max(squares, axis=1, keepdims=True))
    lane = lanes((LD, 128))
    shapes[0:LD, :] = jnp.where(
        lane == 0,
        centers[0],
        jnp.where(
            lane == 1,
            centers[1],
            jnp.where(lane == 2, centers[2], jnp.where(lane == 3, radius, 0.0)),
        ),
    )
    count = LD // 2
    for level in range(1, 8):
        source = LEVEL_OFFSETS[level - 1]
        joined = merge_shape_rows(
            shapes[pl.ds(source, count, stride=2), :],
            shapes[pl.ds(source + 1, count, stride=2), :],
        )
        shapes[pl.ds(LEVEL_OFFSETS[level], count), :] = joined
        count //= 2
    shape_rows = jnp.concatenate(
        [jnp.transpose(shapes[0:128, :])[0:8], jnp.transpose(shapes[128:256, :])[0:8]], axis=1
    )
    shape_ref[...] = shape_rows
    t_high, t_low = halves(doubled_transfer(t_ref))
    pairs = coef[...]
    for level in range(1, 7):
        pairs = pair_lanes(merge_up(pairs, t_high, t_low))
        lev_ref[pl.ds(PAIR_OFFSETS[level], pairs.shape[0])] = pairs
    leaving.append(pltpu.make_async_copy(lev_ref, lev_any, sems.at[2 * CHUNKS + 2]))
    leaving[2].start()
    root = merge_up(pairs, t_high, t_low)[0]

    low = lanes((R // 2, 128)) < K
    block = jnp.concatenate(
        [
            jnp.where(low, root[0 : R // 2], root[R // 2 : R]),
            jnp.broadcast_to(shapes[254:255, :], (8, 128)),
        ],
        axis=0,
    )
    root_ref[...] = jnp.broadcast_to(block[None], root_ref.shape)

    p8[...] = jnp.zeros((8, 512), F32)
    for send, first_pair, group in ((send_next, PAIRS // 2, GROUPS - 1), (send_prev, 0, 0)):

        def copy_pairs(m, carry):
            parts = [halves(coef[first_pair + 8 * m + v]) for v in range(8)]
            for v in range(8):
                send[8 * m + v], send[32 + 8 * m + v] = parts[v]
            return carry

        lax.fori_loop(0, PAIRS // 16, copy_pairs, 0)
        parts = thirds(shape_rows[:, 0:128])
        send[68] = jnp.concatenate(list(parts) + [jnp.zeros((8, 128), F32)], axis=0).astype(BF16)
        p8[0:3, :] = p_ref[:, group * 512 : group * 512 + 512]
        parts = thirds(p8[...])
        for k in range(4):
            send[64 + k] = x_ref[:, group * 512 + k * P_SIZE : group * 512 + (k + 1) * P_SIZE]
        for part in range(3):
            send[69 + part] = jnp.concatenate(
                [parts[part][:, k * P_SIZE : (k + 1) * P_SIZE] for k in range(4)], axis=0
            ).astype(BF16)
    for copy in leaving:
        copy.wait()


def point_features(points8, origin_z):
    row = rows(points8.shape)
    center = jnp.where(row == 2, origin_z + 0.5, 1.0)
    v = jnp.where(row < 3, (points8 - center) * SCALE, 0.0)
    norm = jnp.sum(v * v, axis=0, keepdims=True)
    far = jnp.where(row == 3, norm, jnp.where(row == 4, 1.0, v))
    own = jnp.where(row == 3, 1.0, jnp.where(row == 4, norm, -2.0 * v))
    return far, own


def far_stack(value):
    first, second, third = thirds(value)
    none = jnp.zeros(value.shape, F32)
    return jnp.concatenate(
        [first, first, first, second, second, third, none, none], axis=0
    ).astype(BF16)


def own_stack(value):
    first, second, third = thirds(value)
    none = jnp.zeros(value.shape, F32)
    return jnp.concatenate(
        [first, second, third, first, second, first, none, none], axis=0
    ).astype(BF16)


def identity():
    return jnp.where(rows((128, 128)) == lanes((128, 128)), 1.0, 0.0).astype(BF16)


def near_kernel(
    list_ref, shape_ref, x_any, p_ref, lev_any,
    out_ref, couple_ref,
    x_ref, lev_ref, sems, p8, far_feat, own_feat, tile0, tile1,
):
    copies = [
        pltpu.make_async_copy(x_any, x_ref, sems.at[0]),
        pltpu.make_async_copy(lev_any, lev_ref, sems.at[1]),
    ]
    for copy in copies:
        copy.start()
    first_group = device_index() * GROUPS
    p8[...] = jnp.zeros(p8.shape, F32)
    eye = identity()

    def features(m, carry):
        loaded = [p_ref[:, pl.ds(pl.multiple_of((8 * m + v) * 512, 512), 512)] for v in range(8)]
        for v in range(8):
            p8[v, 0:3, :] = loaded[v]
        made = []
        for v in range(8):
            coords = p8[v]
            origin_z = (first_group + 8 * m + v).astype(F32)
            far, own = point_features(coords, origin_z)
            _, own_up = point_features(coords, origin_z + 1.0)
            far = far_stack(far)
            parts = [far[:, k * P_SIZE : (k + 1) * P_SIZE] for k in range(4)]
            turned = dot_nt(eye, jnp.concatenate(parts, axis=0)).astype(BF16)
            made.append((turned, own_stack(own), own_stack(own_up)))
        for v in range(8):
            g = 8 * m + v
            turned, own, own_up = made[v]
            far_feat[2 * g] = turned[:, 0:128]
            far_feat[2 * g + 1] = turned[:, 128:256]
            for k in range(4):
                part = slice(k * P_SIZE, (k + 1) * P_SIZE)
                own_feat[4 * g + k] = own[:, part]
                own_feat[LD + 4 * g + k] = own_up[:, part]
        return carry

    lax.fori_loop(0, GROUPS // 8, features, 0)

    for copy in copies:
        copy.wait()
    out_ref[...] = x_ref[...].astype(F32)
    for ref in (tile0, tile1):
        ref[...] = jnp.zeros(ref.shape, ref.dtype)

    total = list_ref[4, 0]
    steps = (total + BATCH - 1) // BATCH + 1
    low = lanes((128, 128)) < K

    def leaf_slice(i):
        return pl.ds(pl.multiple_of(i * P_SIZE, P_SIZE), P_SIZE)

    lane_u = lane_nodes()
    row_y, row_z = row_nodes()

    def phase(n, tile_new, tile_old, pairs):
        far, own, sources, updates = [], [], [], []
        siblings = [jnp.minimum(pairs * n + v, PAIRS - 2) for v in range(pairs)]
        levels = [lev_ref[pair] for pair in siblings]
        for u in range(BATCH):
            k = (n + 1) * BATCH + u
            i, j = list_ref[0, k], list_ref[1, k]
            variant = ((j >> 2) - (i >> 2)) * LD
            far.append(far_feat[j >> 1])
            own.append(own_feat[variant + i])
        for u in range(BATCH):
            k = n * BATCH + u
            i, j = list_ref[0, k], list_ref[1, k]
            sources.append((x_ref[:, leaf_slice(j)], x_ref[:, leaf_slice(i)]))
        tiles = []
        for u in range(BATCH // 2):
            pick = jnp.where(low, far[2 * u], far[2 * u + 1])
            dist = dot(pick, block_diagonal(own[2 * u], own[2 * u + 1]))
            tiles.append(decay(dist).astype(BF16))
            weights = block_diagonal(tile_old[u, :, 0:128], tile_old[u, :, 128:256])
            to_i = dot(jnp.concatenate([sources[2 * u][0], sources[2 * u + 1][0]], axis=1), weights)
            to_j = dot_nt(jnp.concatenate([sources[2 * u][1], sources[2 * u + 1][1]], axis=1), weights)
            for h in range(2):
                k = n * BATCH + 2 * u + h
                span = slice(h * 128, (h + 1) * 128)
                updates.append(
                    (
                        to_i[:, span] * list_ref[2, k].astype(F32),
                        to_j[:, span] * list_ref[3, k].astype(F32),
                    )
                )
        for pair, level in zip(siblings, levels):
            cluster = LD + 2 * pair
            left = [shape_ref[d, cluster] for d in range(4)]
            right = [shape_ref[d, cluster + 1] for d in range(4)]
            couple_ref[pair] = sibling_apply(
                sibling_tile(left, right, lane_u, row_y, row_z), level
            )
        for u in range(BATCH // 2):
            tile_new[u] = tiles[u]
        for u in range(BATCH):
            k = n * BATCH + u
            to_i = leaf_slice(list_ref[0, k])
            to_j = leaf_slice(list_ref[1, k])
            out_ref[:, to_i] += updates[u][0]
            out_ref[:, to_j] += updates[u][1]

    def two_phases(pairs, m, carry):
        phase(2 * m, tile0, tile1, pairs)
        phase(2 * m + 1, tile1, tile0, pairs)
        return carry

    rides = PAIRS // (2 * SIBLINGS)
    lax.fori_loop(0, rides, functools.partial(two_phases, SIBLINGS), 0)
    lax.fori_loop(rides, (steps + 1) // 2, functools.partial(two_phases, 0), 0)


def tree_down(t_ref, root_ref, down_ref, couple, pairs_scr, shapes):
    lane_u = lane_nodes()
    row_y, row_z = row_nodes()

    doubled = doubled_transfer(t_ref)
    t_high, t_low = halves(doubled)
    w_high, w_low = down_weights(doubled)
    device = device_index()
    n = root_ref.shape[0]
    low = lanes((R, 128)) < K
    shift = lanes((1, 128)) == 2
    for k in range(n):
        shapes[k : k + 1, :] = root_ref[k, R // 2 : R // 2 + 1, :] + jnp.where(
            shift, (k * GROUPS) * SCALE, 0.0
        )
    for k in range(n // 2):
        left = root_ref[2 * k, 0 : R // 2, :]
        right = root_ref[2 * k + 1, 0 : R // 2, :]
        left = jnp.concatenate([left, pltpu.roll(left, K, 1)], axis=0)
        right = jnp.concatenate([pltpu.roll(right, K, 1), right], axis=0)
        pairs_scr[k] = jnp.where(low, left, right)
    source, count, pair_source = 0, n // 2, 0
    levels = []
    while count >= 1:
        levels.append((source, pair_source))
        if count > 1:
            pairs = pair_lanes(merge_up(pairs_scr[pl.ds(pair_source, count)], t_high, t_low))
            pairs_scr[pl.ds(pair_source + count, count // 2)] = pairs
            joined = merge_shape_rows(
                shapes[pl.ds(source, count, stride=2), :],
                shapes[pl.ds(source + 1, count, stride=2), :],
            )
            shapes[pl.ds(source + 2 * count, count), :] = joined
        source += 2 * count
        pair_source += count
        count //= 2
    couples = []
    for level, (source, pair_source) in enumerate(levels):
        pair = device >> (level + 1)
        left_row = shapes[pl.ds(source + 2 * pair, 1), :]
        right_row = shapes[pl.ds(source + 2 * pair + 1, 1), :]
        left = [jnp.broadcast_to(left_row[:, d : d + 1], (8, 128)) for d in range(4)]
        right = [jnp.broadcast_to(right_row[:, d : d + 1], (8, 128)) for d in range(4)]
        tile = sibling_tile(left, right, lane_u, row_y, row_z)
        couples.append(sibling_apply(tile, pairs_scr[pair_source + pair]))
    incoming = None
    for level in reversed(range(len(levels))):
        value = couples[level]
        if incoming is not None:
            pushed = push_down(incoming[None], w_high, w_low)
            value = value + (pushed[0] + pushed[1])
        side = (device >> level) & 1
        keep_low = jnp.where(low, 1, 0) == (1 - side)
        incoming = jnp.where(keep_low, value, 0.0)
    pushed = push_down(incoming[None], w_high, w_low)
    value = couple[pl.ds(PAIR_OFFSETS[6], 1)] + (pushed[0:1] + pushed[1:2])
    for level in range(5, 0, -1):
        n = PAIRS >> level
        value = couple[pl.ds(PAIR_OFFSETS[level], n)] + push_down(value, w_high, w_low)
    down_ref[...] = push_down(value, w_high, w_low)


UNIT = 4


def couple_leaves(
    entries, shape_ref, prev_ref, next_ref, table_copies, leaf_couple,
    shape_tab, high_tab, low_tab, halo_rows, halo_shape, sems,
    tiles0, lhs0, tiles1, lhs1,
):
    copies = []
    for k, ref in enumerate((prev_ref, next_ref)):
        parts = ref[68].astype(F32)
        halo_rows[k] = parts[0:8] + parts[8:16] + parts[16:24]
        copies.append(pltpu.make_async_copy(halo_rows.at[k], halo_shape.at[k], sems.at[k]))
    for copy in copies:
        copy.start()
    low32 = lanes((R, 128)) < K
    lane_u = lane_nodes()
    row8 = rows((8, 128))
    low8 = lanes((8, 128)) < K

    def shape_rows(read, k, shift):
        return jnp.where(
            row8 == 0,
            read(0, k),
            jnp.where(row8 == 1, read(1, k), jnp.where(row8 == 2, read(2, k) + shift, read(3, k))),
        )

    def own_nodes(m, carry):
        shape_tab[HALF + m] = shape_rows(lambda d, k: shape_ref[d, k], m, 0.0)
        return carry

    lax.fori_loop(0, LD, own_nodes, 0, unroll=8)
    for copy in copies:
        copy.wait()
    for side, ref in enumerate((prev_ref, next_ref)):
        first = LD + side * HALF

        def halo_pairs(m, carry):
            def read(d, k):
                return halo_shape[side, d, k]

            loaded = [
                (tab, 4 * m + v, ref[offset + 4 * m + v])
                for tab, offset in ((high_tab, 0), (low_tab, 32))
                for v in range(4)
            ]
            turned = [pltpu.roll(pair.astype(F32), K, 1).astype(BF16) for _, _, pair in loaded]
            source = HALF if side == 0 else 0
            place = 0 if side == 0 else HALF + LD
            shift = (2.0 * side - 1.0) * GROUPS * SCALE
            for v in range(8):
                shape_tab[place + 8 * m + v] = shape_rows(read, source + 8 * m + v, shift)
            for (tab, pair, value), other in zip(loaded, turned):
                tab[first + pair] = value
                tab[first + PAIRS // 2 + pair] = other
            return carry

        lax.fori_loop(0, PAIRS // 8, halo_pairs, 0)
    high_tab[TABLE - 1] = jnp.zeros((R, 128), BF16)
    low_tab[TABLE - 1] = jnp.zeros((R, 128), BF16)
    for copy in table_copies:
        copy.wait()

    row_y, row_z = row_nodes()

    def couple_tiles(pair, u, tiles, lhs):
        leaves = (2 * pair, 2 * pair + 1)
        for q in range(4):
            span = slice(q * 128, (q + 1) * 128)
            for h in range(2):
                e0, e1 = entries[2 * q, leaves[h]], entries[2 * q + 1, leaves[h]]
                lhs[u, h * R : (h + 1) * R, span] = jnp.where(low32, high_tab[e0], high_tab[e1])
                lhs[u, (2 + h) * R : (3 + h) * R, span] = jnp.where(
                    low32, low_tab[e0], low_tab[e1]
                )
        own = jnp.where(low8, shape_tab[HALF + leaves[0]], shape_tab[HALF + leaves[1]])
        radius = jnp.broadcast_to(own[3:4], (8, 128))
        own = [jnp.broadcast_to(own[d : d + 1], (8, 128)) + radius * lane_u[d] for d in range(3)]
        fars = []
        for s in range(8):
            e0, e1 = entries[8 + s, leaves[0]], entries[8 + s, leaves[1]]
            fars.append(jnp.where(low8, shape_tab[e0], shape_tab[e1]))
        for s, far in enumerate(fars):
            reach = jnp.broadcast_to(far[3:4], (8, 128))
            gap = [own[d] - jnp.broadcast_to(far[d : d + 1], (8, 128)) for d in range(3)]
            tile = tile_from_axes(
                [jnp.square(gap[0] - reach * NODE[b]) for b in range(4)],
                [jnp.square(gap[1] - reach * row_y[h]) for h in range(2)],
                jnp.square(gap[2] - reach * row_z),
            )
            high, low = halves(tile)
            tiles[u, s * K : (s + 1) * K, 0:128] = high
            tiles[u, s * K : (s + 1) * K, 128:256] = low

    def couple_apply(u, tiles, lhs):
        both = dot(lhs[u], tiles[u])
        both = both[0 : 2 * R, 0:128] + (both[2 * R : 4 * R, 0:128] + both[0 : 2 * R, 128:256])
        return jnp.where(low32, both[0:R], both[R : 2 * R])

    def couple_phase(n, new, old):
        for u in range(UNIT):
            couple_tiles(jnp.minimum(n * UNIT + u, PAIRS - 1), u, *new)
            leaf_couple[n * UNIT + u] = couple_apply(u, *old)

    buffers = ((tiles0, lhs0), (tiles1, lhs1))
    for ref in buffers[1]:
        ref[...] = jnp.zeros(ref.shape, ref.dtype)

    def couple_two(m, carry):
        couple_phase(2 * m, buffers[0], buffers[1])
        couple_phase(2 * m + 1, buffers[1], buffers[0])
        return carry

    lax.fori_loop(0, PAIRS // UNIT // 2 + 1, couple_two, 0)


def finish_leaves(b_ref, down_ref, leaf_couple, out_ref, border):
    def finish(m, carry):
        values = []
        for v in range(8):
            c = 8 * m + v
            value = (down_ref[c] + leaf_couple[c + UNIT]).astype(BF16)
            span = pl.ds(pl.multiple_of(c * 256, 256), 256)
            values.append(
                (
                    span,
                    out_ref[:, span]
                    + dot(value, block_diagonal(b_ref[2 * c], b_ref[2 * c + 1])),
                )
            )
        for span, value in values:
            out_ref[:, span] = value
        return carry

    lax.fori_loop(0, PAIRS // 8, finish, 0)
    for side, group in enumerate((0, GROUPS - 1)):
        for i in range(4):
            leaf = 4 * group + i
            out_ref[:, leaf * P_SIZE : (leaf + 1) * P_SIZE] += border[4 * side + i]


def border_blocks(counts, p_ref, prev_ref, next_ref, border, p8, coords):
    device = device_index()

    p8[...] = jnp.zeros(p8.shape, F32)
    eye = identity()
    sides = ((prev_ref, 0), (next_ref, GROUPS - 1))
    for side, (halo_ref, group) in enumerate(sides):
        p8[side, 0:3, :] = p_ref[:, group * 512 : group * 512 + 512]
        coords[side] = halo_ref[69].astype(F32) + halo_ref[70].astype(F32) + halo_ref[71].astype(F32)

    sums = [[0.0] * 4, [0.0] * 4]
    for k in range(4):
        loaded = [
            (halo_ref[64 + k], coords[side, 8 * k : 8 * k + 8, :], p8[side])
            for side, (halo_ref, _) in enumerate(sides)
        ]
        for side, (_, group) in enumerate(sides):
            x_far, far, own = loaded[side]
            origin_z = (device * GROUPS + group).astype(F32)
            _, own = point_features(own, origin_z)
            far, _ = point_features(far, origin_z)
            far = dot_nt(eye, far_stack(far)).astype(BF16)
            tiles = decay(dot(far, own_stack(own))).astype(BF16)
            products = dot(x_far, tiles)
            for i in range(4):
                delta = (4 + i - k) if side == 0 else (4 + k - i)
                weight = counts[8 * (1 - side) + delta, 4 * group + i]
                sums[side][i] = sums[side][i] + products[:, i * P_SIZE : (i + 1) * P_SIZE] * weight
    for side in range(2):
        for i in range(4):
            border[4 * side + i] = sums[side][i]


def couple_kernel(
    entries, shape_ref,
    prev_any, next_any, high_any, low_any,
    leaf_couple,
    prev_ref, next_ref,
    shape_tab, high_tab, low_tab, halo_rows, halo_shape,
    tiles0, lhs0, tiles1, lhs1, sems, halo_sems,
):
    moves = (
        (prev_any, prev_ref),
        (next_any, next_ref),
        (high_any, high_tab.at[0:LD]),
        (low_any, low_tab.at[0:LD]),
    )
    copies = [pltpu.make_async_copy(a, b, sems.at[k]) for k, (a, b) in enumerate(moves)]
    for copy in copies:
        copy.start()
    copies[0].wait()
    copies[1].wait()
    couple_leaves(
        entries, shape_ref, prev_ref, next_ref, copies[2:4], leaf_couple,
        shape_tab, high_tab, low_tab, halo_rows, halo_shape, halo_sems,
        tiles0, lhs0, tiles1, lhs1,
    )


def final_kernel(
    counts,
    t_any, root_any, couple_any, b_any, couple_leaf_any, near_any, prev_any, next_any, p_any,
    out_ref,
    t_ref, root_ref, couple, b_ref, leaf_couple, prev_ref, next_ref, p_ref,
    down, pairs_scr, shapes, p8, coords, border, sems,
):
    moves = (
        (t_any, t_ref),
        (root_any, root_ref),
        (couple_any, couple),
        (prev_any.at[64:SEND], prev_ref.at[64:SEND]),
        (next_any.at[64:SEND], next_ref.at[64:SEND]),
        (p_any, p_ref),
        (b_any, b_ref),
        (couple_leaf_any, leaf_couple),
        (near_any, out_ref),
    )
    copies = [pltpu.make_async_copy(a, b, sems.at[k]) for k, (a, b) in enumerate(moves)]
    for copy in copies:
        copy.start()
    for copy in copies[0:6]:
        copy.wait()
    border_blocks(counts, p_ref, prev_ref, next_ref, border, p8, coords)
    tree_down(t_ref, root_ref, down, couple, pairs_scr, shapes)
    for copy in copies[6:]:
        copy.wait()
    finish_leaves(b_ref, down, leaf_couple, out_ref, border)


def shaped(*shape, dtype=F32):
    return jax.ShapeDtypeStruct(shape, dtype)


def vmem():
    return pl.BlockSpec(memory_space=pltpu.VMEM)


def smem():
    return pl.BlockSpec(memory_space=pltpu.SMEM)


def anywhere():
    return pl.BlockSpec(memory_space=pl.ANY)


PARAMS = pltpu.CompilerParams(vmem_limit_bytes=VMEM_LIMIT)


def per_device(charges, points, basis, transfer, near_list, coupling_list):
    near_rows = near_list.T
    coupling_rows = coupling_list.T
    devices = lax.axis_size("sub") * lax.axis_size("leaf")
    send_next, send_prev, high, low, lev, root, shapes, tasks, counts, entries = pl.pallas_call(
        leaf_kernel,
        name="leaf_up",
        out_shape=(
            shaped(SEND, R, 128, dtype=BF16),
            shaped(SEND, R, 128, dtype=BF16),
            shaped(LD, R, 128, dtype=BF16),
            shaped(LD, R, 128, dtype=BF16),
            shaped(PAIRS - 1, R, 128),
            shaped(devices, R // 2 + 8, 128),
            shaped(8, 256),
            shaped(8, LIST, dtype=jnp.int32),
            shaped(16, 128),
            shaped(16, 128, dtype=jnp.int32),
        ),
        in_specs=[anywhere(), vmem(), anywhere(), vmem(), vmem(), vmem()],
        out_specs=[vmem()] * 2 + [anywhere()] * 3 + [vmem()] * 5,
        scratch_shapes=[
            pltpu.VMEM((R, LD * P_SIZE), BF16),
            pltpu.VMEM((LD, K, P_SIZE), BF16),
            pltpu.VMEM((LD, R, 128), BF16),
            pltpu.VMEM((LD, R, 128), BF16),
            pltpu.VMEM((PAIRS - 1, R, 128), F32),
            pltpu.VMEM((PAIRS, R, 128), F32),
            pltpu.VMEM((3, LD, 128), F32),
            pltpu.VMEM((256, 128), F32),
            pltpu.VMEM((8, 512), F32),
            pltpu.SemaphoreType.DMA((2 * CHUNKS + 3,)),
        ],
        compiler_params=PARAMS,
    )(charges, points, basis, transfer, near_rows, coupling_rows)

    roots = lax.all_to_all(root, AXES, 0, 0, tiled=True)
    forward = [(i, i + 1) for i in range(devices - 1)]
    backward = [(i + 1, i) for i in range(devices - 1)]
    from_prev = lax.ppermute(send_next, AXES, forward)
    from_next = lax.ppermute(send_prev, AXES, backward)

    near, couple = pl.pallas_call(
        near_kernel,
        name="near_field",
        out_shape=(shaped(R, LD * P_SIZE), shaped(PAIRS - 1, R, 128)),
        in_specs=[smem(), smem(), anywhere(), vmem(), anywhere()],
        out_specs=[vmem()] * 2,
        scratch_shapes=[
            pltpu.VMEM((R, LD * P_SIZE), BF16),
            pltpu.VMEM((PAIRS - 1, R, 128), F32),
            pltpu.SemaphoreType.DMA((2,)),
            pltpu.VMEM((8, 8, 512), F32),
            pltpu.VMEM((PAIRS, P_SIZE, 2 * FEATS), BF16),
            pltpu.VMEM((2 * LD, FEATS, P_SIZE), BF16),
            pltpu.VMEM((BATCH // 2, 128, 256), BF16),
            pltpu.VMEM((BATCH // 2, 128, 256), BF16),
        ],
        compiler_params=PARAMS,
        cost_estimate=pl.CostEstimate(
            flops=2 * 460 * 128 * 128 * 128, bytes_accessed=4 << 20, transcendentals=460 * 32768
        ),
    )(tasks, shapes, charges, points, lev)

    near, from_prev, from_next = lax.optimization_barrier((near, from_prev, from_next))
    stages = [
        pltpu.VMEM((UNIT, 512, 256), BF16),
        pltpu.VMEM((UNIT, 4 * R, 512), BF16),
    ]
    leaf_couple = pl.pallas_call(
        couple_kernel,
        name="leaf_couple",
        out_shape=shaped(PAIRS + 2 * UNIT, R, 128),
        in_specs=[smem()] * 2 + [anywhere()] * 4,
        out_specs=vmem(),
        scratch_shapes=[
            pltpu.VMEM((SEND, R, 128), BF16),
            pltpu.VMEM((SEND, R, 128), BF16),
            pltpu.VMEM((2 * LD, 8, 128), F32),
            pltpu.VMEM((TABLE, R, 128), BF16),
            pltpu.VMEM((TABLE, R, 128), BF16),
            pltpu.VMEM((2, 8, 128), F32),
            pltpu.SMEM((2, 8, 128), F32),
        ]
        + stages
        + stages
        + [pltpu.SemaphoreType.DMA((4,)), pltpu.SemaphoreType.DMA((2,))],
        compiler_params=PARAMS,
        cost_estimate=pl.CostEstimate(
            flops=2 * 1024 * 64 * 64 * 32 * 3, bytes_accessed=6 << 20, transcendentals=1024 * 8192
        ),
    )(entries, shapes, from_prev, from_next, high, low)

    leaf_couple, roots = lax.optimization_barrier((leaf_couple, roots))
    return pl.pallas_call(
        final_kernel,
        name="tree_finish",
        out_shape=shaped(R, LD * P_SIZE),
        in_specs=[smem()] + [anywhere()] * 9,
        out_specs=vmem(),
        scratch_shapes=[
            pltpu.VMEM((2, K, K), F32),
            pltpu.VMEM((devices, R // 2 + 8, 128), F32),
            pltpu.VMEM((PAIRS - 1, R, 128), F32),
            pltpu.VMEM((LD, K, P_SIZE), BF16),
            pltpu.VMEM((PAIRS + 2 * UNIT, R, 128), F32),
            pltpu.VMEM((SEND, R, 128), BF16),
            pltpu.VMEM((SEND, R, 128), BF16),
            pltpu.VMEM((3, LD * P_SIZE), F32),
            pltpu.VMEM((PAIRS, R, 128), F32),
            pltpu.VMEM((devices, R, 128), F32),
            pltpu.VMEM((2 * devices, 128), F32),
            pltpu.VMEM((2, 8, 512), F32),
            pltpu.VMEM((2, R, 128), F32),
            pltpu.VMEM((8, R, 128), F32),
            pltpu.SemaphoreType.DMA((9,)),
        ],
        compiler_params=PARAMS,
    )(counts, transfer, roots, couple, basis, leaf_couple, near, from_prev, from_next, points)


def solution(mesh):
    in_specs = (
        P(None, AXES),
        P(None, AXES),
        P(AXES, None, None),
        P(),
        P(AXES, None),
        P(AXES, None),
    )
    return jax.shard_map(
        per_device, mesh=mesh, in_specs=in_specs, out_specs=P(None, AXES), check_vma=False
    )
```

```python
import functools
import math

import jax
import jax.numpy as jnp
from jax import lax
from jax.experimental import pallas as pl
from jax.experimental.pallas import tpu as pltpu
from jax.sharding import PartitionSpec as P

P_SIZE = 128
K = 64
R = 32
LD = 128
PAIRS = LD // 2
GROUPS = LD // 4
TABLE = 257
HALF = LD // 2
NEAR_REACH = 8
FEATS = 64
BATCH = 16
SIBLINGS = 4
LIST = 896
SEND = 72
SCALE = 0.5 * math.log2(math.e)
NODE = [math.cos((2 * a + 1) * math.pi / 8) for a in range(4)]
AXES = ("leaf", "sub")
F32 = jnp.float32
BF16 = jnp.bfloat16
NT = (((1,), (1,)), ((), ()))
TINY = 1e-30
VMEM_LIMIT = 64 * 1024 * 1024


def lanes(shape):
    return lax.broadcasted_iota(jnp.int32, shape, len(shape) - 1)


def rows(shape):
    return lax.broadcasted_iota(jnp.int32, shape, len(shape) - 2)


def dot(a, b):
    return jnp.dot(a, b, preferred_element_type=F32)


def dot_nt(a, b):
    return lax.dot_general(a, b, NT, preferred_element_type=F32)


def halves(value):
    high = value.astype(BF16)
    return high, (value - high.astype(F32)).astype(BF16)


def thirds(value):
    first = value.astype(BF16).astype(F32)
    rest = value - first
    second = rest.astype(BF16).astype(F32)
    return first, second, rest - second


def unit_node(index):
    return jnp.where(
        index == 0,
        NODE[0],
        jnp.where(index == 1, NODE[1], jnp.where(index == 2, NODE[2], NODE[3])),
    ).astype(F32)


def lane_nodes():
    b = lanes((8, 128)) & 63
    return [unit_node(b >> 4), unit_node((b >> 2) & 3), unit_node(b & 3)]


def row_nodes():
    r = rows((8, 128))
    return [unit_node(r >> 2), unit_node((r >> 2) + 2)], unit_node(r & 3)


def decay(t):
    return decay_positive(jnp.maximum(t, TINY))


def decay_positive(t):
    return jnp.exp2(-(t * lax.rsqrt(t)))


def tile_from_axes(x_sq, y_sq, z_sq):
    z_sq = z_sq + TINY
    yz = [y_sq[0] + z_sq, y_sq[1] + z_sq]
    return decay_positive(jnp.concatenate([x_sq[k // 2] + yz[k % 2] for k in range(8)], axis=0))


def doubled_transfer(t_ref):
    flat = t_ref[...].reshape(2 * K, K)
    return jnp.concatenate([flat, flat], axis=1)


def device_index():
    return lax.axis_index("leaf") * lax.axis_size("sub") + lax.axis_index("sub")


def merge_up(pairs, t_high, t_low):
    n = pairs.shape[0]
    high, low = halves(pairs.reshape(n * R, 128))
    out = dot(high, jnp.concatenate([t_high, t_low], axis=1))
    out = out[:, 0:128] + out[:, 128:256] + dot(low, t_high)
    return out.reshape(n, R, 128)


def pair_lanes(clusters):
    n = clusters.shape[0]
    split = clusters.reshape(n // 2, 2, R, 128)
    return jnp.where(lanes((1, R, 128)) < K, split[:, 0], split[:, 1])


def down_weights(doubled):
    low = lanes(doubled.shape) < K
    both = jnp.concatenate(
        [jnp.where(low, doubled, 0.0), jnp.where(low, 0.0, doubled)], axis=0
    )
    return halves(both)


def push_down(value, w_high, w_low):
    n = value.shape[0]
    high, low = halves(value.reshape(n * R, 128))
    out = dot_nt(high, w_high) + dot_nt(high, w_low) + dot_nt(low, w_high)
    out = out.reshape(n, R, 256)
    return jnp.stack([out[:, :, 0:128], out[:, :, 128:256]], axis=1).reshape(2 * n, R, 128)


def merge_shape_rows(left, right):
    lane = lanes(left.shape)
    sep = left - right
    gap = jnp.sqrt(jnp.sum(jnp.where(lane < 3, sep * sep, 0.0), axis=1, keepdims=True))
    radius = jnp.maximum(left, right) + 0.5 * gap
    return jnp.where(lane == 3, radius, jnp.where(lane < 3, 0.5 * (left + right), 0.0))


def sibling_tile(left, right, lane_u, row_y, row_z):
    low = lanes((8, 128)) < K
    alpha = jnp.where(low, left[3], right[3])
    beta = jnp.where(low, right[3], left[3])
    base = [jnp.where(low, left[d] - right[d], right[d] - left[d]) - beta * lane_u[d] for d in range(3)]
    x_sq = [jnp.square(base[0] + alpha * NODE[a]) for a in range(4)]
    y_sq = [jnp.square(base[1] + alpha * row_y[h]) for h in range(2)]
    z_sq = jnp.square(base[2] + alpha * row_z)
    return tile_from_axes(x_sq, y_sq, z_sq)


def sibling_apply(tile, pair):
    low = lanes((K, 128)) < K
    zero = jnp.zeros((K, 128), BF16)
    weights = []
    for part in halves(tile):
        weights.append(
            jnp.concatenate([jnp.where(low, part, zero), jnp.where(low, zero, part)], axis=0)
        )
    high, low_part = halves(pltpu.roll(pair, K, 1))
    out = dot_nt(high, jnp.concatenate(weights, axis=0))
    return out[:, 0:128] + out[:, 128:256] + dot_nt(low_part, weights[0])


LEVEL_OFFSETS = [0, 128, 192, 224, 240, 248, 252, 254]
PAIR_OFFSETS = [0, 0, 32, 48, 56, 60, 62]


def block_diagonal(left, right):
    zero = jnp.zeros(left.shape, left.dtype)
    return jnp.concatenate(
        [jnp.concatenate([left, zero], axis=1), jnp.concatenate([zero, right], axis=1)], axis=0
    )


def make_lists(near_ref, coupling_ref, list_ref, count_ref, index_ref):
    first_leaf = device_index() * LD
    lane8 = lanes((8, 128))
    row8 = rows((8, 128))
    offset = jnp.where(near_ref[...] >= 0, near_ref[...] - first_leaf - lane8, 1000)

    def slots_at(delta):
        return jnp.sum(jnp.where(offset == delta, 1.0, 0.0), axis=0, keepdims=True)

    forward = jnp.concatenate([slots_at(delta) for delta in range(8)], axis=0)
    reverse = jnp.concatenate(
        [jnp.zeros((1, 128), F32)] + [slots_at(-delta) for delta in range(1, 8)], axis=0
    )
    count_ref[0:8, :] = forward
    count_ref[8:16, :] = reverse
    backward = jnp.concatenate(
        [jnp.zeros((1, 128), F32)]
        + [pltpu.roll(reverse[delta : delta + 1, :], 128 - delta, 1) for delta in range(1, 8)],
        axis=0,
    )
    turned = (row8 == 1) & ((lane8 & 3) == 2)
    leaf = lane8.astype(F32)
    other = leaf + row8.astype(F32)
    first = jnp.where(turned, other, leaf)
    second = jnp.where(turned, leaf, other)
    to_first = jnp.where(turned, backward, forward)
    to_second = jnp.where(turned, forward, backward)
    odd = jnp.where(turned, lane8, lane8 + row8) & 1
    wanted = (lane8 + row8 < LD) & (forward + backward > 0.0)
    earlier = jnp.where(rows((128, 128)) < lanes((128, 128)), 1.0, 0.0).astype(BF16)
    place = jnp.full((8, 128), -1.0, F32)
    most = jnp.zeros((1, 1), F32)
    for parity in range(2):
        flags = jnp.where(wanted & (odd == parity), 1.0, 0.0)
        rank = dot(flags.astype(BF16), earlier)
        totals = jnp.sum(flags, axis=1, keepdims=True)
        before = jnp.zeros((1, 1), F32)
        starts = []
        for delta in range(8):
            starts.append(before)
            before = before + totals[delta : delta + 1, :]
        rank = rank + jnp.concatenate(starts, axis=0)
        place = jnp.where(flags > 0.0, 2.0 * rank + (1.0 * BATCH + parity), place)
        most = jnp.maximum(most, before)
    task_rows = []
    for delta in range(8):
        pick = slice(delta, delta + 1)
        task_rows.append(
            jnp.where(
                row8 == 0,
                first[pick],
                jnp.where(
                    row8 == 1,
                    second[pick],
                    jnp.where(
                        row8 == 2, to_first[pick], jnp.where(row8 == 3, to_second[pick], 0.0)
                    ),
                ),
            ).astype(BF16)
        )
    tasks = jnp.concatenate(task_rows, axis=1)
    slot_row = rows((128, 128)).astype(F32)
    for m in range(LIST // 128):
        chosen = jnp.concatenate(
            [
                jnp.where(place[delta : delta + 1, :] == slot_row + 128.0 * m, 1.0, 0.0).astype(BF16)
                for delta in range(8)
            ],
            axis=1,
        )
        part = dot_nt(tasks, chosen)
        part = jnp.where(row8 == 4, 2.0 * most, part)
        list_ref[:, m * 128 : (m + 1) * 128] = part.astype(jnp.int32)

    target = coupling_ref[...]
    reach = target - first_leaf + HALF
    swap = ((reach ^ row8) & 1) * (PAIRS // 2)
    entry = jnp.where(
        reach < HALF,
        LD + (reach >> 1) + swap,
        jnp.where(reach < HALF + LD, reach - HALF, LD + HALF + ((reach - HALF - LD) >> 1) + swap),
    )
    index_ref[0:8, :] = jnp.where(target >= 0, entry, TABLE - 1)
    index_ref[8:16, :] = jnp.where(target >= 0, reach, 0)


CHUNKS = 4


def leaf_kernel(
    x_any, p_ref, b_any, t_ref, near_ref, coupling_ref,
    next_any, prev_any, high_any, low_any, lev_any, root_ref, shape_ref,
    list_ref, count_ref, index_ref,
    send_next, send_prev, x_ref, b_ref, high_ref, low_ref, lev_ref, coef, pts, shapes, p8, sems,
):
    leaves = LD // CHUNKS
    copies = []
    for c in range(CHUNKS):
        span = slice(c * leaves * P_SIZE, (c + 1) * leaves * P_SIZE)
        part = slice(c * leaves, (c + 1) * leaves)
        copies.append(
            (
                pltpu.make_async_copy(x_any.at[:, span], x_ref.at[:, span], sems.at[c]),
                pltpu.make_async_copy(b_any.at[part], b_ref.at[part], sems.at[CHUNKS + c]),
            )
        )
    for pair in copies:
        for copy in pair:
            copy.start()
    origin = (device_index() * GROUPS).astype(F32)
    low32 = lanes((R, 128)) < K

    make_lists(near_ref, coupling_ref, list_ref, count_ref, index_ref)
    def leaf_pairs(m, carry):
        values = []
        for v in range(32):
            leaf = 32 * m + v
            x = x_ref[:, pl.ds(pl.multiple_of(leaf * P_SIZE, P_SIZE), P_SIZE)]
            weights = b_ref[leaf]
            values.append(dot_nt(x, jnp.concatenate([weights, weights], axis=0)))
        for v in range(32):
            high_ref[32 * m + v], low_ref[32 * m + v] = halves(values[v])
        for v in range(16):
            coef[16 * m + v] = jnp.where(low32, values[2 * v], values[2 * v + 1])
        return carry

    for c in range(CHUNKS):
        for copy in copies[c]:
            copy.wait()
        steps = leaves // 32
        lax.fori_loop(c * steps, (c + 1) * steps, leaf_pairs, 0)
    leaving = [
        pltpu.make_async_copy(high_ref, high_any, sems.at[2 * CHUNKS]),
        pltpu.make_async_copy(low_ref, low_any, sems.at[2 * CHUNKS + 1]),
    ]
    for copy in leaving:
        copy.start()

    for i in range(LD):
        for d in range(3):
            pts[d, i : i + 1, :] = p_ref[d : d + 1, i * P_SIZE : (i + 1) * P_SIZE]
    centers, squares = [], 0.0
    for d in range(3):
        coords = (pts[d] - origin if d == 2 else pts[d]) * SCALE
        center = jnp.sum(coords, axis=1, keepdims=True) * (1.0 / P_SIZE)
        centers.append(center)
        squares = squares + jnp.square(coords - center)
    radius = jnp.sqrt(jnp.max(squares, axis=1, keepdims=True))
    lane = lanes((LD, 128))
    shapes[0:LD, :] = jnp.where(
        lane == 0,
        centers[0],
        jnp.where(
            lane == 1,
            centers[1],
            jnp.where(lane == 2, centers[2], jnp.where(lane == 3, radius, 0.0)),
        ),
    )
    count = LD // 2
    for level in range(1, 8):
        source = LEVEL_OFFSETS[level - 1]
        joined = merge_shape_rows(
            shapes[pl.ds(source, count, stride=2), :],
            shapes[pl.ds(source + 1, count, stride=2), :],
        )
        shapes[pl.ds(LEVEL_OFFSETS[level], count), :] = joined
        count //= 2
    shape_rows = jnp.concatenate(
        [jnp.transpose(shapes[0:128, :])[0:8], jnp.transpose(shapes[128:256, :])[0:8]], axis=1
    )
    shape_ref[...] = shape_rows
    p8[...] = jnp.zeros((8, 512), F32)
    for send, first_pair, group in ((send_next, PAIRS // 2, GROUPS - 1), (send_prev, 0, 0)):

        def copy_pairs(m, carry):
            parts = [halves(coef[first_pair + 8 * m + v]) for v in range(8)]
            for v in range(8):
                send[8 * m + v], send[32 + 8 * m + v] = parts[v]
            return carry

        lax.fori_loop(0, PAIRS // 16, copy_pairs, 0)
        parts = thirds(shape_rows[:, 0:128])
        send[68] = jnp.concatenate(list(parts) + [jnp.zeros((8, 128), F32)], axis=0).astype(BF16)
        p8[0:3, :] = p_ref[:, group * 512 : group * 512 + 512]
        parts = thirds(p8[...])
        for k in range(4):
            send[64 + k] = x_ref[:, group * 512 + k * P_SIZE : group * 512 + (k + 1) * P_SIZE]
        for part in range(3):
            send[69 + part] = jnp.concatenate(
                [parts[part][:, k * P_SIZE : (k + 1) * P_SIZE] for k in range(4)], axis=0
            ).astype(BF16)
    for k, (send, out) in enumerate(((send_next, next_any), (send_prev, prev_any))):
        leaving.append(pltpu.make_async_copy(send, out, sems.at[2 * CHUNKS + 3 + k]))
        leaving[-1].start()

    t_high, t_low = halves(doubled_transfer(t_ref))
    pairs = coef[...]
    for level in range(1, 7):
        pairs = pair_lanes(merge_up(pairs, t_high, t_low))
        lev_ref[pl.ds(PAIR_OFFSETS[level], pairs.shape[0])] = pairs
    leaving.append(pltpu.make_async_copy(lev_ref, lev_any, sems.at[2 * CHUNKS + 2]))
    leaving[-1].start()
    root = merge_up(pairs, t_high, t_low)[0]

    low = lanes((R // 2, 128)) < K
    block = jnp.concatenate(
        [
            jnp.where(low, root[0 : R // 2], root[R // 2 : R]),
            jnp.broadcast_to(shapes[254:255, :], (8, 128)),
        ],
        axis=0,
    )
    root_ref[...] = jnp.broadcast_to(block[None], root_ref.shape)

    for copy in leaving:
        copy.wait()


def point_features(points8, origin_z):
    row = rows(points8.shape)
    center = jnp.where(row == 2, origin_z + 0.5, 1.0)
    v = jnp.where(row < 3, (points8 - center) * SCALE, 0.0)
    norm = jnp.sum(v * v, axis=0, keepdims=True)
    far = jnp.where(row == 3, norm, jnp.where(row == 4, 1.0, v))
    own = jnp.where(row == 3, 1.0, jnp.where(row == 4, norm, -2.0 * v))
    return far, own


def far_stack(value):
    first, second, third = thirds(value)
    none = jnp.zeros(value.shape, F32)
    return jnp.concatenate(
        [first, first, first, second, second, third, none, none], axis=0
    ).astype(BF16)


def own_stack(value):
    first, second, third = thirds(value)
    none = jnp.zeros(value.shape, F32)
    return jnp.concatenate(
        [first, second, third, first, second, first, none, none], axis=0
    ).astype(BF16)


def identity():
    return jnp.where(rows((128, 128)) == lanes((128, 128)), 1.0, 0.0).astype(BF16)


def near_kernel(
    list_ref, shape_ref, x_any, p_ref, lev_any,
    out_ref, couple_ref,
    x_ref, lev_ref, sems, p8, far_feat, own_feat, tile0, tile1,
):
    copies = [
        pltpu.make_async_copy(x_any, x_ref, sems.at[0]),
        pltpu.make_async_copy(lev_any, lev_ref, sems.at[1]),
    ]
    for copy in copies:
        copy.start()
    first_group = device_index() * GROUPS
    p8[...] = jnp.zeros(p8.shape, F32)
    eye = identity()

    def features(m, carry):
        loaded = [p_ref[:, pl.ds(pl.multiple_of((16 * m + v) * 512, 512), 512)] for v in range(16)]
        for v in range(16):
            p8[v, 0:3, :] = loaded[v]
        made = []
        for v in range(16):
            coords = p8[v]
            origin_z = (first_group + 16 * m + v).astype(F32)
            far, own = point_features(coords, origin_z)
            _, own_up = point_features(coords, origin_z + 1.0)
            far = far_stack(far)
            parts = [far[:, k * P_SIZE : (k + 1) * P_SIZE] for k in range(4)]
            turned = dot_nt(eye, jnp.concatenate(parts, axis=0)).astype(BF16)
            made.append((turned, own_stack(own), own_stack(own_up)))
        for v in range(16):
            g = 16 * m + v
            turned, own, own_up = made[v]
            far_feat[2 * g] = turned[:, 0:128]
            far_feat[2 * g + 1] = turned[:, 128:256]
            for k in range(4):
                part = slice(k * P_SIZE, (k + 1) * P_SIZE)
                own_feat[4 * g + k] = own[:, part]
                own_feat[LD + 4 * g + k] = own_up[:, part]
        return carry

    lax.fori_loop(0, GROUPS // 16, features, 0)

    for copy in copies:
        copy.wait()
    out_ref[...] = x_ref[...].astype(F32)
    for ref in (tile0, tile1):
        ref[...] = jnp.zeros(ref.shape, ref.dtype)

    total = list_ref[4, 0]
    steps = (total + BATCH - 1) // BATCH + 1
    low = lanes((128, 128)) < K

    def leaf_slice(i):
        return pl.ds(pl.multiple_of(i * P_SIZE, P_SIZE), P_SIZE)

    lane_u = lane_nodes()
    row_y, row_z = row_nodes()

    def phase(n, tile_new, tile_old, pairs):
        far, own, sources, updates = [], [], [], []
        siblings = [jnp.minimum(pairs * n + v, PAIRS - 2) for v in range(pairs)]
        levels = [lev_ref[pair] for pair in siblings]
        for u in range(BATCH):
            k = (n + 1) * BATCH + u
            i, j = list_ref[0, k], list_ref[1, k]
            variant = ((j >> 2) - (i >> 2)) * LD
            far.append(far_feat[j >> 1])
            own.append(own_feat[variant + i])
        for u in range(BATCH):
            k = n * BATCH + u
            i, j = list_ref[0, k], list_ref[1, k]
            sources.append((x_ref[:, leaf_slice(j)], x_ref[:, leaf_slice(i)]))
        tiles = []
        for u in range(BATCH // 2):
            pick = jnp.where(low, far[2 * u], far[2 * u + 1])
            dist = dot(pick, block_diagonal(own[2 * u], own[2 * u + 1]))
            tiles.append(decay(dist).astype(BF16))
            weights = block_diagonal(tile_old[u, :, 0:128], tile_old[u, :, 128:256])
            to_i = dot(jnp.concatenate([sources[2 * u][0], sources[2 * u + 1][0]], axis=1), weights)
            to_j = dot_nt(jnp.concatenate([sources[2 * u][1], sources[2 * u + 1][1]], axis=1), weights)
            for h in range(2):
                k = n * BATCH + 2 * u + h
                span = slice(h * 128, (h + 1) * 128)
                updates.append(
                    (
                        to_i[:, span] * list_ref[2, k].astype(F32),
                        to_j[:, span] * list_ref[3, k].astype(F32),
                    )
                )
        for pair, level in zip(siblings, levels):
            cluster = LD + 2 * pair
            left = [shape_ref[d, cluster] for d in range(4)]
            right = [shape_ref[d, cluster + 1] for d in range(4)]
            couple_ref[pair] = sibling_apply(
                sibling_tile(left, right, lane_u, row_y, row_z), level
            )
        for u in range(BATCH // 2):
            tile_new[u] = tiles[u]
        for u in range(BATCH):
            k = n * BATCH + u
            to_i = leaf_slice(list_ref[0, k])
            to_j = leaf_slice(list_ref[1, k])
            out_ref[:, to_i] += updates[u][0]
            out_ref[:, to_j] += updates[u][1]

    def two_phases(pairs, m, carry):
        phase(2 * m, tile0, tile1, pairs)
        phase(2 * m + 1, tile1, tile0, pairs)
        return carry

    rides = PAIRS // (2 * SIBLINGS)
    lax.fori_loop(0, rides, functools.partial(two_phases, SIBLINGS), 0)
    lax.fori_loop(rides, (steps + 1) // 2, functools.partial(two_phases, 0), 0)


def tree_down(t_ref, root_ref, down_ref, couple, pairs_scr, shapes):
    lane_u = lane_nodes()
    row_y, row_z = row_nodes()

    doubled = doubled_transfer(t_ref)
    t_high, t_low = halves(doubled)
    w_high, w_low = down_weights(doubled)
    device = device_index()
    n = root_ref.shape[0]
    low = lanes((R, 128)) < K
    shift = lanes((1, 128)) == 2
    for k in range(n):
        shapes[k : k + 1, :] = root_ref[k, R // 2 : R // 2 + 1, :] + jnp.where(
            shift, (k * GROUPS) * SCALE, 0.0
        )
    for k in range(n // 2):
        left = root_ref[2 * k, 0 : R // 2, :]
        right = root_ref[2 * k + 1, 0 : R // 2, :]
        left = jnp.concatenate([left, pltpu.roll(left, K, 1)], axis=0)
        right = jnp.concatenate([pltpu.roll(right, K, 1), right], axis=0)
        pairs_scr[k] = jnp.where(low, left, right)
    source, count, pair_source = 0, n // 2, 0
    levels = []
    while count >= 1:
        levels.append((source, pair_source))
        if count > 1:
            pairs = pair_lanes(merge_up(pairs_scr[pl.ds(pair_source, count)], t_high, t_low))
            pairs_scr[pl.ds(pair_source + count, count // 2)] = pairs
            joined = merge_shape_rows(
                shapes[pl.ds(source, count, stride=2), :],
                shapes[pl.ds(source + 1, count, stride=2), :],
            )
            shapes[pl.ds(source + 2 * count, count), :] = joined
        source += 2 * count
        pair_source += count
        count //= 2
    couples = []
    for level, (source, pair_source) in enumerate(levels):
        pair = device >> (level + 1)
        left_row = shapes[pl.ds(source + 2 * pair, 1), :]
        right_row = shapes[pl.ds(source + 2 * pair + 1, 1), :]
        left = [jnp.broadcast_to(left_row[:, d : d + 1], (8, 128)) for d in range(4)]
        right = [jnp.broadcast_to(right_row[:, d : d + 1], (8, 128)) for d in range(4)]
        tile = sibling_tile(left, right, lane_u, row_y, row_z)
        couples.append(sibling_apply(tile, pairs_scr[pair_source + pair]))
    incoming = None
    for level in reversed(range(len(levels))):
        value = couples[level]
        if incoming is not None:
            pushed = push_down(incoming[None], w_high, w_low)
            value = value + (pushed[0] + pushed[1])
        side = (device >> level) & 1
        keep_low = jnp.where(low, 1, 0) == (1 - side)
        incoming = jnp.where(keep_low, value, 0.0)
    pushed = push_down(incoming[None], w_high, w_low)
    value = couple[pl.ds(PAIR_OFFSETS[6], 1)] + (pushed[0:1] + pushed[1:2])
    for level in range(5, 0, -1):
        n = PAIRS >> level
        value = couple[pl.ds(PAIR_OFFSETS[level], n)] + push_down(value, w_high, w_low)
    down_ref[...] = push_down(value, w_high, w_low)


UNIT = 8


def couple_leaves(
    entries, shape_ref, prev_ref, next_ref, table_copies, leaf_couple,
    shape_tab, high_tab, low_tab, halo_rows, halo_shape, sems,
    tiles0, lhs0, tiles1, lhs1,
):
    copies = []
    for k, ref in enumerate((prev_ref, next_ref)):
        parts = ref[68].astype(F32)
        halo_rows[k] = parts[0:8] + parts[8:16] + parts[16:24]
        copies.append(pltpu.make_async_copy(halo_rows.at[k], halo_shape.at[k], sems.at[k]))
    for copy in copies:
        copy.start()
    low32 = lanes((R, 128)) < K
    lane_u = lane_nodes()
    row8 = rows((8, 128))
    low8 = lanes((8, 128)) < K

    def shape_rows(read, k, shift):
        return jnp.where(
            row8 == 0,
            read(0, k),
            jnp.where(row8 == 1, read(1, k), jnp.where(row8 == 2, read(2, k) + shift, read(3, k))),
        )

    def own_nodes(m, carry):
        shape_tab[HALF + m] = shape_rows(lambda d, k: shape_ref[d, k], m, 0.0)
        return carry

    lax.fori_loop(0, LD, own_nodes, 0, unroll=8)
    for copy in copies:
        copy.wait()
    def halo_pairs(m, carry):
        loaded = [
            (tab, LD + side * HALF + 4 * m + v, ref[offset + 4 * m + v])
            for side, ref in enumerate((prev_ref, next_ref))
            for tab, offset in ((high_tab, 0), (low_tab, 32))
            for v in range(4)
        ]
        turned = [pltpu.roll(pair.astype(F32), K, 1).astype(BF16) for _, _, pair in loaded]
        for side in range(2):
            source = HALF if side == 0 else 0
            place = 0 if side == 0 else HALF + LD
            shift = (2.0 * side - 1.0) * GROUPS * SCALE
            for v in range(8):
                shape_tab[place + 8 * m + v] = shape_rows(
                    lambda d, k: halo_shape[side, d, k], source + 8 * m + v, shift
                )
        for (tab, pair, value), other in zip(loaded, turned):
            tab[pair] = value
            tab[PAIRS // 2 + pair] = other
        return carry

    lax.fori_loop(0, PAIRS // 8, halo_pairs, 0)
    high_tab[TABLE - 1] = jnp.zeros((R, 128), BF16)
    low_tab[TABLE - 1] = jnp.zeros((R, 128), BF16)
    for copy in table_copies:
        copy.wait()

    row_y, row_z = row_nodes()

    def couple_tiles(pair, u, tiles, lhs):
        leaves = (2 * pair, 2 * pair + 1)
        for q in range(4):
            span = slice(q * 128, (q + 1) * 128)
            for h in range(2):
                e0, e1 = entries[2 * q, leaves[h]], entries[2 * q + 1, leaves[h]]
                lhs[u, h * R : (h + 1) * R, span] = jnp.where(low32, high_tab[e0], high_tab[e1])
                lhs[u, (2 + h) * R : (3 + h) * R, span] = jnp.where(
                    low32, low_tab[e0], low_tab[e1]
                )
        own = jnp.where(low8, shape_tab[HALF + leaves[0]], shape_tab[HALF + leaves[1]])
        radius = jnp.broadcast_to(own[3:4], (8, 128))
        own = [jnp.broadcast_to(own[d : d + 1], (8, 128)) + radius * lane_u[d] for d in range(3)]
        fars = []
        for s in range(8):
            e0, e1 = entries[8 + s, leaves[0]], entries[8 + s, leaves[1]]
            fars.append(jnp.where(low8, shape_tab[e0], shape_tab[e1]))
        for s, far in enumerate(fars):
            reach = jnp.broadcast_to(far[3:4], (8, 128))
            gap = [own[d] - jnp.broadcast_to(far[d : d + 1], (8, 128)) for d in range(3)]
            tile = tile_from_axes(
                [jnp.square(gap[0] - reach * NODE[b]) for b in range(4)],
                [jnp.square(gap[1] - reach * row_y[h]) for h in range(2)],
                jnp.square(gap[2] - reach * row_z),
            )
            high, low = halves(tile)
            tiles[u, s * K : (s + 1) * K, 0:128] = high
            tiles[u, s * K : (s + 1) * K, 128:256] = low

    def couple_apply(u, tiles, lhs):
        both = dot(lhs[u], tiles[u])
        both = both[0 : 2 * R, 0:128] + (both[2 * R : 4 * R, 0:128] + both[0 : 2 * R, 128:256])
        return jnp.where(low32, both[0:R], both[R : 2 * R])

    def couple_phase(n, new, old):
        for u in range(UNIT):
            couple_tiles(n * UNIT + u, u, *new)
            leaf_couple[n * UNIT + u] = couple_apply(u, *old)

    buffers = ((tiles0, lhs0), (tiles1, lhs1))
    for ref in buffers[1]:
        ref[...] = jnp.zeros(ref.shape, ref.dtype)

    def couple_two(m, carry):
        couple_phase(2 * m, buffers[0], buffers[1])
        couple_phase(2 * m + 1, buffers[1], buffers[0])
        return carry

    lax.fori_loop(0, PAIRS // UNIT // 2, couple_two, 0)
    for u in range(UNIT):
        leaf_couple[PAIRS + u] = couple_apply(u, *buffers[1])


def finish_leaves(b_ref, down_ref, leaf_couple, out_ref, border):
    def finish(m, carry):
        values = []
        for v in range(16):
            c = 16 * m + v
            value = (down_ref[c] + leaf_couple[c + UNIT]).astype(BF16)
            span = pl.ds(pl.multiple_of(c * 256, 256), 256)
            values.append(
                (
                    span,
                    out_ref[:, span]
                    + dot(value, block_diagonal(b_ref[2 * c], b_ref[2 * c + 1])),
                )
            )
        for span, value in values:
            out_ref[:, span] = value
        return carry

    lax.fori_loop(0, PAIRS // 16, finish, 0)
    for side, group in enumerate((0, GROUPS - 1)):
        for i in range(4):
            leaf = 4 * group + i
            out_ref[:, leaf * P_SIZE : (leaf + 1) * P_SIZE] += border[4 * side + i]


def border_blocks(counts, p_ref, prev_ref, next_ref, border, p8, coords):
    device = device_index()

    p8[...] = jnp.zeros(p8.shape, F32)
    eye = identity()
    sides = ((prev_ref, 0), (next_ref, GROUPS - 1))
    for side, (halo_ref, group) in enumerate(sides):
        p8[side, 0:3, :] = p_ref[:, group * 512 : group * 512 + 512]
        coords[side] = halo_ref[69].astype(F32) + halo_ref[70].astype(F32) + halo_ref[71].astype(F32)

    sums = [[0.0] * 4, [0.0] * 4]
    for k in range(4):
        loaded = [
            (halo_ref[64 + k], coords[side, 8 * k : 8 * k + 8, :], p8[side])
            for side, (halo_ref, _) in enumerate(sides)
        ]
        for side, (_, group) in enumerate(sides):
            x_far, far, own = loaded[side]
            origin_z = (device * GROUPS + group).astype(F32)
            _, own = point_features(own, origin_z)
            far, _ = point_features(far, origin_z)
            far = dot_nt(eye, far_stack(far)).astype(BF16)
            tiles = decay(dot(far, own_stack(own))).astype(BF16)
            products = dot(x_far, tiles)
            for i in range(4):
                delta = (4 + i - k) if side == 0 else (4 + k - i)
                weight = counts[8 * (1 - side) + delta, 4 * group + i]
                sums[side][i] = sums[side][i] + products[:, i * P_SIZE : (i + 1) * P_SIZE] * weight
    for side in range(2):
        for i in range(4):
            border[4 * side + i] = sums[side][i]


def tree_kernel(
    t_any, root_any, couple_any, down_ref, t_ref, root_ref, couple, pairs_scr, shapes, sems
):
    moves = ((t_any, t_ref), (root_any, root_ref), (couple_any, couple))
    copies = [pltpu.make_async_copy(a, b, sems.at[k]) for k, (a, b) in enumerate(moves)]
    for copy in copies:
        copy.start()
    for copy in copies:
        copy.wait()
    tree_down(t_ref, root_ref, down_ref, couple, pairs_scr, shapes)


def final_kernel(
    entries, shape_ref, counts,
    prev_any, next_any, p_any, high_any, low_any, b_any, near_any, down_any,
    out_ref,
    prev_ref, next_ref, p_ref, b_ref, down, leaf_couple,
    shape_tab, high_tab, low_tab, halo_rows, halo_shape,
    tiles0, lhs0, tiles1, lhs1, p8, coords, border, sems, halo_sems,
):
    moves = (
        (prev_any, prev_ref),
        (next_any, next_ref),
        (p_any, p_ref),
        (high_any, high_tab.at[0:LD]),
        (low_any, low_tab.at[0:LD]),
        (b_any, b_ref),
        (near_any, out_ref),
        (down_any, down),
    )
    copies = [pltpu.make_async_copy(a, b, sems.at[k]) for k, (a, b) in enumerate(moves)]
    for copy in copies:
        copy.start()
    for copy in copies[0:3]:
        copy.wait()
    border_blocks(counts, p_ref, prev_ref, next_ref, border, p8, coords)
    couple_leaves(
        entries, shape_ref, prev_ref, next_ref, copies[3:5], leaf_couple,
        shape_tab, high_tab, low_tab, halo_rows, halo_shape, halo_sems,
        tiles0, lhs0, tiles1, lhs1,
    )
    for copy in copies[5:]:
        copy.wait()
    finish_leaves(b_ref, down, leaf_couple, out_ref, border)


def shaped(*shape, dtype=F32):
    return jax.ShapeDtypeStruct(shape, dtype)


def vmem():
    return pl.BlockSpec(memory_space=pltpu.VMEM)


def smem():
    return pl.BlockSpec(memory_space=pltpu.SMEM)


def anywhere():
    return pl.BlockSpec(memory_space=pl.ANY)


PARAMS = pltpu.CompilerParams(vmem_limit_bytes=VMEM_LIMIT)


def per_device(charges, points, basis, transfer, near_list, coupling_list):
    near_rows = near_list.T
    coupling_rows = coupling_list.T
    devices = lax.axis_size("sub") * lax.axis_size("leaf")
    send_next, send_prev, high, low, lev, root, shapes, tasks, counts, entries = pl.pallas_call(
        leaf_kernel,
        name="leaf_up",
        out_shape=(
            shaped(SEND, R, 128, dtype=BF16),
            shaped(SEND, R, 128, dtype=BF16),
            shaped(LD, R, 128, dtype=BF16),
            shaped(LD, R, 128, dtype=BF16),
            shaped(PAIRS - 1, R, 128),
            shaped(devices, R // 2 + 8, 128),
            shaped(8, 256),
            shaped(8, LIST, dtype=jnp.int32),
            shaped(16, 128),
            shaped(16, 128, dtype=jnp.int32),
        ),
        in_specs=[anywhere(), vmem(), anywhere(), vmem(), vmem(), vmem()],
        out_specs=[anywhere()] * 5 + [vmem()] * 5,
        scratch_shapes=[
            pltpu.VMEM((SEND, R, 128), BF16),
            pltpu.VMEM((SEND, R, 128), BF16),
            pltpu.VMEM((R, LD * P_SIZE), BF16),
            pltpu.VMEM((LD, K, P_SIZE), BF16),
            pltpu.VMEM((LD, R, 128), BF16),
            pltpu.VMEM((LD, R, 128), BF16),
            pltpu.VMEM((PAIRS - 1, R, 128), F32),
            pltpu.VMEM((PAIRS, R, 128), F32),
            pltpu.VMEM((3, LD, 128), F32),
            pltpu.VMEM((256, 128), F32),
            pltpu.VMEM((8, 512), F32),
            pltpu.SemaphoreType.DMA((2 * CHUNKS + 5,)),
        ],
        compiler_params=PARAMS,
    )(charges, points, basis, transfer, near_rows, coupling_rows)

    roots = lax.all_to_all(root, AXES, 0, 0, tiled=True)
    forward = [(i, i + 1) for i in range(devices - 1)]
    backward = [(i + 1, i) for i in range(devices - 1)]
    from_prev = lax.ppermute(send_next, AXES, forward)
    from_next = lax.ppermute(send_prev, AXES, backward)

    near, couple = pl.pallas_call(
        near_kernel,
        name="near_field",
        out_shape=(shaped(R, LD * P_SIZE), shaped(PAIRS - 1, R, 128)),
        in_specs=[smem(), smem(), anywhere(), vmem(), anywhere()],
        out_specs=[vmem()] * 2,
        scratch_shapes=[
            pltpu.VMEM((R, LD * P_SIZE), BF16),
            pltpu.VMEM((PAIRS - 1, R, 128), F32),
            pltpu.SemaphoreType.DMA((2,)),
            pltpu.VMEM((16, 8, 512), F32),
            pltpu.VMEM((PAIRS, P_SIZE, 2 * FEATS), BF16),
            pltpu.VMEM((2 * LD, FEATS, P_SIZE), BF16),
            pltpu.VMEM((BATCH // 2, 128, 256), BF16),
            pltpu.VMEM((BATCH // 2, 128, 256), BF16),
        ],
        compiler_params=PARAMS,
        cost_estimate=pl.CostEstimate(
            flops=2 * 460 * 128 * 128 * 128, bytes_accessed=4 << 20, transcendentals=460 * 32768
        ),
    )(tasks, shapes, charges, points, lev)

    near, roots = lax.optimization_barrier((near, roots))
    down = pl.pallas_call(
        tree_kernel,
        name="tree_down",
        out_shape=shaped(PAIRS, R, 128),
        in_specs=[anywhere()] * 3,
        out_specs=vmem(),
        scratch_shapes=[
            pltpu.VMEM((2, K, K), F32),
            pltpu.VMEM((devices, R // 2 + 8, 128), F32),
            pltpu.VMEM((PAIRS - 1, R, 128), F32),
            pltpu.VMEM((devices, R, 128), F32),
            pltpu.VMEM((2 * devices, 128), F32),
            pltpu.SemaphoreType.DMA((3,)),
        ],
        compiler_params=PARAMS,
    )(transfer, roots, couple)
    from_prev, from_next, down = lax.optimization_barrier((from_prev, from_next, down))

    stages = [
        pltpu.VMEM((UNIT, 512, 256), BF16),
        pltpu.VMEM((UNIT, 4 * R, 512), BF16),
    ]
    return pl.pallas_call(
        final_kernel,
        name="couple_finish",
        out_shape=shaped(R, LD * P_SIZE),
        in_specs=[smem()] * 3 + [anywhere()] * 8,
        out_specs=vmem(),
        scratch_shapes=[
            pltpu.VMEM((SEND, R, 128), BF16),
            pltpu.VMEM((SEND, R, 128), BF16),
            pltpu.VMEM((3, LD * P_SIZE), F32),
            pltpu.VMEM((LD, K, P_SIZE), BF16),
            pltpu.VMEM((PAIRS, R, 128), F32),
            pltpu.VMEM((PAIRS + UNIT, R, 128), F32),
            pltpu.VMEM((2 * LD, 8, 128), F32),
            pltpu.VMEM((TABLE, R, 128), BF16),
            pltpu.VMEM((TABLE, R, 128), BF16),
            pltpu.VMEM((2, 8, 128), F32),
            pltpu.SMEM((2, 8, 128), F32),
        ]
        + stages
        + stages
        + [
            pltpu.VMEM((2, 8, 512), F32),
            pltpu.VMEM((2, R, 128), F32),
            pltpu.VMEM((8, R, 128), F32),
            pltpu.SemaphoreType.DMA((8,)),
            pltpu.SemaphoreType.DMA((2,)),
        ],
        compiler_params=PARAMS,
    )(
        entries, shapes, counts,
        from_prev, from_next, points, high, low, basis, near, down,
    )


def solution(mesh):
    in_specs = (
        P(None, AXES),
        P(None, AXES),
        P(AXES, None, None),
        P(),
        P(AXES, None),
        P(AXES, None),
    )
    return jax.shard_map(
        per_device, mesh=mesh, in_specs=in_specs, out_specs=P(None, AXES), check_vma=False
    )
```

```python
import functools
import math

import jax
import jax.numpy as jnp
from jax import lax
from jax.experimental import pallas as pl
from jax.experimental.pallas import tpu as pltpu
from jax.sharding import PartitionSpec as P

P_SIZE = 128
K = 64
R = 32
LD = 128
PAIRS = LD // 2
GROUPS = LD // 4
TABLE = 257
HALF = LD // 2
NEAR_REACH = 8
FEATS = 64
BATCH = 16
SIBLINGS = 6
LIST = 1536
SEND = 72
SCALE = 0.5 * math.log2(math.e)
NODE = [math.cos((2 * a + 1) * math.pi / 8) for a in range(4)]
AXES = ("leaf", "sub")
F32 = jnp.float32
BF16 = jnp.bfloat16
NT = (((1,), (1,)), ((), ()))
TINY = 1e-30
VMEM_LIMIT = 64 * 1024 * 1024


def lanes(shape):
    return lax.broadcasted_iota(jnp.int32, shape, len(shape) - 1)


def rows(shape):
    return lax.broadcasted_iota(jnp.int32, shape, len(shape) - 2)


def dot(a, b):
    return jnp.dot(a, b, preferred_element_type=F32)


def dot_nt(a, b):
    return lax.dot_general(a, b, NT, preferred_element_type=F32)


def halves(value):
    high = value.astype(BF16)
    return high, (value - high.astype(F32)).astype(BF16)


def thirds(value):
    first = value.astype(BF16).astype(F32)
    rest = value - first
    second = rest.astype(BF16).astype(F32)
    return first, second, rest - second


def unit_node(index):
    return jnp.where(
        index == 0,
        NODE[0],
        jnp.where(index == 1, NODE[1], jnp.where(index == 2, NODE[2], NODE[3])),
    ).astype(F32)


def lane_nodes():
    b = lanes((8, 128)) & 63
    return [unit_node(b >> 4), unit_node((b >> 2) & 3), unit_node(b & 3)]


def row_nodes():
    r = rows((8, 128))
    return [unit_node(r >> 2), unit_node((r >> 2) + 2)], unit_node(r & 3)


def decay(t):
    return decay_positive(jnp.maximum(t, TINY))


def decay_positive(t):
    return jnp.exp2(-(t * lax.rsqrt(t)))


def tile_from_axes(x_sq, y_sq, z_sq):
    z_sq = z_sq + TINY
    yz = [y_sq[0] + z_sq, y_sq[1] + z_sq]
    return decay_positive(jnp.concatenate([x_sq[k // 2] + yz[k % 2] for k in range(8)], axis=0))


def doubled_transfer(t_ref):
    flat = t_ref[...].reshape(2 * K, K)
    return jnp.concatenate([flat, flat], axis=1)


def device_index():
    return lax.axis_index("leaf") * lax.axis_size("sub") + lax.axis_index("sub")


def merge_up(pairs, t_high, t_low):
    n = pairs.shape[0]
    high, low = halves(pairs.reshape(n * R, 128))
    out = dot(high, jnp.concatenate([t_high, t_low], axis=1))
    out = out[:, 0:128] + out[:, 128:256] + dot(low, t_high)
    return out.reshape(n, R, 128)


def pair_lanes(clusters):
    n = clusters.shape[0]
    split = clusters.reshape(n // 2, 2, R, 128)
    return jnp.where(lanes((1, R, 128)) < K, split[:, 0], split[:, 1])


def down_weights(doubled):
    low = lanes(doubled.shape) < K
    both = jnp.concatenate(
        [jnp.where(low, doubled, 0.0), jnp.where(low, 0.0, doubled)], axis=0
    )
    return halves(both)


def push_down(value, w_high, w_low):
    n = value.shape[0]
    high, low = halves(value.reshape(n * R, 128))
    out = dot_nt(high, w_high) + dot_nt(high, w_low) + dot_nt(low, w_high)
    out = out.reshape(n, R, 256)
    return jnp.stack([out[:, :, 0:128], out[:, :, 128:256]], axis=1).reshape(2 * n, R, 128)


def merge_shape_rows(left, right):
    lane = lanes(left.shape)
    sep = left - right
    gap = jnp.sqrt(jnp.sum(jnp.where(lane < 3, sep * sep, 0.0), axis=1, keepdims=True))
    radius = jnp.maximum(left, right) + 0.5 * gap
    return jnp.where(lane == 3, radius, jnp.where(lane < 3, 0.5 * (left + right), 0.0))


def sibling_tile(left, right, lane_u, row_y, row_z):
    low = lanes((8, 128)) < K
    alpha = jnp.where(low, left[3], right[3])
    beta = jnp.where(low, right[3], left[3])
    base = [jnp.where(low, left[d] - right[d], right[d] - left[d]) - beta * lane_u[d] for d in range(3)]
    x_sq = [jnp.square(base[0] + alpha * NODE[a]) for a in range(4)]
    y_sq = [jnp.square(base[1] + alpha * row_y[h]) for h in range(2)]
    z_sq = jnp.square(base[2] + alpha * row_z)
    return tile_from_axes(x_sq, y_sq, z_sq)


def sibling_apply(tile, pair):
    low = lanes((K, 128)) < K
    zero = jnp.zeros((K, 128), BF16)
    weights = []
    for part in halves(tile):
        weights.append(
            jnp.concatenate([jnp.where(low, part, zero), jnp.where(low, zero, part)], axis=0)
        )
    high, low_part = halves(pltpu.roll(pair, K, 1))
    out = dot_nt(high, jnp.concatenate(weights, axis=0))
    return out[:, 0:128] + out[:, 128:256] + dot_nt(low_part, weights[0])


LEVEL_OFFSETS = [0, 128, 192, 224, 240, 248, 252, 254]
PAIR_OFFSETS = [0, 0, 32, 48, 56, 60, 62]


def block_diagonal(left, right):
    zero = jnp.zeros(left.shape, left.dtype)
    return jnp.concatenate(
        [jnp.concatenate([left, zero], axis=1), jnp.concatenate([zero, right], axis=1)], axis=0
    )


def make_lists(near_ref, coupling_ref, list_ref, count_ref, index_ref):
    first_leaf = device_index() * LD
    lane8 = lanes((8, 128))
    row8 = rows((8, 128))
    offset = jnp.where(near_ref[...] >= 0, near_ref[...] - first_leaf - lane8, 1000)

    def slots_at(delta):
        return jnp.sum(jnp.where(offset == delta, 1.0, 0.0), axis=0, keepdims=True)

    forward = jnp.concatenate([slots_at(delta) for delta in range(8)], axis=0)
    reverse = jnp.concatenate(
        [jnp.zeros((1, 128), F32)] + [slots_at(-delta) for delta in range(1, 8)], axis=0
    )
    count_ref[0:8, :] = forward
    count_ref[8:16, :] = reverse
    backward = jnp.concatenate(
        [jnp.zeros((1, 128), F32)]
        + [pltpu.roll(reverse[delta : delta + 1, :], 128 - delta, 1) for delta in range(1, 8)],
        axis=0,
    )
    wanted = (lane8 + row8 < LD) & (forward + backward > 0.0)
    mutual = (forward > 0.0) & (backward > 0.0)
    turned = ((row8 == 1) & ((lane8 & 3) == 2) & mutual) | (
        (forward == 0.0) & (backward > 0.0)
    )
    leaf = lane8.astype(F32)
    other = leaf + row8.astype(F32)
    first = jnp.where(turned, other, leaf)
    second = jnp.where(turned, leaf, other)
    to_first = jnp.where(turned, backward, forward)
    to_second = jnp.where(turned, forward, backward)
    odd = jnp.where(turned, lane8, lane8 + row8) & 1
    earlier = jnp.where(rows((128, 128)) < lanes((128, 128)), 1.0, 0.0).astype(BF16)
    place = jnp.full((8, 128), -1.0, F32)
    batches = jnp.zeros((1, 1), jnp.int32)
    ends = []
    for kind in range(2):
        most = jnp.zeros((1, 1), F32)
        for parity in range(2):
            chosen = wanted & (odd == parity) & (mutual if kind == 0 else jnp.logical_not(mutual))
            flags = jnp.where(chosen, 1.0, 0.0)
            rank = dot(flags.astype(BF16), earlier)
            totals = jnp.sum(flags, axis=1, keepdims=True)
            before = jnp.zeros((1, 1), F32)
            starts = []
            for delta in range(8):
                starts.append(before)
                before = before + totals[delta : delta + 1, :]
            rank = rank + jnp.concatenate(starts, axis=0)
            base = (batches + 1).astype(F32) * BATCH + parity
            place = jnp.where(flags > 0.0, 2.0 * rank + base, place)
            most = jnp.maximum(most, before)
        needed = (2 * most.astype(jnp.int32) + BATCH - 1) // BATCH
        batches = batches + needed
        if kind == 0:
            batches = batches | 1
        ends.append(batches)
    task_rows = []
    for delta in range(8):
        pick = slice(delta, delta + 1)
        task_rows.append(
            jnp.where(
                row8 == 0,
                first[pick],
                jnp.where(
                    row8 == 1,
                    second[pick],
                    jnp.where(
                        row8 == 2, to_first[pick], jnp.where(row8 == 3, to_second[pick], 0.0)
                    ),
                ),
            ).astype(BF16)
        )
    tasks = jnp.concatenate(task_rows, axis=1)
    slot_row = rows((128, 128)).astype(F32)
    limit = (ends[1][0, 0] + 4) * BATCH

    def fill(m):
        chosen = jnp.concatenate(
            [
                jnp.where(place[delta : delta + 1, :] == slot_row + 128.0 * m, 1.0, 0.0).astype(BF16)
                for delta in range(8)
            ],
            axis=1,
        )
        part = dot_nt(tasks, chosen)
        part = part.astype(jnp.int32)
        part = jnp.where(row8 == 4, ends[0], jnp.where(row8 == 5, ends[1], part))
        list_ref[:, m * 128 : (m + 1) * 128] = part

    for m in range(4):
        fill(m)
    for m in range(4, LIST // 128):
        pl.when(m * 128 < limit)(functools.partial(fill, m))

    target = coupling_ref[...]
    reach = target - first_leaf + HALF
    swap = ((reach ^ row8) & 1) * (PAIRS // 2)
    entry = jnp.where(
        reach < HALF,
        LD + (reach >> 1) + swap,
        jnp.where(reach < HALF + LD, reach - HALF, LD + HALF + ((reach - HALF - LD) >> 1) + swap),
    )
    index_ref[0:8, :] = jnp.where(target >= 0, entry, TABLE - 1)
    index_ref[8:16, :] = jnp.where(target >= 0, reach, 0)


CHUNKS = 4


def leaf_kernel(
    x_any, p_ref, b_any, t_ref, near_ref, coupling_ref,
    next_any, prev_any, high_any, low_any, lev_any, root_ref, shape_ref,
    list_ref, count_ref, index_ref,
    send_next, send_prev, x_ref, b_ref, high_ref, low_ref, lev_ref, coef, pts, shapes, p8, sems,
):
    leaves = LD // CHUNKS
    copies = []
    for c in range(CHUNKS):
        span = slice(c * leaves * P_SIZE, (c + 1) * leaves * P_SIZE)
        part = slice(c * leaves, (c + 1) * leaves)
        copies.append(
            (
                pltpu.make_async_copy(x_any.at[:, span], x_ref.at[:, span], sems.at[c]),
                pltpu.make_async_copy(b_any.at[part], b_ref.at[part], sems.at[CHUNKS + c]),
            )
        )
    for pair in copies:
        for copy in pair:
            copy.start()
    origin = (device_index() * GROUPS).astype(F32)
    low32 = lanes((R, 128)) < K

    make_lists(near_ref, coupling_ref, list_ref, count_ref, index_ref)
    def leaf_pairs(m, carry):
        values = []
        for v in range(32):
            leaf = 32 * m + v
            x = x_ref[:, pl.ds(pl.multiple_of(leaf * P_SIZE, P_SIZE), P_SIZE)]
            weights = b_ref[leaf]
            values.append(dot_nt(x, jnp.concatenate([weights, weights], axis=0)))
        for v in range(32):
            high_ref[32 * m + v], low_ref[32 * m + v] = halves(values[v])
        for v in range(16):
            coef[16 * m + v] = jnp.where(low32, values[2 * v], values[2 * v + 1])
        return carry

    for c in range(CHUNKS):
        for copy in copies[c]:
            copy.wait()
        steps = leaves // 32
        lax.fori_loop(c * steps, (c + 1) * steps, leaf_pairs, 0)
    leaving = [
        pltpu.make_async_copy(high_ref, high_any, sems.at[2 * CHUNKS]),
        pltpu.make_async_copy(low_ref, low_any, sems.at[2 * CHUNKS + 1]),
    ]
    for copy in leaving:
        copy.start()

    for i in range(LD):
        for d in range(3):
            pts[d, i : i + 1, :] = p_ref[d : d + 1, i * P_SIZE : (i + 1) * P_SIZE]
    centers, squares = [], 0.0
    for d in range(3):
        coords = (pts[d] - origin if d == 2 else pts[d]) * SCALE
        center = jnp.sum(coords, axis=1, keepdims=True) * (1.0 / P_SIZE)
        centers.append(center)
        squares = squares + jnp.square(coords - center)
    radius = jnp.sqrt(jnp.max(squares, axis=1, keepdims=True))
    lane = lanes((LD, 128))
    shapes[0:LD, :] = jnp.where(
        lane == 0,
        centers[0],
        jnp.where(
            lane == 1,
            centers[1],
            jnp.where(lane == 2, centers[2], jnp.where(lane == 3, radius, 0.0)),
        ),
    )
    count = LD // 2
    for level in range(1, 8):
        source = LEVEL_OFFSETS[level - 1]
        joined = merge_shape_rows(
            shapes[pl.ds(source, count, stride=2), :],
            shapes[pl.ds(source + 1, count, stride=2), :],
        )
        shapes[pl.ds(LEVEL_OFFSETS[level], count), :] = joined
        count //= 2
    shape_rows = jnp.concatenate(
        [jnp.transpose(shapes[0:128, :])[0:8], jnp.transpose(shapes[128:256, :])[0:8]], axis=1
    )
    shape_ref[...] = shape_rows
    p8[...] = jnp.zeros((8, 512), F32)
    for send, first_pair, group in ((send_next, PAIRS // 2, GROUPS - 1), (send_prev, 0, 0)):

        def copy_pairs(m, carry):
            parts = [halves(coef[first_pair + 8 * m + v]) for v in range(8)]
            for v in range(8):
                send[8 * m + v], send[32 + 8 * m + v] = parts[v]
            return carry

        lax.fori_loop(0, PAIRS // 16, copy_pairs, 0)
        parts = thirds(shape_rows[:, 0:128])
        send[68] = jnp.concatenate(list(parts) + [jnp.zeros((8, 128), F32)], axis=0).astype(BF16)
        p8[0:3, :] = p_ref[:, group * 512 : group * 512 + 512]
        parts = thirds(p8[...])
        for k in range(4):
            send[64 + k] = x_ref[:, group * 512 + k * P_SIZE : group * 512 + (k + 1) * P_SIZE]
        for part in range(3):
            send[69 + part] = jnp.concatenate(
                [parts[part][:, k * P_SIZE : (k + 1) * P_SIZE] for k in range(4)], axis=0
            ).astype(BF16)
    for k, (send, out) in enumerate(((send_next, next_any), (send_prev, prev_any))):
        leaving.append(pltpu.make_async_copy(send, out, sems.at[2 * CHUNKS + 3 + k]))
        leaving[-1].start()

    t_high, t_low = halves(doubled_transfer(t_ref))
    pairs = coef[...]
    for level in range(1, 7):
        pairs = pair_lanes(merge_up(pairs, t_high, t_low))
        lev_ref[pl.ds(PAIR_OFFSETS[level], pairs.shape[0])] = pairs
    leaving.append(pltpu.make_async_copy(lev_ref, lev_any, sems.at[2 * CHUNKS + 2]))
    leaving[-1].start()
    root = merge_up(pairs, t_high, t_low)[0]

    low = lanes((R // 2, 128)) < K
    block = jnp.concatenate(
        [
            jnp.where(low, root[0 : R // 2], root[R // 2 : R]),
            jnp.broadcast_to(shapes[254:255, :], (8, 128)),
        ],
        axis=0,
    )
    root_ref[...] = jnp.broadcast_to(block[None], root_ref.shape)

    for copy in leaving:
        copy.wait()


def point_features(points8, origin_z):
    row = rows(points8.shape)
    center = jnp.where(row == 2, origin_z + 0.5, 1.0)
    v = jnp.where(row < 3, (points8 - center) * SCALE, 0.0)
    norm = jnp.sum(v * v, axis=0, keepdims=True)
    far = jnp.where(row == 3, norm, jnp.where(row == 4, 1.0, v))
    own = jnp.where(row == 3, 1.0, jnp.where(row == 4, norm, -2.0 * v))
    return far, own


def far_stack(value):
    first, second, third = thirds(value)
    none = jnp.zeros(value.shape, F32)
    return jnp.concatenate(
        [first, first, first, second, second, third, none, none], axis=0
    ).astype(BF16)


def own_stack(value):
    first, second, third = thirds(value)
    none = jnp.zeros(value.shape, F32)
    return jnp.concatenate(
        [first, second, third, first, second, first, none, none], axis=0
    ).astype(BF16)


def identity():
    return jnp.where(rows((128, 128)) == lanes((128, 128)), 1.0, 0.0).astype(BF16)


def near_kernel(
    list_ref, shape_ref, x_any, p_ref, lev_any,
    out_ref, couple_ref,
    x_ref, lev_ref, sems, p8, far_feat, own_feat, tile0, tile1,
):
    copies = [
        pltpu.make_async_copy(x_any, x_ref, sems.at[0]),
        pltpu.make_async_copy(lev_any, lev_ref, sems.at[1]),
    ]
    for copy in copies:
        copy.start()
    first_group = device_index() * GROUPS
    p8[...] = jnp.zeros(p8.shape, F32)
    eye = identity()

    def features(m, carry):
        loaded = [p_ref[:, pl.ds(pl.multiple_of((16 * m + v) * 512, 512), 512)] for v in range(16)]
        for v in range(16):
            p8[v, 0:3, :] = loaded[v]
        made = []
        for v in range(16):
            coords = p8[v]
            origin_z = (first_group + 16 * m + v).astype(F32)
            far, own = point_features(coords, origin_z)
            _, own_up = point_features(coords, origin_z + 1.0)
            _, own_down = point_features(coords, origin_z - 1.0)
            far = far_stack(far)
            parts = [far[:, k * P_SIZE : (k + 1) * P_SIZE] for k in range(4)]
            turned = dot_nt(eye, jnp.concatenate(parts, axis=0)).astype(BF16)
            made.append((turned, own_stack(own), own_stack(own_up), own_stack(own_down)))
        for v in range(16):
            g = 16 * m + v
            turned, own, own_up, own_down = made[v]
            far_feat[2 * g] = turned[:, 0:128]
            far_feat[2 * g + 1] = turned[:, 128:256]
            for k in range(4):
                part = slice(k * P_SIZE, (k + 1) * P_SIZE)
                own_feat[4 * g + k] = own[:, part]
                own_feat[LD + 4 * g + k] = own_up[:, part]
                own_feat[2 * LD + 4 * g + k] = own_down[:, part]
        return carry

    lax.fori_loop(0, GROUPS // 16, features, 0)

    for copy in copies:
        copy.wait()
    out_ref[...] = x_ref[...].astype(F32)
    for ref in (tile0, tile1):
        ref[...] = jnp.zeros(ref.shape, ref.dtype)

    mutual_phases = list_ref[4, 0] + 1
    all_phases = list_ref[5, 0] + 1
    low = lanes((128, 128)) < K

    def leaf_slice(i):
        return pl.ds(pl.multiple_of(i * P_SIZE, P_SIZE), P_SIZE)

    lane_u = lane_nodes()
    row_y, row_z = row_nodes()

    def phase(n, tile_new, tile_old, pairs, sides):
        far, own, sources, updates = [], [], [], []
        siblings = [jnp.minimum(pairs * n + v, PAIRS - 2) for v in range(pairs)]
        levels = [lev_ref[pair] for pair in siblings]
        for u in range(BATCH):
            k = (n + 1) * BATCH + u
            i, j = list_ref[0, k], list_ref[1, k]
            step = (j >> 2) - (i >> 2)
            variant = jnp.where(step < 0, 2, step) * LD
            far.append(far_feat[j >> 1])
            own.append(own_feat[variant + i])
        for u in range(BATCH):
            k = n * BATCH + u
            i, j = list_ref[0, k], list_ref[1, k]
            sources.append((x_ref[:, leaf_slice(j)], x_ref[:, leaf_slice(i)]))
        tiles = []
        for u in range(BATCH // 2):
            pick = jnp.where(low, far[2 * u], far[2 * u + 1])
            dist = dot(pick, block_diagonal(own[2 * u], own[2 * u + 1]))
            tiles.append(decay(dist).astype(BF16))
            weights = block_diagonal(tile_old[u, :, 0:128], tile_old[u, :, 128:256])
            to_i = dot(jnp.concatenate([sources[2 * u][0], sources[2 * u + 1][0]], axis=1), weights)
            to_j = None
            if sides == 2:
                to_j = dot_nt(
                    jnp.concatenate([sources[2 * u][1], sources[2 * u + 1][1]], axis=1), weights
                )
            for h in range(2):
                k = n * BATCH + 2 * u + h
                span = slice(h * 128, (h + 1) * 128)
                updates.append(
                    (
                        to_i[:, span] * list_ref[2, k].astype(F32),
                        to_j[:, span] * list_ref[3, k].astype(F32) if sides == 2 else None,
                    )
                )
        for pair, level in zip(siblings, levels):
            cluster = LD + 2 * pair
            left = [shape_ref[d, cluster] for d in range(4)]
            right = [shape_ref[d, cluster + 1] for d in range(4)]
            couple_ref[pair] = sibling_apply(
                sibling_tile(left, right, lane_u, row_y, row_z), level
            )
        for u in range(BATCH // 2):
            tile_new[u] = tiles[u]
        for u in range(BATCH):
            k = n * BATCH + u
            to_i = leaf_slice(list_ref[0, k])
            to_j = leaf_slice(list_ref[1, k])
            out_ref[:, to_i] += updates[u][0]
            if sides == 2:
                out_ref[:, to_j] += updates[u][1]

    def two_phases(pairs, sides, m, carry):
        phase(2 * m, tile0, tile1, pairs, sides)
        phase(2 * m + 1, tile1, tile0, pairs, sides)
        return carry

    rides = -(-(PAIRS - 1) // (2 * SIBLINGS))
    middle = mutual_phases // 2
    lax.fori_loop(0, rides, functools.partial(two_phases, SIBLINGS, 2), 0)
    lax.fori_loop(rides, middle, functools.partial(two_phases, 0, 2), 0)
    lax.fori_loop(middle, (all_phases + 1) // 2, functools.partial(two_phases, 0, 1), 0)


def tree_down(t_ref, root_ref, down_ref, couple, pairs_scr, shapes):
    lane_u = lane_nodes()
    row_y, row_z = row_nodes()

    doubled = doubled_transfer(t_ref)
    t_high, t_low = halves(doubled)
    w_high, w_low = down_weights(doubled)
    device = device_index()
    n = root_ref.shape[0]
    low = lanes((R, 128)) < K
    shift = lanes((1, 128)) == 2
    for k in range(n):
        shapes[k : k + 1, :] = root_ref[k, R // 2 : R // 2 + 1, :] + jnp.where(
            shift, (k * GROUPS) * SCALE, 0.0
        )
    for k in range(n // 2):
        left = root_ref[2 * k, 0 : R // 2, :]
        right = root_ref[2 * k + 1, 0 : R // 2, :]
        left = jnp.concatenate([left, pltpu.roll(left, K, 1)], axis=0)
        right = jnp.concatenate([pltpu.roll(right, K, 1), right], axis=0)
        pairs_scr[k] = jnp.where(low, left, right)
    source, count, pair_source = 0, n // 2, 0
    levels = []
    while count >= 1:
        levels.append((source, pair_source))
        if count > 1:
            pairs = pair_lanes(merge_up(pairs_scr[pl.ds(pair_source, count)], t_high, t_low))
            pairs_scr[pl.ds(pair_source + count, count // 2)] = pairs
            joined = merge_shape_rows(
                shapes[pl.ds(source, count, stride=2), :],
                shapes[pl.ds(source + 1, count, stride=2), :],
            )
            shapes[pl.ds(source + 2 * count, count), :] = joined
        source += 2 * count
        pair_source += count
        count //= 2
    couples = []
    for level, (source, pair_source) in enumerate(levels):
        pair = device >> (level + 1)
        left_row = shapes[pl.ds(source + 2 * pair, 1), :]
        right_row = shapes[pl.ds(source + 2 * pair + 1, 1), :]
        left = [jnp.broadcast_to(left_row[:, d : d + 1], (8, 128)) for d in range(4)]
        right = [jnp.broadcast_to(right_row[:, d : d + 1], (8, 128)) for d in range(4)]
        tile = sibling_tile(left, right, lane_u, row_y, row_z)
        couples.append(sibling_apply(tile, pairs_scr[pair_source + pair]))
    incoming = None
    for level in reversed(range(len(levels))):
        value = couples[level]
        if incoming is not None:
            pushed = push_down(incoming[None], w_high, w_low)
            value = value + (pushed[0] + pushed[1])
        side = (device >> level) & 1
        keep_low = jnp.where(low, 1, 0) == (1 - side)
        incoming = jnp.where(keep_low, value, 0.0)
    pushed = push_down(incoming[None], w_high, w_low)
    value = couple[pl.ds(PAIR_OFFSETS[6], 1)] + (pushed[0:1] + pushed[1:2])
    for level in range(5, 0, -1):
        n = PAIRS >> level
        value = couple[pl.ds(PAIR_OFFSETS[level], n)] + push_down(value, w_high, w_low)
    down_ref[...] = push_down(value, w_high, w_low)


UNIT = 8


def couple_leaves(
    entries, shape_ref, prev_ref, next_ref, table_copies, leaf_couple,
    shape_tab, high_tab, low_tab, halo_rows, halo_shape, sems,
    tiles0, lhs0, tiles1, lhs1,
):
    copies = []
    for k, ref in enumerate((prev_ref, next_ref)):
        parts = ref[68].astype(F32)
        halo_rows[k] = parts[0:8] + parts[8:16] + parts[16:24]
        copies.append(pltpu.make_async_copy(halo_rows.at[k], halo_shape.at[k], sems.at[k]))
    for copy in copies:
        copy.start()
    low32 = lanes((R, 128)) < K
    lane_u = lane_nodes()
    row8 = rows((8, 128))
    low8 = lanes((8, 128)) < K

    def shape_rows(read, k, shift):
        return jnp.where(
            row8 == 0,
            read(0, k),
            jnp.where(row8 == 1, read(1, k), jnp.where(row8 == 2, read(2, k) + shift, read(3, k))),
        )

    def own_nodes(m, carry):
        shape_tab[HALF + m] = shape_rows(lambda d, k: shape_ref[d, k], m, 0.0)
        return carry

    lax.fori_loop(0, LD, own_nodes, 0, unroll=8)
    for copy in copies:
        copy.wait()
    def halo_pairs(m, carry):
        loaded = [
            (tab, LD + side * HALF + 4 * m + v, ref[offset + 4 * m + v])
            for side, ref in enumerate((prev_ref, next_ref))
            for tab, offset in ((high_tab, 0), (low_tab, 32))
            for v in range(4)
        ]
        turned = [pltpu.roll(pair.astype(F32), K, 1).astype(BF16) for _, _, pair in loaded]
        for side in range(2):
            source = HALF if side == 0 else 0
            place = 0 if side == 0 else HALF + LD
            shift = (2.0 * side - 1.0) * GROUPS * SCALE
            for v in range(8):
                shape_tab[place + 8 * m + v] = shape_rows(
                    lambda d, k: halo_shape[side, d, k], source + 8 * m + v, shift
                )
        for (tab, pair, value), other in zip(loaded, turned):
            tab[pair] = value
            tab[PAIRS // 2 + pair] = other
        return carry

    lax.fori_loop(0, PAIRS // 8, halo_pairs, 0)
    high_tab[TABLE - 1] = jnp.zeros((R, 128), BF16)
    low_tab[TABLE - 1] = jnp.zeros((R, 128), BF16)
    for copy in table_copies:
        copy.wait()

    row_y, row_z = row_nodes()

    def couple_tiles(pair, u, tiles, lhs):
        leaves = (2 * pair, 2 * pair + 1)
        for q in range(4):
            span = slice(q * 128, (q + 1) * 128)
            for h in range(2):
                e0, e1 = entries[2 * q, leaves[h]], entries[2 * q + 1, leaves[h]]
                lhs[u, h * R : (h + 1) * R, span] = jnp.where(low32, high_tab[e0], high_tab[e1])
                lhs[u, (2 + h) * R : (3 + h) * R, span] = jnp.where(
                    low32, low_tab[e0], low_tab[e1]
                )
        own = jnp.where(low8, shape_tab[HALF + leaves[0]], shape_tab[HALF + leaves[1]])
        radius = jnp.broadcast_to(own[3:4], (8, 128))
        own = [jnp.broadcast_to(own[d : d + 1], (8, 128)) + radius * lane_u[d] for d in range(3)]
        fars = []
        for s in range(8):
            e0, e1 = entries[8 + s, leaves[0]], entries[8 + s, leaves[1]]
            fars.append(jnp.where(low8, shape_tab[e0], shape_tab[e1]))
        for s, far in enumerate(fars):
            reach = jnp.broadcast_to(far[3:4], (8, 128))
            gap = [own[d] - jnp.broadcast_to(far[d : d + 1], (8, 128)) for d in range(3)]
            tile = tile_from_axes(
                [jnp.square(gap[0] - reach * NODE[b]) for b in range(4)],
                [jnp.square(gap[1] - reach * row_y[h]) for h in range(2)],
                jnp.square(gap[2] - reach * row_z),
            )
            high, low = halves(tile)
            tiles[u, s * K : (s + 1) * K, 0:128] = high
            tiles[u, s * K : (s + 1) * K, 128:256] = low

    def couple_apply(u, tiles, lhs):
        both = dot(lhs[u], tiles[u])
        both = both[0 : 2 * R, 0:128] + (both[2 * R : 4 * R, 0:128] + both[0 : 2 * R, 128:256])
        return jnp.where(low32, both[0:R], both[R : 2 * R])

    def couple_phase(n, new, old):
        for u in range(UNIT):
            couple_tiles(n * UNIT + u, u, *new)
            leaf_couple[n * UNIT + u] = couple_apply(u, *old)

    buffers = ((tiles0, lhs0), (tiles1, lhs1))
    for ref in buffers[1]:
        ref[...] = jnp.zeros(ref.shape, ref.dtype)

    def couple_two(m, carry):
        couple_phase(2 * m, buffers[0], buffers[1])
        couple_phase(2 * m + 1, buffers[1], buffers[0])
        return carry

    lax.fori_loop(0, PAIRS // UNIT // 2, couple_two, 0)
    for u in range(UNIT):
        leaf_couple[PAIRS + u] = couple_apply(u, *buffers[1])


def finish_leaves(b_ref, down_ref, leaf_couple, out_ref, border):
    def finish(m, carry):
        values = []
        for v in range(16):
            c = 16 * m + v
            value = (down_ref[c] + leaf_couple[c + UNIT]).astype(BF16)
            span = pl.ds(pl.multiple_of(c * 256, 256), 256)
            values.append(
                (
                    span,
                    out_ref[:, span]
                    + dot(value, block_diagonal(b_ref[2 * c], b_ref[2 * c + 1])),
                )
            )
        for span, value in values:
            out_ref[:, span] = value
        return carry

    lax.fori_loop(0, PAIRS // 16, finish, 0)
    for side, group in enumerate((0, GROUPS - 1)):
        for i in range(4):
            leaf = 4 * group + i
            out_ref[:, leaf * P_SIZE : (leaf + 1) * P_SIZE] += border[4 * side + i]


def border_blocks(counts, p_ref, prev_ref, next_ref, border, p8, coords):
    device = device_index()

    p8[...] = jnp.zeros(p8.shape, F32)
    eye = identity()
    sides = ((prev_ref, 0), (next_ref, GROUPS - 1))
    for side, (halo_ref, group) in enumerate(sides):
        p8[side, 0:3, :] = p_ref[:, group * 512 : group * 512 + 512]
        coords[side] = halo_ref[69].astype(F32) + halo_ref[70].astype(F32) + halo_ref[71].astype(F32)

    sums = [[0.0] * 4, [0.0] * 4]
    for k in range(4):
        loaded = [
            (halo_ref[64 + k], coords[side, 8 * k : 8 * k + 8, :], p8[side])
            for side, (halo_ref, _) in enumerate(sides)
        ]
        for side, (_, group) in enumerate(sides):
            x_far, far, own = loaded[side]
            origin_z = (device * GROUPS + group).astype(F32)
            _, own = point_features(own, origin_z)
            far, _ = point_features(far, origin_z)
            far = dot_nt(eye, far_stack(far)).astype(BF16)
            tiles = decay(dot(far, own_stack(own))).astype(BF16)
            products = dot(x_far, tiles)
            for i in range(4):
                delta = (4 + i - k) if side == 0 else (4 + k - i)
                weight = counts[8 * (1 - side) + delta, 4 * group + i]
                sums[side][i] = sums[side][i] + products[:, i * P_SIZE : (i + 1) * P_SIZE] * weight
    for side in range(2):
        for i in range(4):
            border[4 * side + i] = sums[side][i]


def tree_kernel(
    t_any, root_any, couple_any, down_ref, t_ref, root_ref, couple, pairs_scr, shapes, sems
):
    moves = ((t_any, t_ref), (root_any, root_ref), (couple_any, couple))
    copies = [pltpu.make_async_copy(a, b, sems.at[k]) for k, (a, b) in enumerate(moves)]
    for copy in copies:
        copy.start()
    for copy in copies:
        copy.wait()
    tree_down(t_ref, root_ref, down_ref, couple, pairs_scr, shapes)


def final_kernel(
    entries, shape_ref, counts,
    prev_any, next_any, p_any, high_any, low_any, b_any, near_any, down_any,
    out_ref,
    prev_ref, next_ref, p_ref, b_ref, down, leaf_couple,
    shape_tab, high_tab, low_tab, halo_rows, halo_shape,
    tiles0, lhs0, tiles1, lhs1, p8, coords, border, sems, halo_sems,
):
    moves = (
        (prev_any, prev_ref),
        (next_any, next_ref),
        (p_any, p_ref),
        (high_any, high_tab.at[0:LD]),
        (low_any, low_tab.at[0:LD]),
        (b_any, b_ref),
        (near_any, out_ref),
        (down_any, down),
    )
    copies = [pltpu.make_async_copy(a, b, sems.at[k]) for k, (a, b) in enumerate(moves)]
    for copy in copies:
        copy.start()
    for copy in copies[0:3]:
        copy.wait()
    border_blocks(counts, p_ref, prev_ref, next_ref, border, p8, coords)
    couple_leaves(
        entries, shape_ref, prev_ref, next_ref, copies[3:5], leaf_couple,
        shape_tab, high_tab, low_tab, halo_rows, halo_shape, halo_sems,
        tiles0, lhs0, tiles1, lhs1,
    )
    for copy in copies[5:]:
        copy.wait()
    finish_leaves(b_ref, down, leaf_couple, out_ref, border)


def shaped(*shape, dtype=F32):
    return jax.ShapeDtypeStruct(shape, dtype)


def vmem():
    return pl.BlockSpec(memory_space=pltpu.VMEM)


def smem():
    return pl.BlockSpec(memory_space=pltpu.SMEM)


def anywhere():
    return pl.BlockSpec(memory_space=pl.ANY)


PARAMS = pltpu.CompilerParams(vmem_limit_bytes=VMEM_LIMIT)


def per_device(charges, points, basis, transfer, near_list, coupling_list):
    near_rows = near_list.T
    coupling_rows = coupling_list.T
    devices = lax.axis_size("sub") * lax.axis_size("leaf")
    send_next, send_prev, high, low, lev, root, shapes, tasks, counts, entries = pl.pallas_call(
        leaf_kernel,
        name="leaf_up",
        out_shape=(
            shaped(SEND, R, 128, dtype=BF16),
            shaped(SEND, R, 128, dtype=BF16),
            shaped(LD, R, 128, dtype=BF16),
            shaped(LD, R, 128, dtype=BF16),
            shaped(PAIRS - 1, R, 128),
            shaped(devices, R // 2 + 8, 128),
            shaped(8, 256),
            shaped(8, LIST, dtype=jnp.int32),
            shaped(16, 128),
            shaped(16, 128, dtype=jnp.int32),
        ),
        in_specs=[anywhere(), vmem(), anywhere(), vmem(), vmem(), vmem()],
        out_specs=[anywhere()] * 5 + [vmem()] * 5,
        scratch_shapes=[
            pltpu.VMEM((SEND, R, 128), BF16),
            pltpu.VMEM((SEND, R, 128), BF16),
            pltpu.VMEM((R, LD * P_SIZE), BF16),
            pltpu.VMEM((LD, K, P_SIZE), BF16),
            pltpu.VMEM((LD, R, 128), BF16),
            pltpu.VMEM((LD, R, 128), BF16),
            pltpu.VMEM((PAIRS - 1, R, 128), F32),
            pltpu.VMEM((PAIRS, R, 128), F32),
            pltpu.VMEM((3, LD, 128), F32),
            pltpu.VMEM((256, 128), F32),
            pltpu.VMEM((8, 512), F32),
            pltpu.SemaphoreType.DMA((2 * CHUNKS + 5,)),
        ],
        compiler_params=PARAMS,
    )(charges, points, basis, transfer, near_rows, coupling_rows)

    roots = lax.all_to_all(root, AXES, 0, 0, tiled=True)
    forward = [(i, i + 1) for i in range(devices - 1)]
    backward = [(i + 1, i) for i in range(devices - 1)]
    from_prev = lax.ppermute(send_next, AXES, forward)
    from_next = lax.ppermute(send_prev, AXES, backward)

    near, couple = pl.pallas_call(
        near_kernel,
        name="near_field",
        out_shape=(shaped(R, LD * P_SIZE), shaped(PAIRS - 1, R, 128)),
        in_specs=[smem(), smem(), anywhere(), vmem(), anywhere()],
        out_specs=[vmem()] * 2,
        scratch_shapes=[
            pltpu.VMEM((R, LD * P_SIZE), BF16),
            pltpu.VMEM((PAIRS - 1, R, 128), F32),
            pltpu.SemaphoreType.DMA((2,)),
            pltpu.VMEM((16, 8, 512), F32),
            pltpu.VMEM((PAIRS, P_SIZE, 2 * FEATS), BF16),
            pltpu.VMEM((3 * LD, FEATS, P_SIZE), BF16),
            pltpu.VMEM((BATCH // 2, 128, 256), BF16),
            pltpu.VMEM((BATCH // 2, 128, 256), BF16),
        ],
        compiler_params=PARAMS,
        cost_estimate=pl.CostEstimate(
            flops=2 * 460 * 128 * 128 * 128, bytes_accessed=4 << 20, transcendentals=460 * 32768
        ),
    )(tasks, shapes, charges, points, lev)

    near, roots = lax.optimization_barrier((near, roots))
    down = pl.pallas_call(
        tree_kernel,
        name="tree_down",
        out_shape=shaped(PAIRS, R, 128),
        in_specs=[anywhere()] * 3,
        out_specs=vmem(),
        scratch_shapes=[
            pltpu.VMEM((2, K, K), F32),
            pltpu.VMEM((devices, R // 2 + 8, 128), F32),
            pltpu.VMEM((PAIRS - 1, R, 128), F32),
            pltpu.VMEM((devices, R, 128), F32),
            pltpu.VMEM((2 * devices, 128), F32),
            pltpu.SemaphoreType.DMA((3,)),
        ],
        compiler_params=PARAMS,
    )(transfer, roots, couple)
    from_prev, from_next, down = lax.optimization_barrier((from_prev, from_next, down))

    stages = [
        pltpu.VMEM((UNIT, 512, 256), BF16),
        pltpu.VMEM((UNIT, 4 * R, 512), BF16),
    ]
    return pl.pallas_call(
        final_kernel,
        name="couple_finish",
        out_shape=shaped(R, LD * P_SIZE),
        in_specs=[smem()] * 3 + [anywhere()] * 8,
        out_specs=vmem(),
        scratch_shapes=[
            pltpu.VMEM((SEND, R, 128), BF16),
            pltpu.VMEM((SEND, R, 128), BF16),
            pltpu.VMEM((3, LD * P_SIZE), F32),
            pltpu.VMEM((LD, K, P_SIZE), BF16),
            pltpu.VMEM((PAIRS, R, 128), F32),
            pltpu.VMEM((PAIRS + UNIT, R, 128), F32),
            pltpu.VMEM((2 * LD, 8, 128), F32),
            pltpu.VMEM((TABLE, R, 128), BF16),
            pltpu.VMEM((TABLE, R, 128), BF16),
            pltpu.VMEM((2, 8, 128), F32),
            pltpu.SMEM((2, 8, 128), F32),
        ]
        + stages
        + stages
        + [
            pltpu.VMEM((2, 8, 512), F32),
            pltpu.VMEM((2, R, 128), F32),
            pltpu.VMEM((8, R, 128), F32),
            pltpu.SemaphoreType.DMA((8,)),
            pltpu.SemaphoreType.DMA((2,)),
        ],
        compiler_params=PARAMS,
    )(
        entries, shapes, counts,
        from_prev, from_next, points, high, low, basis, near, down,
    )


def solution(mesh):
    in_specs = (
        P(None, AXES),
        P(None, AXES),
        P(AXES, None, None),
        P(),
        P(AXES, None),
        P(AXES, None),
    )
    return jax.shard_map(
        per_device, mesh=mesh, in_specs=in_specs, out_specs=P(None, AXES), check_vma=False
    )
```

```python
import functools
import math

import jax
import jax.numpy as jnp
from jax import lax
from jax.experimental import pallas as pl
from jax.experimental.pallas import tpu as pltpu
from jax.sharding import PartitionSpec as P

P_SIZE = 128
K = 64
R = 32
LD = 128
PAIRS = LD // 2
GROUPS = LD // 4
TABLE = 257
HALF = LD // 2
NEAR_REACH = 8
FEATS = 64
BATCH = 16
SIBLINGS = 6
LIST = 1536
SEND = 72
SCALE = 0.5 * math.log2(math.e)
NODE = [math.cos((2 * a + 1) * math.pi / 8) for a in range(4)]
AXES = ("leaf", "sub")
F32 = jnp.float32
BF16 = jnp.bfloat16
NT = (((1,), (1,)), ((), ()))
TINY = 1e-30
VMEM_LIMIT = 64 * 1024 * 1024


def lanes(shape):
    return lax.broadcasted_iota(jnp.int32, shape, len(shape) - 1)


def rows(shape):
    return lax.broadcasted_iota(jnp.int32, shape, len(shape) - 2)


def dot(a, b):
    return jnp.dot(a, b, preferred_element_type=F32)


def dot_nt(a, b):
    return lax.dot_general(a, b, NT, preferred_element_type=F32)


def halves(value):
    high = value.astype(BF16)
    return high, (value - high.astype(F32)).astype(BF16)


def thirds(value):
    first = value.astype(BF16).astype(F32)
    rest = value - first
    second = rest.astype(BF16).astype(F32)
    return first, second, rest - second


def unit_node(index):
    return jnp.where(
        index == 0,
        NODE[0],
        jnp.where(index == 1, NODE[1], jnp.where(index == 2, NODE[2], NODE[3])),
    ).astype(F32)


def lane_nodes():
    b = lanes((8, 128)) & 63
    return [unit_node(b >> 4), unit_node((b >> 2) & 3), unit_node(b & 3)]


def row_nodes():
    r = rows((8, 128))
    return [unit_node(r >> 2), unit_node((r >> 2) + 2)], unit_node(r & 3)


def decay(t):
    return decay_positive(jnp.maximum(t, TINY))


def decay_positive(t):
    return jnp.exp2(-(t * lax.rsqrt(t)))


def tile_from_axes(x_sq, y_sq, z_sq):
    z_sq = z_sq + TINY
    yz = [y_sq[0] + z_sq, y_sq[1] + z_sq]
    return decay_positive(jnp.concatenate([x_sq[k // 2] + yz[k % 2] for k in range(8)], axis=0))


def doubled_transfer(t_ref):
    flat = t_ref[...].reshape(2 * K, K)
    return jnp.concatenate([flat, flat], axis=1)


def device_index():
    return lax.axis_index("leaf") * lax.axis_size("sub") + lax.axis_index("sub")


def merge_up(pairs, t_high, t_low):
    n = pairs.shape[0]
    high, low = halves(pairs.reshape(n * R, 128))
    out = dot(high, jnp.concatenate([t_high, t_low], axis=1))
    out = out[:, 0:128] + out[:, 128:256] + dot(low, t_high)
    return out.reshape(n, R, 128)


def pair_lanes(clusters):
    n = clusters.shape[0]
    split = clusters.reshape(n // 2, 2, R, 128)
    return jnp.where(lanes((1, R, 128)) < K, split[:, 0], split[:, 1])


def down_weights(doubled):
    low = lanes(doubled.shape) < K
    both = jnp.concatenate(
        [jnp.where(low, doubled, 0.0), jnp.where(low, 0.0, doubled)], axis=0
    )
    return halves(both)


def push_down(value, w_high, w_low):
    n = value.shape[0]
    high, low = halves(value.reshape(n * R, 128))
    out = dot_nt(high, w_high) + dot_nt(high, w_low) + dot_nt(low, w_high)
    out = out.reshape(n, R, 256)
    return jnp.stack([out[:, :, 0:128], out[:, :, 128:256]], axis=1).reshape(2 * n, R, 128)


def merge_shape_rows(left, right):
    lane = lanes(left.shape)
    sep = left - right
    gap = jnp.sqrt(jnp.sum(jnp.where(lane < 3, sep * sep, 0.0), axis=1, keepdims=True))
    radius = jnp.maximum(left, right) + 0.5 * gap
    return jnp.where(lane == 3, radius, jnp.where(lane < 3, 0.5 * (left + right), 0.0))


def sibling_tile(left, right, lane_u, row_y, row_z):
    low = lanes((8, 128)) < K
    alpha = jnp.where(low, left[3], right[3])
    beta = jnp.where(low, right[3], left[3])
    base = [jnp.where(low, left[d] - right[d], right[d] - left[d]) - beta * lane_u[d] for d in range(3)]
    x_sq = [jnp.square(base[0] + alpha * NODE[a]) for a in range(4)]
    y_sq = [jnp.square(base[1] + alpha * row_y[h]) for h in range(2)]
    z_sq = jnp.square(base[2] + alpha * row_z)
    return tile_from_axes(x_sq, y_sq, z_sq)


def sibling_apply(tile, pair):
    low = lanes((K, 128)) < K
    zero = jnp.zeros((K, 128), BF16)
    weights = []
    for part in halves(tile):
        weights.append(
            jnp.concatenate([jnp.where(low, part, zero), jnp.where(low, zero, part)], axis=0)
        )
    high, low_part = halves(pltpu.roll(pair, K, 1))
    out = dot_nt(high, jnp.concatenate(weights, axis=0))
    return out[:, 0:128] + out[:, 128:256] + dot_nt(low_part, weights[0])


LEVEL_OFFSETS = [0, 128, 192, 224, 240, 248, 252, 254]
PAIR_OFFSETS = [0, 0, 32, 48, 56, 60, 62]


def block_diagonal(left, right):
    zero = jnp.zeros(left.shape, left.dtype)
    return jnp.concatenate(
        [jnp.concatenate([left, zero], axis=1), jnp.concatenate([zero, right], axis=1)], axis=0
    )


def make_lists(near_ref, coupling_ref, list_ref, count_ref, index_ref):
    first_leaf = device_index() * LD
    lane8 = lanes((8, 128))
    row8 = rows((8, 128))
    offset = jnp.where(near_ref[...] >= 0, near_ref[...] - first_leaf - lane8, 1000)

    def slots_at(delta):
        return jnp.sum(jnp.where(offset == delta, 1.0, 0.0), axis=0, keepdims=True)

    forward = jnp.concatenate([slots_at(delta) for delta in range(8)], axis=0)
    reverse = jnp.concatenate(
        [jnp.zeros((1, 128), F32)] + [slots_at(-delta) for delta in range(1, 8)], axis=0
    )
    count_ref[0:8, :] = forward
    count_ref[8:16, :] = reverse
    backward = jnp.concatenate(
        [jnp.zeros((1, 128), F32)]
        + [pltpu.roll(reverse[delta : delta + 1, :], 128 - delta, 1) for delta in range(1, 8)],
        axis=0,
    )
    wanted = (lane8 + row8 < LD) & (forward + backward > 0.0)
    mutual = (forward > 0.0) & (backward > 0.0)
    turned = ((row8 == 1) & ((lane8 & 3) == 2) & mutual) | (
        (forward == 0.0) & (backward > 0.0)
    )
    leaf = lane8.astype(F32)
    other = leaf + row8.astype(F32)
    first = jnp.where(turned, other, leaf)
    second = jnp.where(turned, leaf, other)
    to_first = jnp.where(turned, backward, forward)
    to_second = jnp.where(turned, forward, backward)
    odd = jnp.where(turned, lane8, lane8 + row8) & 1
    earlier = jnp.where(rows((128, 128)) < lanes((128, 128)), 1.0, 0.0).astype(BF16)
    place = jnp.full((8, 128), -1.0, F32)
    batches = jnp.zeros((1, 1), jnp.int32)
    ends = []
    for kind in range(2):
        most = jnp.zeros((1, 1), F32)
        for parity in range(2):
            chosen = wanted & (odd == parity) & (mutual if kind == 0 else jnp.logical_not(mutual))
            flags = jnp.where(chosen, 1.0, 0.0)
            rank = dot(flags.astype(BF16), earlier)
            totals = jnp.sum(flags, axis=1, keepdims=True)
            before = jnp.zeros((1, 1), F32)
            starts = []
            for delta in range(8):
                starts.append(before)
                before = before + totals[delta : delta + 1, :]
            rank = rank + jnp.concatenate(starts, axis=0)
            base = (batches + 1).astype(F32) * BATCH + parity
            place = jnp.where(flags > 0.0, 2.0 * rank + base, place)
            most = jnp.maximum(most, before)
        needed = (2 * most.astype(jnp.int32) + BATCH - 1) // BATCH
        batches = batches + needed
        if kind == 0:
            batches = batches | 1
        ends.append(batches)
    task_rows = []
    for delta in range(8):
        pick = slice(delta, delta + 1)
        task_rows.append(
            jnp.where(
                row8 == 0,
                first[pick],
                jnp.where(
                    row8 == 1,
                    second[pick],
                    jnp.where(
                        row8 == 2, to_first[pick], jnp.where(row8 == 3, to_second[pick], 0.0)
                    ),
                ),
            ).astype(BF16)
        )
    tasks = jnp.concatenate(task_rows, axis=1)
    slot_row = rows((128, 128)).astype(F32)
    limit = (ends[1][0, 0] + 4) * BATCH

    def fill(m):
        chosen = jnp.concatenate(
            [
                jnp.where(place[delta : delta + 1, :] == slot_row + 128.0 * m, 1.0, 0.0).astype(BF16)
                for delta in range(8)
            ],
            axis=1,
        )
        part = dot_nt(tasks, chosen)
        part = part.astype(jnp.int32)
        part = jnp.where(row8 == 4, ends[0], jnp.where(row8 == 5, ends[1], part))
        list_ref[:, m * 128 : (m + 1) * 128] = part

    for m in range(4):
        fill(m)
    for m in range(4, LIST // 128):
        pl.when(m * 128 < limit)(functools.partial(fill, m))

    target = coupling_ref[...]
    reach = target - first_leaf + HALF
    swap = ((reach ^ row8) & 1) * (PAIRS // 2)
    entry = jnp.where(
        reach < HALF,
        LD + (reach >> 1) + swap,
        jnp.where(reach < HALF + LD, reach - HALF, LD + HALF + ((reach - HALF - LD) >> 1) + swap),
    )
    index_ref[0:8, :] = jnp.where(target >= 0, entry, TABLE - 1)
    index_ref[8:16, :] = jnp.where(target >= 0, reach, 0)


CHUNKS = 4


def leaf_kernel(
    x_any, p_ref, b_any, t_ref, near_ref, coupling_ref,
    next_any, prev_any, high_any, low_any, lev_any, root_ref, shape_ref,
    list_ref, count_ref, index_ref,
    send_next, send_prev, x_ref, b_ref, high_ref, low_ref, lev_ref, coef, pts, shapes, p8, sems,
):
    leaves = LD // CHUNKS
    copies = []
    for c in range(CHUNKS):
        span = slice(c * leaves * P_SIZE, (c + 1) * leaves * P_SIZE)
        part = slice(c * leaves, (c + 1) * leaves)
        copies.append(
            (
                pltpu.make_async_copy(x_any.at[:, span], x_ref.at[:, span], sems.at[c]),
                pltpu.make_async_copy(b_any.at[part], b_ref.at[part], sems.at[CHUNKS + c]),
            )
        )
    for pair in copies:
        for copy in pair:
            copy.start()
    origin = (device_index() * GROUPS).astype(F32)
    low32 = lanes((R, 128)) < K

    make_lists(near_ref, coupling_ref, list_ref, count_ref, index_ref)
    def leaf_pairs(m, carry):
        values = []
        for v in range(32):
            leaf = 32 * m + v
            x = x_ref[:, pl.ds(pl.multiple_of(leaf * P_SIZE, P_SIZE), P_SIZE)]
            weights = b_ref[leaf]
            values.append(dot_nt(x, jnp.concatenate([weights, weights], axis=0)))
        for v in range(32):
            high_ref[32 * m + v], low_ref[32 * m + v] = halves(values[v])
        for v in range(16):
            coef[16 * m + v] = jnp.where(low32, values[2 * v], values[2 * v + 1])
        return carry

    for c in range(CHUNKS):
        for copy in copies[c]:
            copy.wait()
        steps = leaves // 32
        lax.fori_loop(c * steps, (c + 1) * steps, leaf_pairs, 0)
    leaving = [
        pltpu.make_async_copy(high_ref, high_any, sems.at[2 * CHUNKS]),
        pltpu.make_async_copy(low_ref, low_any, sems.at[2 * CHUNKS + 1]),
    ]
    for copy in leaving:
        copy.start()

    for i in range(LD):
        for d in range(3):
            pts[d, i : i + 1, :] = p_ref[d : d + 1, i * P_SIZE : (i + 1) * P_SIZE]
    centers, squares = [], 0.0
    for d in range(3):
        coords = (pts[d] - origin if d == 2 else pts[d]) * SCALE
        center = jnp.sum(coords, axis=1, keepdims=True) * (1.0 / P_SIZE)
        centers.append(center)
        squares = squares + jnp.square(coords - center)
    radius = jnp.sqrt(jnp.max(squares, axis=1, keepdims=True))
    lane = lanes((LD, 128))
    shapes[0:LD, :] = jnp.where(
        lane == 0,
        centers[0],
        jnp.where(
            lane == 1,
            centers[1],
            jnp.where(lane == 2, centers[2], jnp.where(lane == 3, radius, 0.0)),
        ),
    )
    count = LD // 2
    for level in range(1, 8):
        source = LEVEL_OFFSETS[level - 1]
        joined = merge_shape_rows(
            shapes[pl.ds(source, count, stride=2), :],
            shapes[pl.ds(source + 1, count, stride=2), :],
        )
        shapes[pl.ds(LEVEL_OFFSETS[level], count), :] = joined
        count //= 2
    shape_rows = jnp.concatenate(
        [jnp.transpose(shapes[0:128, :])[0:8], jnp.transpose(shapes[128:256, :])[0:8]], axis=1
    )
    shape_ref[...] = shape_rows
    p8[...] = jnp.zeros((8, 512), F32)
    for send, first_pair, group in ((send_next, PAIRS // 2, GROUPS - 1), (send_prev, 0, 0)):

        def copy_pairs(m, carry):
            parts = [halves(coef[first_pair + 8 * m + v]) for v in range(8)]
            for v in range(8):
                send[8 * m + v], send[32 + 8 * m + v] = parts[v]
            return carry

        lax.fori_loop(0, PAIRS // 16, copy_pairs, 0)
        parts = thirds(shape_rows[:, 0:128])
        send[68] = jnp.concatenate(list(parts) + [jnp.zeros((8, 128), F32)], axis=0).astype(BF16)
        p8[0:3, :] = p_ref[:, group * 512 : group * 512 + 512]
        parts = thirds(p8[...])
        for k in range(4):
            send[64 + k] = x_ref[:, group * 512 + k * P_SIZE : group * 512 + (k + 1) * P_SIZE]
        for part in range(3):
            send[69 + part] = jnp.concatenate(
                [parts[part][:, k * P_SIZE : (k + 1) * P_SIZE] for k in range(4)], axis=0
            ).astype(BF16)
    for k, (send, out) in enumerate(((send_next, next_any), (send_prev, prev_any))):
        leaving.append(pltpu.make_async_copy(send, out, sems.at[2 * CHUNKS + 3 + k]))
        leaving[-1].start()

    t_high, t_low = halves(doubled_transfer(t_ref))
    pairs = coef[...]
    for level in range(1, 7):
        pairs = pair_lanes(merge_up(pairs, t_high, t_low))
        lev_ref[pl.ds(PAIR_OFFSETS[level], pairs.shape[0])] = pairs
    leaving.append(pltpu.make_async_copy(lev_ref, lev_any, sems.at[2 * CHUNKS + 2]))
    leaving[-1].start()
    root = merge_up(pairs, t_high, t_low)[0]

    low = lanes((R // 2, 128)) < K
    block = jnp.concatenate(
        [
            jnp.where(low, root[0 : R // 2], root[R // 2 : R]),
            jnp.broadcast_to(shapes[254:255, :], (8, 128)),
        ],
        axis=0,
    )
    root_ref[...] = jnp.broadcast_to(block[None], root_ref.shape)

    for copy in leaving:
        copy.wait()


def point_features(points8, origin_z):
    row = rows(points8.shape)
    center = jnp.where(row == 2, origin_z + 0.5, 1.0)
    v = jnp.where(row < 3, (points8 - center) * SCALE, 0.0)
    norm = jnp.sum(v * v, axis=0, keepdims=True)
    far = jnp.where(row == 3, norm, jnp.where(row == 4, 1.0, v))
    own = jnp.where(row == 3, 1.0, jnp.where(row == 4, norm, -2.0 * v))
    return far, own


def far_stack(value):
    first, second, third = thirds(value)
    none = jnp.zeros(value.shape, F32)
    return jnp.concatenate(
        [first, first, first, second, second, third, none, none], axis=0
    ).astype(BF16)


def own_stack(value):
    first, second, third = thirds(value)
    none = jnp.zeros(value.shape, F32)
    return jnp.concatenate(
        [first, second, third, first, second, first, none, none], axis=0
    ).astype(BF16)


def identity():
    return jnp.where(rows((128, 128)) == lanes((128, 128)), 1.0, 0.0).astype(BF16)


def near_kernel(
    list_ref, shape_ref, x_any, p_ref, lev_any,
    out_ref, couple_ref,
    x_ref, lev_ref, sems, p8, far_feat, own_feat, tile0, tile1,
):
    copies = [
        pltpu.make_async_copy(x_any, x_ref, sems.at[0]),
        pltpu.make_async_copy(lev_any, lev_ref, sems.at[1]),
    ]
    for copy in copies:
        copy.start()
    first_group = device_index() * GROUPS
    p8[...] = jnp.zeros(p8.shape, F32)
    eye = identity()

    def features(m, carry):
        loaded = [p_ref[:, pl.ds(pl.multiple_of((16 * m + v) * 512, 512), 512)] for v in range(16)]
        for v in range(16):
            p8[v, 0:3, :] = loaded[v]
        made = []
        for v in range(16):
            coords = p8[v]
            origin_z = (first_group + 16 * m + v).astype(F32)
            far, own = point_features(coords, origin_z)
            _, own_up = point_features(coords, origin_z + 1.0)
            _, own_down = point_features(coords, origin_z - 1.0)
            far = far_stack(far)
            parts = [far[:, k * P_SIZE : (k + 1) * P_SIZE] for k in range(4)]
            turned = dot_nt(eye, jnp.concatenate(parts, axis=0)).astype(BF16)
            made.append((turned, own_stack(own), own_stack(own_up), own_stack(own_down)))
        for v in range(16):
            g = 16 * m + v
            turned, own, own_up, own_down = made[v]
            far_feat[2 * g] = turned[:, 0:128]
            far_feat[2 * g + 1] = turned[:, 128:256]
            for k in range(4):
                part = slice(k * P_SIZE, (k + 1) * P_SIZE)
                own_feat[4 * g + k] = own[:, part]
                own_feat[LD + 4 * g + k] = own_up[:, part]
                own_feat[2 * LD + 4 * g + k] = own_down[:, part]
        return carry

    lax.fori_loop(0, GROUPS // 16, features, 0)

    for copy in copies:
        copy.wait()
    out_ref[...] = x_ref[...].astype(F32)
    for ref in (tile0, tile1):
        ref[...] = jnp.zeros(ref.shape, ref.dtype)

    mutual_phases = list_ref[4, 0] + 1
    all_phases = list_ref[5, 0] + 1
    low = lanes((128, 128)) < K

    def leaf_slice(i):
        return pl.ds(pl.multiple_of(i * P_SIZE, P_SIZE), P_SIZE)

    lane_u = lane_nodes()
    row_y, row_z = row_nodes()

    def phase(n, tile_new, tile_old, pairs, sides):
        far, own, sources, updates = [], [], [], []
        siblings = [jnp.minimum(pairs * n + v, PAIRS - 2) for v in range(pairs)]
        levels = [lev_ref[pair] for pair in siblings]
        for u in range(BATCH):
            k = (n + 1) * BATCH + u
            i, j = list_ref[0, k], list_ref[1, k]
            step = (j >> 2) - (i >> 2)
            variant = jnp.where(step < 0, 2, step) * LD
            far.append(far_feat[j >> 1])
            own.append(own_feat[variant + i])
        for u in range(BATCH):
            k = n * BATCH + u
            i, j = list_ref[0, k], list_ref[1, k]
            sources.append((x_ref[:, leaf_slice(j)], x_ref[:, leaf_slice(i)]))
        tiles = []
        for u in range(BATCH // 2):
            pick = jnp.where(low, far[2 * u], far[2 * u + 1])
            dist = dot(pick, block_diagonal(own[2 * u], own[2 * u + 1]))
            tiles.append(decay(dist).astype(BF16))
            weights = block_diagonal(tile_old[u, :, 0:128], tile_old[u, :, 128:256])
            to_i = dot(jnp.concatenate([sources[2 * u][0], sources[2 * u + 1][0]], axis=1), weights)
            to_j = None
            if sides == 2:
                to_j = dot_nt(
                    jnp.concatenate([sources[2 * u][1], sources[2 * u + 1][1]], axis=1), weights
                )
            for h in range(2):
                k = n * BATCH + 2 * u + h
                span = slice(h * 128, (h + 1) * 128)
                updates.append(
                    (
                        to_i[:, span] * list_ref[2, k].astype(F32),
                        to_j[:, span] * list_ref[3, k].astype(F32) if sides == 2 else None,
                    )
                )
        for pair, level in zip(siblings, levels):
            cluster = LD + 2 * pair
            left = [shape_ref[d, cluster] for d in range(4)]
            right = [shape_ref[d, cluster + 1] for d in range(4)]
            couple_ref[pair] = sibling_apply(
                sibling_tile(left, right, lane_u, row_y, row_z), level
            )
        for u in range(BATCH // 2):
            tile_new[u] = tiles[u]
        for u in range(BATCH):
            k = n * BATCH + u
            to_i = leaf_slice(list_ref[0, k])
            to_j = leaf_slice(list_ref[1, k])
            out_ref[:, to_i] += updates[u][0]
            if sides == 2:
                out_ref[:, to_j] += updates[u][1]

    def two_phases(pairs, sides, m, carry):
        phase(2 * m, tile0, tile1, pairs, sides)
        phase(2 * m + 1, tile1, tile0, pairs, sides)
        return carry

    rides = -(-(PAIRS - 1) // (2 * SIBLINGS))
    middle = mutual_phases // 2
    lax.fori_loop(0, rides, functools.partial(two_phases, SIBLINGS, 2), 0)
    lax.fori_loop(rides, middle, functools.partial(two_phases, 0, 2), 0)
    lax.fori_loop(middle, (all_phases + 1) // 2, functools.partial(two_phases, 0, 1), 0)


def tree_down(t_ref, root_ref, down_ref, couple, pairs_scr, shapes):
    lane_u = lane_nodes()
    row_y, row_z = row_nodes()

    doubled = doubled_transfer(t_ref)
    t_high, t_low = halves(doubled)
    w_high, w_low = down_weights(doubled)
    device = device_index()
    n = root_ref.shape[0]
    low = lanes((R, 128)) < K
    shift = lanes((1, 128)) == 2
    for k in range(n):
        shapes[k : k + 1, :] = root_ref[k, R // 2 : R // 2 + 1, :] + jnp.where(
            shift, (k * GROUPS) * SCALE, 0.0
        )
    for k in range(n // 2):
        left = root_ref[2 * k, 0 : R // 2, :]
        right = root_ref[2 * k + 1, 0 : R // 2, :]
        left = jnp.concatenate([left, pltpu.roll(left, K, 1)], axis=0)
        right = jnp.concatenate([pltpu.roll(right, K, 1), right], axis=0)
        pairs_scr[k] = jnp.where(low, left, right)
    source, count, pair_source = 0, n // 2, 0
    levels = []
    while count >= 1:
        levels.append((source, pair_source))
        if count > 1:
            pairs = pair_lanes(merge_up(pairs_scr[pl.ds(pair_source, count)], t_high, t_low))
            pairs_scr[pl.ds(pair_source + count, count // 2)] = pairs
            joined = merge_shape_rows(
                shapes[pl.ds(source, count, stride=2), :],
                shapes[pl.ds(source + 1, count, stride=2), :],
            )
            shapes[pl.ds(source + 2 * count, count), :] = joined
        source += 2 * count
        pair_source += count
        count //= 2
    couples = []
    for level, (source, pair_source) in enumerate(levels):
        pair = device >> (level + 1)
        left_row = shapes[pl.ds(source + 2 * pair, 1), :]
        right_row = shapes[pl.ds(source + 2 * pair + 1, 1), :]
        left = [jnp.broadcast_to(left_row[:, d : d + 1], (8, 128)) for d in range(4)]
        right = [jnp.broadcast_to(right_row[:, d : d + 1], (8, 128)) for d in range(4)]
        tile = sibling_tile(left, right, lane_u, row_y, row_z)
        couples.append(sibling_apply(tile, pairs_scr[pair_source + pair]))
    incoming = None
    for level in reversed(range(len(levels))):
        value = couples[level]
        if incoming is not None:
            pushed = push_down(incoming[None], w_high, w_low)
            value = value + (pushed[0] + pushed[1])
        side = (device >> level) & 1
        keep_low = jnp.where(low, 1, 0) == (1 - side)
        incoming = jnp.where(keep_low, value, 0.0)
    pushed = push_down(incoming[None], w_high, w_low)
    value = couple[pl.ds(PAIR_OFFSETS[6], 1)] + (pushed[0:1] + pushed[1:2])
    for level in range(5, 0, -1):
        n = PAIRS >> level
        value = couple[pl.ds(PAIR_OFFSETS[level], n)] + push_down(value, w_high, w_low)
    down_ref[...] = push_down(value, w_high, w_low)


UNIT = 8


def couple_leaves(
    entries, shape_ref, prev_ref, next_ref, table_copies, leaf_couple,
    shape_tab, high_tab, low_tab, halo_rows, halo_shape, sems,
    tiles0, lhs0, tiles1, lhs1,
):
    copies = []
    for k, ref in enumerate((prev_ref, next_ref)):
        parts = ref[68].astype(F32)
        halo_rows[k] = parts[0:8] + parts[8:16] + parts[16:24]
        copies.append(pltpu.make_async_copy(halo_rows.at[k], halo_shape.at[k], sems.at[k]))
    for copy in copies:
        copy.start()
    low32 = lanes((R, 128)) < K
    lane_u = lane_nodes()
    row8 = rows((8, 128))
    low8 = lanes((8, 128)) < K

    def shape_rows(read, k, shift):
        return jnp.where(
            row8 == 0,
            read(0, k),
            jnp.where(row8 == 1, read(1, k), jnp.where(row8 == 2, read(2, k) + shift, read(3, k))),
        )

    def own_nodes(m, carry):
        shape_tab[HALF + m] = shape_rows(lambda d, k: shape_ref[d, k], m, 0.0)
        return carry

    lax.fori_loop(0, LD, own_nodes, 0, unroll=8)
    for copy in copies:
        copy.wait()
    def halo_pairs(m, carry):
        loaded = [
            (tab, LD + side * HALF + 4 * m + v, ref[offset + 4 * m + v])
            for side, ref in enumerate((prev_ref, next_ref))
            for tab, offset in ((high_tab, 0), (low_tab, 32))
            for v in range(4)
        ]
        turned = [pltpu.roll(pair.astype(F32), K, 1).astype(BF16) for _, _, pair in loaded]
        for side in range(2):
            source = HALF if side == 0 else 0
            place = 0 if side == 0 else HALF + LD
            shift = (2.0 * side - 1.0) * GROUPS * SCALE
            for v in range(8):
                shape_tab[place + 8 * m + v] = shape_rows(
                    lambda d, k: halo_shape[side, d, k], source + 8 * m + v, shift
                )
        for (tab, pair, value), other in zip(loaded, turned):
            tab[pair] = value
            tab[PAIRS // 2 + pair] = other
        return carry

    lax.fori_loop(0, PAIRS // 8, halo_pairs, 0)
    high_tab[TABLE - 1] = jnp.zeros((R, 128), BF16)
    low_tab[TABLE - 1] = jnp.zeros((R, 128), BF16)
    for copy in table_copies:
        copy.wait()

    row_y, row_z = row_nodes()

    def couple_tiles(pair, u, tiles, lhs):
        leaves = (2 * pair, 2 * pair + 1)
        for q in range(4):
            span = slice(q * 128, (q + 1) * 128)
            for h in range(2):
                e0, e1 = entries[2 * q, leaves[h]], entries[2 * q + 1, leaves[h]]
                lhs[u, h * R : (h + 1) * R, span] = jnp.where(low32, high_tab[e0], high_tab[e1])
                lhs[u, (2 + h) * R : (3 + h) * R, span] = jnp.where(
                    low32, low_tab[e0], low_tab[e1]
                )
        own = jnp.where(low8, shape_tab[HALF + leaves[0]], shape_tab[HALF + leaves[1]])
        radius = jnp.broadcast_to(own[3:4], (8, 128))
        own = [jnp.broadcast_to(own[d : d + 1], (8, 128)) + radius * lane_u[d] for d in range(3)]
        fars = []
        for s in range(8):
            e0, e1 = entries[8 + s, leaves[0]], entries[8 + s, leaves[1]]
            fars.append(jnp.where(low8, shape_tab[e0], shape_tab[e1]))
        for s, far in enumerate(fars):
            reach = jnp.broadcast_to(far[3:4], (8, 128))
            gap = [own[d] - jnp.broadcast_to(far[d : d + 1], (8, 128)) for d in range(3)]
            tile = tile_from_axes(
                [jnp.square(gap[0] - reach * NODE[b]) for b in range(4)],
                [jnp.square(gap[1] - reach * row_y[h]) for h in range(2)],
                jnp.square(gap[2] - reach * row_z),
            )
            high, low = halves(tile)
            tiles[u, s * K : (s + 1) * K, 0:128] = high
            tiles[u, s * K : (s + 1) * K, 128:256] = low

    def couple_apply(u, tiles, lhs):
        both = dot(lhs[u], tiles[u])
        both = both[0 : 2 * R, 0:128] + (both[2 * R : 4 * R, 0:128] + both[0 : 2 * R, 128:256])
        return jnp.where(low32, both[0:R], both[R : 2 * R])

    def couple_phase(n, new, old):
        for u in range(UNIT):
            couple_tiles(n * UNIT + u, u, *new)
            leaf_couple[n * UNIT + u] = couple_apply(u, *old)

    buffers = ((tiles0, lhs0), (tiles1, lhs1))
    for ref in buffers[1]:
        ref[...] = jnp.zeros(ref.shape, ref.dtype)

    def couple_two(m, carry):
        couple_phase(2 * m, buffers[0], buffers[1])
        couple_phase(2 * m + 1, buffers[1], buffers[0])
        return carry

    lax.fori_loop(0, PAIRS // UNIT // 2, couple_two, 0)
    for u in range(UNIT):
        leaf_couple[PAIRS + u] = couple_apply(u, *buffers[1])


def finish_leaves(b_ref, down_ref, leaf_couple, out_ref, border, out_any, sems):
    def finish(m, carry):
        values = []
        for v in range(16):
            c = 16 * m + v
            value = (down_ref[c] + leaf_couple[c + UNIT]).astype(BF16)
            span = pl.ds(pl.multiple_of(c * 256, 256), 256)
            values.append(
                (
                    span,
                    out_ref[:, span]
                    + dot(value, block_diagonal(b_ref[2 * c], b_ref[2 * c + 1])),
                )
            )
        for span, value in values:
            out_ref[:, span] = value
        return carry

    parts = PAIRS // 16
    leaving = []
    for c in range(parts):
        lax.fori_loop(c, c + 1, finish, 0)
        for side, (part, group) in enumerate(((0, 0), (parts - 1, GROUPS - 1))):
            if c == part:
                for i in range(4):
                    leaf = 4 * group + i
                    out_ref[:, leaf * P_SIZE : (leaf + 1) * P_SIZE] += border[4 * side + i]
        span = slice(c * 16 * 256, (c + 1) * 16 * 256)
        leaving.append(
            pltpu.make_async_copy(out_ref.at[:, span], out_any.at[:, span], sems.at[c])
        )
        leaving[c].start()
    for copy in leaving:
        copy.wait()


def border_blocks(counts, p_ref, prev_ref, next_ref, border, p8, coords):
    device = device_index()

    p8[...] = jnp.zeros(p8.shape, F32)
    eye = identity()
    sides = ((prev_ref, 0), (next_ref, GROUPS - 1))
    for side, (halo_ref, group) in enumerate(sides):
        p8[side, 0:3, :] = p_ref[:, group * 512 : group * 512 + 512]
        coords[side] = halo_ref[69].astype(F32) + halo_ref[70].astype(F32) + halo_ref[71].astype(F32)

    sums = [[0.0] * 4, [0.0] * 4]
    for k in range(4):
        loaded = [
            (halo_ref[64 + k], coords[side, 8 * k : 8 * k + 8, :], p8[side])
            for side, (halo_ref, _) in enumerate(sides)
        ]
        for side, (_, group) in enumerate(sides):
            x_far, far, own = loaded[side]
            origin_z = (device * GROUPS + group).astype(F32)
            _, own = point_features(own, origin_z)
            far, _ = point_features(far, origin_z)
            far = dot_nt(eye, far_stack(far)).astype(BF16)
            tiles = decay(dot(far, own_stack(own))).astype(BF16)
            products = dot(x_far, tiles)
            for i in range(4):
                delta = (4 + i - k) if side == 0 else (4 + k - i)
                weight = counts[8 * (1 - side) + delta, 4 * group + i]
                sums[side][i] = sums[side][i] + products[:, i * P_SIZE : (i + 1) * P_SIZE] * weight
    for side in range(2):
        for i in range(4):
            border[4 * side + i] = sums[side][i]


def tree_kernel(
    t_any, root_any, couple_any, down_ref, t_ref, root_ref, couple, pairs_scr, shapes, sems
):
    moves = ((t_any, t_ref), (root_any, root_ref), (couple_any, couple))
    copies = [pltpu.make_async_copy(a, b, sems.at[k]) for k, (a, b) in enumerate(moves)]
    for copy in copies:
        copy.start()
    for copy in copies:
        copy.wait()
    tree_down(t_ref, root_ref, down_ref, couple, pairs_scr, shapes)


def final_kernel(
    entries, shape_ref, counts,
    prev_any, next_any, p_any, high_any, low_any, b_any, near_any, down_any,
    out_any,
    out_ref, prev_ref, next_ref, p_ref, b_ref, down, leaf_couple,
    shape_tab, high_tab, low_tab, halo_rows, halo_shape,
    tiles0, lhs0, tiles1, lhs1, p8, coords, border, sems, halo_sems, out_sems,
):
    moves = (
        (prev_any, prev_ref),
        (next_any, next_ref),
        (p_any, p_ref),
        (high_any, high_tab.at[0:LD]),
        (low_any, low_tab.at[0:LD]),
        (b_any, b_ref),
        (near_any, out_ref),
        (down_any, down),
    )
    copies = [pltpu.make_async_copy(a, b, sems.at[k]) for k, (a, b) in enumerate(moves)]
    for copy in copies:
        copy.start()
    for copy in copies[0:3]:
        copy.wait()
    border_blocks(counts, p_ref, prev_ref, next_ref, border, p8, coords)
    couple_leaves(
        entries, shape_ref, prev_ref, next_ref, copies[3:5], leaf_couple,
        shape_tab, high_tab, low_tab, halo_rows, halo_shape, halo_sems,
        tiles0, lhs0, tiles1, lhs1,
    )
    for copy in copies[5:]:
        copy.wait()
    finish_leaves(b_ref, down, leaf_couple, out_ref, border, out_any, out_sems)


def shaped(*shape, dtype=F32):
    return jax.ShapeDtypeStruct(shape, dtype)


def vmem():
    return pl.BlockSpec(memory_space=pltpu.VMEM)


def smem():
    return pl.BlockSpec(memory_space=pltpu.SMEM)


def anywhere():
    return pl.BlockSpec(memory_space=pl.ANY)


PARAMS = pltpu.CompilerParams(vmem_limit_bytes=VMEM_LIMIT)


def per_device(charges, points, basis, transfer, near_list, coupling_list):
    near_rows = near_list.T
    coupling_rows = coupling_list.T
    devices = lax.axis_size("sub") * lax.axis_size("leaf")
    send_next, send_prev, high, low, lev, root, shapes, tasks, counts, entries = pl.pallas_call(
        leaf_kernel,
        name="leaf_up",
        out_shape=(
            shaped(SEND, R, 128, dtype=BF16),
            shaped(SEND, R, 128, dtype=BF16),
            shaped(LD, R, 128, dtype=BF16),
            shaped(LD, R, 128, dtype=BF16),
            shaped(PAIRS - 1, R, 128),
            shaped(devices, R // 2 + 8, 128),
            shaped(8, 256),
            shaped(8, LIST, dtype=jnp.int32),
            shaped(16, 128),
            shaped(16, 128, dtype=jnp.int32),
        ),
        in_specs=[anywhere(), vmem(), anywhere(), vmem(), vmem(), vmem()],
        out_specs=[anywhere()] * 5 + [vmem()] * 5,
        scratch_shapes=[
            pltpu.VMEM((SEND, R, 128), BF16),
            pltpu.VMEM((SEND, R, 128), BF16),
            pltpu.VMEM((R, LD * P_SIZE), BF16),
            pltpu.VMEM((LD, K, P_SIZE), BF16),
            pltpu.VMEM((LD, R, 128), BF16),
            pltpu.VMEM((LD, R, 128), BF16),
            pltpu.VMEM((PAIRS - 1, R, 128), F32),
            pltpu.VMEM((PAIRS, R, 128), F32),
            pltpu.VMEM((3, LD, 128), F32),
            pltpu.VMEM((256, 128), F32),
            pltpu.VMEM((8, 512), F32),
            pltpu.SemaphoreType.DMA((2 * CHUNKS + 5,)),
        ],
        compiler_params=PARAMS,
    )(charges, points, basis, transfer, near_rows, coupling_rows)

    roots = lax.all_to_all(root, AXES, 0, 0, tiled=True)
    forward = [(i, i + 1) for i in range(devices - 1)]
    backward = [(i + 1, i) for i in range(devices - 1)]
    from_prev = lax.ppermute(send_next, AXES, forward)
    from_next = lax.ppermute(send_prev, AXES, backward)

    near, couple = pl.pallas_call(
        near_kernel,
        name="near_field",
        out_shape=(shaped(R, LD * P_SIZE), shaped(PAIRS - 1, R, 128)),
        in_specs=[smem(), smem(), anywhere(), vmem(), anywhere()],
        out_specs=[vmem()] * 2,
        scratch_shapes=[
            pltpu.VMEM((R, LD * P_SIZE), BF16),
            pltpu.VMEM((PAIRS - 1, R, 128), F32),
            pltpu.SemaphoreType.DMA((2,)),
            pltpu.VMEM((16, 8, 512), F32),
            pltpu.VMEM((PAIRS, P_SIZE, 2 * FEATS), BF16),
            pltpu.VMEM((3 * LD, FEATS, P_SIZE), BF16),
            pltpu.VMEM((BATCH // 2, 128, 256), BF16),
            pltpu.VMEM((BATCH // 2, 128, 256), BF16),
        ],
        compiler_params=PARAMS,
        cost_estimate=pl.CostEstimate(
            flops=2 * 460 * 128 * 128 * 128, bytes_accessed=4 << 20, transcendentals=460 * 32768
        ),
    )(tasks, shapes, charges, points, lev)

    near, roots = lax.optimization_barrier((near, roots))
    down = pl.pallas_call(
        tree_kernel,
        name="tree_down",
        out_shape=shaped(PAIRS, R, 128),
        in_specs=[anywhere()] * 3,
        out_specs=vmem(),
        scratch_shapes=[
            pltpu.VMEM((2, K, K), F32),
            pltpu.VMEM((devices, R // 2 + 8, 128), F32),
            pltpu.VMEM((PAIRS - 1, R, 128), F32),
            pltpu.VMEM((devices, R, 128), F32),
            pltpu.VMEM((2 * devices, 128), F32),
            pltpu.SemaphoreType.DMA((3,)),
        ],
        compiler_params=PARAMS,
    )(transfer, roots, couple)
    from_prev, from_next, down = lax.optimization_barrier((from_prev, from_next, down))

    stages = [
        pltpu.VMEM((UNIT, 512, 256), BF16),
        pltpu.VMEM((UNIT, 4 * R, 512), BF16),
    ]
    return pl.pallas_call(
        final_kernel,
        name="couple_finish",
        out_shape=shaped(R, LD * P_SIZE),
        in_specs=[smem()] * 3 + [anywhere()] * 8,
        out_specs=anywhere(),
        scratch_shapes=[
            pltpu.VMEM((R, LD * P_SIZE), F32),
            pltpu.VMEM((SEND, R, 128), BF16),
            pltpu.VMEM((SEND, R, 128), BF16),
            pltpu.VMEM((3, LD * P_SIZE), F32),
            pltpu.VMEM((LD, K, P_SIZE), BF16),
            pltpu.VMEM((PAIRS, R, 128), F32),
            pltpu.VMEM((PAIRS + UNIT, R, 128), F32),
            pltpu.VMEM((2 * LD, 8, 128), F32),
            pltpu.VMEM((TABLE, R, 128), BF16),
            pltpu.VMEM((TABLE, R, 128), BF16),
            pltpu.VMEM((2, 8, 128), F32),
            pltpu.SMEM((2, 8, 128), F32),
        ]
        + stages
        + stages
        + [
            pltpu.VMEM((2, 8, 512), F32),
            pltpu.VMEM((2, R, 128), F32),
            pltpu.VMEM((8, R, 128), F32),
            pltpu.SemaphoreType.DMA((8,)),
            pltpu.SemaphoreType.DMA((2,)),
            pltpu.SemaphoreType.DMA((PAIRS // 16,)),
        ],
        compiler_params=PARAMS,
    )(
        entries, shapes, counts,
        from_prev, from_next, points, high, low, basis, near, down,
    )


def solution(mesh):
    in_specs = (
        P(None, AXES),
        P(None, AXES),
        P(AXES, None, None),
        P(),
        P(AXES, None),
        P(AXES, None),
    )
    return jax.shard_map(
        per_device, mesh=mesh, in_specs=in_specs, out_specs=P(None, AXES), check_vma=False
    )
```

```python
import functools
import math

import jax
import jax.numpy as jnp
from jax import lax
from jax.experimental import pallas as pl
from jax.experimental.pallas import tpu as pltpu
from jax.sharding import PartitionSpec as P

P_SIZE = 128
K = 64
R = 32
LD = 128
PAIRS = LD // 2
GROUPS = LD // 4
TABLE = 257
HALF = LD // 2
NEAR_REACH = 8
FEATS = 64
BATCH = 16
SIBLINGS = 6
LIST = 1536
SEND = 72
SCALE = 0.5 * math.log2(math.e)
NODE = [math.cos((2 * a + 1) * math.pi / 8) for a in range(4)]
AXES = ("leaf", "sub")
F32 = jnp.float32
BF16 = jnp.bfloat16
NT = (((1,), (1,)), ((), ()))
TINY = 1e-30
VMEM_LIMIT = 64 * 1024 * 1024


def lanes(shape):
    return lax.broadcasted_iota(jnp.int32, shape, len(shape) - 1)


def rows(shape):
    return lax.broadcasted_iota(jnp.int32, shape, len(shape) - 2)


def dot(a, b):
    return jnp.dot(a, b, preferred_element_type=F32)


def dot_nt(a, b):
    return lax.dot_general(a, b, NT, preferred_element_type=F32)


def halves(value):
    high = value.astype(BF16)
    return high, (value - high.astype(F32)).astype(BF16)


def thirds(value):
    first = value.astype(BF16).astype(F32)
    rest = value - first
    second = rest.astype(BF16).astype(F32)
    return first, second, rest - second


def unit_node(index):
    return jnp.where(
        index == 0,
        NODE[0],
        jnp.where(index == 1, NODE[1], jnp.where(index == 2, NODE[2], NODE[3])),
    ).astype(F32)


def lane_nodes():
    b = lanes((8, 128)) & 63
    return [unit_node(b >> 4), unit_node((b >> 2) & 3), unit_node(b & 3)]


def row_nodes():
    r = rows((8, 128))
    return [unit_node(r >> 2), unit_node((r >> 2) + 2)], unit_node(r & 3)


def decay(t):
    return decay_positive(jnp.maximum(t, TINY))


def decay_positive(t):
    return jnp.exp2(-(t * lax.rsqrt(t)))


def tile_from_axes(x_sq, y_sq, z_sq):
    z_sq = z_sq + TINY
    yz = [y_sq[0] + z_sq, y_sq[1] + z_sq]
    return decay_positive(jnp.concatenate([x_sq[k // 2] + yz[k % 2] for k in range(8)], axis=0))


def doubled_transfer(t_ref):
    flat = t_ref[...].reshape(2 * K, K)
    return jnp.concatenate([flat, flat], axis=1)


def device_index():
    return lax.axis_index("leaf") * lax.axis_size("sub") + lax.axis_index("sub")


def merge_up(pairs, t_high, t_low):
    n = pairs.shape[0]
    high, low = halves(pairs.reshape(n * R, 128))
    out = dot(high, jnp.concatenate([t_high, t_low], axis=1))
    out = out[:, 0:128] + out[:, 128:256] + dot(low, t_high)
    return out.reshape(n, R, 128)


def pair_lanes(clusters):
    n = clusters.shape[0]
    split = clusters.reshape(n // 2, 2, R, 128)
    return jnp.where(lanes((1, R, 128)) < K, split[:, 0], split[:, 1])


def down_weights(doubled):
    low = lanes(doubled.shape) < K
    both = jnp.concatenate(
        [jnp.where(low, doubled, 0.0), jnp.where(low, 0.0, doubled)], axis=0
    )
    return halves(both)


def push_down(value, w_high, w_low):
    n = value.shape[0]
    high, low = halves(value.reshape(n * R, 128))
    out = dot_nt(high, w_high) + dot_nt(high, w_low) + dot_nt(low, w_high)
    out = out.reshape(n, R, 256)
    return jnp.stack([out[:, :, 0:128], out[:, :, 128:256]], axis=1).reshape(2 * n, R, 128)


def merge_shape_rows(left, right):
    lane = lanes(left.shape)
    sep = left - right
    gap = jnp.sqrt(jnp.sum(jnp.where(lane < 3, sep * sep, 0.0), axis=1, keepdims=True))
    radius = jnp.maximum(left, right) + 0.5 * gap
    return jnp.where(lane == 3, radius, jnp.where(lane < 3, 0.5 * (left + right), 0.0))


def sibling_tile(left, right, lane_u, row_y, row_z):
    low = lanes((8, 128)) < K
    alpha = jnp.where(low, left[3], right[3])
    beta = jnp.where(low, right[3], left[3])
    base = [jnp.where(low, left[d] - right[d], right[d] - left[d]) - beta * lane_u[d] for d in range(3)]
    x_sq = [jnp.square(base[0] + alpha * NODE[a]) for a in range(4)]
    y_sq = [jnp.square(base[1] + alpha * row_y[h]) for h in range(2)]
    z_sq = jnp.square(base[2] + alpha * row_z)
    return tile_from_axes(x_sq, y_sq, z_sq)


def sibling_apply(tile, pair):
    low = lanes((K, 128)) < K
    zero = jnp.zeros((K, 128), BF16)
    weights = []
    for part in halves(tile):
        weights.append(
            jnp.concatenate([jnp.where(low, part, zero), jnp.where(low, zero, part)], axis=0)
        )
    high, low_part = halves(pltpu.roll(pair, K, 1))
    out = dot_nt(high, jnp.concatenate(weights, axis=0))
    return out[:, 0:128] + out[:, 128:256] + dot_nt(low_part, weights[0])


LEVEL_OFFSETS = [0, 128, 192, 224, 240, 248, 252, 254]
PAIR_OFFSETS = [0, 0, 32, 48, 56, 60, 62]


def block_diagonal(left, right):
    zero = jnp.zeros(left.shape, left.dtype)
    return jnp.concatenate(
        [jnp.concatenate([left, zero], axis=1), jnp.concatenate([zero, right], axis=1)], axis=0
    )


def make_lists(near_ref, coupling_ref, list_ref, count_ref, index_ref):
    first_leaf = device_index() * LD
    lane8 = lanes((8, 128))
    row8 = rows((8, 128))
    offset = jnp.where(near_ref[...] >= 0, near_ref[...] - first_leaf - lane8, 1000)

    def slots_at(delta):
        return jnp.sum(jnp.where(offset == delta, 1.0, 0.0), axis=0, keepdims=True)

    forward = jnp.concatenate([slots_at(delta) for delta in range(8)], axis=0)
    reverse = jnp.concatenate(
        [jnp.zeros((1, 128), F32)] + [slots_at(-delta) for delta in range(1, 8)], axis=0
    )
    count_ref[0:8, :] = forward
    count_ref[8:16, :] = reverse
    backward = jnp.concatenate(
        [jnp.zeros((1, 128), F32)]
        + [pltpu.roll(reverse[delta : delta + 1, :], 128 - delta, 1) for delta in range(1, 8)],
        axis=0,
    )
    wanted = (lane8 + row8 < LD) & (forward + backward > 0.0)
    mutual = (forward > 0.0) & (backward > 0.0)
    turned = ((row8 == 1) & ((lane8 & 3) == 2) & mutual) | (
        (forward == 0.0) & (backward > 0.0)
    )
    leaf = lane8.astype(F32)
    other = leaf + row8.astype(F32)
    first = jnp.where(turned, other, leaf)
    second = jnp.where(turned, leaf, other)
    to_first = jnp.where(turned, backward, forward)
    to_second = jnp.where(turned, forward, backward)
    odd = jnp.where(turned, lane8, lane8 + row8) & 1
    earlier = jnp.where(rows((128, 128)) < lanes((128, 128)), 1.0, 0.0).astype(BF16)
    place = jnp.full((8, 128), -1.0, F32)
    batches = jnp.zeros((1, 1), jnp.int32)
    ends = []
    for kind in range(2):
        most = jnp.zeros((1, 1), F32)
        for parity in range(2):
            chosen = wanted & (odd == parity) & (mutual if kind == 0 else jnp.logical_not(mutual))
            flags = jnp.where(chosen, 1.0, 0.0)
            rank = dot(flags.astype(BF16), earlier)
            totals = jnp.sum(flags, axis=1, keepdims=True)
            before = jnp.zeros((1, 1), F32)
            starts = []
            for delta in range(8):
                starts.append(before)
                before = before + totals[delta : delta + 1, :]
            rank = rank + jnp.concatenate(starts, axis=0)
            base = (batches + 1).astype(F32) * BATCH + parity
            place = jnp.where(flags > 0.0, 2.0 * rank + base, place)
            most = jnp.maximum(most, before)
        needed = (2 * most.astype(jnp.int32) + BATCH - 1) // BATCH
        batches = batches + needed
        if kind == 0:
            batches = batches | 1
        ends.append(batches)
    task_rows = []
    for delta in range(8):
        pick = slice(delta, delta + 1)
        task_rows.append(
            jnp.where(
                row8 == 0,
                first[pick],
                jnp.where(
                    row8 == 1,
                    second[pick],
                    jnp.where(
                        row8 == 2, to_first[pick], jnp.where(row8 == 3, to_second[pick], 0.0)
                    ),
                ),
            ).astype(BF16)
        )
    tasks = jnp.concatenate(task_rows, axis=1)
    slot_row = rows((128, 128)).astype(F32)
    limit = (ends[1][0, 0] + 4) * BATCH

    def fill(m):
        chosen = jnp.concatenate(
            [
                jnp.where(place[delta : delta + 1, :] == slot_row + 128.0 * m, 1.0, 0.0).astype(BF16)
                for delta in range(8)
            ],
            axis=1,
        )
        part = dot_nt(tasks, chosen)
        part = part.astype(jnp.int32)
        part = jnp.where(row8 == 4, ends[0], jnp.where(row8 == 5, ends[1], part))
        list_ref[:, m * 128 : (m + 1) * 128] = part

    for m in range(4):
        fill(m)
    for m in range(4, LIST // 128):
        pl.when(m * 128 < limit)(functools.partial(fill, m))

    target = coupling_ref[...]
    reach = target - first_leaf + HALF
    swap = ((reach ^ row8) & 1) * (PAIRS // 2)
    entry = jnp.where(
        reach < HALF,
        LD + (reach >> 1) + swap,
        jnp.where(reach < HALF + LD, reach - HALF, LD + HALF + ((reach - HALF - LD) >> 1) + swap),
    )
    index_ref[0:8, :] = jnp.where(target >= 0, entry, TABLE - 1)
    index_ref[8:16, :] = jnp.where(target >= 0, reach, 0)


CHUNKS = 4


def leaf_kernel(
    x_any, p_ref, b_any, t_ref, near_ref, coupling_ref,
    next_any, prev_any, high_any, low_any, lev_any, root_ref, shape_ref,
    list_ref, count_ref, index_ref,
    send_next, send_prev, x_ref, b_ref, high_ref, low_ref, lev_ref, coef, pts, shapes, p8, sems,
):
    leaves = LD // CHUNKS
    copies = []
    for c in range(CHUNKS):
        span = slice(c * leaves * P_SIZE, (c + 1) * leaves * P_SIZE)
        part = slice(c * leaves, (c + 1) * leaves)
        copies.append(
            (
                pltpu.make_async_copy(x_any.at[:, span], x_ref.at[:, span], sems.at[c]),
                pltpu.make_async_copy(b_any.at[part], b_ref.at[part], sems.at[CHUNKS + c]),
            )
        )
    for pair in copies:
        for copy in pair:
            copy.start()
    origin = (device_index() * GROUPS).astype(F32)
    low32 = lanes((R, 128)) < K

    make_lists(near_ref, coupling_ref, list_ref, count_ref, index_ref)
    def leaf_pairs(m, carry):
        values = []
        for v in range(32):
            leaf = 32 * m + v
            x = x_ref[:, pl.ds(pl.multiple_of(leaf * P_SIZE, P_SIZE), P_SIZE)]
            weights = b_ref[leaf]
            values.append(dot_nt(x, jnp.concatenate([weights, weights], axis=0)))
        for v in range(32):
            high_ref[32 * m + v], low_ref[32 * m + v] = halves(values[v])
        for v in range(16):
            coef[16 * m + v] = jnp.where(low32, values[2 * v], values[2 * v + 1])
        return carry

    for c in range(CHUNKS):
        for copy in copies[c]:
            copy.wait()
        steps = leaves // 32
        lax.fori_loop(c * steps, (c + 1) * steps, leaf_pairs, 0)
    leaving = [
        pltpu.make_async_copy(high_ref, high_any, sems.at[2 * CHUNKS]),
        pltpu.make_async_copy(low_ref, low_any, sems.at[2 * CHUNKS + 1]),
    ]
    for copy in leaving:
        copy.start()

    for i in range(LD):
        for d in range(3):
            pts[d, i : i + 1, :] = p_ref[d : d + 1, i * P_SIZE : (i + 1) * P_SIZE]
    centers, squares = [], 0.0
    for d in range(3):
        coords = (pts[d] - origin if d == 2 else pts[d]) * SCALE
        center = jnp.sum(coords, axis=1, keepdims=True) * (1.0 / P_SIZE)
        centers.append(center)
        squares = squares + jnp.square(coords - center)
    radius = jnp.sqrt(jnp.max(squares, axis=1, keepdims=True))
    lane = lanes((LD, 128))
    shapes[0:LD, :] = jnp.where(
        lane == 0,
        centers[0],
        jnp.where(
            lane == 1,
            centers[1],
            jnp.where(lane == 2, centers[2], jnp.where(lane == 3, radius, 0.0)),
        ),
    )
    count = LD // 2
    for level in range(1, 8):
        source = LEVEL_OFFSETS[level - 1]
        joined = merge_shape_rows(
            shapes[pl.ds(source, count, stride=2), :],
            shapes[pl.ds(source + 1, count, stride=2), :],
        )
        shapes[pl.ds(LEVEL_OFFSETS[level], count), :] = joined
        count //= 2
    shape_rows = jnp.concatenate(
        [jnp.transpose(shapes[0:128, :])[0:8], jnp.transpose(shapes[128:256, :])[0:8]], axis=1
    )
    shape_ref[...] = shape_rows
    p8[...] = jnp.zeros((8, 512), F32)
    for send, first_pair, group in ((send_next, PAIRS // 2, GROUPS - 1), (send_prev, 0, 0)):

        def copy_pairs(m, carry):
            parts = [halves(coef[first_pair + 8 * m + v]) for v in range(8)]
            for v in range(8):
                send[8 * m + v], send[32 + 8 * m + v] = parts[v]
            return carry

        lax.fori_loop(0, PAIRS // 16, copy_pairs, 0)
        parts = thirds(shape_rows[:, 0:128])
        send[68] = jnp.concatenate(list(parts) + [jnp.zeros((8, 128), F32)], axis=0).astype(BF16)
        p8[0:3, :] = p_ref[:, group * 512 : group * 512 + 512]
        parts = thirds(p8[...])
        for k in range(4):
            send[64 + k] = x_ref[:, group * 512 + k * P_SIZE : group * 512 + (k + 1) * P_SIZE]
        for part in range(3):
            send[69 + part] = jnp.concatenate(
                [parts[part][:, k * P_SIZE : (k + 1) * P_SIZE] for k in range(4)], axis=0
            ).astype(BF16)
    for k, (send, out) in enumerate(((send_next, next_any), (send_prev, prev_any))):
        leaving.append(pltpu.make_async_copy(send, out, sems.at[2 * CHUNKS + 3 + k]))
        leaving[-1].start()

    t_high, t_low = halves(doubled_transfer(t_ref))
    pairs = coef[...]
    for level in range(1, 7):
        pairs = pair_lanes(merge_up(pairs, t_high, t_low))
        lev_ref[pl.ds(PAIR_OFFSETS[level], pairs.shape[0])] = pairs
    leaving.append(pltpu.make_async_copy(lev_ref, lev_any, sems.at[2 * CHUNKS + 2]))
    leaving[-1].start()
    root = merge_up(pairs, t_high, t_low)[0]

    low = lanes((R // 2, 128)) < K
    block = jnp.concatenate(
        [
            jnp.where(low, root[0 : R // 2], root[R // 2 : R]),
            jnp.broadcast_to(shapes[254:255, :], (8, 128)),
        ],
        axis=0,
    )
    root_ref[...] = jnp.broadcast_to(block[None], root_ref.shape)

    for copy in leaving:
        copy.wait()


def point_features(points8, origin_z):
    row = rows(points8.shape)
    center = jnp.where(row == 2, origin_z + 0.5, 1.0)
    v = jnp.where(row < 3, (points8 - center) * SCALE, 0.0)
    norm = jnp.sum(v * v, axis=0, keepdims=True)
    far = jnp.where(row == 3, norm, jnp.where(row == 4, 1.0, v))
    own = jnp.where(row == 3, 1.0, jnp.where(row == 4, norm, -2.0 * v))
    return far, own


def far_stack(value):
    first, second, third = thirds(value)
    none = jnp.zeros(value.shape, F32)
    return jnp.concatenate(
        [first, first, first, second, second, third, none, none], axis=0
    ).astype(BF16)


def own_stack(value):
    first, second, third = thirds(value)
    none = jnp.zeros(value.shape, F32)
    return jnp.concatenate(
        [first, second, third, first, second, first, none, none], axis=0
    ).astype(BF16)


def identity():
    return jnp.where(rows((128, 128)) == lanes((128, 128)), 1.0, 0.0).astype(BF16)


def near_kernel(
    list_ref, shape_ref, x_any, p_ref, lev_any,
    out_ref, couple_any,
    couple_ref, x_ref, lev_ref, sems, p8, far_feat, own_feat, tile0, tile1,
):
    copies = [
        pltpu.make_async_copy(x_any, x_ref, sems.at[0]),
        pltpu.make_async_copy(lev_any, lev_ref, sems.at[1]),
    ]
    for copy in copies:
        copy.start()
    first_group = device_index() * GROUPS
    p8[...] = jnp.zeros(p8.shape, F32)
    eye = identity()

    def features(m, carry):
        loaded = [p_ref[:, pl.ds(pl.multiple_of((16 * m + v) * 512, 512), 512)] for v in range(16)]
        for v in range(16):
            p8[v, 0:3, :] = loaded[v]
        made = []
        for v in range(16):
            coords = p8[v]
            origin_z = (first_group + 16 * m + v).astype(F32)
            far, own = point_features(coords, origin_z)
            _, own_up = point_features(coords, origin_z + 1.0)
            _, own_down = point_features(coords, origin_z - 1.0)
            far = far_stack(far)
            parts = [far[:, k * P_SIZE : (k + 1) * P_SIZE] for k in range(4)]
            turned = dot_nt(eye, jnp.concatenate(parts, axis=0)).astype(BF16)
            made.append((turned, own_stack(own), own_stack(own_up), own_stack(own_down)))
        for v in range(16):
            g = 16 * m + v
            turned, own, own_up, own_down = made[v]
            far_feat[2 * g] = turned[:, 0:128]
            far_feat[2 * g + 1] = turned[:, 128:256]
            for k in range(4):
                part = slice(k * P_SIZE, (k + 1) * P_SIZE)
                own_feat[4 * g + k] = own[:, part]
                own_feat[LD + 4 * g + k] = own_up[:, part]
                own_feat[2 * LD + 4 * g + k] = own_down[:, part]
        return carry

    lax.fori_loop(0, GROUPS // 16, features, 0)

    for copy in copies:
        copy.wait()
    out_ref[...] = x_ref[...].astype(F32)
    for ref in (tile0, tile1):
        ref[...] = jnp.zeros(ref.shape, ref.dtype)

    mutual_phases = list_ref[4, 0] + 1
    all_phases = list_ref[5, 0] + 1
    low = lanes((128, 128)) < K

    def leaf_slice(i):
        return pl.ds(pl.multiple_of(i * P_SIZE, P_SIZE), P_SIZE)

    lane_u = lane_nodes()
    row_y, row_z = row_nodes()

    def phase(n, tile_new, tile_old, pairs, sides):
        far, own, sources, updates = [], [], [], []
        siblings = [jnp.minimum(pairs * n + v, PAIRS - 2) for v in range(pairs)]
        levels = [lev_ref[pair] for pair in siblings]
        for u in range(BATCH):
            k = (n + 1) * BATCH + u
            i, j = list_ref[0, k], list_ref[1, k]
            step = (j >> 2) - (i >> 2)
            variant = jnp.where(step < 0, 2, step) * LD
            far.append(far_feat[j >> 1])
            own.append(own_feat[variant + i])
        for u in range(BATCH):
            k = n * BATCH + u
            i, j = list_ref[0, k], list_ref[1, k]
            sources.append((x_ref[:, leaf_slice(j)], x_ref[:, leaf_slice(i)]))
        tiles = []
        for u in range(BATCH // 2):
            pick = jnp.where(low, far[2 * u], far[2 * u + 1])
            dist = dot(pick, block_diagonal(own[2 * u], own[2 * u + 1]))
            tiles.append(decay(dist).astype(BF16))
            weights = block_diagonal(tile_old[u, :, 0:128], tile_old[u, :, 128:256])
            to_i = dot(jnp.concatenate([sources[2 * u][0], sources[2 * u + 1][0]], axis=1), weights)
            to_j = None
            if sides == 2:
                to_j = dot_nt(
                    jnp.concatenate([sources[2 * u][1], sources[2 * u + 1][1]], axis=1), weights
                )
            for h in range(2):
                k = n * BATCH + 2 * u + h
                span = slice(h * 128, (h + 1) * 128)
                updates.append(
                    (
                        to_i[:, span] * list_ref[2, k].astype(F32),
                        to_j[:, span] * list_ref[3, k].astype(F32) if sides == 2 else None,
                    )
                )
        for pair, level in zip(siblings, levels):
            cluster = LD + 2 * pair
            left = [shape_ref[d, cluster] for d in range(4)]
            right = [shape_ref[d, cluster + 1] for d in range(4)]
            couple_ref[pair] = sibling_apply(
                sibling_tile(left, right, lane_u, row_y, row_z), level
            )
        for u in range(BATCH // 2):
            tile_new[u] = tiles[u]
        for u in range(BATCH):
            k = n * BATCH + u
            to_i = leaf_slice(list_ref[0, k])
            to_j = leaf_slice(list_ref[1, k])
            out_ref[:, to_i] += updates[u][0]
            if sides == 2:
                out_ref[:, to_j] += updates[u][1]

    def two_phases(pairs, sides, m, carry):
        phase(2 * m, tile0, tile1, pairs, sides)
        phase(2 * m + 1, tile1, tile0, pairs, sides)
        return carry

    rides = -(-(PAIRS - 1) // (2 * SIBLINGS))
    middle = mutual_phases // 2
    lax.fori_loop(0, rides, functools.partial(two_phases, SIBLINGS, 2), 0)
    leaving = pltpu.make_async_copy(couple_ref, couple_any, sems.at[2])
    leaving.start()
    lax.fori_loop(rides, middle, functools.partial(two_phases, 0, 2), 0)
    lax.fori_loop(middle, (all_phases + 1) // 2, functools.partial(two_phases, 0, 1), 0)
    leaving.wait()


def tree_down(t_ref, root_ref, down_ref, couple, pairs_scr, shapes):
    lane_u = lane_nodes()
    row_y, row_z = row_nodes()

    doubled = doubled_transfer(t_ref)
    t_high, t_low = halves(doubled)
    w_high, w_low = down_weights(doubled)
    device = device_index()
    n = root_ref.shape[0]
    low = lanes((R, 128)) < K
    shift = lanes((1, 128)) == 2
    for k in range(n):
        shapes[k : k + 1, :] = root_ref[k, R // 2 : R // 2 + 1, :] + jnp.where(
            shift, (k * GROUPS) * SCALE, 0.0
        )
    for k in range(n // 2):
        left = root_ref[2 * k, 0 : R // 2, :]
        right = root_ref[2 * k + 1, 0 : R // 2, :]
        left = jnp.concatenate([left, pltpu.roll(left, K, 1)], axis=0)
        right = jnp.concatenate([pltpu.roll(right, K, 1), right], axis=0)
        pairs_scr[k] = jnp.where(low, left, right)
    source, count, pair_source = 0, n // 2, 0
    levels = []
    while count >= 1:
        levels.append((source, pair_source))
        if count > 1:
            pairs = pair_lanes(merge_up(pairs_scr[pl.ds(pair_source, count)], t_high, t_low))
            pairs_scr[pl.ds(pair_source + count, count // 2)] = pairs
            joined = merge_shape_rows(
                shapes[pl.ds(source, count, stride=2), :],
                shapes[pl.ds(source + 1, count, stride=2), :],
            )
            shapes[pl.ds(source + 2 * count, count), :] = joined
        source += 2 * count
        pair_source += count
        count //= 2
    couples = []
    for level, (source, pair_source) in enumerate(levels):
        pair = device >> (level + 1)
        left_row = shapes[pl.ds(source + 2 * pair, 1), :]
        right_row = shapes[pl.ds(source + 2 * pair + 1, 1), :]
        left = [jnp.broadcast_to(left_row[:, d : d + 1], (8, 128)) for d in range(4)]
        right = [jnp.broadcast_to(right_row[:, d : d + 1], (8, 128)) for d in range(4)]
        tile = sibling_tile(left, right, lane_u, row_y, row_z)
        couples.append(sibling_apply(tile, pairs_scr[pair_source + pair]))
    incoming = None
    for level in reversed(range(len(levels))):
        value = couples[level]
        if incoming is not None:
            pushed = push_down(incoming[None], w_high, w_low)
            value = value + (pushed[0] + pushed[1])
        side = (device >> level) & 1
        keep_low = jnp.where(low, 1, 0) == (1 - side)
        incoming = jnp.where(keep_low, value, 0.0)
    pushed = push_down(incoming[None], w_high, w_low)
    value = couple[pl.ds(PAIR_OFFSETS[6], 1)] + (pushed[0:1] + pushed[1:2])
    for level in range(5, 0, -1):
        n = PAIRS >> level
        value = couple[pl.ds(PAIR_OFFSETS[level], n)] + push_down(value, w_high, w_low)
    down_ref[...] = push_down(value, w_high, w_low)


UNIT = 8


def couple_leaves(
    entries, shape_ref, prev_ref, next_ref, table_copies, leaf_couple,
    shape_tab, high_tab, low_tab, halo_rows, halo_shape, sems,
    tiles0, lhs0, tiles1, lhs1,
):
    copies = []
    for k, ref in enumerate((prev_ref, next_ref)):
        parts = ref[68].astype(F32)
        halo_rows[k] = parts[0:8] + parts[8:16] + parts[16:24]
        copies.append(pltpu.make_async_copy(halo_rows.at[k], halo_shape.at[k], sems.at[k]))
    for copy in copies:
        copy.start()
    low32 = lanes((R, 128)) < K
    lane_u = lane_nodes()
    row8 = rows((8, 128))
    low8 = lanes((8, 128)) < K

    def shape_rows(read, k, shift):
        return jnp.where(
            row8 == 0,
            read(0, k),
            jnp.where(row8 == 1, read(1, k), jnp.where(row8 == 2, read(2, k) + shift, read(3, k))),
        )

    def own_nodes(m, carry):
        shape_tab[HALF + m] = shape_rows(lambda d, k: shape_ref[d, k], m, 0.0)
        return carry

    lax.fori_loop(0, LD, own_nodes, 0, unroll=32)
    for copy in copies:
        copy.wait()
    def halo_pairs(m, carry):
        loaded = [
            (tab, LD + side * HALF + 4 * m + v, ref[offset + 4 * m + v])
            for side, ref in enumerate((prev_ref, next_ref))
            for tab, offset in ((high_tab, 0), (low_tab, 32))
            for v in range(4)
        ]
        turned = [pltpu.roll(pair.astype(F32), K, 1).astype(BF16) for _, _, pair in loaded]
        for side in range(2):
            source = HALF if side == 0 else 0
            place = 0 if side == 0 else HALF + LD
            shift = (2.0 * side - 1.0) * GROUPS * SCALE
            for v in range(8):
                shape_tab[place + 8 * m + v] = shape_rows(
                    lambda d, k: halo_shape[side, d, k], source + 8 * m + v, shift
                )
        for (tab, pair, value), other in zip(loaded, turned):
            tab[pair] = value
            tab[PAIRS // 2 + pair] = other
        return carry

    lax.fori_loop(0, PAIRS // 8, halo_pairs, 0)
    high_tab[TABLE - 1] = jnp.zeros((R, 128), BF16)
    low_tab[TABLE - 1] = jnp.zeros((R, 128), BF16)
    for copy in table_copies:
        copy.wait()

    row_y, row_z = row_nodes()

    def couple_tiles(pair, u, tiles, lhs):
        leaves = (2 * pair, 2 * pair + 1)
        for q in range(4):
            span = slice(q * 128, (q + 1) * 128)
            for h in range(2):
                e0, e1 = entries[2 * q, leaves[h]], entries[2 * q + 1, leaves[h]]
                lhs[u, h * R : (h + 1) * R, span] = jnp.where(low32, high_tab[e0], high_tab[e1])
                lhs[u, (2 + h) * R : (3 + h) * R, span] = jnp.where(
                    low32, low_tab[e0], low_tab[e1]
                )
        own = jnp.where(low8, shape_tab[HALF + leaves[0]], shape_tab[HALF + leaves[1]])
        radius = jnp.broadcast_to(own[3:4], (8, 128))
        own = [jnp.broadcast_to(own[d : d + 1], (8, 128)) + radius * lane_u[d] for d in range(3)]
        fars = []
        for s in range(8):
            e0, e1 = entries[8 + s, leaves[0]], entries[8 + s, leaves[1]]
            fars.append(jnp.where(low8, shape_tab[e0], shape_tab[e1]))
        for s, far in enumerate(fars):
            reach = jnp.broadcast_to(far[3:4], (8, 128))
            gap = [own[d] - jnp.broadcast_to(far[d : d + 1], (8, 128)) for d in range(3)]
            tile = tile_from_axes(
                [jnp.square(gap[0] - reach * NODE[b]) for b in range(4)],
                [jnp.square(gap[1] - reach * row_y[h]) for h in range(2)],
                jnp.square(gap[2] - reach * row_z),
            )
            high, low = halves(tile)
            tiles[u, s * K : (s + 1) * K, 0:128] = high
            tiles[u, s * K : (s + 1) * K, 128:256] = low

    def couple_apply(u, tiles, lhs):
        both = dot(lhs[u], tiles[u])
        both = both[0 : 2 * R, 0:128] + (both[2 * R : 4 * R, 0:128] + both[0 : 2 * R, 128:256])
        return jnp.where(low32, both[0:R], both[R : 2 * R])

    def couple_phase(n, new, old):
        for u in range(UNIT):
            couple_tiles(n * UNIT + u, u, *new)
            leaf_couple[n * UNIT + u] = couple_apply(u, *old)

    buffers = ((tiles0, lhs0), (tiles1, lhs1))
    for ref in buffers[1]:
        ref[...] = jnp.zeros(ref.shape, ref.dtype)

    def couple_two(m, carry):
        couple_phase(2 * m, buffers[0], buffers[1])
        couple_phase(2 * m + 1, buffers[1], buffers[0])
        return carry

    lax.fori_loop(0, PAIRS // UNIT // 2, couple_two, 0)
    for u in range(UNIT):
        leaf_couple[PAIRS + u] = couple_apply(u, *buffers[1])


def finish_leaves(b_ref, down_ref, leaf_couple, out_ref, border, out_any, sems):
    def finish(m, carry):
        values = []
        for v in range(16):
            c = 16 * m + v
            value = (down_ref[c] + leaf_couple[c + UNIT]).astype(BF16)
            span = pl.ds(pl.multiple_of(c * 256, 256), 256)
            values.append(
                (
                    span,
                    out_ref[:, span]
                    + dot(value, block_diagonal(b_ref[2 * c], b_ref[2 * c + 1])),
                )
            )
        for span, value in values:
            out_ref[:, span] = value
        return carry

    parts = PAIRS // 16
    leaving = []
    for c in range(parts):
        lax.fori_loop(c, c + 1, finish, 0)
        for side, (part, group) in enumerate(((0, 0), (parts - 1, GROUPS - 1))):
            if c == part:
                for i in range(4):
                    leaf = 4 * group + i
                    out_ref[:, leaf * P_SIZE : (leaf + 1) * P_SIZE] += border[4 * side + i]
        span = slice(c * 16 * 256, (c + 1) * 16 * 256)
        leaving.append(
            pltpu.make_async_copy(out_ref.at[:, span], out_any.at[:, span], sems.at[c])
        )
        leaving[c].start()
    for copy in leaving:
        copy.wait()


def border_blocks(counts, p_ref, prev_ref, next_ref, border, p8, coords):
    device = device_index()

    p8[...] = jnp.zeros(p8.shape, F32)
    eye = identity()
    sides = ((prev_ref, 0), (next_ref, GROUPS - 1))
    for side, (halo_ref, group) in enumerate(sides):
        p8[side, 0:3, :] = p_ref[:, group * 512 : group * 512 + 512]
        coords[side] = halo_ref[69].astype(F32) + halo_ref[70].astype(F32) + halo_ref[71].astype(F32)

    sums = [[0.0] * 4, [0.0] * 4]
    for k in range(4):
        loaded = [
            (halo_ref[64 + k], coords[side, 8 * k : 8 * k + 8, :], p8[side])
            for side, (halo_ref, _) in enumerate(sides)
        ]
        for side, (_, group) in enumerate(sides):
            x_far, far, own = loaded[side]
            origin_z = (device * GROUPS + group).astype(F32)
            _, own = point_features(own, origin_z)
            far, _ = point_features(far, origin_z)
            far = dot_nt(eye, far_stack(far)).astype(BF16)
            tiles = decay(dot(far, own_stack(own))).astype(BF16)
            products = dot(x_far, tiles)
            for i in range(4):
                delta = (4 + i - k) if side == 0 else (4 + k - i)
                weight = counts[8 * (1 - side) + delta, 4 * group + i]
                sums[side][i] = sums[side][i] + products[:, i * P_SIZE : (i + 1) * P_SIZE] * weight
    for side in range(2):
        for i in range(4):
            border[4 * side + i] = sums[side][i]


def tree_kernel(
    t_any, root_any, couple_any, down_ref, t_ref, root_ref, couple, pairs_scr, shapes, sems
):
    moves = ((t_any, t_ref), (root_any, root_ref), (couple_any, couple))
    copies = [pltpu.make_async_copy(a, b, sems.at[k]) for k, (a, b) in enumerate(moves)]
    for copy in copies:
        copy.start()
    for copy in copies:
        copy.wait()
    tree_down(t_ref, root_ref, down_ref, couple, pairs_scr, shapes)


def final_kernel(
    entries, shape_ref, counts,
    prev_any, next_any, p_any, high_any, low_any, b_any, near_any, down_any,
    out_any,
    out_ref, prev_ref, next_ref, p_ref, b_ref, down, leaf_couple,
    shape_tab, high_tab, low_tab, halo_rows, halo_shape,
    tiles0, lhs0, tiles1, lhs1, p8, coords, border, sems, halo_sems, out_sems,
):
    moves = (
        (prev_any, prev_ref),
        (next_any, next_ref),
        (p_any, p_ref),
        (high_any, high_tab.at[0:LD]),
        (low_any, low_tab.at[0:LD]),
        (b_any, b_ref),
        (near_any, out_ref),
        (down_any, down),
    )
    copies = [pltpu.make_async_copy(a, b, sems.at[k]) for k, (a, b) in enumerate(moves)]
    for copy in copies:
        copy.start()
    for copy in copies[0:3]:
        copy.wait()
    border_blocks(counts, p_ref, prev_ref, next_ref, border, p8, coords)
    couple_leaves(
        entries, shape_ref, prev_ref, next_ref, copies[3:5], leaf_couple,
        shape_tab, high_tab, low_tab, halo_rows, halo_shape, halo_sems,
        tiles0, lhs0, tiles1, lhs1,
    )
    for copy in copies[5:]:
        copy.wait()
    finish_leaves(b_ref, down, leaf_couple, out_ref, border, out_any, out_sems)


def shaped(*shape, dtype=F32):
    return jax.ShapeDtypeStruct(shape, dtype)


def vmem():
    return pl.BlockSpec(memory_space=pltpu.VMEM)


def smem():
    return pl.BlockSpec(memory_space=pltpu.SMEM)


def anywhere():
    return pl.BlockSpec(memory_space=pl.ANY)


PARAMS = pltpu.CompilerParams(vmem_limit_bytes=VMEM_LIMIT)


def per_device(charges, points, basis, transfer, near_list, coupling_list):
    near_rows = near_list.T
    coupling_rows = coupling_list.T
    devices = lax.axis_size("sub") * lax.axis_size("leaf")
    send_next, send_prev, high, low, lev, root, shapes, tasks, counts, entries = pl.pallas_call(
        leaf_kernel,
        name="leaf_up",
        out_shape=(
            shaped(SEND, R, 128, dtype=BF16),
            shaped(SEND, R, 128, dtype=BF16),
            shaped(LD, R, 128, dtype=BF16),
            shaped(LD, R, 128, dtype=BF16),
            shaped(PAIRS - 1, R, 128),
            shaped(devices, R // 2 + 8, 128),
            shaped(8, 256),
            shaped(8, LIST, dtype=jnp.int32),
            shaped(16, 128),
            shaped(16, 128, dtype=jnp.int32),
        ),
        in_specs=[anywhere(), vmem(), anywhere(), vmem(), vmem(), vmem()],
        out_specs=[anywhere()] * 5 + [vmem()] * 5,
        scratch_shapes=[
            pltpu.VMEM((SEND, R, 128), BF16),
            pltpu.VMEM((SEND, R, 128), BF16),
            pltpu.VMEM((R, LD * P_SIZE), BF16),
            pltpu.VMEM((LD, K, P_SIZE), BF16),
            pltpu.VMEM((LD, R, 128), BF16),
            pltpu.VMEM((LD, R, 128), BF16),
            pltpu.VMEM((PAIRS - 1, R, 128), F32),
            pltpu.VMEM((PAIRS, R, 128), F32),
            pltpu.VMEM((3, LD, 128), F32),
            pltpu.VMEM((256, 128), F32),
            pltpu.VMEM((8, 512), F32),
            pltpu.SemaphoreType.DMA((2 * CHUNKS + 5,)),
        ],
        compiler_params=PARAMS,
    )(charges, points, basis, transfer, near_rows, coupling_rows)

    roots = lax.all_to_all(root, AXES, 0, 0, tiled=True)
    forward = [(i, i + 1) for i in range(devices - 1)]
    backward = [(i + 1, i) for i in range(devices - 1)]
    from_prev = lax.ppermute(send_next, AXES, forward)
    from_next = lax.ppermute(send_prev, AXES, backward)

    near, couple = pl.pallas_call(
        near_kernel,
        name="near_field",
        out_shape=(shaped(R, LD * P_SIZE), shaped(PAIRS - 1, R, 128)),
        in_specs=[smem(), smem(), anywhere(), vmem(), anywhere()],
        out_specs=[vmem(), anywhere()],
        scratch_shapes=[
            pltpu.VMEM((PAIRS - 1, R, 128), F32),
            pltpu.VMEM((R, LD * P_SIZE), BF16),
            pltpu.VMEM((PAIRS - 1, R, 128), F32),
            pltpu.SemaphoreType.DMA((3,)),
            pltpu.VMEM((16, 8, 512), F32),
            pltpu.VMEM((PAIRS, P_SIZE, 2 * FEATS), BF16),
            pltpu.VMEM((3 * LD, FEATS, P_SIZE), BF16),
            pltpu.VMEM((BATCH // 2, 128, 256), BF16),
            pltpu.VMEM((BATCH // 2, 128, 256), BF16),
        ],
        compiler_params=PARAMS,
        cost_estimate=pl.CostEstimate(
            flops=2 * 460 * 128 * 128 * 128, bytes_accessed=4 << 20, transcendentals=460 * 32768
        ),
    )(tasks, shapes, charges, points, lev)

    near, roots = lax.optimization_barrier((near, roots))
    down = pl.pallas_call(
        tree_kernel,
        name="tree_down",
        out_shape=shaped(PAIRS, R, 128),
        in_specs=[anywhere()] * 3,
        out_specs=vmem(),
        scratch_shapes=[
            pltpu.VMEM((2, K, K), F32),
            pltpu.VMEM((devices, R // 2 + 8, 128), F32),
            pltpu.VMEM((PAIRS - 1, R, 128), F32),
            pltpu.VMEM((devices, R, 128), F32),
            pltpu.VMEM((2 * devices, 128), F32),
            pltpu.SemaphoreType.DMA((3,)),
        ],
        compiler_params=PARAMS,
    )(transfer, roots, couple)
    from_prev, from_next, down = lax.optimization_barrier((from_prev, from_next, down))

    stages = [
        pltpu.VMEM((UNIT, 512, 256), BF16),
        pltpu.VMEM((UNIT, 4 * R, 512), BF16),
    ]
    return pl.pallas_call(
        final_kernel,
        name="couple_finish",
        out_shape=shaped(R, LD * P_SIZE),
        in_specs=[smem()] * 3 + [anywhere()] * 8,
        out_specs=anywhere(),
        scratch_shapes=[
            pltpu.VMEM((R, LD * P_SIZE), F32),
            pltpu.VMEM((SEND, R, 128), BF16),
            pltpu.VMEM((SEND, R, 128), BF16),
            pltpu.VMEM((3, LD * P_SIZE), F32),
            pltpu.VMEM((LD, K, P_SIZE), BF16),
            pltpu.VMEM((PAIRS, R, 128), F32),
            pltpu.VMEM((PAIRS + UNIT, R, 128), F32),
            pltpu.VMEM((2 * LD, 8, 128), F32),
            pltpu.VMEM((TABLE, R, 128), BF16),
            pltpu.VMEM((TABLE, R, 128), BF16),
            pltpu.VMEM((2, 8, 128), F32),
            pltpu.SMEM((2, 8, 128), F32),
        ]
        + stages
        + stages
        + [
            pltpu.VMEM((2, 8, 512), F32),
            pltpu.VMEM((2, R, 128), F32),
            pltpu.VMEM((8, R, 128), F32),
            pltpu.SemaphoreType.DMA((8,)),
            pltpu.SemaphoreType.DMA((2,)),
            pltpu.SemaphoreType.DMA((PAIRS // 16,)),
        ],
        compiler_params=PARAMS,
    )(
        entries, shapes, counts,
        from_prev, from_next, points, high, low, basis, near, down,
    )


def solution(mesh):
    in_specs = (
        P(None, AXES),
        P(None, AXES),
        P(AXES, None, None),
        P(),
        P(AXES, None),
        P(AXES, None),
    )
    return jax.shard_map(
        per_device, mesh=mesh, in_specs=in_specs, out_specs=P(None, AXES), check_vma=False
    )
```
